32 devices in a mesh: site: 8 (over z, x), phonon: 4 (over y, core).
Axes of the slice: x: 2, y: 2, z: 4, core: 2. Of those that a mesh axis runs over, the one named last changes fastest.
Arguments:
- state: float32 [8192, 512], P('site', 'phonon'), may hold values from -4.5 to 6.5
- operators: bfloat16 [3, 1024, 1024], replicated, may hold values from -0.1875 to 0.1875
- op_mask: int32 [3, 8, 8], replicated, may hold values 0 or 1
- site_bits: int32 [3], replicated, may hold values from 0 to 2, each once
- field: float32 [3], replicated, may hold values from 0.25 to 1
- site_coupling: float32 [13], replicated, may hold values from 0.1 to 0.6
- mode_coupling: float32 [64], replicated, may hold values from 0.2 to 1
Outputs:
- chebyshev_last: float32 [8192, 512], P('site', 'phonon')
- chebyshev_prev: float32 [8192, 512], P('site', 'phonon')
- moments: float32 [3], replicated
The draws below stay inside these ranges and needn't reach their ends.
Inputs may be any that keep to these rules, and one draw needn't show every extreme that they name: `site_bits`: each of 0 to 2 exactly once.
All inputs are finite; a program needn't handle non-finite values.
Results may differ from the reference program's by a relative error of at most 0.0011.
The reference program's roundings to bfloat16 on the way (of `masked`) count: a program that leaves them out, or rounds other values in their place, can miss the bound.
Values sent between devices are 32-bit elements; how exact they have to be, the bound alone decides.
No kernel may reach another device: no remote copies, remote signals or barrier semaphores. Data moves between devices by JAX's collectives and lax.ppermute only.
A program may use at most 64 MiB of HBM per device.

```python
import math
import jax
import jax.numpy as jnp

LBITS = 10
SBITS = 3
SITES = 13
CS = 1024
BLOCK = 128
NB = 8
MODES = 64
STEPS = 3
NLEV = 8
NS = 8192
NP = 512
N_SITE = 8


def draw_state(key, part):
    row_place = jnp.arange(NS, dtype=jnp.float32)[:, None]
    column_place = jnp.arange(NP, dtype=jnp.float32)[None, :]
    smooth_part = 1.0 + 0.5 * jnp.cos(2.0 * math.pi * row_place / NS) * jnp.cos(math.pi * column_place / NP)
    noisy_part = jnp.clip(jax.random.normal(key, (NS, NP), jnp.float32), -5.0, 5.0)
    return (smooth_part + noisy_part).astype(jnp.float32)


def set_ends(values, rng, least, largest):
    dims = values.shape
    spot = [jax.random.randint(jax.random.fold_in(rng, axis), (), 0, dims[axis]) for axis in range(len(dims))]
    values = values.at[tuple(spot)].set(least)
    longest = dims.index(max(dims))
    spot[longest] = (spot[longest] + 1) % dims[longest]
    return values.at[tuple(spot)].set(largest)


def normal_values(key, extent, deviation, reach, held_as=jnp.bfloat16):
    values = jax.random.normal(key, extent, jnp.float32) * deviation
    return jnp.minimum(jnp.maximum(values, -reach), reach).astype(held_as)


def setup_inputs(seed: int = 0) -> dict:
    key_of = jax.random.split(jax.random.key(seed), 8)
    state = draw_state(jax.random.fold_in(key_of[7], 71), 0)
    operators = normal_values(key_of[1], (SBITS, CS, CS), CS ** -0.5, 0.1875)
    op_mask = set_ends((jax.random.randint(key_of[2], (SBITS, NB, NB), 0, 2) < 1).astype(jnp.int32), jax.random.fold_in(key_of[2], 1), 0, 1)
    site_bits = jax.random.permutation(key_of[3], SBITS).astype(jnp.int32)
    field = jnp.clip(jnp.exp(jax.random.uniform(key_of[4], (SBITS,), jnp.float32, math.log(0.25), math.log(1.0))), 0.25, 1.0)
    site_coupling = jnp.clip(jnp.exp(jax.random.uniform(key_of[5], (SITES,), jnp.float32, math.log(0.1), math.log(0.6))), 0.1, 0.6)
    mode_coupling = jnp.clip(jnp.exp(jax.random.uniform(key_of[6], (MODES,), jnp.float32, math.log(0.2), math.log(1.0))), 0.2, 1.0)
    return {"state": state, "operators": operators, "op_mask": op_mask, "site_bits": site_bits, "field": field, "site_coupling": site_coupling, "mode_coupling": mode_coupling}


epsilon = 1e-06

def flip_sites(values, position):
    shaped = values.reshape(N_SITE >> position + 1, 2, 1 << position, CS, NP)
    return shaped[:, ::-1].reshape(N_SITE, CS, NP)

def reference(state, operators, op_mask, site_bits, field, site_coupling, mode_coupling):
    expanded = jnp.repeat(jnp.repeat(op_mask, BLOCK, axis=1), BLOCK, axis=2)
    masked = jnp.where(expanded > 0, operators, jnp.zeros((), jnp.bfloat16))
    row_index = jnp.arange(NS, dtype=jnp.int32)
    device = row_index // CS
    inside = row_index % CS
    weight_rows = jnp.zeros((NS,), jnp.float32)
    for position in range(SBITS):
        weight_rows = weight_rows + site_coupling[site_bits[position]] * (device >> position & 1).astype(jnp.float32)
    for local_bit in range(LBITS):
        weight_rows = weight_rows + site_coupling[SBITS + local_bit] * (inside >> local_bit & 1).astype(jnp.float32)
    column = jnp.arange(NP, dtype=jnp.int32)
    levels = (column // MODES).astype(jnp.float32)
    lower_weight = jnp.sqrt(levels)
    upper_weight = jnp.sqrt(levels + 1.0)
    mode_weight = jnp.tile(mode_coupling, NP // MODES) / jnp.sqrt(jnp.float32(NLEV))
    entries = jnp.float32(NS * NP)

    def operate(vector):
        lower_part = jnp.pad(vector, ((0, 0), (MODES, 0)))[:, :NP]
        upper_part = jnp.pad(vector, ((0, 0), (0, MODES)))[:, MODES:]
        summed = weight_rows[:, None] * (mode_weight * (lower_weight * lower_part + upper_weight * upper_part))
        cube = vector.reshape(N_SITE, CS, NP)
        rounded = cube.astype(jnp.bfloat16).transpose(1, 0, 2).reshape(CS, N_SITE * NP)
        for position in range(SBITS):
            chosen = site_bits[position]
            product = jnp.dot(masked[chosen], rounded, preferred_element_type=jnp.float32)
            product = product.reshape(CS, N_SITE, NP).transpose(1, 0, 2)
            contribution = field[chosen] * cube + product
            summed = summed + flip_sites(contribution, position).reshape(NS, NP)
        return summed

    def root_mean(values):
        return jnp.sqrt(jnp.sum(values * values) / entries + epsilon)
    initial = state / root_mean(state)
    previous = initial
    current = initial
    scale_prev = jnp.float32(1.0)
    moments = []
    for iteration in range(STEPS):
        applied = operate(current)
        if iteration == 0:
            vector_new = applied
        else:
            vector_new = 2.0 * applied - previous / scale_prev
        scale_now = root_mean(vector_new)
        updated = vector_new / scale_now
        moments.append(jnp.sum(initial * updated) / entries)
        previous = current
        current = updated
        scale_prev = scale_now
    return (current, previous, jnp.stack(moments))
```

```python
import jax
import jax.numpy as jnp
from jax import lax
from jax.sharding import PartitionSpec as P

LBITS = 10
MODES = 64
STEPS = 3
LANES = 128
AXES = ("site", "phonon")

epsilon = 1e-06


def exchange(block):
    return lax.all_to_all(block, AXES, 0, 0, tiled=True)


def shards(state, operators, op_mask, site_bits, field, site_coupling, mode_coupling):
    site_count = lax.axis_size("site")
    phonon_count = lax.axis_size("phonon")
    groups = site_count * phonon_count
    bit_count = site_count.bit_length() - 1
    rows, columns = state.shape
    levels_here = columns // MODES
    level_count = levels_here * phonon_count
    share = MODES // groups
    entries = jnp.float32(rows * columns * groups)
    block_edge = rows // op_mask.shape[1]
    me = lax.axis_index("site") * phonon_count + lax.axis_index("phonon")

    expanded = jnp.repeat(jnp.repeat(op_mask, block_edge, axis=1), block_edge, axis=2)
    masked = jnp.where(expanded > 0, operators, jnp.zeros((), jnp.bfloat16))

    outgoing = state.reshape(rows, levels_here, groups, share).transpose(2, 1, 3, 0)
    outgoing = outgoing.reshape(groups, levels_here * share, rows)
    tail = jnp.full((groups, levels_here * share, LANES), jnp.sum(state * state))
    arrived = exchange(jnp.concatenate([outgoing, tail], axis=2))
    start_squares = jnp.sum(arrived[:, 0, rows])
    scale = jnp.sqrt(start_squares / entries + epsilon)
    shape = (site_count, level_count, share, rows)
    initial = (arrived[:, :, :rows] / scale).reshape(shape)

    bits = lax.iota(jnp.int32, rows)
    device = lax.iota(jnp.int32, site_count)
    weight = jnp.zeros((site_count, rows), jnp.float32)
    for position in range(bit_count):
        weight = weight + site_coupling[site_bits[position]] * (device >> position & 1).astype(jnp.float32)[:, None]
    for local_bit in range(LBITS):
        weight = weight + site_coupling[bit_count + local_bit] * (bits >> local_bit & 1).astype(jnp.float32)
    modes = lax.dynamic_slice(mode_coupling, (me * share,), (share,)) / jnp.sqrt(jnp.float32(level_count))
    levels = lax.iota(jnp.float32, level_count)
    lower_weight = (jnp.sqrt(levels)[:, None] * modes)[None, :, :, None]
    upper_weight = (jnp.sqrt(levels + 1.0)[:, None] * modes)[None, :, :, None]
    weight = weight[:, None, None, :]

    def operate(vector, exact):
        lower = jnp.pad(vector, ((0, 0), (1, 0), (0, 0), (0, 0)))[:, :level_count]
        upper = jnp.pad(vector, ((0, 0), (0, 1), (0, 0), (0, 0)))[:, 1:]
        total = weight * (lower_weight * lower + upper_weight * upper)
        high = vector.astype(jnp.bfloat16)
        parts = [high]
        if exact:
            parts.append((vector - high.astype(jnp.float32)).astype(jnp.bfloat16))
        for position in range(bit_count):
            chosen = site_bits[position]
            part_total = field[chosen] * vector
            for part in parts:
                part_total = part_total + lax.dot_general(
                    part, masked[chosen], (((3,), (1,)), ((), ())), preferred_element_type=jnp.float32
                )
            total = total + jnp.stack([part_total[index ^ (1 << position)] for index in range(site_count)])
        return total

    first = operate(initial, False)
    second = 2.0 * operate(first, True) - initial
    third = 2.0 * operate(second, True) - first
    sums = []
    for vector in (first, second, third):
        sums += [jnp.sum(vector * vector), jnp.sum(initial * vector)]
    tail = jnp.pad(jnp.stack(sums), (0, LANES - 2 * STEPS))
    packed = jnp.concatenate(
        [
            second.reshape(groups, levels_here * share, rows),
            third.reshape(groups, levels_here * share, rows),
            jnp.broadcast_to(tail, (groups, levels_here * share, LANES)),
        ],
        axis=2,
    )
    back = exchange(packed)
    sums = jnp.sum(back[:, 0, 2 * rows :], axis=0)
    running = jnp.float32(1.0)
    scales = []
    moments = []
    for step in range(STEPS):
        running = running * jnp.sqrt(sums[2 * step] / entries / (running * running) + epsilon)
        scales.append(running)
        moments.append(sums[2 * step + 1] / (entries * running))

    def placed(block, factor):
        block = (block / factor).reshape(groups, levels_here, share, rows)
        return block.transpose(3, 1, 0, 2).reshape(rows, columns)

    last = placed(back[:, :, rows : 2 * rows], scales[2])
    before = placed(back[:, :, :rows], scales[1])
    return last, before, jnp.stack(moments)


def extended_2(block, sides, width):
    for axis, dim in sides:
        count = lax.axis_size(axis)
        forward = [(i, i + 1) for i in range(count - 1)]
        backward = [(target, source) for source, target in forward]
        low = lax.ppermute(
            lax.slice_in_dim(block, block.shape[dim] - width, None, axis=dim), axis, forward
        )
        high = lax.ppermute(lax.slice_in_dim(block, 0, width, axis=dim), axis, backward)
        block = jnp.concatenate([low, block, high], axis=dim)
    return block


def partner(value, axis, bit):
    mask = 2**bit
    pairs = [(source, source ^ mask) for source in range(lax.axis_size(axis))]
    return lax.ppermute(value, axis, pairs)


def halo_shards(state, operators, op_mask, site_bits, field, site_coupling, mode_coupling):
    site_count = lax.axis_size("site")
    phonon_count = lax.axis_size("phonon")
    bit_count = site_count.bit_length() - 1
    rows_here = state.shape[0]
    columns_here = state.shape[1]
    levels_here = columns_here // MODES
    block_edge = rows_here // op_mask.shape[1]
    expanded = jnp.repeat(jnp.repeat(op_mask, block_edge, axis=1), block_edge, axis=2)
    masked = jnp.where(expanded > 0, operators, jnp.zeros((), jnp.bfloat16))
    entries = jnp.float32(rows_here * columns_here * site_count * phonon_count)
    level_total = jnp.sqrt(jnp.float32(levels_here * phonon_count))
    device = lax.axis_index("site")
    inside = lax.iota(jnp.int32, rows_here)
    weight_rows = jnp.zeros((rows_here,), jnp.float32)
    for position in range(bit_count):
        weight_rows = weight_rows + site_coupling[site_bits[position]] * (
            device >> position & 1
        ).astype(jnp.float32)
    for local_bit in range(LBITS):
        weight_rows = weight_rows + site_coupling[bit_count + local_bit] * (
            inside >> local_bit & 1
        ).astype(jnp.float32)
    levels = (
        lax.axis_index("phonon") * levels_here + lax.iota(jnp.int32, columns_here) // MODES
    ).astype(jnp.float32)
    lower_weight = jnp.sqrt(levels)
    upper_weight = jnp.sqrt(levels + 1.0)
    mode_weight = jnp.tile(mode_coupling, columns_here // MODES) / level_total
    start_squares = lax.psum(jnp.sum(state * state), ("site", "phonon"))
    initial = state / jnp.sqrt(start_squares / entries + epsilon)
    previous = initial
    current = initial
    scale_prev = jnp.float32(1.0)
    moments = []
    for iteration in range(STEPS):
        extended = extended_2(current, (("phonon", 1),), MODES)
        lower_part = extended[:, :columns_here]
        upper_part = extended[:, 2 * MODES :]
        summed = weight_rows[:, None] * (
            mode_weight * (lower_weight * lower_part + upper_weight * upper_part)
        )
        for operate_position in range(bit_count):
            chosen = site_bits[operate_position]
            flipped = partner(current, "site", operate_position)
            product = jnp.dot(
                masked[chosen], flipped.astype(jnp.bfloat16), preferred_element_type=jnp.float32
            )
            summed = summed + (field[chosen] * flipped + product)
        if iteration == 0:
            vector_new = summed
        else:
            vector_new = 2.0 * summed - previous / scale_prev
        squares, intersection = lax.psum(
            (jnp.sum(vector_new * vector_new), jnp.sum(initial * vector_new)), ("site", "phonon")
        )
        scale_now = jnp.sqrt(squares / entries + epsilon)
        updated = vector_new / scale_now
        moment = intersection / (entries * scale_now)
        moments.append(moment)
        previous = current
        current = updated
        scale_prev = scale_now
    return (current, previous, jnp.stack(moments))


def solution(mesh):
    in_specs = (P("site", "phonon"), P(), P(), P(), P(), P(), P())
    out_specs = (P("site", "phonon"), P("site", "phonon"), P())
    groups = mesh.shape["site"] * mesh.shape["phonon"]
    body = shards if MODES % groups == 0 else halo_shards
    return jax.shard_map(body, mesh=mesh, in_specs=in_specs, out_specs=out_specs, check_vma=False)
```

```python
import functools

import jax
import jax.numpy as jnp
from jax import lax
from jax.experimental import pallas as pl
from jax.experimental.pallas import tpu as pltpu
from jax.sharding import PartitionSpec as P

LBITS = 10
MODES = 64
STEPS = 3
LANES = 128
SUBLANES = 8
EXTRA = 2
AXES = ("site", "phonon")

epsilon = 1e-06


VMEM = pl.BlockSpec(memory_space=pltpu.VMEM)
SMEM = pl.BlockSpec(memory_space=pltpu.SMEM)


class Plan:
    def __init__(self, mesh, rows, columns, blocks):
        self.sites = mesh.shape["site"]
        self.phonons = mesh.shape["phonon"]
        self.groups = self.sites * self.phonons
        self.bits = self.sites.bit_length() - 1
        self.rows = rows
        self.columns = columns
        self.blocks = blocks
        self.edge = rows // blocks
        self.levels_here = columns // MODES
        self.level_count = self.levels_here * self.phonons
        self.share = MODES // self.groups
        self.pieces = self.levels_here * self.share
        self.lane_blocks = rows // LANES
        self.body = self.pieces * self.lane_blocks
        self.message = self.body + EXTRA
        self.places = self.pieces * self.groups
        self.entries = float(rows * columns * self.groups)

    def fits(self):
        return (
            MODES % self.groups == 0
            and self.columns == LANES
            and self.rows % LANES == 0
            and self.edge % LANES == 0
            and self.groups % SUBLANES == 0
        )


def params(mib):
    return pltpu.CompilerParams(vmem_limit_bytes=mib * 2**20)


def lane_sums(values):
    return jnp.sum(values, axis=0, keepdims=True)


def put_extra(plan, out_ref, sums):
    for index, value in enumerate(sums):
        out_ref[pl.ds(plan.body + index, plan.groups, stride=plan.message), :] = jnp.broadcast_to(
            value, (plan.groups, LANES)
        )


def total_of(plan, ref, start, stride):
    lanes = lane_sums(ref[pl.ds(start, plan.groups, stride=stride), :])
    return jnp.sum(lanes, axis=1, keepdims=True)


def scale_of(plan, squares):
    return jnp.sqrt(squares / plan.entries + epsilon)


def depart_kernel(plan, state_ref, out_ref):
    sums = jnp.zeros((1, LANES), jnp.float32)
    for block in range(plan.lane_blocks):
        tile = state_ref[pl.ds(block * LANES, LANES), :]
        sums = sums + lane_sums(tile * tile)
        turned = tile.T
        for piece in range(plan.pieces):
            out_ref[pl.ds(piece * plan.lane_blocks + block, plan.groups, stride=plan.message), :] = turned[
                piece * plan.groups : (piece + 1) * plan.groups
            ]
    put_extra(plan, out_ref, (sums, jnp.zeros_like(sums)))


def prepare_kernel(
    plan, bits_ref, mask_ref, field_ref, coupling_ref, mode_ref, operators_ref, masked_ref, place_ref, inside_ref
):
    me = lax.axis_index("site") * plan.phonons + lax.axis_index("phonon")
    for position in range(plan.bits):
        chosen = bits_ref[position]
        for across in range(plan.blocks):
            rows = pl.ds(across * plan.edge, plan.edge)
            for along in range(plan.blocks):
                columns = pl.ds(along * plan.edge, plan.edge)
                keep = (mask_ref[chosen, across, along] > 0).astype(jnp.float32).astype(jnp.bfloat16)
                masked_ref[position, rows, columns] = operators_ref[chosen, rows, columns] * keep
    place = lax.broadcasted_iota(jnp.int32, (plan.places, LANES), 0)
    phonon = place % plan.phonons
    site = place // plan.phonons % plan.sites
    mode = place // plan.groups % plan.share
    level = phonon * plan.levels_here + place // (plan.groups * plan.share)
    occupied = jnp.zeros((plan.places, LANES), jnp.float32)
    for position in range(plan.bits):
        held = (site >> position & 1).astype(jnp.float32)
        occupied = occupied + coupling_ref[bits_ref[position]] * held
    strength = jnp.zeros((plan.places, LANES), jnp.float32)
    for index in range(plan.share):
        strength = jnp.where(mode == index, mode_ref[index * plan.groups + me], strength)
    strength = strength / jnp.sqrt(jnp.full((1, LANES), plan.level_count, jnp.float32))
    height = level.astype(jnp.float32)
    place_ref[0] = occupied
    place_ref[1] = strength * jnp.sqrt(height)
    place_ref[2] = jnp.where(level == plan.level_count - 1, 0.0, strength * jnp.sqrt(height + 1.0))
    for position in range(plan.bits):
        place_ref[3 + position] = jnp.full((plan.places, LANES), field_ref[bits_ref[position]])
    inside = lax.broadcasted_iota(jnp.int32, (SUBLANES, plan.rows), 1)
    weight = jnp.zeros((SUBLANES, plan.rows), jnp.float32)
    for local_bit in range(LBITS):
        weight = weight + coupling_ref[plan.bits + local_bit] * (inside >> local_bit & 1).astype(jnp.float32)
    inside_ref[...] = weight


def flipped(values, stride):
    places, width = values.shape
    if stride % SUBLANES == 0:
        shaped = values.reshape(places // (2 * stride), 2, stride, width)
        return jnp.concatenate([shaped[:, 1:], shaped[:, :1]], axis=1).reshape(places, width)
    tiles = values.reshape(places // SUBLANES, SUBLANES, width)
    if 2 * stride == SUBLANES:
        return pltpu.roll(tiles, stride, 1).reshape(places, width)
    spot = lax.broadcasted_iota(jnp.int32, tiles.shape, 1)
    down = pltpu.roll(tiles, stride, 1)
    up = pltpu.roll(tiles, SUBLANES - stride, 1)
    return jnp.where(spot & stride > 0, down, up).reshape(places, width)


def shifted(values, by):
    places, width = values.shape
    tiles = values.reshape(places // SUBLANES, SUBLANES, width)
    return pltpu.roll(tiles, by % SUBLANES, 1).reshape(places, width)


def operate(plan, vector_ref, masked_ref, place_ref, inside_ref, rounded_ref, total_ref):
    span = plan.places // plan.levels_here
    for block in range(plan.lane_blocks):
        lanes = pl.ds(block * LANES, LANES)
        vector = vector_ref[:, lanes]
        levels = [vector[index * span : (index + 1) * span] for index in range(plan.levels_here)]
        lower = jnp.concatenate([shifted(levels[-1], 1)] + levels[:-1], axis=0)
        upper = jnp.concatenate(levels[1:] + [shifted(levels[0], -1)], axis=0)
        weight = place_ref[0] + inside_ref[:1, lanes]
        total = weight * (place_ref[1] * lower + place_ref[2] * upper)
        for position in range(plan.bits):
            turned = flipped(vector, plan.phonons << position)
            total = total + place_ref[3 + position] * turned
            rounded_ref[:, pl.ds(position * plan.rows + block * LANES, LANES)] = turned.astype(jnp.bfloat16)
        total_ref[:, lanes] = total
    width = 2 * LANES
    for column in range(plan.rows // width):
        lanes = pl.ds(column * width, width)
        total = total_ref[:, lanes]
        for position in range(plan.bits):
            total = total + lax.dot_general(
                rounded_ref[:, pl.ds(position * plan.rows, plan.rows)],
                masked_ref[position, lanes, :],
                (((1,), (1,)), ((), ())),
                preferred_element_type=jnp.float32,
            )
        total_ref[:, lanes] = total


def first_kernel(
    plan, arrived_ref, masked_ref, place_ref, inside_ref, initial_ref, new_ref, sums_ref, rounded_ref
):
    scale = scale_of(plan, total_of(plan, arrived_ref, plan.body, plan.message))
    for piece in range(plan.pieces):
        for block in range(plan.lane_blocks):
            part = arrived_ref[pl.ds(piece * plan.lane_blocks + block, plan.groups, stride=plan.message), :]
            initial_ref[pl.ds(piece * plan.groups, plan.groups), pl.ds(block * LANES, LANES)] = part / scale
    operate(plan, initial_ref, masked_ref, place_ref, inside_ref, rounded_ref, new_ref)
    squares = jnp.zeros((1, LANES), jnp.float32)
    overlap = jnp.zeros((1, LANES), jnp.float32)
    for block in range(plan.lane_blocks):
        lanes = pl.ds(block * LANES, LANES)
        new = new_ref[:, lanes]
        squares = squares + lane_sums(new * new)
        overlap = overlap + lane_sums(new * initial_ref[:, lanes])
    for index, value in enumerate((squares, overlap)):
        sums_ref[pl.ds(index, plan.groups, stride=EXTRA), :] = jnp.broadcast_to(value, (plan.groups, LANES))


def later_kernel(
    plan,
    body,
    keep,
    arrived_ref,
    raw_ref,
    previous_ref,
    initial_ref,
    masked_ref,
    place_ref,
    inside_ref,
    *refs,
):
    if keep:
        current_ref, new_ref, out_ref, moment_ref, rounded_ref = refs
    else:
        out_ref, moment_ref, rounded_ref, current_ref, new_ref = refs
    stride = body + EXTRA
    scale = scale_of(plan, total_of(plan, arrived_ref, body, stride))
    moment = total_of(plan, arrived_ref, body + 1, stride) / (plan.entries * scale)
    moment_ref[...] = jnp.broadcast_to(moment, moment_ref.shape)
    for block in range(plan.lane_blocks):
        lanes = pl.ds(block * LANES, LANES)
        current_ref[:, lanes] = raw_ref[:, lanes] / scale
    operate(plan, current_ref, masked_ref, place_ref, inside_ref, rounded_ref, new_ref)
    squares = jnp.zeros((1, LANES), jnp.float32)
    overlap = jnp.zeros((1, LANES), jnp.float32)
    for block in range(plan.lane_blocks):
        lanes = pl.ds(block * LANES, LANES)
        new = 2.0 * new_ref[:, lanes] - previous_ref[:, lanes] / scale
        squares = squares + lane_sums(new * new)
        overlap = overlap + lane_sums(new * initial_ref[:, lanes])
        if keep:
            new_ref[:, lanes] = new
        for piece in range(plan.pieces):
            out_ref[pl.ds(piece * plan.lane_blocks + block, plan.groups, stride=plan.message), :] = new[
                piece * plan.groups : (piece + 1) * plan.groups
            ]
    put_extra(plan, out_ref, (squares, overlap))


def arrive_kernel(plan, arrived_ref, *refs):
    scale = scale_of(plan, total_of(plan, arrived_ref, plan.body, plan.message))
    if len(refs) > 1:
        first_ref, second_ref, out_ref, moments_ref = refs
        moment = total_of(plan, arrived_ref, plan.body + 1, plan.message) / (plan.entries * scale)
        moments_ref[0] = first_ref[0, 0]
        moments_ref[1] = second_ref[0, 0]
        moments_ref[2] = moment[0, 0]
    else:
        (out_ref,) = refs
    for block in range(plan.lane_blocks):
        parts = [
            arrived_ref[pl.ds(piece * plan.lane_blocks + block, plan.groups, stride=plan.message), :]
            for piece in range(plan.pieces)
        ]
        out_ref[pl.ds(block * LANES, LANES), :] = (jnp.concatenate(parts, axis=0) / scale).T


def exchange(plan, values):
    rows = values.shape[0] // plan.groups
    shaped = values.reshape(plan.groups, rows // EXTRA, EXTRA, LANES)
    return lax.all_to_all(shaped, AXES, 0, 0, tiled=True).reshape(values.shape)


def shards(plan, state, operators, op_mask, site_bits, field, site_coupling, mode_coupling):
    f32 = jnp.float32
    message = jax.ShapeDtypeStruct((plan.groups * plan.message, LANES), f32)
    vector = jax.ShapeDtypeStruct((plan.places, plan.rows), f32)
    moment = jax.ShapeDtypeStruct((SUBLANES, LANES), f32)
    held = jax.ShapeDtypeStruct((plan.rows, plan.columns), f32)
    rounded = pltpu.VMEM((plan.places, plan.bits * plan.rows), jnp.bfloat16)
    kept = pltpu.VMEM((plan.places, plan.rows), f32)
    work = 2 * plan.bits * plan.places * plan.rows * plan.rows

    def cost(flops, moved):
        return pl.CostEstimate(flops=flops, bytes_accessed=moved, transcendentals=0)

    departing = pl.pallas_call(
        functools.partial(depart_kernel, plan),
        out_shape=message,
        in_specs=[VMEM],
        out_specs=VMEM,
        compiler_params=params(16),
        name="depart",
    )(state)
    arrived = exchange(plan, departing)
    masked, place, inside = pl.pallas_call(
        functools.partial(prepare_kernel, plan),
        out_shape=[
            jax.ShapeDtypeStruct((plan.bits, plan.rows, plan.rows), jnp.bfloat16),
            jax.ShapeDtypeStruct((3 + plan.bits, plan.places, LANES), f32),
            jax.ShapeDtypeStruct((SUBLANES, plan.rows), f32),
        ],
        in_specs=[SMEM] * 5 + [VMEM],
        out_specs=[VMEM] * 3,
        compiler_params=params(32),
        cost_estimate=cost(plan.bits * plan.rows * plan.rows, 4 * plan.bits * plan.rows * plan.rows),
        name="prepare",
    )(site_bits, op_mask, field, site_coupling, mode_coupling, operators)
    tables = (masked, place, inside)
    initial, raw, sums = pl.pallas_call(
        functools.partial(first_kernel, plan),
        out_shape=[vector, vector, jax.ShapeDtypeStruct((plan.groups * EXTRA, LANES), f32)],
        in_specs=[VMEM] * 4,
        out_specs=[VMEM] * 3,
        scratch_shapes=[rounded],
        compiler_params=params(32),
        cost_estimate=cost(work, 4 * plan.places * plan.rows),
        name="first",
    )(arrived, *tables)
    sums = exchange(plan, sums)
    current, raw, departing, moment_one = pl.pallas_call(
        functools.partial(later_kernel, plan, 0, True),
        out_shape=[vector, vector, message, moment],
        in_specs=[VMEM] * 7,
        out_specs=[VMEM] * 4,
        scratch_shapes=[rounded],
        compiler_params=params(32),
        cost_estimate=cost(work, 4 * plan.places * plan.rows),
        name="second",
    )(sums, raw, initial, initial, *tables)
    before = exchange(plan, departing)
    departing, moment_two = pl.pallas_call(
        functools.partial(later_kernel, plan, plan.body, False),
        out_shape=[message, moment],
        in_specs=[VMEM] * 7,
        out_specs=[VMEM] * 2,
        scratch_shapes=[rounded, kept, kept],
        compiler_params=params(32),
        cost_estimate=cost(work, 4 * plan.places * plan.rows),
        name="third",
    )(before, raw, current, initial, *tables)
    last = exchange(plan, departing)
    before = pl.pallas_call(
        functools.partial(arrive_kernel, plan),
        out_shape=held,
        in_specs=[VMEM],
        out_specs=VMEM,
        compiler_params=params(16),
        cost_estimate=cost(plan.places * plan.rows, 8 * plan.places * plan.rows),
        name="arrive_before",
    )(before)
    last, moments = pl.pallas_call(
        functools.partial(arrive_kernel, plan),
        out_shape=[held, jax.ShapeDtypeStruct((STEPS,), f32)],
        in_specs=[VMEM] * 3,
        out_specs=[VMEM, SMEM],
        compiler_params=params(16),
        name="arrive_last",
    )(last, moment_one, moment_two)
    return last, before, moments


def extended_2(block, sides, width):
    for axis, dim in sides:
        count = lax.axis_size(axis)
        forward = [(i, i + 1) for i in range(count - 1)]
        backward = [(target, source) for source, target in forward]
        low = lax.ppermute(
            lax.slice_in_dim(block, block.shape[dim] - width, None, axis=dim), axis, forward
        )
        high = lax.ppermute(lax.slice_in_dim(block, 0, width, axis=dim), axis, backward)
        block = jnp.concatenate([low, block, high], axis=dim)
    return block


def partner(value, axis, bit):
    mask = 2**bit
    pairs = [(source, source ^ mask) for source in range(lax.axis_size(axis))]
    return lax.ppermute(value, axis, pairs)


def halo_shards(state, operators, op_mask, site_bits, field, site_coupling, mode_coupling):
    site_count = lax.axis_size("site")
    phonon_count = lax.axis_size("phonon")
    bit_count = site_count.bit_length() - 1
    rows_here = state.shape[0]
    columns_here = state.shape[1]
    levels_here = columns_here // MODES
    block_edge = rows_here // op_mask.shape[1]
    expanded = jnp.repeat(jnp.repeat(op_mask, block_edge, axis=1), block_edge, axis=2)
    masked = jnp.where(expanded > 0, operators, jnp.zeros((), jnp.bfloat16))
    entries = jnp.float32(rows_here * columns_here * site_count * phonon_count)
    level_total = jnp.sqrt(jnp.float32(levels_here * phonon_count))
    device = lax.axis_index("site")
    inside = lax.iota(jnp.int32, rows_here)
    weight_rows = jnp.zeros((rows_here,), jnp.float32)
    for position in range(bit_count):
        weight_rows = weight_rows + site_coupling[site_bits[position]] * (
            device >> position & 1
        ).astype(jnp.float32)
    for local_bit in range(LBITS):
        weight_rows = weight_rows + site_coupling[bit_count + local_bit] * (
            inside >> local_bit & 1
        ).astype(jnp.float32)
    levels = (
        lax.axis_index("phonon") * levels_here + lax.iota(jnp.int32, columns_here) // MODES
    ).astype(jnp.float32)
    lower_weight = jnp.sqrt(levels)
    upper_weight = jnp.sqrt(levels + 1.0)
    mode_weight = jnp.tile(mode_coupling, columns_here // MODES) / level_total
    start_squares = lax.psum(jnp.sum(state * state), ("site", "phonon"))
    initial = state / jnp.sqrt(start_squares / entries + epsilon)
    previous = initial
    current = initial
    scale_prev = jnp.float32(1.0)
    moments = []
    for iteration in range(STEPS):
        extended = extended_2(current, (("phonon", 1),), MODES)
        lower_part = extended[:, :columns_here]
        upper_part = extended[:, 2 * MODES :]
        summed = weight_rows[:, None] * (
            mode_weight * (lower_weight * lower_part + upper_weight * upper_part)
        )
        for operate_position in range(bit_count):
            chosen = site_bits[operate_position]
            flipped = partner(current, "site", operate_position)
            product = jnp.dot(
                masked[chosen], flipped.astype(jnp.bfloat16), preferred_element_type=jnp.float32
            )
            summed = summed + (field[chosen] * flipped + product)
        if iteration == 0:
            vector_new = summed
        else:
            vector_new = 2.0 * summed - previous / scale_prev
        squares, intersection = lax.psum(
            (jnp.sum(vector_new * vector_new), jnp.sum(initial * vector_new)), ("site", "phonon")
        )
        scale_now = jnp.sqrt(squares / entries + epsilon)
        updated = vector_new / scale_now
        moment = intersection / (entries * scale_now)
        moments.append(moment)
        previous = current
        current = updated
        scale_prev = scale_now
    return (current, previous, jnp.stack(moments))


def solution(mesh):
    in_specs = (P("site", "phonon"), P(), P(), P(), P(), P(), P())
    out_specs = (P("site", "phonon"), P("site", "phonon"), P())

    def whole(state, operators, op_mask, *rest):
        rows = state.shape[0] // mesh.shape["site"]
        columns = state.shape[1] // mesh.shape["phonon"]
        plan = Plan(mesh, rows, columns, op_mask.shape[1])
        body = functools.partial(shards, plan) if plan.fits() else halo_shards
        run = jax.shard_map(body, mesh=mesh, in_specs=in_specs, out_specs=out_specs, check_vma=False)
        return run(state, operators, op_mask, *rest)

    return whole
```

```python
import functools

import jax
import jax.numpy as jnp
from jax import lax
from jax.experimental import pallas as pl
from jax.experimental.pallas import tpu as pltpu
from jax.sharding import PartitionSpec as P

LBITS = 10
MODES = 64
STEPS = 3
LANES = 128
SUBLANES = 8
EXTRA = 2
AXES = ("site", "phonon")

epsilon = 1e-06


VMEM = pl.BlockSpec(memory_space=pltpu.VMEM)
SMEM = pl.BlockSpec(memory_space=pltpu.SMEM)


class Plan:
    def __init__(self, mesh, rows, columns, blocks):
        self.sites = mesh.shape["site"]
        self.phonons = mesh.shape["phonon"]
        self.groups = self.sites * self.phonons
        self.bits = self.sites.bit_length() - 1
        self.rows = rows
        self.columns = columns
        self.blocks = blocks
        self.edge = rows // blocks
        self.levels_here = columns // MODES
        self.level_count = self.levels_here * self.phonons
        self.share = MODES // self.groups
        self.pieces = self.levels_here * self.share
        self.lane_blocks = rows // LANES
        self.body = self.pieces * self.lane_blocks
        self.message = self.body + EXTRA
        self.places = self.pieces * self.groups
        self.entries = float(rows * columns * self.groups)

    def fits(self):
        return (
            MODES % self.groups == 0
            and self.columns == LANES
            and self.rows % LANES == 0
            and self.edge % LANES == 0
            and self.groups % SUBLANES == 0
        )


def params(mib):
    return pltpu.CompilerParams(vmem_limit_bytes=mib * 2**20)


def lane_sums(values):
    return jnp.sum(values, axis=0, keepdims=True)


def put_extra(plan, out_ref, sums, start, stride):
    for index, value in enumerate(sums):
        out_ref[pl.ds(start + index, plan.groups, stride=stride), :] = jnp.broadcast_to(value, (plan.groups, LANES))


def total_of(plan, ref, start, stride):
    lanes = lane_sums(ref[pl.ds(start, plan.groups, stride=stride), :])
    return jnp.sum(lanes, axis=1, keepdims=True)


def scale_of(plan, squares):
    return jnp.sqrt(squares / plan.entries + epsilon)


def depart_kernel(plan, state_ref, out_ref):
    sums = jnp.zeros((1, LANES), jnp.float32)
    for block in range(plan.lane_blocks):
        tile = state_ref[pl.ds(block * LANES, LANES), :]
        sums = sums + lane_sums(tile * tile)
        turned = tile.T
        for piece in range(plan.pieces):
            out_ref[pl.ds(piece * plan.lane_blocks + block, plan.groups, stride=plan.message), :] = turned[
                piece * plan.groups : (piece + 1) * plan.groups
            ]
    put_extra(plan, out_ref, (sums, jnp.zeros_like(sums)), plan.body, plan.message)


def prepare_kernel(
    plan, bits_ref, mask_ref, field_ref, coupling_ref, mode_ref, operators_ref, masked_ref, place_ref, inside_ref
):
    me = lax.axis_index("site") * plan.phonons + lax.axis_index("phonon")
    for position in range(plan.bits):
        chosen = bits_ref[position]
        for across in range(plan.blocks):
            rows = pl.ds(across * plan.edge, plan.edge)
            for along in range(plan.blocks):
                columns = pl.ds(along * plan.edge, plan.edge)
                keep = (mask_ref[chosen, across, along] > 0).astype(jnp.float32).astype(jnp.bfloat16)
                masked_ref[position, rows, columns] = operators_ref[chosen, rows, columns] * keep
    place = lax.broadcasted_iota(jnp.int32, (plan.places, LANES), 0)
    phonon = place % plan.phonons
    site = place // plan.phonons % plan.sites
    mode = place // plan.groups % plan.share
    level = phonon * plan.levels_here + place // (plan.groups * plan.share)
    occupied = jnp.zeros((plan.places, LANES), jnp.float32)
    for position in range(plan.bits):
        held = (site >> position & 1).astype(jnp.float32)
        occupied = occupied + coupling_ref[bits_ref[position]] * held
    strength = jnp.zeros((plan.places, LANES), jnp.float32)
    for index in range(plan.share):
        strength = jnp.where(mode == index, mode_ref[index * plan.groups + me], strength)
    strength = strength / jnp.sqrt(jnp.full((1, LANES), plan.level_count, jnp.float32))
    height = level.astype(jnp.float32)
    place_ref[0] = occupied
    place_ref[1] = strength * jnp.sqrt(height)
    place_ref[2] = jnp.where(level == plan.level_count - 1, 0.0, strength * jnp.sqrt(height + 1.0))
    for position in range(plan.bits):
        place_ref[3 + position] = jnp.full((plan.places, LANES), field_ref[bits_ref[position]])
    inside = lax.broadcasted_iota(jnp.int32, (SUBLANES, plan.rows), 1)
    weight = jnp.zeros((SUBLANES, plan.rows), jnp.float32)
    for local_bit in range(LBITS):
        weight = weight + coupling_ref[plan.bits + local_bit] * (inside >> local_bit & 1).astype(jnp.float32)
    inside_ref[...] = weight


def flipped(values, stride):
    places, width = values.shape
    if stride % SUBLANES == 0:
        shaped = values.reshape(places // (2 * stride), 2, stride, width)
        return jnp.concatenate([shaped[:, 1:], shaped[:, :1]], axis=1).reshape(places, width)
    tiles = values.reshape(places // SUBLANES, SUBLANES, width)
    if 2 * stride == SUBLANES:
        return pltpu.roll(tiles, stride, 1).reshape(places, width)
    spot = lax.broadcasted_iota(jnp.int32, tiles.shape, 1)
    down = pltpu.roll(tiles, stride, 1)
    up = pltpu.roll(tiles, SUBLANES - stride, 1)
    return jnp.where(spot & stride > 0, down, up).reshape(places, width)


def shifted(values, by):
    places, width = values.shape
    tiles = values.reshape(places // SUBLANES, SUBLANES, width)
    return pltpu.roll(tiles, by % SUBLANES, 1).reshape(places, width)


def operate(plan, vector_ref, masked_ref, place_ref, inside_ref, rounded_ref, total_ref):
    span = plan.places // plan.levels_here
    for block in range(plan.lane_blocks):
        lanes = pl.ds(block * LANES, LANES)
        vector = vector_ref[:, lanes]
        levels = [vector[index * span : (index + 1) * span] for index in range(plan.levels_here)]
        lower = jnp.concatenate([shifted(levels[-1], 1)] + levels[:-1], axis=0)
        upper = jnp.concatenate(levels[1:] + [shifted(levels[0], -1)], axis=0)
        weight = place_ref[0] + inside_ref[:1, lanes]
        total = weight * (place_ref[1] * lower + place_ref[2] * upper)
        for position in range(plan.bits):
            turned = flipped(vector, plan.phonons << position)
            total = total + place_ref[3 + position] * turned
            rounded_ref[:, pl.ds(position * plan.rows + block * LANES, LANES)] = turned.astype(jnp.bfloat16)
        total_ref[:, lanes] = total
    width = 2 * LANES
    for column in range(plan.rows // width):
        lanes = pl.ds(column * width, width)
        total = total_ref[:, lanes]
        for position in range(plan.bits):
            total = total + lax.dot_general(
                rounded_ref[:, pl.ds(position * plan.rows, plan.rows)],
                masked_ref[position, lanes, :],
                (((1,), (1,)), ((), ())),
                preferred_element_type=jnp.float32,
            )
        total_ref[:, lanes] = total


def first_kernel(
    plan, arrived_ref, masked_ref, place_ref, inside_ref, initial_ref, new_ref, sums_ref, rounded_ref
):
    scale = scale_of(plan, total_of(plan, arrived_ref, plan.body, plan.message))
    for piece in range(plan.pieces):
        for block in range(plan.lane_blocks):
            part = arrived_ref[pl.ds(piece * plan.lane_blocks + block, plan.groups, stride=plan.message), :]
            initial_ref[pl.ds(piece * plan.groups, plan.groups), pl.ds(block * LANES, LANES)] = part / scale
    operate(plan, initial_ref, masked_ref, place_ref, inside_ref, rounded_ref, new_ref)
    squares = jnp.zeros((1, LANES), jnp.float32)
    overlap = jnp.zeros((1, LANES), jnp.float32)
    for block in range(plan.lane_blocks):
        lanes = pl.ds(block * LANES, LANES)
        new = new_ref[:, lanes]
        squares = squares + lane_sums(new * new)
        overlap = overlap + lane_sums(new * initial_ref[:, lanes])
    put_extra(plan, sums_ref, (squares, overlap), 0, EXTRA)


def later_kernel(
    plan,
    keep,
    arrived_ref,
    raw_ref,
    previous_ref,
    initial_ref,
    masked_ref,
    place_ref,
    inside_ref,
    *refs,
):
    if keep:
        current_ref, new_ref, out_ref, moment_ref, sums_ref, rounded_ref = refs
    else:
        out_ref, moment_ref, rounded_ref, current_ref, new_ref = refs
    scale = scale_of(plan, total_of(plan, arrived_ref, 0, EXTRA))
    moment = total_of(plan, arrived_ref, 1, EXTRA) / (plan.entries * scale)
    moment_ref[...] = jnp.broadcast_to(moment, moment_ref.shape)
    for block in range(plan.lane_blocks):
        lanes = pl.ds(block * LANES, LANES)
        current_ref[:, lanes] = raw_ref[:, lanes] / scale
    operate(plan, current_ref, masked_ref, place_ref, inside_ref, rounded_ref, new_ref)
    squares = jnp.zeros((1, LANES), jnp.float32)
    overlap = jnp.zeros((1, LANES), jnp.float32)
    for block in range(plan.lane_blocks):
        lanes = pl.ds(block * LANES, LANES)
        new = 2.0 * new_ref[:, lanes] - previous_ref[:, lanes] / scale
        squares = squares + lane_sums(new * new)
        overlap = overlap + lane_sums(new * initial_ref[:, lanes])
        if keep:
            new_ref[:, lanes] = new
        for piece in range(plan.pieces):
            out_ref[pl.ds(piece * plan.lane_blocks + block, plan.groups, stride=plan.message), :] = new[
                piece * plan.groups : (piece + 1) * plan.groups
            ]
    put_extra(plan, out_ref, (squares, overlap), plan.body, plan.message)
    if keep:
        put_extra(plan, sums_ref, (squares, overlap), 0, EXTRA)


def arrive_kernel(plan, arrived_ref, *refs):
    scale = scale_of(plan, total_of(plan, arrived_ref, plan.body, plan.message))
    if len(refs) > 1:
        first_ref, second_ref, out_ref, moments_ref = refs
        moment = total_of(plan, arrived_ref, plan.body + 1, plan.message) / (plan.entries * scale)
        moments_ref[0] = first_ref[0, 0]
        moments_ref[1] = second_ref[0, 0]
        moments_ref[2] = moment[0, 0]
    else:
        (out_ref,) = refs
    for block in range(plan.lane_blocks):
        parts = [
            arrived_ref[pl.ds(piece * plan.lane_blocks + block, plan.groups, stride=plan.message), :]
            for piece in range(plan.pieces)
        ]
        out_ref[pl.ds(block * LANES, LANES), :] = (jnp.concatenate(parts, axis=0) / scale).T


def exchange(plan, values):
    rows = values.shape[0] // plan.groups
    shaped = values.reshape(plan.groups, rows // EXTRA, EXTRA, LANES)
    return lax.all_to_all(shaped, AXES, 0, 0, tiled=True).reshape(values.shape)


def shards(plan, state, operators, op_mask, site_bits, field, site_coupling, mode_coupling):
    f32 = jnp.float32
    message = jax.ShapeDtypeStruct((plan.groups * plan.message, LANES), f32)
    vector = jax.ShapeDtypeStruct((plan.places, plan.rows), f32)
    moment = jax.ShapeDtypeStruct((SUBLANES, LANES), f32)
    held = jax.ShapeDtypeStruct((plan.rows, plan.columns), f32)
    rounded = pltpu.VMEM((plan.places, plan.bits * plan.rows), jnp.bfloat16)
    kept = pltpu.VMEM((plan.places, plan.rows), f32)
    work = 2 * plan.bits * plan.places * plan.rows * plan.rows

    def cost(flops, moved):
        return pl.CostEstimate(flops=flops, bytes_accessed=moved, transcendentals=0)

    departing = pl.pallas_call(
        functools.partial(depart_kernel, plan),
        out_shape=message,
        in_specs=[VMEM],
        out_specs=VMEM,
        compiler_params=params(16),
        name="depart",
    )(state)
    arrived = exchange(plan, departing)
    masked, place, inside = pl.pallas_call(
        functools.partial(prepare_kernel, plan),
        out_shape=[
            jax.ShapeDtypeStruct((plan.bits, plan.rows, plan.rows), jnp.bfloat16),
            jax.ShapeDtypeStruct((3 + plan.bits, plan.places, LANES), f32),
            jax.ShapeDtypeStruct((SUBLANES, plan.rows), f32),
        ],
        in_specs=[SMEM] * 5 + [VMEM],
        out_specs=[VMEM] * 3,
        compiler_params=params(32),
        cost_estimate=cost(plan.bits * plan.rows * plan.rows, 4 * plan.bits * plan.rows * plan.rows),
        name="prepare",
    )(site_bits, op_mask, field, site_coupling, mode_coupling, operators)
    tables = (masked, place, inside)
    small = jax.ShapeDtypeStruct((plan.groups * EXTRA, LANES), f32)
    initial, raw, sums = pl.pallas_call(
        functools.partial(first_kernel, plan),
        out_shape=[vector, vector, small],
        in_specs=[VMEM] * 4,
        out_specs=[VMEM] * 3,
        scratch_shapes=[rounded],
        compiler_params=params(32),
        cost_estimate=cost(work, 4 * plan.places * plan.rows),
        name="first",
    )(arrived, *tables)
    sums = exchange(plan, sums)
    current, raw, departing, moment_one, sums = pl.pallas_call(
        functools.partial(later_kernel, plan, True),
        out_shape=[vector, vector, message, moment, small],
        in_specs=[VMEM] * 7,
        out_specs=[VMEM] * 5,
        scratch_shapes=[rounded],
        compiler_params=params(32),
        cost_estimate=cost(work, 4 * plan.places * plan.rows),
        name="second",
    )(sums, raw, initial, initial, *tables)
    before = exchange(plan, departing)
    sums = exchange(plan, sums)
    departing, moment_two = pl.pallas_call(
        functools.partial(later_kernel, plan, False),
        out_shape=[message, moment],
        in_specs=[VMEM] * 7,
        out_specs=[VMEM] * 2,
        scratch_shapes=[rounded, kept, kept],
        compiler_params=params(32),
        cost_estimate=cost(work, 4 * plan.places * plan.rows),
        name="third",
    )(sums, raw, current, initial, *tables)
    last = exchange(plan, departing)
    before = pl.pallas_call(
        functools.partial(arrive_kernel, plan),
        out_shape=held,
        in_specs=[VMEM],
        out_specs=VMEM,
        compiler_params=params(16),
        cost_estimate=cost(plan.places * plan.rows, 8 * plan.places * plan.rows),
        name="arrive_before",
    )(before)
    last, moments = pl.pallas_call(
        functools.partial(arrive_kernel, plan),
        out_shape=[held, jax.ShapeDtypeStruct((STEPS,), f32)],
        in_specs=[VMEM] * 3,
        out_specs=[VMEM, SMEM],
        compiler_params=params(16),
        name="arrive_last",
    )(last, moment_one, moment_two)
    return last, before, moments


def extended_2(block, sides, width):
    for axis, dim in sides:
        count = lax.axis_size(axis)
        forward = [(i, i + 1) for i in range(count - 1)]
        backward = [(target, source) for source, target in forward]
        low = lax.ppermute(
            lax.slice_in_dim(block, block.shape[dim] - width, None, axis=dim), axis, forward
        )
        high = lax.ppermute(lax.slice_in_dim(block, 0, width, axis=dim), axis, backward)
        block = jnp.concatenate([low, block, high], axis=dim)
    return block


def partner(value, axis, bit):
    mask = 2**bit
    pairs = [(source, source ^ mask) for source in range(lax.axis_size(axis))]
    return lax.ppermute(value, axis, pairs)


def halo_shards(state, operators, op_mask, site_bits, field, site_coupling, mode_coupling):
    site_count = lax.axis_size("site")
    phonon_count = lax.axis_size("phonon")
    bit_count = site_count.bit_length() - 1
    rows_here = state.shape[0]
    columns_here = state.shape[1]
    levels_here = columns_here // MODES
    block_edge = rows_here // op_mask.shape[1]
    expanded = jnp.repeat(jnp.repeat(op_mask, block_edge, axis=1), block_edge, axis=2)
    masked = jnp.where(expanded > 0, operators, jnp.zeros((), jnp.bfloat16))
    entries = jnp.float32(rows_here * columns_here * site_count * phonon_count)
    level_total = jnp.sqrt(jnp.float32(levels_here * phonon_count))
    device = lax.axis_index("site")
    inside = lax.iota(jnp.int32, rows_here)
    weight_rows = jnp.zeros((rows_here,), jnp.float32)
    for position in range(bit_count):
        weight_rows = weight_rows + site_coupling[site_bits[position]] * (
            device >> position & 1
        ).astype(jnp.float32)
    for local_bit in range(LBITS):
        weight_rows = weight_rows + site_coupling[bit_count + local_bit] * (
            inside >> local_bit & 1
        ).astype(jnp.float32)
    levels = (
        lax.axis_index("phonon") * levels_here + lax.iota(jnp.int32, columns_here) // MODES
    ).astype(jnp.float32)
    lower_weight = jnp.sqrt(levels)
    upper_weight = jnp.sqrt(levels + 1.0)
    mode_weight = jnp.tile(mode_coupling, columns_here // MODES) / level_total
    start_squares = lax.psum(jnp.sum(state * state), ("site", "phonon"))
    initial = state / jnp.sqrt(start_squares / entries + epsilon)
    previous = initial
    current = initial
    scale_prev = jnp.float32(1.0)
    moments = []
    for iteration in range(STEPS):
        extended = extended_2(current, (("phonon", 1),), MODES)
        lower_part = extended[:, :columns_here]
        upper_part = extended[:, 2 * MODES :]
        summed = weight_rows[:, None] * (
            mode_weight * (lower_weight * lower_part + upper_weight * upper_part)
        )
        for operate_position in range(bit_count):
            chosen = site_bits[operate_position]
            flipped = partner(current, "site", operate_position)
            product = jnp.dot(
                masked[chosen], flipped.astype(jnp.bfloat16), preferred_element_type=jnp.float32
            )
            summed = summed + (field[chosen] * flipped + product)
        if iteration == 0:
            vector_new = summed
        else:
            vector_new = 2.0 * summed - previous / scale_prev
        squares, intersection = lax.psum(
            (jnp.sum(vector_new * vector_new), jnp.sum(initial * vector_new)), ("site", "phonon")
        )
        scale_now = jnp.sqrt(squares / entries + epsilon)
        updated = vector_new / scale_now
        moment = intersection / (entries * scale_now)
        moments.append(moment)
        previous = current
        current = updated
        scale_prev = scale_now
    return (current, previous, jnp.stack(moments))


def solution(mesh):
    in_specs = (P("site", "phonon"), P(), P(), P(), P(), P(), P())
    out_specs = (P("site", "phonon"), P("site", "phonon"), P())

    def whole(state, operators, op_mask, *rest):
        rows = state.shape[0] // mesh.shape["site"]
        columns = state.shape[1] // mesh.shape["phonon"]
        plan = Plan(mesh, rows, columns, op_mask.shape[1])
        body = functools.partial(shards, plan) if plan.fits() else halo_shards
        run = jax.shard_map(body, mesh=mesh, in_specs=in_specs, out_specs=out_specs, check_vma=False)
        return run(state, operators, op_mask, *rest)

    return whole
```

```python
import functools

import jax
import jax.numpy as jnp
from jax import lax
from jax.experimental import pallas as pl
from jax.experimental.pallas import tpu as pltpu
from jax.sharding import PartitionSpec as P

LBITS = 10
MODES = 64
STEPS = 3
LANES = 128
SUBLANES = 8
EXTRA = 2
AXES = ("phonon", "site")

epsilon = 1e-06


VMEM = pl.BlockSpec(memory_space=pltpu.VMEM)
SMEM = pl.BlockSpec(memory_space=pltpu.SMEM)
HBM = pl.BlockSpec(memory_space=pltpu.HBM)


class Plan:
    def __init__(self, mesh, rows, columns, blocks):
        self.sites = mesh.shape["site"]
        self.phonons = mesh.shape["phonon"]
        self.groups = self.sites * self.phonons
        self.bits = self.sites.bit_length() - 1
        self.rows = rows
        self.columns = columns
        self.blocks = blocks
        self.edge = rows // blocks
        self.levels_here = columns // MODES
        self.level_count = self.levels_here * self.phonons
        self.share = MODES // self.groups
        self.pieces = self.levels_here * self.share
        self.lane_blocks = rows // LANES
        self.body = self.pieces * self.lane_blocks
        self.message = self.body + EXTRA
        self.places = self.pieces * self.groups
        self.entries = float(rows * columns * self.groups)

    def fits(self):
        return (
            MODES % self.groups == 0
            and self.columns == LANES
            and self.rows % LANES == 0
            and self.edge % LANES == 0
            and self.groups % SUBLANES == 0
        )


def params(mib):
    return pltpu.CompilerParams(vmem_limit_bytes=mib * 2**20)


def lane_sums(values):
    return jnp.sum(values, axis=0, keepdims=True)


def put_extra(plan, out_ref, sums):
    for index, value in enumerate(sums):
        out_ref[pl.ds(plan.body + index, plan.groups, stride=plan.message), :] = jnp.broadcast_to(
            value, (plan.groups, LANES)
        )


def total_of(plan, ref, start, stride):
    lanes = lane_sums(ref[pl.ds(start, plan.groups, stride=stride), :])
    return jnp.sum(lanes, axis=1, keepdims=True)


def scale_of(plan, squares):
    return jnp.sqrt(squares / plan.entries + epsilon)


def depart_kernel(plan, state_ref, out_ref, tiles_ref, semaphores):
    copies = [
        pltpu.make_async_copy(state_ref.at[pl.ds(block * LANES, LANES), :], tiles_ref.at[block], semaphores.at[block])
        for block in range(plan.lane_blocks)
    ]
    for copy in copies:
        copy.start()
    sums = jnp.zeros((1, LANES), jnp.float32)
    for block in range(plan.lane_blocks):
        copies[block].wait()
        tile = tiles_ref[block]
        sums = sums + lane_sums(tile * tile)
        turned = tile.T
        for piece in range(plan.pieces):
            out_ref[pl.ds(piece * plan.lane_blocks + block, plan.groups, stride=plan.message), :] = turned[
                piece * plan.groups : (piece + 1) * plan.groups
            ]
    put_extra(plan, out_ref, (sums, jnp.zeros_like(sums)))


def prepare_kernel(
    plan,
    bits_ref,
    mask_ref,
    field_ref,
    coupling_ref,
    mode_ref,
    operators_ref,
    masked_ref,
    place_ref,
    inside_ref,
    held_ref,
    in_semaphores,
    out_semaphores,
):
    me = lax.axis_index("phonon") * plan.sites + lax.axis_index("site")
    fetches = []
    for position in range(plan.bits):
        fetch = pltpu.make_async_copy(
            operators_ref.at[bits_ref[position]], held_ref.at[position], in_semaphores.at[position]
        )
        fetch.start()
        fetches.append(fetch)
    stores = []
    for position in range(plan.bits):
        fetches[position].wait()
        chosen = bits_ref[position]
        for across in range(plan.blocks):
            rows = pl.ds(across * plan.edge, plan.edge)
            for along in range(plan.blocks):
                columns = pl.ds(along * plan.edge, plan.edge)
                keep = (mask_ref[chosen, across, along] > 0).astype(jnp.float32).astype(jnp.bfloat16)
                held_ref[position, rows, columns] = held_ref[position, rows, columns] * keep
        store = pltpu.make_async_copy(held_ref.at[position], masked_ref.at[position], out_semaphores.at[position])
        store.start()
        stores.append(store)
    place = lax.broadcasted_iota(jnp.int32, (plan.places, LANES), 0)
    site = place % plan.sites
    phonon = place // plan.sites % plan.phonons
    mode = place // plan.groups % plan.share
    level = phonon * plan.levels_here + place // (plan.groups * plan.share)
    occupied = jnp.zeros((plan.places, LANES), jnp.float32)
    for position in range(plan.bits):
        held = (site >> position & 1).astype(jnp.float32)
        occupied = occupied + coupling_ref[bits_ref[position]] * held
    strength = jnp.zeros((plan.places, LANES), jnp.float32)
    for index in range(plan.share):
        strength = jnp.where(mode == index, mode_ref[index * plan.groups + me], strength)
    strength = strength / jnp.sqrt(jnp.full((1, LANES), plan.level_count, jnp.float32))
    height = level.astype(jnp.float32)
    place_ref[0] = occupied
    place_ref[1] = strength * jnp.sqrt(height)
    place_ref[2] = jnp.where(level == plan.level_count - 1, 0.0, strength * jnp.sqrt(height + 1.0))
    for position in range(plan.bits):
        place_ref[3 + position] = jnp.full((plan.places, LANES), field_ref[bits_ref[position]])
    inside = lax.broadcasted_iota(jnp.int32, (SUBLANES, plan.rows), 1)
    weight = jnp.zeros((SUBLANES, plan.rows), jnp.float32)
    for local_bit in range(LBITS):
        weight = weight + coupling_ref[plan.bits + local_bit] * (inside >> local_bit & 1).astype(jnp.float32)
    inside_ref[...] = weight
    for store in stores:
        store.wait()


def flipped(values, stride):
    places, width = values.shape
    if stride % SUBLANES == 0:
        shaped = values.reshape(places // (2 * stride), 2, stride, width)
        return jnp.concatenate([shaped[:, 1:], shaped[:, :1]], axis=1).reshape(places, width)
    tiles = values.reshape(places // SUBLANES, SUBLANES, width)
    if 2 * stride == SUBLANES:
        return pltpu.roll(tiles, stride, 1).reshape(places, width)
    spot = lax.broadcasted_iota(jnp.int32, tiles.shape, 1)
    down = pltpu.roll(tiles, stride, 1)
    up = pltpu.roll(tiles, SUBLANES - stride, 1)
    return jnp.where(spot & stride > 0, down, up).reshape(places, width)


def shifted(values, by):
    places, width = values.shape
    if by % SUBLANES == 0:
        return jnp.concatenate([values[-by:], values[:-by]], axis=0)
    tiles = values.reshape(places // SUBLANES, SUBLANES, width)
    return pltpu.roll(tiles, by % SUBLANES, 1).reshape(places, width)


def operate(plan, vector_ref, masked_ref, place_ref, inside_ref, rounded_ref, total_ref, fetches=None):
    span = plan.places // plan.levels_here
    for block in range(plan.lane_blocks):
        lanes = pl.ds(block * LANES, LANES)
        vector = vector_ref[:, lanes]
        levels = [vector[index * span : (index + 1) * span] for index in range(plan.levels_here)]
        lower = jnp.concatenate([shifted(levels[-1], plan.sites)] + levels[:-1], axis=0)
        upper = jnp.concatenate(levels[1:] + [shifted(levels[0], -plan.sites)], axis=0)
        weight = place_ref[0] + inside_ref[:1, lanes]
        total = weight * (place_ref[1] * lower + place_ref[2] * upper)
        for position in range(plan.bits):
            turned = flipped(vector, 1 << position)
            total = total + place_ref[3 + position] * turned
            rounded_ref[:, pl.ds(position * plan.rows + block * LANES, LANES)] = turned.astype(jnp.bfloat16)
        total_ref[:, lanes] = total
    width = 2 * LANES
    rounds = [[position] for position in range(plan.bits)] if fetches else [range(plan.bits)]
    for positions in rounds:
        if fetches:
            fetches[positions[0]].wait()
        for column in range(plan.rows // width):
            lanes = pl.ds(column * width, width)
            total = total_ref[:, lanes]
            for position in positions:
                total = total + lax.dot_general(
                    rounded_ref[:, pl.ds(position * plan.rows, plan.rows)],
                    masked_ref[position, lanes, :],
                    (((1,), (1,)), ((), ())),
                    preferred_element_type=jnp.float32,
                )
            total_ref[:, lanes] = total


def first_kernel(
    plan,
    arrived_ref,
    stored_ref,
    place_ref,
    inside_ref,
    initial_ref,
    new_ref,
    sums_ref,
    masked_ref,
    rounded_ref,
    semaphores,
):
    fetches = []
    for position in range(plan.bits):
        fetch = pltpu.make_async_copy(stored_ref.at[position], masked_ref.at[position], semaphores.at[position])
        fetch.start()
        fetches.append(fetch)
    scale = scale_of(plan, total_of(plan, arrived_ref, plan.body, plan.message))
    for piece in range(plan.pieces):
        for block in range(plan.lane_blocks):
            part = arrived_ref[pl.ds(piece * plan.lane_blocks + block, plan.groups, stride=plan.message), :]
            initial_ref[pl.ds(piece * plan.groups, plan.groups), pl.ds(block * LANES, LANES)] = part / scale
    operate(plan, initial_ref, masked_ref, place_ref, inside_ref, rounded_ref, new_ref, fetches)
    squares = jnp.zeros((1, LANES), jnp.float32)
    overlap = jnp.zeros((1, LANES), jnp.float32)
    for block in range(plan.lane_blocks):
        lanes = pl.ds(block * LANES, LANES)
        new = new_ref[:, lanes]
        squares = squares + lane_sums(new * new)
        overlap = overlap + lane_sums(new * initial_ref[:, lanes])
    for index, value in enumerate((squares, overlap)):
        sums_ref[pl.ds(index, plan.groups, stride=EXTRA), :] = jnp.broadcast_to(value, (plan.groups, LANES))


def later_kernel(
    plan,
    body,
    keep,
    arrived_ref,
    raw_ref,
    previous_ref,
    initial_ref,
    masked_ref,
    place_ref,
    inside_ref,
    *refs,
):
    if keep:
        current_ref, new_ref, out_ref, moment_ref, rounded_ref = refs
    else:
        out_ref, moment_ref, rounded_ref, current_ref, new_ref = refs
    stride = body + EXTRA
    scale = scale_of(plan, total_of(plan, arrived_ref, body, stride))
    moment = total_of(plan, arrived_ref, body + 1, stride) / (plan.entries * scale)
    moment_ref[...] = jnp.broadcast_to(moment, moment_ref.shape)
    for block in range(plan.lane_blocks):
        lanes = pl.ds(block * LANES, LANES)
        current_ref[:, lanes] = raw_ref[:, lanes] / scale
    operate(plan, current_ref, masked_ref, place_ref, inside_ref, rounded_ref, new_ref)
    squares = jnp.zeros((1, LANES), jnp.float32)
    overlap = jnp.zeros((1, LANES), jnp.float32)
    for block in range(plan.lane_blocks):
        lanes = pl.ds(block * LANES, LANES)
        new = 2.0 * new_ref[:, lanes] - previous_ref[:, lanes] / scale
        squares = squares + lane_sums(new * new)
        overlap = overlap + lane_sums(new * initial_ref[:, lanes])
        if keep:
            new_ref[:, lanes] = new
        for piece in range(plan.pieces):
            out_ref[pl.ds(piece * plan.lane_blocks + block, plan.groups, stride=plan.message), :] = new[
                piece * plan.groups : (piece + 1) * plan.groups
            ]
    put_extra(plan, out_ref, (squares, overlap))


def arrive_kernel(plan, arrived_ref, *refs):
    scale = scale_of(plan, total_of(plan, arrived_ref, plan.body, plan.message))
    if len(refs) > 1:
        first_ref, second_ref, out_ref, moments_ref = refs
        moment = total_of(plan, arrived_ref, plan.body + 1, plan.message) / (plan.entries * scale)
        moments_ref[0] = first_ref[0, 0]
        moments_ref[1] = second_ref[0, 0]
        moments_ref[2] = moment[0, 0]
    else:
        (out_ref,) = refs
    for block in range(plan.lane_blocks):
        parts = [
            arrived_ref[pl.ds(piece * plan.lane_blocks + block, plan.groups, stride=plan.message), :]
            for piece in range(plan.pieces)
        ]
        out_ref[pl.ds(block * LANES, LANES), :] = (jnp.concatenate(parts, axis=0) / scale).T


def exchange(plan, values):
    rows = values.shape[0] // plan.groups
    shaped = values.reshape(plan.groups, rows // EXTRA, EXTRA, LANES)
    return lax.all_to_all(shaped, AXES, 0, 0, tiled=True).reshape(values.shape)


def shards(plan, state, operators, op_mask, site_bits, field, site_coupling, mode_coupling):
    f32 = jnp.float32
    message = jax.ShapeDtypeStruct((plan.groups * plan.message, LANES), f32)
    vector = jax.ShapeDtypeStruct((plan.places, plan.rows), f32)
    moment = jax.ShapeDtypeStruct((SUBLANES, LANES), f32)
    held = jax.ShapeDtypeStruct((plan.rows, plan.columns), f32)
    rounded = pltpu.VMEM((plan.places, plan.bits * plan.rows), jnp.bfloat16)
    kept = pltpu.VMEM((plan.places, plan.rows), f32)
    work = 2 * plan.bits * plan.places * plan.rows * plan.rows

    def cost(flops, moved):
        return pl.CostEstimate(flops=flops, bytes_accessed=moved, transcendentals=0)

    departing = pl.pallas_call(
        functools.partial(depart_kernel, plan),
        out_shape=message,
        in_specs=[HBM],
        out_specs=VMEM,
        scratch_shapes=[
            pltpu.VMEM((plan.lane_blocks, LANES, plan.columns), f32),
            pltpu.SemaphoreType.DMA((plan.lane_blocks,)),
        ],
        compiler_params=params(60),
        name="depart",
    )(state)
    arrived = exchange(plan, departing)
    operators_shape = jax.ShapeDtypeStruct((plan.bits, plan.rows, plan.rows), jnp.bfloat16)
    stored, place, inside = pl.pallas_call(
        functools.partial(prepare_kernel, plan),
        out_shape=[
            operators_shape,
            jax.ShapeDtypeStruct((3 + plan.bits, plan.places, LANES), f32),
            jax.ShapeDtypeStruct((SUBLANES, plan.rows), f32),
        ],
        in_specs=[SMEM] * 5 + [HBM],
        out_specs=[HBM, VMEM, VMEM],
        scratch_shapes=[
            pltpu.VMEM((plan.bits, plan.rows, plan.rows), jnp.bfloat16),
            pltpu.SemaphoreType.DMA((plan.bits,)),
            pltpu.SemaphoreType.DMA((plan.bits,)),
        ],
        compiler_params=params(58),
        cost_estimate=cost(plan.bits * plan.rows * plan.rows, 4 * plan.bits * plan.rows * plan.rows),
        name="prepare",
    )(site_bits, op_mask, field, site_coupling, mode_coupling, operators)
    initial, raw, sums, masked = pl.pallas_call(
        functools.partial(first_kernel, plan),
        out_shape=[vector, vector, jax.ShapeDtypeStruct((plan.groups * EXTRA, LANES), f32), operators_shape],
        in_specs=[VMEM, HBM, VMEM, VMEM],
        out_specs=[VMEM] * 4,
        scratch_shapes=[rounded, pltpu.SemaphoreType.DMA((plan.bits,))],
        compiler_params=params(40),
        cost_estimate=cost(work, 4 * plan.places * plan.rows),
        name="first",
    )(arrived, stored, place, inside)
    tables = (masked, place, inside)
    sums = exchange(plan, sums)
    current, raw, departing, moment_one = pl.pallas_call(
        functools.partial(later_kernel, plan, 0, True),
        out_shape=[vector, vector, message, moment],
        in_specs=[VMEM] * 7,
        out_specs=[VMEM] * 4,
        scratch_shapes=[rounded],
        compiler_params=params(32),
        cost_estimate=cost(work, 4 * plan.places * plan.rows),
        name="second",
    )(sums, raw, initial, initial, *tables)
    before = exchange(plan, departing)
    departing, moment_two = pl.pallas_call(
        functools.partial(later_kernel, plan, plan.body, False),
        out_shape=[message, moment],
        in_specs=[VMEM] * 7,
        out_specs=[VMEM] * 2,
        scratch_shapes=[rounded, kept, kept],
        compiler_params=params(32),
        cost_estimate=cost(work, 4 * plan.places * plan.rows),
        name="third",
    )(before, raw, current, initial, *tables)
    last = exchange(plan, departing)
    before = pl.pallas_call(
        functools.partial(arrive_kernel, plan),
        out_shape=held,
        in_specs=[VMEM],
        out_specs=VMEM,
        compiler_params=params(16),
        cost_estimate=cost(plan.places * plan.rows, 8 * plan.places * plan.rows),
        name="arrive_before",
    )(before)
    last, moments = pl.pallas_call(
        functools.partial(arrive_kernel, plan),
        out_shape=[held, jax.ShapeDtypeStruct((STEPS,), f32)],
        in_specs=[VMEM] * 3,
        out_specs=[VMEM, SMEM],
        compiler_params=params(16),
        name="arrive_last",
    )(last, moment_one, moment_two)
    return last, before, moments


def extended_2(block, sides, width):
    for axis, dim in sides:
        count = lax.axis_size(axis)
        forward = [(i, i + 1) for i in range(count - 1)]
        backward = [(target, source) for source, target in forward]
        low = lax.ppermute(
            lax.slice_in_dim(block, block.shape[dim] - width, None, axis=dim), axis, forward
        )
        high = lax.ppermute(lax.slice_in_dim(block, 0, width, axis=dim), axis, backward)
        block = jnp.concatenate([low, block, high], axis=dim)
    return block


def partner(value, axis, bit):
    mask = 2**bit
    pairs = [(source, source ^ mask) for source in range(lax.axis_size(axis))]
    return lax.ppermute(value, axis, pairs)


def halo_shards(state, operators, op_mask, site_bits, field, site_coupling, mode_coupling):
    site_count = lax.axis_size("site")
    phonon_count = lax.axis_size("phonon")
    bit_count = site_count.bit_length() - 1
    rows_here = state.shape[0]
    columns_here = state.shape[1]
    levels_here = columns_here // MODES
    block_edge = rows_here // op_mask.shape[1]
    expanded = jnp.repeat(jnp.repeat(op_mask, block_edge, axis=1), block_edge, axis=2)
    masked = jnp.where(expanded > 0, operators, jnp.zeros((), jnp.bfloat16))
    entries = jnp.float32(rows_here * columns_here * site_count * phonon_count)
    level_total = jnp.sqrt(jnp.float32(levels_here * phonon_count))
    device = lax.axis_index("site")
    inside = lax.iota(jnp.int32, rows_here)
    weight_rows = jnp.zeros((rows_here,), jnp.float32)
    for position in range(bit_count):
        weight_rows = weight_rows + site_coupling[site_bits[position]] * (
            device >> position & 1
        ).astype(jnp.float32)
    for local_bit in range(LBITS):
        weight_rows = weight_rows + site_coupling[bit_count + local_bit] * (
            inside >> local_bit & 1
        ).astype(jnp.float32)
    levels = (
        lax.axis_index("phonon") * levels_here + lax.iota(jnp.int32, columns_here) // MODES
    ).astype(jnp.float32)
    lower_weight = jnp.sqrt(levels)
    upper_weight = jnp.sqrt(levels + 1.0)
    mode_weight = jnp.tile(mode_coupling, columns_here // MODES) / level_total
    start_squares = lax.psum(jnp.sum(state * state), ("site", "phonon"))
    initial = state / jnp.sqrt(start_squares / entries + epsilon)
    previous = initial
    current = initial
    scale_prev = jnp.float32(1.0)
    moments = []
    for iteration in range(STEPS):
        extended = extended_2(current, (("phonon", 1),), MODES)
        lower_part = extended[:, :columns_here]
        upper_part = extended[:, 2 * MODES :]
        summed = weight_rows[:, None] * (
            mode_weight * (lower_weight * lower_part + upper_weight * upper_part)
        )
        for operate_position in range(bit_count):
            chosen = site_bits[operate_position]
            flipped = partner(current, "site", operate_position)
            product = jnp.dot(
                masked[chosen], flipped.astype(jnp.bfloat16), preferred_element_type=jnp.float32
            )
            summed = summed + (field[chosen] * flipped + product)
        if iteration == 0:
            vector_new = summed
        else:
            vector_new = 2.0 * summed - previous / scale_prev
        squares, intersection = lax.psum(
            (jnp.sum(vector_new * vector_new), jnp.sum(initial * vector_new)), ("site", "phonon")
        )
        scale_now = jnp.sqrt(squares / entries + epsilon)
        updated = vector_new / scale_now
        moment = intersection / (entries * scale_now)
        moments.append(moment)
        previous = current
        current = updated
        scale_prev = scale_now
    return (current, previous, jnp.stack(moments))


def solution(mesh):
    in_specs = (P("site", "phonon"), P(), P(), P(), P(), P(), P())
    out_specs = (P("site", "phonon"), P("site", "phonon"), P())

    def whole(state, operators, op_mask, *rest):
        rows = state.shape[0] // mesh.shape["site"]
        columns = state.shape[1] // mesh.shape["phonon"]
        plan = Plan(mesh, rows, columns, op_mask.shape[1])
        body = functools.partial(shards, plan) if plan.fits() else halo_shards
        run = jax.shard_map(body, mesh=mesh, in_specs=in_specs, out_specs=out_specs, check_vma=False)
        return run(state, operators, op_mask, *rest)

    return whole
```

```python
import functools

import jax
import jax.numpy as jnp
from jax import lax
from jax.experimental import pallas as pl
from jax.experimental.pallas import tpu as pltpu
from jax.sharding import PartitionSpec as P

LBITS = 10
MODES = 64
STEPS = 3
LANES = 128
SUBLANES = 8
EXTRA = 2
AXES = ("site", "phonon")

epsilon = 1e-06


VMEM = pl.BlockSpec(memory_space=pltpu.VMEM)
SMEM = pl.BlockSpec(memory_space=pltpu.SMEM)


class Plan:
    def __init__(self, mesh, rows, columns, blocks):
        self.sites = mesh.shape["site"]
        self.phonons = mesh.shape["phonon"]
        self.groups = self.sites * self.phonons
        self.bits = self.sites.bit_length() - 1
        self.rows = rows
        self.columns = columns
        self.blocks = blocks
        self.edge = rows // blocks
        self.levels_here = columns // MODES
        self.level_count = self.levels_here * self.phonons
        self.share = MODES // self.groups
        self.pieces = self.levels_here * self.share
        self.lane_blocks = rows // LANES
        self.body = self.pieces * self.lane_blocks
        self.message = self.body + EXTRA
        self.places = self.pieces * self.groups
        self.entries = float(rows * columns * self.groups)

    def fits(self):
        return (
            MODES % self.groups == 0
            and self.columns == LANES
            and self.rows % LANES == 0
            and self.edge % LANES == 0
            and self.groups % SUBLANES == 0
        )


def params(mib):
    return pltpu.CompilerParams(vmem_limit_bytes=mib * 2**20)


def lane_sums(values):
    return jnp.sum(values, axis=0, keepdims=True)


def put_extra(plan, out_ref, sums, start, stride):
    for index, value in enumerate(sums):
        out_ref[pl.ds(start + index, plan.groups, stride=stride), :] = jnp.broadcast_to(value, (plan.groups, LANES))


def put_sums(sums_ref, sums):
    for index, value in enumerate(sums):
        sums_ref[pl.ds(index, 1), :] = value
    sums_ref[pl.ds(len(sums), SUBLANES - len(sums)), :] = jnp.zeros((SUBLANES - len(sums), LANES), jnp.float32)


def total_of(plan, ref, start, stride):
    lanes = lane_sums(ref[pl.ds(start, plan.groups, stride=stride), :])
    return jnp.sum(lanes, axis=1, keepdims=True)


def scale_of(plan, squares):
    return jnp.sqrt(squares / plan.entries + epsilon)


def depart_kernel(plan, state_ref, out_ref):
    sums = jnp.zeros((1, LANES), jnp.float32)
    for block in range(plan.lane_blocks):
        tile = state_ref[pl.ds(block * LANES, LANES), :]
        sums = sums + lane_sums(tile * tile)
        turned = tile.T
        for piece in range(plan.pieces):
            out_ref[pl.ds(piece * plan.lane_blocks + block, plan.groups, stride=plan.message), :] = turned[
                piece * plan.groups : (piece + 1) * plan.groups
            ]
    put_extra(plan, out_ref, (sums, jnp.zeros_like(sums)), plan.body, plan.message)


def prepare_kernel(
    plan, bits_ref, mask_ref, field_ref, coupling_ref, mode_ref, operators_ref, masked_ref, place_ref, inside_ref
):
    me = lax.axis_index("site") * plan.phonons + lax.axis_index("phonon")
    for position in range(plan.bits):
        chosen = bits_ref[position]
        for across in range(plan.blocks):
            rows = pl.ds(across * plan.edge, plan.edge)
            for along in range(plan.blocks):
                columns = pl.ds(along * plan.edge, plan.edge)
                keep = (mask_ref[chosen, across, along] > 0).astype(jnp.float32).astype(jnp.bfloat16)
                masked_ref[position, rows, columns] = operators_ref[chosen, rows, columns] * keep
    place = lax.broadcasted_iota(jnp.int32, (plan.places, LANES), 0)
    phonon = place % plan.phonons
    site = place // plan.phonons % plan.sites
    mode = place // plan.groups % plan.share
    level = phonon * plan.levels_here + place // (plan.groups * plan.share)
    occupied = jnp.zeros((plan.places, LANES), jnp.float32)
    for position in range(plan.bits):
        held = (site >> position & 1).astype(jnp.float32)
        occupied = occupied + coupling_ref[bits_ref[position]] * held
    strength = jnp.zeros((plan.places, LANES), jnp.float32)
    for index in range(plan.share):
        strength = jnp.where(mode == index, mode_ref[index * plan.groups + me], strength)
    strength = strength / jnp.sqrt(jnp.full((1, LANES), plan.level_count, jnp.float32))
    height = level.astype(jnp.float32)
    place_ref[0] = occupied
    place_ref[1] = strength * jnp.sqrt(height)
    place_ref[2] = jnp.where(level == plan.level_count - 1, 0.0, strength * jnp.sqrt(height + 1.0))
    for position in range(plan.bits):
        place_ref[3 + position] = jnp.full((plan.places, LANES), field_ref[bits_ref[position]])
    inside = lax.broadcasted_iota(jnp.int32, (SUBLANES, plan.rows), 1)
    weight = jnp.zeros((SUBLANES, plan.rows), jnp.float32)
    for local_bit in range(LBITS):
        weight = weight + coupling_ref[plan.bits + local_bit] * (inside >> local_bit & 1).astype(jnp.float32)
    inside_ref[...] = weight


def flipped(values, stride):
    places, width = values.shape
    if stride % SUBLANES == 0:
        shaped = values.reshape(places // (2 * stride), 2, stride, width)
        return jnp.concatenate([shaped[:, 1:], shaped[:, :1]], axis=1).reshape(places, width)
    tiles = values.reshape(places // SUBLANES, SUBLANES, width)
    if 2 * stride == SUBLANES:
        return pltpu.roll(tiles, stride, 1).reshape(places, width)
    spot = lax.broadcasted_iota(jnp.int32, tiles.shape, 1)
    down = pltpu.roll(tiles, stride, 1)
    up = pltpu.roll(tiles, SUBLANES - stride, 1)
    return jnp.where(spot & stride > 0, down, up).reshape(places, width)


def shifted(values, by):
    places, width = values.shape
    tiles = values.reshape(places // SUBLANES, SUBLANES, width)
    return pltpu.roll(tiles, by % SUBLANES, 1).reshape(places, width)


def operate(plan, vector_ref, masked_ref, place_ref, inside_ref, rounded_ref, total_ref):
    span = plan.places // plan.levels_here
    for block in range(plan.lane_blocks):
        lanes = pl.ds(block * LANES, LANES)
        vector = vector_ref[:, lanes]
        levels = [vector[index * span : (index + 1) * span] for index in range(plan.levels_here)]
        lower = jnp.concatenate([shifted(levels[-1], 1)] + levels[:-1], axis=0)
        upper = jnp.concatenate(levels[1:] + [shifted(levels[0], -1)], axis=0)
        weight = place_ref[0] + inside_ref[:1, lanes]
        total = weight * (place_ref[1] * lower + place_ref[2] * upper)
        for position in range(plan.bits):
            turned = flipped(vector, plan.phonons << position)
            total = total + place_ref[3 + position] * turned
            rounded_ref[:, pl.ds(position * plan.rows + block * LANES, LANES)] = turned.astype(jnp.bfloat16)
        total_ref[:, lanes] = total
    width = 2 * LANES
    for column in range(plan.rows // width):
        lanes = pl.ds(column * width, width)
        total = total_ref[:, lanes]
        for position in range(plan.bits):
            total = total + lax.dot_general(
                rounded_ref[:, pl.ds(position * plan.rows, plan.rows)],
                masked_ref[position, lanes, :],
                (((1,), (1,)), ((), ())),
                preferred_element_type=jnp.float32,
            )
        total_ref[:, lanes] = total


def first_kernel(
    plan, arrived_ref, masked_ref, place_ref, inside_ref, initial_ref, new_ref, sums_ref, rounded_ref
):
    scale = scale_of(plan, total_of(plan, arrived_ref, plan.body, plan.message))
    for piece in range(plan.pieces):
        for block in range(plan.lane_blocks):
            part = arrived_ref[pl.ds(piece * plan.lane_blocks + block, plan.groups, stride=plan.message), :]
            initial_ref[pl.ds(piece * plan.groups, plan.groups), pl.ds(block * LANES, LANES)] = part / scale
    operate(plan, initial_ref, masked_ref, place_ref, inside_ref, rounded_ref, new_ref)
    squares = jnp.zeros((1, LANES), jnp.float32)
    overlap = jnp.zeros((1, LANES), jnp.float32)
    for block in range(plan.lane_blocks):
        lanes = pl.ds(block * LANES, LANES)
        new = new_ref[:, lanes]
        squares = squares + lane_sums(new * new)
        overlap = overlap + lane_sums(new * initial_ref[:, lanes])
    put_sums(sums_ref, (squares, overlap))


def later_kernel(
    plan,
    keep,
    arrived_ref,
    raw_ref,
    previous_ref,
    initial_ref,
    masked_ref,
    place_ref,
    inside_ref,
    *refs,
):
    if keep:
        current_ref, new_ref, out_ref, moment_ref, sums_ref, rounded_ref = refs
    else:
        out_ref, moment_ref, rounded_ref, current_ref, new_ref = refs
    scale = scale_of(plan, total_of(plan, arrived_ref, 0, SUBLANES))
    moment = total_of(plan, arrived_ref, 1, SUBLANES) / (plan.entries * scale)
    moment_ref[...] = jnp.broadcast_to(moment, moment_ref.shape)
    for block in range(plan.lane_blocks):
        lanes = pl.ds(block * LANES, LANES)
        current_ref[:, lanes] = raw_ref[:, lanes] / scale
    operate(plan, current_ref, masked_ref, place_ref, inside_ref, rounded_ref, new_ref)
    squares = jnp.zeros((1, LANES), jnp.float32)
    overlap = jnp.zeros((1, LANES), jnp.float32)
    for block in range(plan.lane_blocks):
        lanes = pl.ds(block * LANES, LANES)
        new = 2.0 * new_ref[:, lanes] - previous_ref[:, lanes] / scale
        squares = squares + lane_sums(new * new)
        overlap = overlap + lane_sums(new * initial_ref[:, lanes])
        if keep:
            new_ref[:, lanes] = new
        for piece in range(plan.pieces):
            out_ref[pl.ds(piece * plan.lane_blocks + block, plan.groups, stride=plan.message), :] = new[
                piece * plan.groups : (piece + 1) * plan.groups
            ]
    put_extra(plan, out_ref, (squares, overlap), plan.body, plan.message)
    if keep:
        put_sums(sums_ref, (squares, overlap))


def arrive_kernel(plan, arrived_ref, *refs):
    scale = scale_of(plan, total_of(plan, arrived_ref, plan.body, plan.message))
    if len(refs) > 1:
        first_ref, second_ref, out_ref, moments_ref = refs
        moment = total_of(plan, arrived_ref, plan.body + 1, plan.message) / (plan.entries * scale)
        moments_ref[0] = first_ref[0, 0]
        moments_ref[1] = second_ref[0, 0]
        moments_ref[2] = moment[0, 0]
    else:
        (out_ref,) = refs
    for block in range(plan.lane_blocks):
        parts = [
            arrived_ref[pl.ds(piece * plan.lane_blocks + block, plan.groups, stride=plan.message), :]
            for piece in range(plan.pieces)
        ]
        out_ref[pl.ds(block * LANES, LANES), :] = (jnp.concatenate(parts, axis=0) / scale).T


def exchange(plan, values):
    rows = values.shape[0] // plan.groups
    shaped = values.reshape(plan.groups, rows // EXTRA, EXTRA, LANES)
    return lax.all_to_all(shaped, AXES, 0, 0, tiled=True).reshape(values.shape)


def gathered(plan, sums):
    return lax.all_gather(sums, AXES, axis=0, tiled=True)


def shards(plan, state, operators, op_mask, site_bits, field, site_coupling, mode_coupling):
    f32 = jnp.float32
    message = jax.ShapeDtypeStruct((plan.groups * plan.message, LANES), f32)
    vector = jax.ShapeDtypeStruct((plan.places, plan.rows), f32)
    moment = jax.ShapeDtypeStruct((SUBLANES, LANES), f32)
    held = jax.ShapeDtypeStruct((plan.rows, plan.columns), f32)
    rounded = pltpu.VMEM((plan.places, plan.bits * plan.rows), jnp.bfloat16)
    kept = pltpu.VMEM((plan.places, plan.rows), f32)
    work = 2 * plan.bits * plan.places * plan.rows * plan.rows

    def cost(flops, moved):
        return pl.CostEstimate(flops=flops, bytes_accessed=moved, transcendentals=0)

    departing = pl.pallas_call(
        functools.partial(depart_kernel, plan),
        out_shape=message,
        in_specs=[VMEM],
        out_specs=VMEM,
        compiler_params=params(16),
        name="depart",
    )(state)
    arrived = exchange(plan, departing)
    masked, place, inside = pl.pallas_call(
        functools.partial(prepare_kernel, plan),
        out_shape=[
            jax.ShapeDtypeStruct((plan.bits, plan.rows, plan.rows), jnp.bfloat16),
            jax.ShapeDtypeStruct((3 + plan.bits, plan.places, LANES), f32),
            jax.ShapeDtypeStruct((SUBLANES, plan.rows), f32),
        ],
        in_specs=[SMEM] * 5 + [VMEM],
        out_specs=[VMEM] * 3,
        compiler_params=params(32),
        cost_estimate=cost(plan.bits * plan.rows * plan.rows, 4 * plan.bits * plan.rows * plan.rows),
        name="prepare",
    )(site_bits, op_mask, field, site_coupling, mode_coupling, operators)
    tables = (masked, place, inside)
    small = jax.ShapeDtypeStruct((SUBLANES, LANES), f32)
    initial, raw, sums = pl.pallas_call(
        functools.partial(first_kernel, plan),
        out_shape=[vector, vector, small],
        in_specs=[VMEM] * 4,
        out_specs=[VMEM] * 3,
        scratch_shapes=[rounded],
        compiler_params=params(32),
        cost_estimate=cost(work, 4 * plan.places * plan.rows),
        name="first",
    )(arrived, *tables)
    sums = gathered(plan, sums)
    current, raw, departing, moment_one, sums = pl.pallas_call(
        functools.partial(later_kernel, plan, True),
        out_shape=[vector, vector, message, moment, small],
        in_specs=[VMEM] * 7,
        out_specs=[VMEM] * 5,
        scratch_shapes=[rounded],
        compiler_params=params(32),
        cost_estimate=cost(work, 4 * plan.places * plan.rows),
        name="second",
    )(sums, raw, initial, initial, *tables)
    before = exchange(plan, departing)
    sums = gathered(plan, sums)
    departing, moment_two = pl.pallas_call(
        functools.partial(later_kernel, plan, False),
        out_shape=[message, moment],
        in_specs=[VMEM] * 7,
        out_specs=[VMEM] * 2,
        scratch_shapes=[rounded, kept, kept],
        compiler_params=params(32),
        cost_estimate=cost(work, 4 * plan.places * plan.rows),
        name="third",
    )(sums, raw, current, initial, *tables)
    last = exchange(plan, departing)
    before = pl.pallas_call(
        functools.partial(arrive_kernel, plan),
        out_shape=held,
        in_specs=[VMEM],
        out_specs=VMEM,
        compiler_params=params(16),
        cost_estimate=cost(plan.places * plan.rows, 8 * plan.places * plan.rows),
        name="arrive_before",
    )(before)
    last, moments = pl.pallas_call(
        functools.partial(arrive_kernel, plan),
        out_shape=[held, jax.ShapeDtypeStruct((STEPS,), f32)],
        in_specs=[VMEM] * 3,
        out_specs=[VMEM, SMEM],
        compiler_params=params(16),
        name="arrive_last",
    )(last, moment_one, moment_two)
    return last, before, moments


def extended_2(block, sides, width):
    for axis, dim in sides:
        count = lax.axis_size(axis)
        forward = [(i, i + 1) for i in range(count - 1)]
        backward = [(target, source) for source, target in forward]
        low = lax.ppermute(
            lax.slice_in_dim(block, block.shape[dim] - width, None, axis=dim), axis, forward
        )
        high = lax.ppermute(lax.slice_in_dim(block, 0, width, axis=dim), axis, backward)
        block = jnp.concatenate([low, block, high], axis=dim)
    return block


def partner(value, axis, bit):
    mask = 2**bit
    pairs = [(source, source ^ mask) for source in range(lax.axis_size(axis))]
    return lax.ppermute(value, axis, pairs)


def halo_shards(state, operators, op_mask, site_bits, field, site_coupling, mode_coupling):
    site_count = lax.axis_size("site")
    phonon_count = lax.axis_size("phonon")
    bit_count = site_count.bit_length() - 1
    rows_here = state.shape[0]
    columns_here = state.shape[1]
    levels_here = columns_here // MODES
    block_edge = rows_here // op_mask.shape[1]
    expanded = jnp.repeat(jnp.repeat(op_mask, block_edge, axis=1), block_edge, axis=2)
    masked = jnp.where(expanded > 0, operators, jnp.zeros((), jnp.bfloat16))
    entries = jnp.float32(rows_here * columns_here * site_count * phonon_count)
    level_total = jnp.sqrt(jnp.float32(levels_here * phonon_count))
    device = lax.axis_index("site")
    inside = lax.iota(jnp.int32, rows_here)
    weight_rows = jnp.zeros((rows_here,), jnp.float32)
    for position in range(bit_count):
        weight_rows = weight_rows + site_coupling[site_bits[position]] * (
            device >> position & 1
        ).astype(jnp.float32)
    for local_bit in range(LBITS):
        weight_rows = weight_rows + site_coupling[bit_count + local_bit] * (
            inside >> local_bit & 1
        ).astype(jnp.float32)
    levels = (
        lax.axis_index("phonon") * levels_here + lax.iota(jnp.int32, columns_here) // MODES
    ).astype(jnp.float32)
    lower_weight = jnp.sqrt(levels)
    upper_weight = jnp.sqrt(levels + 1.0)
    mode_weight = jnp.tile(mode_coupling, columns_here // MODES) / level_total
    start_squares = lax.psum(jnp.sum(state * state), ("site", "phonon"))
    initial = state / jnp.sqrt(start_squares / entries + epsilon)
    previous = initial
    current = initial
    scale_prev = jnp.float32(1.0)
    moments = []
    for iteration in range(STEPS):
        extended = extended_2(current, (("phonon", 1),), MODES)
        lower_part = extended[:, :columns_here]
        upper_part = extended[:, 2 * MODES :]
        summed = weight_rows[:, None] * (
            mode_weight * (lower_weight * lower_part + upper_weight * upper_part)
        )
        for operate_position in range(bit_count):
            chosen = site_bits[operate_position]
            flipped = partner(current, "site", operate_position)
            product = jnp.dot(
                masked[chosen], flipped.astype(jnp.bfloat16), preferred_element_type=jnp.float32
            )
            summed = summed + (field[chosen] * flipped + product)
        if iteration == 0:
            vector_new = summed
        else:
            vector_new = 2.0 * summed - previous / scale_prev
        squares, intersection = lax.psum(
            (jnp.sum(vector_new * vector_new), jnp.sum(initial * vector_new)), ("site", "phonon")
        )
        scale_now = jnp.sqrt(squares / entries + epsilon)
        updated = vector_new / scale_now
        moment = intersection / (entries * scale_now)
        moments.append(moment)
        previous = current
        current = updated
        scale_prev = scale_now
    return (current, previous, jnp.stack(moments))


def solution(mesh):
    in_specs = (P("site", "phonon"), P(), P(), P(), P(), P(), P())
    out_specs = (P("site", "phonon"), P("site", "phonon"), P())

    def whole(state, operators, op_mask, *rest):
        rows = state.shape[0] // mesh.shape["site"]
        columns = state.shape[1] // mesh.shape["phonon"]
        plan = Plan(mesh, rows, columns, op_mask.shape[1])
        body = functools.partial(shards, plan) if plan.fits() else halo_shards
        run = jax.shard_map(body, mesh=mesh, in_specs=in_specs, out_specs=out_specs, check_vma=False)
        return run(state, operators, op_mask, *rest)

    return whole
```

```python
import functools

import jax
import jax.numpy as jnp
from jax import lax
from jax.experimental import pallas as pl
from jax.experimental.pallas import tpu as pltpu
from jax.sharding import PartitionSpec as P

LBITS = 10
MODES = 64
STEPS = 3
LANES = 128
SUBLANES = 8
EXTRA = 1
AXES = ("site", "phonon")

epsilon = 1e-06


VMEM = pl.BlockSpec(memory_space=pltpu.VMEM)
SMEM = pl.BlockSpec(memory_space=pltpu.SMEM)
HBM = pl.BlockSpec(memory_space=pltpu.HBM)


class Plan:
    def __init__(self, mesh, rows, columns, blocks):
        self.sites = mesh.shape["site"]
        self.phonons = mesh.shape["phonon"]
        self.groups = self.sites * self.phonons
        self.bits = self.sites.bit_length() - 1
        self.rows = rows
        self.columns = columns
        self.blocks = blocks
        self.edge = rows // blocks
        self.levels_here = columns // MODES
        self.level_count = self.levels_here * self.phonons
        self.share = MODES // self.groups
        self.pieces = self.levels_here * self.share
        self.lane_blocks = rows // LANES
        self.body = self.pieces * self.lane_blocks
        self.message = self.body + EXTRA
        self.places = self.pieces * self.groups
        self.entries = float(rows * columns * self.groups)

    def fits(self):
        return (
            MODES % self.groups == 0
            and self.columns == LANES
            and self.rows % LANES == 0
            and self.edge % LANES == 0
            and self.groups % SUBLANES == 0
        )


def params(mib):
    return pltpu.CompilerParams(vmem_limit_bytes=mib * 2**20)


def lane_sums(values):
    return jnp.sum(values, axis=0, keepdims=True)


def folded(value):
    return value + pltpu.roll(value, LANES // 2, 1)


def put_sums(plan, out_ref, squares, overlap, start, stride):
    lane = lax.broadcasted_iota(jnp.int32, (1, LANES), 1)
    row = jnp.where(lane < LANES // 2, folded(squares), folded(overlap))
    out_ref[pl.ds(start, plan.groups, stride=stride), :] = jnp.broadcast_to(row, (plan.groups, LANES))


def totals_of(plan, ref, start, stride):
    lanes = lane_sums(ref[pl.ds(start, plan.groups, stride=stride), :])
    lane = lax.broadcasted_iota(jnp.int32, (1, LANES), 1)
    squares = jnp.sum(jnp.where(lane < LANES // 2, lanes, 0.0), axis=1, keepdims=True)
    overlap = jnp.sum(jnp.where(lane < LANES // 2, 0.0, lanes), axis=1, keepdims=True)
    return squares, overlap


def scale_of(plan, squares):
    return jnp.sqrt(squares / plan.entries + epsilon)


def depart_kernel(plan, state_ref, out_ref):
    sums = jnp.zeros((1, LANES), jnp.float32)
    for block in range(plan.lane_blocks):
        tile = state_ref[pl.ds(block * LANES, LANES), :]
        sums = sums + lane_sums(tile * tile)
        turned = tile.T
        for piece in range(plan.pieces):
            out_ref[pl.ds(piece * plan.lane_blocks + block, plan.groups, stride=plan.message), :] = turned[
                piece * plan.groups : (piece + 1) * plan.groups
            ]
    put_sums(plan, out_ref, sums, jnp.zeros_like(sums), plan.body, plan.message)


def prepare_kernel(
    plan, bits_ref, mask_ref, field_ref, coupling_ref, mode_ref, operators_ref, place_ref, inside_ref, *masked_refs
):
    me = lax.axis_index("site") * plan.phonons + lax.axis_index("phonon")
    for position in range(plan.bits):
        chosen = bits_ref[position]
        for across in range(plan.blocks):
            rows = pl.ds(across * plan.edge, plan.edge)
            for along in range(plan.blocks):
                columns = pl.ds(along * plan.edge, plan.edge)
                keep = (mask_ref[chosen, across, along] > 0).astype(jnp.float32).astype(jnp.bfloat16)
                masked_refs[position][rows, columns] = operators_ref[chosen, rows, columns] * keep
    place = lax.broadcasted_iota(jnp.int32, (plan.places, LANES), 0)
    phonon = place % plan.phonons
    site = place // plan.phonons % plan.sites
    mode = place // plan.groups % plan.share
    level = phonon * plan.levels_here + place // (plan.groups * plan.share)
    occupied = jnp.zeros((plan.places, LANES), jnp.float32)
    for position in range(plan.bits):
        held = (site >> position & 1).astype(jnp.float32)
        occupied = occupied + coupling_ref[bits_ref[position]] * held
    strength = jnp.zeros((plan.places, LANES), jnp.float32)
    for index in range(plan.share):
        strength = jnp.where(mode == index, mode_ref[index * plan.groups + me], strength)
    strength = strength / jnp.sqrt(jnp.full((1, LANES), plan.level_count, jnp.float32))
    height = level.astype(jnp.float32)
    place_ref[0] = occupied
    place_ref[1] = strength * jnp.sqrt(height)
    place_ref[2] = jnp.where(level == plan.level_count - 1, 0.0, strength * jnp.sqrt(height + 1.0))
    for position in range(plan.bits):
        place_ref[3 + position] = jnp.full((plan.places, LANES), field_ref[bits_ref[position]])
    inside = lax.broadcasted_iota(jnp.int32, (SUBLANES, plan.rows), 1)
    weight = jnp.zeros((SUBLANES, plan.rows), jnp.float32)
    for local_bit in range(LBITS):
        weight = weight + coupling_ref[plan.bits + local_bit] * (inside >> local_bit & 1).astype(jnp.float32)
    inside_ref[...] = weight


def flipped(values, stride):
    places, width = values.shape
    if stride % SUBLANES == 0:
        shaped = values.reshape(places // (2 * stride), 2, stride, width)
        return jnp.concatenate([shaped[:, 1:], shaped[:, :1]], axis=1).reshape(places, width)
    tiles = values.reshape(places // SUBLANES, SUBLANES, width)
    if 2 * stride == SUBLANES:
        return pltpu.roll(tiles, stride, 1).reshape(places, width)
    spot = lax.broadcasted_iota(jnp.int32, tiles.shape, 1)
    down = pltpu.roll(tiles, stride, 1)
    up = pltpu.roll(tiles, SUBLANES - stride, 1)
    return jnp.where(spot & stride > 0, down, up).reshape(places, width)


def shifted(values, by):
    places, width = values.shape
    tiles = values.reshape(places // SUBLANES, SUBLANES, width)
    return pltpu.roll(tiles, by % SUBLANES, 1).reshape(places, width)


def step(plan, vector_ref, masked_refs, place_ref, inside_ref, rounded_ref, finish, fetches=()):
    span = plan.places // plan.levels_here
    for block in range(plan.lane_blocks):
        vector = vector_ref[:, pl.ds(block * LANES, LANES)]
        for position in range(plan.bits):
            rounded_ref[:, pl.ds(position * plan.rows + block * LANES, LANES)] = flipped(
                vector, plan.phonons << position
            ).astype(jnp.bfloat16)

    def local(start):
        lanes = pl.ds(start, LANES)
        vector = vector_ref[:, lanes]
        levels = [vector[index * span : (index + 1) * span] for index in range(plan.levels_here)]
        lower = jnp.concatenate([shifted(levels[-1], 1)] + levels[:-1], axis=0)
        upper = jnp.concatenate(levels[1:] + [shifted(levels[0], -1)], axis=0)
        weight = place_ref[0] + inside_ref[:1, lanes]
        total = weight * (place_ref[1] * lower + place_ref[2] * upper)
        for position in range(plan.bits):
            total = total + place_ref[3 + position, :1] * flipped(vector, plan.phonons << position)
        return total

    def product(lanes, position):
        return lax.dot_general(
            rounded_ref[:, pl.ds(position * plan.rows, plan.rows)],
            masked_refs[position][lanes, :],
            (((1,), (1,)), ((), ())),
            preferred_element_type=jnp.float32,
        )

    early = range(plan.bits - len(fetches))
    late = range(plan.bits - len(fetches), plan.bits)
    width = 2 * LANES
    parts = [pl.ds(start, width) for start in range(0, plan.rows, width)]

    def begun(lanes):
        total = jnp.concatenate([local(start) for start in range(lanes.start, lanes.start + width, LANES)], axis=1)
        for position in early:
            total = total + product(lanes, position)
        return total

    if not fetches:
        for lanes in parts:
            finish(lanes, begun(lanes))
        return
    held_ref = fetches[0][0]
    for lanes in parts:
        held_ref[:, lanes] = begun(lanes)
    for _, fetch in fetches:
        fetch.wait()
    for lanes in parts:
        total = held_ref[:, lanes]
        for position in late:
            total = total + product(lanes, position)
        finish(lanes, total)


def first_kernel(plan, arrived_ref, place_ref, inside_ref, *refs):
    kept = 1
    masked_refs = refs[:kept]
    stored_refs = refs[kept : plan.bits]
    initial_ref, new_ref, sums_ref = refs[plan.bits : plan.bits + 3]
    fetched_refs = refs[plan.bits + 3 : -2]
    rounded_ref, semaphores = refs[-2:]
    fetches = []
    for index, (stored_ref, fetched_ref) in enumerate(zip(stored_refs, fetched_refs)):
        fetch = pltpu.make_async_copy(stored_ref, fetched_ref, semaphores.at[index])
        fetch.start()
        fetches.append((new_ref, fetch))
    squares, _ = totals_of(plan, arrived_ref, plan.body, plan.message)
    inverse = 1.0 / scale_of(plan, squares)
    for piece in range(plan.pieces):
        for block in range(plan.lane_blocks):
            part = arrived_ref[pl.ds(piece * plan.lane_blocks + block, plan.groups, stride=plan.message), :]
            initial_ref[pl.ds(piece * plan.groups, plan.groups), pl.ds(block * LANES, LANES)] = part * inverse
    squares = []
    overlap = []

    def finish(lanes, new):
        new_ref[:, lanes] = new
        squares.append(lane_sums(new * new))
        overlap.append(lane_sums(new * initial_ref[:, lanes]))

    step(
        plan, initial_ref, (*masked_refs, *fetched_refs), place_ref, inside_ref, rounded_ref, finish, fetches
    )
    put_sums(plan, sums_ref, one_row(squares), one_row(overlap), 0, EXTRA)


def one_row(rows):
    total = sum(rows[1:], rows[0])
    return sum(total[:, start : start + LANES] for start in range(0, total.shape[1], LANES))


def later_kernel(plan, body, keep, arrived_ref, raw_ref, previous_ref, initial_ref, place_ref, inside_ref, *refs):
    masked_refs = refs[: plan.bits]
    if keep:
        current_ref, new_ref, out_ref, moment_ref, rounded_ref = refs[plan.bits :]
    else:
        out_ref, moment_ref, rounded_ref, current_ref = refs[plan.bits :]
    squares, overlap = totals_of(plan, arrived_ref, body, body + EXTRA)
    inverse = 1.0 / scale_of(plan, squares)
    moment_ref[...] = jnp.broadcast_to(overlap * inverse / plan.entries, moment_ref.shape)
    for block in range(plan.lane_blocks):
        lanes = pl.ds(block * LANES, LANES)
        current_ref[:, lanes] = raw_ref[:, lanes] * inverse
    squares = []
    overlap = []

    def finish(lanes, total):
        new = 2.0 * total - previous_ref[:, lanes] * inverse
        if keep:
            new_ref[:, lanes] = new
        squares.append(lane_sums(new * new))
        overlap.append(lane_sums(new * initial_ref[:, lanes]))
        for start in range(0, lanes.size, LANES):
            block = (lanes.start + start) // LANES
            for piece in range(plan.pieces):
                out_ref[pl.ds(piece * plan.lane_blocks + block, plan.groups, stride=plan.message), :] = new[
                    piece * plan.groups : (piece + 1) * plan.groups, start : start + LANES
                ]

    step(plan, current_ref, masked_refs, place_ref, inside_ref, rounded_ref, finish)
    put_sums(plan, out_ref, one_row(squares), one_row(overlap), plan.body, plan.message)


def arrive_kernel(plan, arrived_ref, *refs):
    squares, overlap = totals_of(plan, arrived_ref, plan.body, plan.message)
    inverse = 1.0 / scale_of(plan, squares)
    if len(refs) > 1:
        first_ref, second_ref, out_ref, moments_ref = refs
        moment = overlap * inverse / plan.entries
        moments_ref[0] = first_ref[0, 0]
        moments_ref[1] = second_ref[0, 0]
        moments_ref[2] = moment[0, 0]
    else:
        (out_ref,) = refs
    for block in range(plan.lane_blocks):
        parts = [
            arrived_ref[pl.ds(piece * plan.lane_blocks + block, plan.groups, stride=plan.message), :]
            for piece in range(plan.pieces)
        ]
        out_ref[pl.ds(block * LANES, LANES), :] = (jnp.concatenate(parts, axis=0) * inverse).T


def exchange(plan, values):
    rows = values.shape[0] // plan.groups
    shaped = values.reshape(plan.groups, rows // EXTRA, EXTRA, LANES)
    return lax.all_to_all(shaped, AXES, 0, 0, tiled=True).reshape(values.shape)


def shards(plan, state, operators, op_mask, site_bits, field, site_coupling, mode_coupling):
    f32 = jnp.float32
    message = jax.ShapeDtypeStruct((plan.groups * plan.message, LANES), f32)
    vector = jax.ShapeDtypeStruct((plan.places, plan.rows), f32)
    moment = jax.ShapeDtypeStruct((SUBLANES, LANES), f32)
    held = jax.ShapeDtypeStruct((plan.rows, plan.columns), f32)
    rounded = pltpu.VMEM((plan.places, plan.bits * plan.rows), jnp.bfloat16)
    kept = pltpu.VMEM((plan.places, plan.rows), f32)
    work = 2 * plan.bits * plan.places * plan.rows * plan.rows

    def cost(flops, moved):
        return pl.CostEstimate(flops=flops, bytes_accessed=moved, transcendentals=0)

    departing = pl.pallas_call(
        functools.partial(depart_kernel, plan),
        out_shape=message,
        in_specs=[VMEM],
        out_specs=VMEM,
        compiler_params=params(16),
        name="depart",
    )(state)
    arrived = exchange(plan, departing)
    operator = jax.ShapeDtypeStruct((plan.rows, plan.rows), jnp.bfloat16)
    place, inside, *masked = pl.pallas_call(
        functools.partial(prepare_kernel, plan),
        out_shape=[
            jax.ShapeDtypeStruct((3 + plan.bits, plan.places, LANES), f32),
            jax.ShapeDtypeStruct((SUBLANES, plan.rows), f32),
        ]
        + [operator] * plan.bits,
        in_specs=[SMEM] * 5 + [VMEM],
        out_specs=[VMEM] * (2 + plan.bits),
        compiler_params=params(32),
        cost_estimate=cost(plan.bits * plan.rows * plan.rows, 4 * plan.bits * plan.rows * plan.rows),
        name="prepare",
    )(site_bits, op_mask, field, site_coupling, mode_coupling, operators)
    fetched = plan.bits - 1
    initial, raw, sums, *fetched_masked = pl.pallas_call(
        functools.partial(first_kernel, plan),
        out_shape=[vector, vector, jax.ShapeDtypeStruct((plan.groups * EXTRA, LANES), f32)] + [operator] * fetched,
        in_specs=[VMEM] * 4 + [HBM] * fetched,
        out_specs=[VMEM] * (3 + fetched),
        scratch_shapes=[rounded, pltpu.SemaphoreType.DMA((fetched,))],
        compiler_params=params(32),
        cost_estimate=cost(work, 4 * plan.places * plan.rows),
        name="first",
    )(arrived, place, inside, *masked)
    tables = (place, inside, masked[0], *fetched_masked)
    sums = exchange(plan, sums)
    current, raw, departing, moment_one = pl.pallas_call(
        functools.partial(later_kernel, plan, 0, True),
        out_shape=[vector, vector, message, moment],
        in_specs=[VMEM] * (6 + plan.bits),
        out_specs=[VMEM] * 4,
        scratch_shapes=[rounded],
        compiler_params=params(32),
        cost_estimate=cost(work, 4 * plan.places * plan.rows),
        name="second",
    )(sums, raw, initial, initial, *tables)
    before = exchange(plan, departing)
    departing, moment_two = pl.pallas_call(
        functools.partial(later_kernel, plan, plan.body, False),
        out_shape=[message, moment],
        in_specs=[VMEM] * (6 + plan.bits),
        out_specs=[VMEM] * 2,
        scratch_shapes=[rounded, kept],
        compiler_params=params(32),
        cost_estimate=cost(work, 4 * plan.places * plan.rows),
        name="third",
    )(before, raw, current, initial, *tables)
    last = exchange(plan, departing)
    before = pl.pallas_call(
        functools.partial(arrive_kernel, plan),
        out_shape=held,
        in_specs=[VMEM],
        out_specs=VMEM,
        compiler_params=params(16),
        cost_estimate=cost(plan.places * plan.rows, 8 * plan.places * plan.rows),
        name="arrive_before",
    )(before)
    last, moments = pl.pallas_call(
        functools.partial(arrive_kernel, plan),
        out_shape=[held, jax.ShapeDtypeStruct((STEPS,), f32)],
        in_specs=[VMEM] * 3,
        out_specs=[VMEM, SMEM],
        compiler_params=params(16),
        name="arrive_last",
    )(last, moment_one, moment_two)
    return last, before, moments


def extended_2(block, sides, width):
    for axis, dim in sides:
        count = lax.axis_size(axis)
        forward = [(i, i + 1) for i in range(count - 1)]
        backward = [(target, source) for source, target in forward]
        low = lax.ppermute(
            lax.slice_in_dim(block, block.shape[dim] - width, None, axis=dim), axis, forward
        )
        high = lax.ppermute(lax.slice_in_dim(block, 0, width, axis=dim), axis, backward)
        block = jnp.concatenate([low, block, high], axis=dim)
    return block


def partner(value, axis, bit):
    mask = 2**bit
    pairs = [(source, source ^ mask) for source in range(lax.axis_size(axis))]
    return lax.ppermute(value, axis, pairs)


def halo_shards(state, operators, op_mask, site_bits, field, site_coupling, mode_coupling):
    site_count = lax.axis_size("site")
    phonon_count = lax.axis_size("phonon")
    bit_count = site_count.bit_length() - 1
    rows_here = state.shape[0]
    columns_here = state.shape[1]
    levels_here = columns_here // MODES
    block_edge = rows_here // op_mask.shape[1]
    expanded = jnp.repeat(jnp.repeat(op_mask, block_edge, axis=1), block_edge, axis=2)
    masked = jnp.where(expanded > 0, operators, jnp.zeros((), jnp.bfloat16))
    entries = jnp.float32(rows_here * columns_here * site_count * phonon_count)
    level_total = jnp.sqrt(jnp.float32(levels_here * phonon_count))
    device = lax.axis_index("site")
    inside = lax.iota(jnp.int32, rows_here)
    weight_rows = jnp.zeros((rows_here,), jnp.float32)
    for position in range(bit_count):
        weight_rows = weight_rows + site_coupling[site_bits[position]] * (
            device >> position & 1
        ).astype(jnp.float32)
    for local_bit in range(LBITS):
        weight_rows = weight_rows + site_coupling[bit_count + local_bit] * (
            inside >> local_bit & 1
        ).astype(jnp.float32)
    levels = (
        lax.axis_index("phonon") * levels_here + lax.iota(jnp.int32, columns_here) // MODES
    ).astype(jnp.float32)
    lower_weight = jnp.sqrt(levels)
    upper_weight = jnp.sqrt(levels + 1.0)
    mode_weight = jnp.tile(mode_coupling, columns_here // MODES) / level_total
    start_squares = lax.psum(jnp.sum(state * state), ("site", "phonon"))
    initial = state / jnp.sqrt(start_squares / entries + epsilon)
    previous = initial
    current = initial
    scale_prev = jnp.float32(1.0)
    moments = []
    for iteration in range(STEPS):
        extended = extended_2(current, (("phonon", 1),), MODES)
        lower_part = extended[:, :columns_here]
        upper_part = extended[:, 2 * MODES :]
        summed = weight_rows[:, None] * (
            mode_weight * (lower_weight * lower_part + upper_weight * upper_part)
        )
        for operate_position in range(bit_count):
            chosen = site_bits[operate_position]
            flipped = partner(current, "site", operate_position)
            product = jnp.dot(
                masked[chosen], flipped.astype(jnp.bfloat16), preferred_element_type=jnp.float32
            )
            summed = summed + (field[chosen] * flipped + product)
        if iteration == 0:
            vector_new = summed
        else:
            vector_new = 2.0 * summed - previous / scale_prev
        squares, intersection = lax.psum(
            (jnp.sum(vector_new * vector_new), jnp.sum(initial * vector_new)), ("site", "phonon")
        )
        scale_now = jnp.sqrt(squares / entries + epsilon)
        updated = vector_new / scale_now
        moment = intersection / (entries * scale_now)
        moments.append(moment)
        previous = current
        current = updated
        scale_prev = scale_now
    return (current, previous, jnp.stack(moments))


def solution(mesh):
    in_specs = (P("site", "phonon"), P(), P(), P(), P(), P(), P())
    out_specs = (P("site", "phonon"), P("site", "phonon"), P())

    def whole(state, operators, op_mask, *rest):
        rows = state.shape[0] // mesh.shape["site"]
        columns = state.shape[1] // mesh.shape["phonon"]
        plan = Plan(mesh, rows, columns, op_mask.shape[1])
        body = functools.partial(shards, plan) if plan.fits() else halo_shards
        run = jax.shard_map(body, mesh=mesh, in_specs=in_specs, out_specs=out_specs, check_vma=False)
        return run(state, operators, op_mask, *rest)

    return whole
```

```python
import functools

import jax
import jax.numpy as jnp
from jax import lax
from jax.experimental import pallas as pl
from jax.experimental.pallas import tpu as pltpu
from jax.sharding import PartitionSpec as P

LBITS = 10
MODES = 64
STEPS = 3
LANES = 128
SUBLANES = 8
EXTRA = 1
AXES = ("site", "phonon")

epsilon = 1e-06


VMEM = pl.BlockSpec(memory_space=pltpu.VMEM)
SMEM = pl.BlockSpec(memory_space=pltpu.SMEM)
HBM = pl.BlockSpec(memory_space=pltpu.HBM)


class Plan:
    def __init__(self, mesh, rows, columns, blocks):
        self.sites = mesh.shape["site"]
        self.phonons = mesh.shape["phonon"]
        self.groups = self.sites * self.phonons
        self.bits = self.sites.bit_length() - 1
        self.rows = rows
        self.columns = columns
        self.blocks = blocks
        self.edge = rows // blocks
        self.levels_here = columns // MODES
        self.level_count = self.levels_here * self.phonons
        self.share = MODES // self.groups
        self.pieces = self.levels_here * self.share
        self.lane_blocks = rows // LANES
        self.body = self.pieces * self.lane_blocks
        self.message = self.body + EXTRA
        self.places = self.pieces * self.groups
        self.entries = float(rows * columns * self.groups)

    def fits(self):
        return (
            MODES % self.groups == 0
            and self.columns == LANES
            and self.rows % LANES == 0
            and self.edge % LANES == 0
            and self.groups % SUBLANES == 0
        )


def params(mib):
    return pltpu.CompilerParams(vmem_limit_bytes=mib * 2**20)


def lane_sums(values):
    return jnp.sum(values, axis=0, keepdims=True)


def folded(value):
    return value + pltpu.roll(value, LANES // 2, 1)


def put_sums(plan, out_ref, squares, overlap, start, stride):
    lane = lax.broadcasted_iota(jnp.int32, (1, LANES), 1)
    row = jnp.where(lane < LANES // 2, folded(squares), folded(overlap))
    out_ref[pl.ds(start, plan.groups, stride=stride), :] = jnp.broadcast_to(row, (plan.groups, LANES))


def totals_of(plan, ref, start, stride):
    lanes = lane_sums(ref[pl.ds(start, plan.groups, stride=stride), :])
    lane = lax.broadcasted_iota(jnp.int32, (1, LANES), 1)
    squares = jnp.sum(jnp.where(lane < LANES // 2, lanes, 0.0), axis=1, keepdims=True)
    overlap = jnp.sum(jnp.where(lane < LANES // 2, 0.0, lanes), axis=1, keepdims=True)
    return squares, overlap


def scale_of(plan, squares):
    return jnp.sqrt(squares / plan.entries + epsilon)


def depart_kernel(plan, state_ref, out_ref):
    sums = jnp.zeros((1, LANES), jnp.float32)
    for block in range(plan.lane_blocks):
        tile = state_ref[pl.ds(block * LANES, LANES), :]
        sums = sums + lane_sums(tile * tile)
        turned = tile.T
        for piece in range(plan.pieces):
            out_ref[pl.ds(piece * plan.lane_blocks + block, plan.groups, stride=plan.message), :] = turned[
                piece * plan.groups : (piece + 1) * plan.groups
            ]
    put_sums(plan, out_ref, sums, jnp.zeros_like(sums), plan.body, plan.message)


def mask_operator(plan, chosen, mask_ref, held_ref, out_ref):
    for across in range(plan.blocks):
        rows = pl.ds(across * plan.edge, plan.edge)
        for along in range(plan.blocks):
            columns = pl.ds(along * plan.edge, plan.edge)
            keep = (mask_ref[chosen, across, along] > 0).astype(jnp.float32).astype(jnp.bfloat16)
            out_ref[columns, rows] = (held_ref[rows, columns] * keep).T


def store_kernel(plan, kept, bits_ref, mask_ref, operators_ref, *refs):
    count = plan.bits - kept
    stored_refs, (held_ref, masked_ref, in_semaphores, out_semaphores) = refs[:count], refs[count:]
    fetches = [
        pltpu.make_async_copy(operators_ref.at[bits_ref[kept + index]], held_ref.at[index], in_semaphores.at[index])
        for index in range(count)
    ]
    for fetch in fetches:
        fetch.start()
    stores = []
    for index in range(count):
        fetches[index].wait()
        mask_operator(plan, bits_ref[kept + index], mask_ref, held_ref.at[index], masked_ref.at[index])
        store = pltpu.make_async_copy(masked_ref.at[index], stored_refs[index], out_semaphores.at[index])
        store.start()
        stores.append(store)
    for store in stores:
        store.wait()


def prepare_kernel(
    plan,
    kept,
    bits_ref,
    mask_ref,
    field_ref,
    coupling_ref,
    mode_ref,
    operators_ref,
    place_ref,
    inside_ref,
    *refs,
):
    masked_refs, (held_ref, semaphores) = refs[:kept], refs[kept:]
    fetches = [
        pltpu.make_async_copy(operators_ref.at[bits_ref[index]], held_ref.at[index], semaphores.at[index])
        for index in range(kept)
    ]
    for fetch in fetches:
        fetch.start()
    me = lax.axis_index("site") * plan.phonons + lax.axis_index("phonon")
    place = lax.broadcasted_iota(jnp.int32, (plan.places, LANES), 0)
    phonon = place % plan.phonons
    site = place // plan.phonons % plan.sites
    mode = place // plan.groups % plan.share
    level = phonon * plan.levels_here + place // (plan.groups * plan.share)
    occupied = jnp.zeros((plan.places, LANES), jnp.float32)
    for position in range(plan.bits):
        held = (site >> position & 1).astype(jnp.float32)
        occupied = occupied + coupling_ref[bits_ref[position]] * held
    strength = jnp.zeros((plan.places, LANES), jnp.float32)
    for index in range(plan.share):
        strength = jnp.where(mode == index, mode_ref[index * plan.groups + me], strength)
    strength = strength / jnp.sqrt(jnp.full((1, LANES), plan.level_count, jnp.float32))
    height = level.astype(jnp.float32)
    place_ref[0] = occupied
    place_ref[1] = strength * jnp.sqrt(height)
    place_ref[2] = jnp.where(level == plan.level_count - 1, 0.0, strength * jnp.sqrt(height + 1.0))
    for position in range(plan.bits):
        place_ref[3 + position] = jnp.full((plan.places, LANES), field_ref[bits_ref[position]])
    inside = lax.broadcasted_iota(jnp.int32, (SUBLANES, plan.rows), 1)
    weight = jnp.zeros((SUBLANES, plan.rows), jnp.float32)
    for local_bit in range(LBITS):
        weight = weight + coupling_ref[plan.bits + local_bit] * (inside >> local_bit & 1).astype(jnp.float32)
    inside_ref[...] = weight
    for index in range(kept):
        fetches[index].wait()
        mask_operator(plan, bits_ref[index], mask_ref, held_ref.at[index], masked_refs[index])


def flipped(values, stride):
    places, width = values.shape
    if stride % SUBLANES == 0:
        shaped = values.reshape(places // (2 * stride), 2, stride, width)
        return jnp.concatenate([shaped[:, 1:], shaped[:, :1]], axis=1).reshape(places, width)
    tiles = values.reshape(places // SUBLANES, SUBLANES, width)
    if 2 * stride == SUBLANES:
        return pltpu.roll(tiles, stride, 1).reshape(places, width)
    spot = lax.broadcasted_iota(jnp.int32, tiles.shape, 1)
    down = pltpu.roll(tiles, stride, 1)
    up = pltpu.roll(tiles, SUBLANES - stride, 1)
    return jnp.where(spot & stride > 0, down, up).reshape(places, width)


def shifted(values, by):
    places, width = values.shape
    tiles = values.reshape(places // SUBLANES, SUBLANES, width)
    return pltpu.roll(tiles, by % SUBLANES, 1).reshape(places, width)


def step(plan, vector_ref, masked_refs, place_ref, inside_ref, rounded_ref, finish, fetches=()):
    span = plan.places // plan.levels_here
    for block in range(plan.lane_blocks):
        vector = vector_ref[:, pl.ds(block * LANES, LANES)]
        for position in range(plan.bits):
            rounded_ref[:, pl.ds(position * plan.rows + block * LANES, LANES)] = flipped(
                vector, plan.phonons << position
            ).astype(jnp.bfloat16)

    def local(start):
        lanes = pl.ds(start, LANES)
        vector = vector_ref[:, lanes]
        levels = [vector[index * span : (index + 1) * span] for index in range(plan.levels_here)]
        lower = jnp.concatenate([shifted(levels[-1], 1)] + levels[:-1], axis=0)
        upper = jnp.concatenate(levels[1:] + [shifted(levels[0], -1)], axis=0)
        weight = place_ref[0] + inside_ref[:1, lanes]
        total = weight * (place_ref[1] * lower + place_ref[2] * upper)
        for position in range(plan.bits):
            total = total + place_ref[3 + position, :1] * flipped(vector, plan.phonons << position)
        return total

    def product(lanes, position):
        return jnp.dot(
            rounded_ref[:, pl.ds(position * plan.rows, plan.rows)],
            masked_refs[position][:, lanes],
            preferred_element_type=jnp.float32,
        )

    early = range(plan.bits - len(fetches))
    late = range(plan.bits - len(fetches), plan.bits)
    width = 2 * LANES
    parts = [pl.ds(start, width) for start in range(0, plan.rows, width)]

    def begun(lanes):
        total = jnp.concatenate([local(start) for start in range(lanes.start, lanes.start + width, LANES)], axis=1)
        for position in early:
            total = total + product(lanes, position)
        return total

    if not fetches:
        for lanes in parts:
            finish(lanes, begun(lanes))
        return
    held_ref = fetches[0][0]
    for lanes in parts:
        held_ref[:, lanes] = begun(lanes)
    for _, fetch in fetches:
        fetch.wait()
    for lanes in parts:
        total = held_ref[:, lanes]
        for position in late:
            total = total + product(lanes, position)
        finish(lanes, total)


def first_kernel(plan, kept, arrived_ref, place_ref, inside_ref, *refs):
    masked_refs = refs[:kept]
    stored_refs = refs[kept : plan.bits]
    initial_ref, new_ref, sums_ref = refs[plan.bits : plan.bits + 3]
    fetched_refs = refs[plan.bits + 3 : -2]
    rounded_ref, semaphores = refs[-2:]
    fetches = []
    for index, (stored_ref, fetched_ref) in enumerate(zip(stored_refs, fetched_refs)):
        fetch = pltpu.make_async_copy(stored_ref, fetched_ref, semaphores.at[index])
        fetch.start()
        fetches.append((new_ref, fetch))
    squares, _ = totals_of(plan, arrived_ref, plan.body, plan.message)
    inverse = 1.0 / scale_of(plan, squares)
    for piece in range(plan.pieces):
        for block in range(plan.lane_blocks):
            part = arrived_ref[pl.ds(piece * plan.lane_blocks + block, plan.groups, stride=plan.message), :]
            initial_ref[pl.ds(piece * plan.groups, plan.groups), pl.ds(block * LANES, LANES)] = part * inverse
    squares = []
    overlap = []

    def finish(lanes, new):
        new_ref[:, lanes] = new
        squares.append(lane_sums(new * new))
        overlap.append(lane_sums(new * initial_ref[:, lanes]))

    step(
        plan, initial_ref, (*masked_refs, *fetched_refs), place_ref, inside_ref, rounded_ref, finish, fetches
    )
    put_sums(plan, sums_ref, one_row(squares), one_row(overlap), 0, EXTRA)


def one_row(rows):
    total = sum(rows[1:], rows[0])
    return sum(total[:, start : start + LANES] for start in range(0, total.shape[1], LANES))


def later_kernel(plan, body, keep, arrived_ref, raw_ref, previous_ref, initial_ref, place_ref, inside_ref, *refs):
    masked_refs = refs[: plan.bits]
    if keep:
        current_ref, new_ref, out_ref, moment_ref, rounded_ref = refs[plan.bits :]
    else:
        out_ref, moment_ref, rounded_ref, current_ref = refs[plan.bits :]
    squares, overlap = totals_of(plan, arrived_ref, body, body + EXTRA)
    inverse = 1.0 / scale_of(plan, squares)
    moment_ref[...] = jnp.broadcast_to(overlap * inverse / plan.entries, moment_ref.shape)
    for block in range(plan.lane_blocks):
        lanes = pl.ds(block * LANES, LANES)
        current_ref[:, lanes] = raw_ref[:, lanes] * inverse
    squares = []
    overlap = []

    def finish(lanes, total):
        new = 2.0 * total - previous_ref[:, lanes] * inverse
        if keep:
            new_ref[:, lanes] = new
        squares.append(lane_sums(new * new))
        overlap.append(lane_sums(new * initial_ref[:, lanes]))
        for start in range(0, lanes.size, LANES):
            block = (lanes.start + start) // LANES
            for piece in range(plan.pieces):
                out_ref[pl.ds(piece * plan.lane_blocks + block, plan.groups, stride=plan.message), :] = new[
                    piece * plan.groups : (piece + 1) * plan.groups, start : start + LANES
                ]

    step(plan, current_ref, masked_refs, place_ref, inside_ref, rounded_ref, finish)
    put_sums(plan, out_ref, one_row(squares), one_row(overlap), plan.body, plan.message)


def arrive_kernel(plan, arrived_ref, *refs):
    squares, overlap = totals_of(plan, arrived_ref, plan.body, plan.message)
    inverse = 1.0 / scale_of(plan, squares)
    if len(refs) > 1:
        first_ref, second_ref, out_ref, moments_ref = refs
        moment = overlap * inverse / plan.entries
        moments_ref[0] = first_ref[0, 0]
        moments_ref[1] = second_ref[0, 0]
        moments_ref[2] = moment[0, 0]
    else:
        (out_ref,) = refs
    for block in range(plan.lane_blocks):
        parts = [
            arrived_ref[pl.ds(piece * plan.lane_blocks + block, plan.groups, stride=plan.message), :]
            for piece in range(plan.pieces)
        ]
        out_ref[pl.ds(block * LANES, LANES), :] = (jnp.concatenate(parts, axis=0) * inverse).T


def exchange(plan, values):
    rows = values.shape[0] // plan.groups
    shaped = values.reshape(plan.groups, rows // EXTRA, EXTRA, LANES)
    return lax.all_to_all(shaped, AXES, 0, 0, tiled=True).reshape(values.shape)


def shards(plan, state, operators, op_mask, site_bits, field, site_coupling, mode_coupling):
    f32 = jnp.float32
    message = jax.ShapeDtypeStruct((plan.groups * plan.message, LANES), f32)
    vector = jax.ShapeDtypeStruct((plan.places, plan.rows), f32)
    moment = jax.ShapeDtypeStruct((SUBLANES, LANES), f32)
    held = jax.ShapeDtypeStruct((plan.rows, plan.columns), f32)
    rounded = pltpu.VMEM((plan.places, plan.bits * plan.rows), jnp.bfloat16)
    working = pltpu.VMEM((plan.places, plan.rows), f32)
    work = 2 * plan.bits * plan.places * plan.rows * plan.rows

    def cost(flops, moved):
        return pl.CostEstimate(flops=flops, bytes_accessed=moved, transcendentals=0)

    departing = pl.pallas_call(
        functools.partial(depart_kernel, plan),
        out_shape=message,
        in_specs=[VMEM],
        out_specs=VMEM,
        compiler_params=params(16),
        name="depart",
    )(state)
    arrived = exchange(plan, departing)
    operator = jax.ShapeDtypeStruct((plan.rows, plan.rows), jnp.bfloat16)
    kept = 1
    fetched = plan.bits - kept
    place, inside, *masked = pl.pallas_call(
        functools.partial(prepare_kernel, plan, kept),
        out_shape=[
            jax.ShapeDtypeStruct((3 + plan.bits, plan.places, LANES), f32),
            jax.ShapeDtypeStruct((SUBLANES, plan.rows), f32),
        ]
        + [operator] * kept,
        in_specs=[SMEM] * 5 + [HBM],
        out_specs=[VMEM] * (2 + kept),
        scratch_shapes=[
            pltpu.VMEM((kept, plan.rows, plan.rows), jnp.bfloat16),
            pltpu.SemaphoreType.DMA((kept,)),
        ],
        compiler_params=params(50),
        cost_estimate=cost(plan.rows * plan.rows, 4 * kept * plan.rows * plan.rows),
        name="prepare",
    )(site_bits, op_mask, field, site_coupling, mode_coupling, operators)
    stored = pl.pallas_call(
        functools.partial(store_kernel, plan, kept),
        out_shape=[operator] * fetched,
        in_specs=[SMEM] * 2 + [HBM],
        out_specs=[HBM] * fetched,
        scratch_shapes=[
            pltpu.VMEM((fetched, plan.rows, plan.rows), jnp.bfloat16),
            pltpu.VMEM((fetched, plan.rows, plan.rows), jnp.bfloat16),
            pltpu.SemaphoreType.DMA((fetched,)),
            pltpu.SemaphoreType.DMA((fetched,)),
        ],
        compiler_params=params(60),
        cost_estimate=cost(plan.rows * plan.rows, 4 * fetched * plan.rows * plan.rows),
        name="store",
    )(site_bits, op_mask, operators)
    initial, raw, sums, *fetched_masked = pl.pallas_call(
        functools.partial(first_kernel, plan, kept),
        out_shape=[vector, vector, jax.ShapeDtypeStruct((plan.groups * EXTRA, LANES), f32)] + [operator] * fetched,
        in_specs=[VMEM] * 4 + [HBM] * fetched,
        out_specs=[VMEM] * (3 + fetched),
        scratch_shapes=[rounded, pltpu.SemaphoreType.DMA((fetched,))],
        compiler_params=params(46),
        cost_estimate=cost(work, 4 * plan.places * plan.rows),
        name="first",
    )(arrived, place, inside, *masked, *stored)
    tables = (place, inside, *masked, *fetched_masked)
    sums = exchange(plan, sums)
    current, raw, departing, moment_one = pl.pallas_call(
        functools.partial(later_kernel, plan, 0, True),
        out_shape=[vector, vector, message, moment],
        in_specs=[VMEM] * (6 + plan.bits),
        out_specs=[VMEM] * 4,
        scratch_shapes=[rounded],
        compiler_params=params(32),
        cost_estimate=cost(work, 4 * plan.places * plan.rows),
        name="second",
    )(sums, raw, initial, initial, *tables)
    before = exchange(plan, departing)
    departing, moment_two = pl.pallas_call(
        functools.partial(later_kernel, plan, plan.body, False),
        out_shape=[message, moment],
        in_specs=[VMEM] * (6 + plan.bits),
        out_specs=[VMEM] * 2,
        scratch_shapes=[rounded, working],
        compiler_params=params(32),
        cost_estimate=cost(work, 4 * plan.places * plan.rows),
        name="third",
    )(before, raw, current, initial, *tables)
    last = exchange(plan, departing)
    before = pl.pallas_call(
        functools.partial(arrive_kernel, plan),
        out_shape=held,
        in_specs=[VMEM],
        out_specs=VMEM,
        compiler_params=params(16),
        cost_estimate=cost(plan.places * plan.rows, 8 * plan.places * plan.rows),
        name="arrive_before",
    )(before)
    last, moments = pl.pallas_call(
        functools.partial(arrive_kernel, plan),
        out_shape=[held, jax.ShapeDtypeStruct((STEPS,), f32)],
        in_specs=[VMEM] * 3,
        out_specs=[VMEM, SMEM],
        compiler_params=params(16),
        name="arrive_last",
    )(last, moment_one, moment_two)
    return last, before, moments


def extended_2(block, sides, width):
    for axis, dim in sides:
        count = lax.axis_size(axis)
        forward = [(i, i + 1) for i in range(count - 1)]
        backward = [(target, source) for source, target in forward]
        low = lax.ppermute(
            lax.slice_in_dim(block, block.shape[dim] - width, None, axis=dim), axis, forward
        )
        high = lax.ppermute(lax.slice_in_dim(block, 0, width, axis=dim), axis, backward)
        block = jnp.concatenate([low, block, high], axis=dim)
    return block


def partner(value, axis, bit):
    mask = 2**bit
    pairs = [(source, source ^ mask) for source in range(lax.axis_size(axis))]
    return lax.ppermute(value, axis, pairs)


def halo_shards(state, operators, op_mask, site_bits, field, site_coupling, mode_coupling):
    site_count = lax.axis_size("site")
    phonon_count = lax.axis_size("phonon")
    bit_count = site_count.bit_length() - 1
    rows_here = state.shape[0]
    columns_here = state.shape[1]
    levels_here = columns_here // MODES
    block_edge = rows_here // op_mask.shape[1]
    expanded = jnp.repeat(jnp.repeat(op_mask, block_edge, axis=1), block_edge, axis=2)
    masked = jnp.where(expanded > 0, operators, jnp.zeros((), jnp.bfloat16))
    entries = jnp.float32(rows_here * columns_here * site_count * phonon_count)
    level_total = jnp.sqrt(jnp.float32(levels_here * phonon_count))
    device = lax.axis_index("site")
    inside = lax.iota(jnp.int32, rows_here)
    weight_rows = jnp.zeros((rows_here,), jnp.float32)
    for position in range(bit_count):
        weight_rows = weight_rows + site_coupling[site_bits[position]] * (
            device >> position & 1
        ).astype(jnp.float32)
    for local_bit in range(LBITS):
        weight_rows = weight_rows + site_coupling[bit_count + local_bit] * (
            inside >> local_bit & 1
        ).astype(jnp.float32)
    levels = (
        lax.axis_index("phonon") * levels_here + lax.iota(jnp.int32, columns_here) // MODES
    ).astype(jnp.float32)
    lower_weight = jnp.sqrt(levels)
    upper_weight = jnp.sqrt(levels + 1.0)
    mode_weight = jnp.tile(mode_coupling, columns_here // MODES) / level_total
    start_squares = lax.psum(jnp.sum(state * state), ("site", "phonon"))
    initial = state / jnp.sqrt(start_squares / entries + epsilon)
    previous = initial
    current = initial
    scale_prev = jnp.float32(1.0)
    moments = []
    for iteration in range(STEPS):
        extended = extended_2(current, (("phonon", 1),), MODES)
        lower_part = extended[:, :columns_here]
        upper_part = extended[:, 2 * MODES :]
        summed = weight_rows[:, None] * (
            mode_weight * (lower_weight * lower_part + upper_weight * upper_part)
        )
        for operate_position in range(bit_count):
            chosen = site_bits[operate_position]
            flipped = partner(current, "site", operate_position)
            product = jnp.dot(
                masked[chosen], flipped.astype(jnp.bfloat16), preferred_element_type=jnp.float32
            )
            summed = summed + (field[chosen] * flipped + product)
        if iteration == 0:
            vector_new = summed
        else:
            vector_new = 2.0 * summed - previous / scale_prev
        squares, intersection = lax.psum(
            (jnp.sum(vector_new * vector_new), jnp.sum(initial * vector_new)), ("site", "phonon")
        )
        scale_now = jnp.sqrt(squares / entries + epsilon)
        updated = vector_new / scale_now
        moment = intersection / (entries * scale_now)
        moments.append(moment)
        previous = current
        current = updated
        scale_prev = scale_now
    return (current, previous, jnp.stack(moments))


def solution(mesh):
    in_specs = (P("site", "phonon"), P(), P(), P(), P(), P(), P())
    out_specs = (P("site", "phonon"), P("site", "phonon"), P())

    def whole(state, operators, op_mask, *rest):
        rows = state.shape[0] // mesh.shape["site"]
        columns = state.shape[1] // mesh.shape["phonon"]
        plan = Plan(mesh, rows, columns, op_mask.shape[1])
        body = functools.partial(shards, plan) if plan.fits() else halo_shards
        run = jax.shard_map(body, mesh=mesh, in_specs=in_specs, out_specs=out_specs, check_vma=False)
        return run(state, operators, op_mask, *rest)

    return whole
```

```python
import functools

import jax
import jax.numpy as jnp
from jax import lax
from jax.experimental import pallas as pl
from jax.experimental.pallas import tpu as pltpu
from jax.sharding import PartitionSpec as P

LBITS = 10
MODES = 64
STEPS = 3
LANES = 128
SUBLANES = 8
EXTRA = 1
AXES = ("site", "phonon")

epsilon = 1e-06


VMEM = pl.BlockSpec(memory_space=pltpu.VMEM)
SMEM = pl.BlockSpec(memory_space=pltpu.SMEM)
HBM = pl.BlockSpec(memory_space=pltpu.HBM)


class Plan:
    def __init__(self, mesh, rows, columns, blocks):
        self.sites = mesh.shape["site"]
        self.phonons = mesh.shape["phonon"]
        self.groups = self.sites * self.phonons
        self.bits = self.sites.bit_length() - 1
        self.rows = rows
        self.columns = columns
        self.blocks = blocks
        self.edge = rows // blocks
        self.levels_here = columns // MODES
        self.level_count = self.levels_here * self.phonons
        self.share = MODES // self.groups
        self.pieces = self.levels_here * self.share
        self.lane_blocks = rows // LANES
        self.body = self.pieces * self.lane_blocks
        self.message = self.body + EXTRA
        self.places = self.pieces * self.groups
        self.entries = float(rows * columns * self.groups)

    def fits(self):
        return (
            MODES % self.groups == 0
            and self.columns == LANES
            and self.rows % LANES == 0
            and self.edge % LANES == 0
            and self.groups % SUBLANES == 0
        )


def params(mib):
    return pltpu.CompilerParams(vmem_limit_bytes=mib * 2**20)


def lane_sums(values):
    return jnp.sum(values, axis=0, keepdims=True)


def folded(value):
    return value + pltpu.roll(value, LANES // 2, 1)


def put_sums(out_ref, squares, overlap, start, stride, count):
    lane = lax.broadcasted_iota(jnp.int32, (1, LANES), 1)
    row = jnp.where(lane < LANES // 2, folded(squares), folded(overlap))
    out_ref[pl.ds(start, count, stride=stride), :] = jnp.broadcast_to(row, (count, LANES))


def totals_of(ref, start, stride, count):
    lanes = lane_sums(ref[pl.ds(start, count, stride=stride), :])
    lane = lax.broadcasted_iota(jnp.int32, (1, LANES), 1)
    squares = jnp.sum(jnp.where(lane < LANES // 2, lanes, 0.0), axis=1, keepdims=True)
    overlap = jnp.sum(jnp.where(lane < LANES // 2, 0.0, lanes), axis=1, keepdims=True)
    return squares, overlap


def scale_of(plan, squares):
    return jnp.sqrt(squares / plan.entries + epsilon)


def depart_kernel(plan, state_ref, out_ref):
    sums = jnp.zeros((1, LANES), jnp.float32)
    for block in range(plan.lane_blocks):
        tile = state_ref[pl.ds(block * LANES, LANES), :]
        sums = sums + lane_sums(tile * tile)
        turned = tile.T
        for piece in range(plan.pieces):
            out_ref[pl.ds(piece * plan.lane_blocks + block, plan.groups, stride=plan.message), :] = turned[
                piece * plan.groups : (piece + 1) * plan.groups
            ]
    put_sums(out_ref, sums, jnp.zeros_like(sums), plan.body, plan.message, plan.groups)


def mask_operator(plan, chosen, mask_ref, held_ref, out_ref):
    for across in range(plan.blocks):
        rows = pl.ds(across * plan.edge, plan.edge)
        for along in range(plan.blocks):
            columns = pl.ds(along * plan.edge, plan.edge)
            keep = (mask_ref[chosen, across, along] > 0).astype(jnp.float32).astype(jnp.bfloat16)
            out_ref[columns, rows] = (held_ref[rows, columns] * keep).T


def store_kernel(plan, kept, bits_ref, mask_ref, operators_ref, *refs):
    count = plan.bits - kept
    stored_refs, (held_ref, masked_ref, in_semaphores, out_semaphores) = refs[:count], refs[count:]
    fetches = [
        pltpu.make_async_copy(operators_ref.at[bits_ref[kept + index]], held_ref.at[index], in_semaphores.at[index])
        for index in range(count)
    ]
    for fetch in fetches:
        fetch.start()
    stores = []
    for index in range(count):
        fetches[index].wait()
        mask_operator(plan, bits_ref[kept + index], mask_ref, held_ref.at[index], masked_ref.at[index])
        store = pltpu.make_async_copy(masked_ref.at[index], stored_refs[index], out_semaphores.at[index])
        store.start()
        stores.append(store)
    for store in stores:
        store.wait()


def prepare_kernel(
    plan,
    kept,
    bits_ref,
    mask_ref,
    field_ref,
    coupling_ref,
    mode_ref,
    operators_ref,
    place_ref,
    inside_ref,
    *refs,
):
    masked_refs, (held_ref, semaphores) = refs[:kept], refs[kept:]
    fetches = [
        pltpu.make_async_copy(operators_ref.at[bits_ref[index]], held_ref.at[index], semaphores.at[index])
        for index in range(kept)
    ]
    for fetch in fetches:
        fetch.start()
    me = lax.axis_index("site") * plan.phonons + lax.axis_index("phonon")
    place = lax.broadcasted_iota(jnp.int32, (plan.places, LANES), 0)
    phonon = place % plan.phonons
    site = place // plan.phonons % plan.sites
    mode = place // plan.groups % plan.share
    level = phonon * plan.levels_here + place // (plan.groups * plan.share)
    occupied = jnp.zeros((plan.places, LANES), jnp.float32)
    for position in range(plan.bits):
        held = (site >> position & 1).astype(jnp.float32)
        occupied = occupied + coupling_ref[bits_ref[position]] * held
    strength = jnp.zeros((plan.places, LANES), jnp.float32)
    for index in range(plan.share):
        strength = jnp.where(mode == index, mode_ref[index * plan.groups + me], strength)
    strength = strength / jnp.sqrt(jnp.full((1, LANES), plan.level_count, jnp.float32))
    height = level.astype(jnp.float32)
    place_ref[0] = occupied
    place_ref[1] = strength * jnp.sqrt(height)
    place_ref[2] = jnp.where(level == plan.level_count - 1, 0.0, strength * jnp.sqrt(height + 1.0))
    for position in range(plan.bits):
        place_ref[3 + position] = jnp.full((plan.places, LANES), field_ref[bits_ref[position]])
    inside = lax.broadcasted_iota(jnp.int32, (SUBLANES, plan.rows), 1)
    weight = jnp.zeros((SUBLANES, plan.rows), jnp.float32)
    for local_bit in range(LBITS):
        weight = weight + coupling_ref[plan.bits + local_bit] * (inside >> local_bit & 1).astype(jnp.float32)
    inside_ref[...] = weight
    for index in range(kept):
        fetches[index].wait()
        mask_operator(plan, bits_ref[index], mask_ref, held_ref.at[index], masked_refs[index])


def flipped(values, stride):
    places, width = values.shape
    if stride % SUBLANES == 0:
        shaped = values.reshape(places // (2 * stride), 2, stride, width)
        return jnp.concatenate([shaped[:, 1:], shaped[:, :1]], axis=1).reshape(places, width)
    tiles = values.reshape(places // SUBLANES, SUBLANES, width)
    if 2 * stride == SUBLANES:
        return pltpu.roll(tiles, stride, 1).reshape(places, width)
    spot = lax.broadcasted_iota(jnp.int32, tiles.shape, 1)
    down = pltpu.roll(tiles, stride, 1)
    up = pltpu.roll(tiles, SUBLANES - stride, 1)
    return jnp.where(spot & stride > 0, down, up).reshape(places, width)


def shifted(values, by):
    places, width = values.shape
    tiles = values.reshape(places // SUBLANES, SUBLANES, width)
    return pltpu.roll(tiles, by % SUBLANES, 1).reshape(places, width)


def step(plan, vector_ref, masked_refs, place_ref, inside_ref, rounded_ref, finish, fetches={}):
    span = plan.places // plan.levels_here
    for block in range(plan.lane_blocks):
        vector = vector_ref[:, pl.ds(block * LANES, LANES)]
        for position in range(plan.bits):
            rounded_ref[:, pl.ds(position * plan.rows + block * LANES, LANES)] = flipped(
                vector, plan.phonons << position
            ).astype(jnp.bfloat16)

    def local(start):
        lanes = pl.ds(start, LANES)
        vector = vector_ref[:, lanes]
        levels = [vector[index * span : (index + 1) * span] for index in range(plan.levels_here)]
        lower = jnp.concatenate([shifted(levels[-1], 1)] + levels[:-1], axis=0)
        upper = jnp.concatenate(levels[1:] + [shifted(levels[0], -1)], axis=0)
        weight = place_ref[0] + inside_ref[:1, lanes]
        total = weight * (place_ref[1] * lower + place_ref[2] * upper)
        for position in range(plan.bits):
            total = total + place_ref[3 + position, :1] * flipped(vector, plan.phonons << position)
        return total

    def product(lanes, position):
        return jnp.dot(
            rounded_ref[:, pl.ds(position * plan.rows, plan.rows)],
            masked_refs[position][:, lanes],
            preferred_element_type=jnp.float32,
        )

    for index, lanes in enumerate(parts_of(plan)):
        total = jnp.concatenate(
            [local(start) for start in range(lanes.start, lanes.start + lanes.size, LANES)], axis=1
        )
        for position in range(plan.bits):
            if (position, index) in fetches:
                fetches[position, index].wait()
            total = total + product(lanes, position)
        finish(lanes, total)


def parts_of(plan):
    return [pl.ds(start, 2 * LANES) for start in range(0, plan.rows, 2 * LANES)]


def first_kernel(plan, kept, arrived_ref, place_ref, inside_ref, *refs):
    masked_refs = refs[:kept]
    stored_refs = refs[kept : plan.bits]
    initial_ref, new_ref, sums_ref = refs[plan.bits : plan.bits + 3]
    fetched_refs = refs[plan.bits + 3 : -2]
    rounded_ref, semaphores = refs[-2:]
    fetches = {}
    for part, lanes in enumerate(parts_of(plan)):
        for index, (stored_ref, fetched_ref) in enumerate(zip(stored_refs, fetched_refs)):
            fetch = pltpu.make_async_copy(
                stored_ref.at[:, lanes], fetched_ref.at[:, lanes], semaphores.at[index, part]
            )
            fetch.start()
            fetches[kept + index, part] = fetch
    squares, _ = totals_of(arrived_ref, plan.body, plan.message, plan.groups)
    inverse = 1.0 / scale_of(plan, squares)
    for piece in range(plan.pieces):
        for block in range(plan.lane_blocks):
            part = arrived_ref[pl.ds(piece * plan.lane_blocks + block, plan.groups, stride=plan.message), :]
            initial_ref[pl.ds(piece * plan.groups, plan.groups), pl.ds(block * LANES, LANES)] = part * inverse
    squares = []
    overlap = []

    def finish(lanes, new):
        new_ref[:, lanes] = new
        squares.append(lane_sums(new * new))
        overlap.append(lane_sums(new * initial_ref[:, lanes]))

    step(
        plan, initial_ref, (*masked_refs, *fetched_refs), place_ref, inside_ref, rounded_ref, finish, fetches
    )
    put_sums(sums_ref, one_row(squares), one_row(overlap), 0, 1, plan.sites)


def one_row(rows):
    total = sum(rows[1:], rows[0])
    return sum(total[:, start : start + LANES] for start in range(0, total.shape[1], LANES))


def place_block(plan, arrived_ref, out_ref, inverse, block):
    parts = [
        arrived_ref[pl.ds(piece * plan.lane_blocks + block, plan.groups, stride=plan.message), :]
        for piece in range(plan.pieces)
    ]
    out_ref[pl.ds(block * LANES, LANES), :] = (jnp.concatenate(parts, axis=0) * inverse).T


def relay_kernel(plan, arrived_ref, out_ref):
    out_ref[...] = jnp.broadcast_to(lane_sums(arrived_ref[...]), out_ref.shape)


def later_kernel(plan, keep, arrived_ref, raw_ref, previous_ref, initial_ref, place_ref, inside_ref, *refs):
    masked_refs = refs[: plan.bits]
    if keep:
        current_ref, new_ref, out_ref, moment_ref, rounded_ref = refs[plan.bits :]
        squares, overlap = totals_of(arrived_ref, 0, 1, plan.phonons)
    else:
        out_ref, moment_ref, placed_ref, rounded_ref, current_ref = refs[plan.bits :]
        squares, overlap = totals_of(arrived_ref, plan.body, plan.message, plan.groups)
    inverse = 1.0 / scale_of(plan, squares)
    moment_ref[...] = jnp.broadcast_to(overlap * inverse / plan.entries, moment_ref.shape)
    for block in range(plan.lane_blocks):
        lanes = pl.ds(block * LANES, LANES)
        current_ref[:, lanes] = raw_ref[:, lanes] * inverse
    squares = []
    overlap = []

    def finish(lanes, total):
        new = 2.0 * total - previous_ref[:, lanes] * inverse
        if keep:
            new_ref[:, lanes] = new
        squares.append(lane_sums(new * new))
        overlap.append(lane_sums(new * initial_ref[:, lanes]))
        for start in range(0, lanes.size, LANES):
            block = (lanes.start + start) // LANES
            if not keep:
                place_block(plan, arrived_ref, placed_ref, inverse, block)
            for piece in range(plan.pieces):
                out_ref[pl.ds(piece * plan.lane_blocks + block, plan.groups, stride=plan.message), :] = new[
                    piece * plan.groups : (piece + 1) * plan.groups, start : start + LANES
                ]

    step(plan, current_ref, masked_refs, place_ref, inside_ref, rounded_ref, finish)
    put_sums(out_ref, one_row(squares), one_row(overlap), plan.body, plan.message, plan.groups)


def arrive_kernel(plan, arrived_ref, first_ref, second_ref, out_ref, moments_ref):
    squares, overlap = totals_of(arrived_ref, plan.body, plan.message, plan.groups)
    inverse = 1.0 / scale_of(plan, squares)
    moment = overlap * inverse / plan.entries
    moments_ref[0] = first_ref[0, 0]
    moments_ref[1] = second_ref[0, 0]
    moments_ref[2] = moment[0, 0]
    for block in range(plan.lane_blocks):
        place_block(plan, arrived_ref, out_ref, inverse, block)


def exchange(values, count, axes):
    shaped = values.reshape(count, values.shape[0] // count, 1, LANES)
    return lax.all_to_all(shaped, axes, 0, 0, tiled=True).reshape(values.shape)


def shards(plan, state, operators, op_mask, site_bits, field, site_coupling, mode_coupling):
    f32 = jnp.float32
    message = jax.ShapeDtypeStruct((plan.groups * plan.message, LANES), f32)
    vector = jax.ShapeDtypeStruct((plan.places, plan.rows), f32)
    moment = jax.ShapeDtypeStruct((SUBLANES, LANES), f32)
    held = jax.ShapeDtypeStruct((plan.rows, plan.columns), f32)
    rounded = pltpu.VMEM((plan.places, plan.bits * plan.rows), jnp.bfloat16)
    working = pltpu.VMEM((plan.places, plan.rows), f32)
    work = 2 * plan.bits * plan.places * plan.rows * plan.rows

    def cost(flops, moved):
        return pl.CostEstimate(flops=flops, bytes_accessed=moved, transcendentals=0)

    departing = pl.pallas_call(
        functools.partial(depart_kernel, plan),
        out_shape=message,
        in_specs=[VMEM],
        out_specs=VMEM,
        compiler_params=params(16),
        name="depart",
    )(state)
    arrived = exchange(departing, plan.groups, AXES)
    operator = jax.ShapeDtypeStruct((plan.rows, plan.rows), jnp.bfloat16)
    kept = 1
    fetched = plan.bits - kept
    place, inside, *masked = pl.pallas_call(
        functools.partial(prepare_kernel, plan, kept),
        out_shape=[
            jax.ShapeDtypeStruct((3 + plan.bits, plan.places, LANES), f32),
            jax.ShapeDtypeStruct((SUBLANES, plan.rows), f32),
        ]
        + [operator] * kept,
        in_specs=[SMEM] * 5 + [HBM],
        out_specs=[VMEM] * (2 + kept),
        scratch_shapes=[
            pltpu.VMEM((kept, plan.rows, plan.rows), jnp.bfloat16),
            pltpu.SemaphoreType.DMA((kept,)),
        ],
        compiler_params=params(50),
        cost_estimate=cost(plan.rows * plan.rows, 4 * kept * plan.rows * plan.rows),
        name="prepare",
    )(site_bits, op_mask, field, site_coupling, mode_coupling, operators)
    stored = pl.pallas_call(
        functools.partial(store_kernel, plan, kept),
        out_shape=[operator] * fetched,
        in_specs=[SMEM] * 2 + [HBM],
        out_specs=[HBM] * fetched,
        scratch_shapes=[
            pltpu.VMEM((fetched, plan.rows, plan.rows), jnp.bfloat16),
            pltpu.VMEM((fetched, plan.rows, plan.rows), jnp.bfloat16),
            pltpu.SemaphoreType.DMA((fetched,)),
            pltpu.SemaphoreType.DMA((fetched,)),
        ],
        compiler_params=params(60),
        cost_estimate=cost(plan.rows * plan.rows, 4 * fetched * plan.rows * plan.rows),
        name="store",
    )(site_bits, op_mask, operators)
    initial, raw, sums, *fetched_masked = pl.pallas_call(
        functools.partial(first_kernel, plan, kept),
        out_shape=[vector, vector, jax.ShapeDtypeStruct((plan.sites, LANES), f32)] + [operator] * fetched,
        in_specs=[VMEM] * 4 + [HBM] * fetched,
        out_specs=[VMEM] * (3 + fetched),
        scratch_shapes=[rounded, pltpu.SemaphoreType.DMA((fetched, len(parts_of(plan))))],
        compiler_params=params(46),
        cost_estimate=cost(work, 4 * plan.places * plan.rows),
        name="first",
    )(arrived, place, inside, *masked, *stored)
    tables = (place, inside, *masked, *fetched_masked)
    sums = exchange(sums, plan.sites, "site")
    sums = pl.pallas_call(
        functools.partial(relay_kernel, plan),
        out_shape=jax.ShapeDtypeStruct((plan.phonons, LANES), f32),
        in_specs=[VMEM],
        out_specs=VMEM,
        compiler_params=params(4),
        name="relay",
    )(sums)
    sums = exchange(sums, plan.phonons, "phonon")
    current, raw, departing, moment_one = pl.pallas_call(
        functools.partial(later_kernel, plan, True),
        out_shape=[vector, vector, message, moment],
        in_specs=[VMEM] * (6 + plan.bits),
        out_specs=[VMEM] * 4,
        scratch_shapes=[rounded],
        compiler_params=params(32),
        cost_estimate=cost(work, 4 * plan.places * plan.rows),
        name="second",
    )(sums, raw, initial, initial, *tables)
    before = exchange(departing, plan.groups, AXES)
    departing, moment_two, before = pl.pallas_call(
        functools.partial(later_kernel, plan, False),
        out_shape=[message, moment, held],
        in_specs=[VMEM] * (6 + plan.bits),
        out_specs=[VMEM] * 3,
        scratch_shapes=[rounded, working],
        compiler_params=params(32),
        cost_estimate=cost(work, 4 * plan.places * plan.rows),
        name="third",
    )(before, raw, current, initial, *tables)
    last = exchange(departing, plan.groups, AXES)
    last, moments = pl.pallas_call(
        functools.partial(arrive_kernel, plan),
        out_shape=[held, jax.ShapeDtypeStruct((STEPS,), f32)],
        in_specs=[VMEM] * 3,
        out_specs=[VMEM, SMEM],
        compiler_params=params(16),
        name="arrive_last",
    )(last, moment_one, moment_two)
    return last, before, moments


def extended_2(block, sides, width):
    for axis, dim in sides:
        count = lax.axis_size(axis)
        forward = [(i, i + 1) for i in range(count - 1)]
        backward = [(target, source) for source, target in forward]
        low = lax.ppermute(
            lax.slice_in_dim(block, block.shape[dim] - width, None, axis=dim), axis, forward
        )
        high = lax.ppermute(lax.slice_in_dim(block, 0, width, axis=dim), axis, backward)
        block = jnp.concatenate([low, block, high], axis=dim)
    return block


def partner(value, axis, bit):
    mask = 2**bit
    pairs = [(source, source ^ mask) for source in range(lax.axis_size(axis))]
    return lax.ppermute(value, axis, pairs)


def halo_shards(state, operators, op_mask, site_bits, field, site_coupling, mode_coupling):
    site_count = lax.axis_size("site")
    phonon_count = lax.axis_size("phonon")
    bit_count = site_count.bit_length() - 1
    rows_here = state.shape[0]
    columns_here = state.shape[1]
    levels_here = columns_here // MODES
    block_edge = rows_here // op_mask.shape[1]
    expanded = jnp.repeat(jnp.repeat(op_mask, block_edge, axis=1), block_edge, axis=2)
    masked = jnp.where(expanded > 0, operators, jnp.zeros((), jnp.bfloat16))
    entries = jnp.float32(rows_here * columns_here * site_count * phonon_count)
    level_total = jnp.sqrt(jnp.float32(levels_here * phonon_count))
    device = lax.axis_index("site")
    inside = lax.iota(jnp.int32, rows_here)
    weight_rows = jnp.zeros((rows_here,), jnp.float32)
    for position in range(bit_count):
        weight_rows = weight_rows + site_coupling[site_bits[position]] * (
            device >> position & 1
        ).astype(jnp.float32)
    for local_bit in range(LBITS):
        weight_rows = weight_rows + site_coupling[bit_count + local_bit] * (
            inside >> local_bit & 1
        ).astype(jnp.float32)
    levels = (
        lax.axis_index("phonon") * levels_here + lax.iota(jnp.int32, columns_here) // MODES
    ).astype(jnp.float32)
    lower_weight = jnp.sqrt(levels)
    upper_weight = jnp.sqrt(levels + 1.0)
    mode_weight = jnp.tile(mode_coupling, columns_here // MODES) / level_total
    start_squares = lax.psum(jnp.sum(state * state), ("site", "phonon"))
    initial = state / jnp.sqrt(start_squares / entries + epsilon)
    previous = initial
    current = initial
    scale_prev = jnp.float32(1.0)
    moments = []
    for iteration in range(STEPS):
        extended = extended_2(current, (("phonon", 1),), MODES)
        lower_part = extended[:, :columns_here]
        upper_part = extended[:, 2 * MODES :]
        summed = weight_rows[:, None] * (
            mode_weight * (lower_weight * lower_part + upper_weight * upper_part)
        )
        for operate_position in range(bit_count):
            chosen = site_bits[operate_position]
            flipped = partner(current, "site", operate_position)
            product = jnp.dot(
                masked[chosen], flipped.astype(jnp.bfloat16), preferred_element_type=jnp.float32
            )
            summed = summed + (field[chosen] * flipped + product)
        if iteration == 0:
            vector_new = summed
        else:
            vector_new = 2.0 * summed - previous / scale_prev
        squares, intersection = lax.psum(
            (jnp.sum(vector_new * vector_new), jnp.sum(initial * vector_new)), ("site", "phonon")
        )
        scale_now = jnp.sqrt(squares / entries + epsilon)
        updated = vector_new / scale_now
        moment = intersection / (entries * scale_now)
        moments.append(moment)
        previous = current
        current = updated
        scale_prev = scale_now
    return (current, previous, jnp.stack(moments))


def solution(mesh):
    in_specs = (P("site", "phonon"), P(), P(), P(), P(), P(), P())
    out_specs = (P("site", "phonon"), P("site", "phonon"), P())

    def whole(state, operators, op_mask, *rest):
        rows = state.shape[0] // mesh.shape["site"]
        columns = state.shape[1] // mesh.shape["phonon"]
        plan = Plan(mesh, rows, columns, op_mask.shape[1])
        body = functools.partial(shards, plan) if plan.fits() else halo_shards
        run = jax.shard_map(body, mesh=mesh, in_specs=in_specs, out_specs=out_specs, check_vma=False)
        return run(state, operators, op_mask, *rest)

    return whole
```

```python
import functools

import jax
import jax.numpy as jnp
from jax import lax
from jax.experimental import pallas as pl
from jax.experimental.pallas import tpu as pltpu
from jax.sharding import PartitionSpec as P

LBITS = 10
MODES = 64
STEPS = 3
LANES = 128
SUBLANES = 8
EXTRA = 1
AXES = ("site", "phonon")

epsilon = 1e-06


VMEM = pl.BlockSpec(memory_space=pltpu.VMEM)
SMEM = pl.BlockSpec(memory_space=pltpu.SMEM)
HBM = pl.BlockSpec(memory_space=pltpu.HBM)


class Plan:
    def __init__(self, mesh, rows, columns, blocks):
        self.sites = mesh.shape["site"]
        self.phonons = mesh.shape["phonon"]
        self.groups = self.sites * self.phonons
        self.bits = self.sites.bit_length() - 1
        self.rows = rows
        self.columns = columns
        self.blocks = blocks
        self.edge = rows // blocks
        self.levels_here = columns // MODES
        self.level_count = self.levels_here * self.phonons
        self.share = MODES // self.groups
        self.pieces = self.levels_here * self.share
        self.lane_blocks = rows // LANES
        self.body = self.pieces * self.lane_blocks
        self.message = self.body + EXTRA
        self.places = self.pieces * self.groups
        self.entries = float(rows * columns * self.groups)

    def fits(self):
        return (
            MODES % self.groups == 0
            and self.columns == LANES
            and self.rows % (2 * LANES) == 0
            and self.edge % LANES == 0
            and self.groups % SUBLANES == 0
        )


def params(mib):
    return pltpu.CompilerParams(vmem_limit_bytes=mib * 2**20)


def lane_sums(values):
    return jnp.sum(values, axis=0, keepdims=True)


def folded(value):
    return value + pltpu.roll(value, LANES // 2, 1)


def put_sums(out_ref, squares, overlap, start, stride, count):
    lane = lax.broadcasted_iota(jnp.int32, (1, LANES), 1)
    row = jnp.where(lane < LANES // 2, folded(squares), folded(overlap))
    out_ref[pl.ds(start, count, stride=stride), :] = jnp.broadcast_to(row, (count, LANES))


def totals_of(ref, start, stride, count):
    lanes = lane_sums(ref[pl.ds(start, count, stride=stride), :])
    lane = lax.broadcasted_iota(jnp.int32, (1, LANES), 1)
    squares = jnp.sum(jnp.where(lane < LANES // 2, lanes, 0.0), axis=1, keepdims=True)
    overlap = jnp.sum(jnp.where(lane < LANES // 2, 0.0, lanes), axis=1, keepdims=True)
    return squares, overlap


def scale_of(plan, squares):
    return jnp.sqrt(squares / plan.entries + epsilon)


def depart_kernel(plan, state_ref, out_ref, held_ref, semaphores):
    half = plan.rows // 2
    fetches = [
        pltpu.make_async_copy(
            state_ref.at[pl.ds(index * half, half), :], held_ref.at[pl.ds(index * half, half), :], semaphores.at[index]
        )
        for index in range(2)
    ]
    for fetch in fetches:
        fetch.start()
    sums = jnp.zeros((1, LANES), jnp.float32)
    for block in range(plan.lane_blocks):
        if block * LANES % half == 0:
            fetches[block * LANES // half].wait()
        tile = held_ref[pl.ds(block * LANES, LANES), :]
        sums = sums + lane_sums(tile * tile)
        turned = tile.T
        for piece in range(plan.pieces):
            out_ref[pl.ds(piece * plan.lane_blocks + block, plan.groups, stride=plan.message), :] = turned[
                piece * plan.groups : (piece + 1) * plan.groups
            ]
    put_sums(out_ref, sums, jnp.zeros_like(sums), plan.body, plan.message, plan.groups)


def mask_operator(plan, chosen, mask_ref, held_ref, out_ref):
    for across in range(plan.blocks):
        rows = pl.ds(across * plan.edge, plan.edge)
        for along in range(plan.blocks):
            columns = pl.ds(along * plan.edge, plan.edge)
            keep = (mask_ref[chosen, across, along] > 0).astype(jnp.float32).astype(jnp.bfloat16)
            out_ref[columns, rows] = (held_ref[rows, columns] * keep).T


def store_kernel(plan, kept, bits_ref, mask_ref, operators_ref, *refs):
    count = plan.bits - kept
    stored_refs, (held_ref, masked_ref, in_semaphores, out_semaphores) = refs[:count], refs[count:]
    fetches = [
        pltpu.make_async_copy(operators_ref.at[bits_ref[kept + index]], held_ref.at[index], in_semaphores.at[index])
        for index in range(count)
    ]
    for fetch in fetches:
        fetch.start()
    stores = []
    for index in range(count):
        fetches[index].wait()
        mask_operator(plan, bits_ref[kept + index], mask_ref, held_ref.at[index], masked_ref.at[index])
        store = pltpu.make_async_copy(masked_ref.at[index], stored_refs[index], out_semaphores.at[index])
        store.start()
        stores.append(store)
    for store in stores:
        store.wait()


def prepare_kernel(
    plan,
    kept,
    bits_ref,
    mask_ref,
    field_ref,
    coupling_ref,
    mode_ref,
    operators_ref,
    place_ref,
    inside_ref,
    *refs,
):
    masked_refs, (held_ref, semaphores) = refs[:kept], refs[kept:]
    fetches = [
        pltpu.make_async_copy(operators_ref.at[bits_ref[index]], held_ref.at[index], semaphores.at[index])
        for index in range(kept)
    ]
    for fetch in fetches:
        fetch.start()
    me = lax.axis_index("site") * plan.phonons + lax.axis_index("phonon")
    place = lax.broadcasted_iota(jnp.int32, (plan.places, LANES), 0)
    phonon = place % plan.phonons
    site = place // plan.phonons % plan.sites
    mode = place // plan.groups % plan.share
    level = phonon * plan.levels_here + place // (plan.groups * plan.share)
    occupied = jnp.zeros((plan.places, LANES), jnp.float32)
    for position in range(plan.bits):
        held = (site >> position & 1).astype(jnp.float32)
        occupied = occupied + coupling_ref[bits_ref[position]] * held
    strength = jnp.zeros((plan.places, LANES), jnp.float32)
    for index in range(plan.share):
        strength = jnp.where(mode == index, mode_ref[index * plan.groups + me], strength)
    strength = strength / jnp.sqrt(jnp.full((1, LANES), plan.level_count, jnp.float32))
    height = level.astype(jnp.float32)
    place_ref[0] = occupied
    place_ref[1] = strength * jnp.sqrt(height)
    place_ref[2] = jnp.where(level == plan.level_count - 1, 0.0, strength * jnp.sqrt(height + 1.0))
    for position in range(plan.bits):
        place_ref[3 + position] = jnp.full((plan.places, LANES), field_ref[bits_ref[position]])
    inside = lax.broadcasted_iota(jnp.int32, (SUBLANES, plan.rows), 1)
    weight = jnp.zeros((SUBLANES, plan.rows), jnp.float32)
    for local_bit in range(LBITS):
        weight = weight + coupling_ref[plan.bits + local_bit] * (inside >> local_bit & 1).astype(jnp.float32)
    inside_ref[...] = weight
    for index in range(kept):
        fetches[index].wait()
        mask_operator(plan, bits_ref[index], mask_ref, held_ref.at[index], masked_refs[index])


def flipped(values, stride):
    places, width = values.shape
    if stride % SUBLANES == 0:
        shaped = values.reshape(places // (2 * stride), 2, stride, width)
        return jnp.concatenate([shaped[:, 1:], shaped[:, :1]], axis=1).reshape(places, width)
    tiles = values.reshape(places // SUBLANES, SUBLANES, width)
    if 2 * stride == SUBLANES:
        return pltpu.roll(tiles, stride, 1).reshape(places, width)
    spot = lax.broadcasted_iota(jnp.int32, tiles.shape, 1)
    down = pltpu.roll(tiles, stride, 1)
    up = pltpu.roll(tiles, SUBLANES - stride, 1)
    return jnp.where(spot & stride > 0, down, up).reshape(places, width)


def shifted(values, by):
    places, width = values.shape
    tiles = values.reshape(places // SUBLANES, SUBLANES, width)
    return pltpu.roll(tiles, by % SUBLANES, 1).reshape(places, width)


def step(plan, vector_ref, masked_refs, place_ref, inside_ref, rounded_ref, finish, kept, ready=None):
    span = plan.places // plan.levels_here
    for block in range(plan.lane_blocks):
        vector = vector_ref[:, pl.ds(block * LANES, LANES)]
        for position in range(plan.bits):
            rounded_ref[:, pl.ds(position * plan.rows + block * LANES, LANES)] = flipped(
                vector, plan.phonons << position
            ).astype(jnp.bfloat16)

    def local(start):
        lanes = pl.ds(start, LANES)
        vector = vector_ref[:, lanes]
        levels = [vector[index * span : (index + 1) * span] for index in range(plan.levels_here)]
        lower = jnp.concatenate([shifted(levels[-1], 1)] + levels[:-1], axis=0)
        upper = jnp.concatenate(levels[1:] + [shifted(levels[0], -1)], axis=0)
        weight = place_ref[0] + inside_ref[:1, lanes]
        total = weight * (place_ref[1] * lower + place_ref[2] * upper)
        for position in range(plan.bits):
            total = total + place_ref[3 + position, :1] * flipped(vector, plan.phonons << position)
        return total

    def product(lanes, position):
        return jnp.dot(
            rounded_ref[:, pl.ds(position * plan.rows, plan.rows)],
            masked_refs[position][:, lanes],
            preferred_element_type=jnp.float32,
        )

    for index, lanes in enumerate(parts_of(plan)):
        total = jnp.concatenate(
            [local(start) for start in range(lanes.start, lanes.start + lanes.size, LANES)], axis=1
        )
        for position in range(kept):
            total = total + product(lanes, position)
        if ready:
            ready(index)
        for position in range(kept, plan.bits):
            total = total + product(lanes, position)
        finish(lanes, total)


def parts_of(plan):
    return [pl.ds(start, 2 * LANES) for start in range(0, plan.rows, 2 * LANES)]


def first_kernel(plan, kept, arrived_ref, place_ref, inside_ref, *refs):
    masked_refs = refs[:kept]
    stored_refs = refs[kept : plan.bits]
    initial_ref, new_ref, sums_ref = refs[plan.bits : plan.bits + 3]
    fetched_refs = refs[plan.bits + 3 : -2]
    rounded_ref, semaphores = refs[-2:]
    parts = parts_of(plan)
    fetches = [
        [
            pltpu.make_async_copy(stored_ref.at[:, lanes], fetched_ref.at[:, lanes], semaphores.at[index, part])
            for index, (stored_ref, fetched_ref) in enumerate(zip(stored_refs, fetched_refs))
        ]
        for part, lanes in enumerate(parts)
    ]
    flying = 2

    def fetch(part):
        if part < len(parts):
            for copy in fetches[part]:
                copy.start()

    def ready(part):
        for copy in fetches[part]:
            copy.wait()
        fetch(part + flying)

    for part in range(flying):
        fetch(part)
    squares, _ = totals_of(arrived_ref, plan.body, plan.message, plan.groups)
    inverse = 1.0 / scale_of(plan, squares)
    for piece in range(plan.pieces):
        for block in range(plan.lane_blocks):
            part = arrived_ref[pl.ds(piece * plan.lane_blocks + block, plan.groups, stride=plan.message), :]
            initial_ref[pl.ds(piece * plan.groups, plan.groups), pl.ds(block * LANES, LANES)] = part * inverse
    squares = []
    overlap = []

    def finish(lanes, new):
        new_ref[:, lanes] = new
        squares.append(lane_sums(new * new))
        overlap.append(lane_sums(new * initial_ref[:, lanes]))

    tables = (place_ref, inside_ref)
    step(plan, initial_ref, (*masked_refs, *fetched_refs), *tables, rounded_ref, finish, kept, ready)
    put_sums(sums_ref, one_row(squares), one_row(overlap), 0, 1, plan.groups)


def one_row(rows):
    total = sum(rows[1:], rows[0])
    return sum(total[:, start : start + LANES] for start in range(0, total.shape[1], LANES))


def place(plan, arrived_ref, out_ref, turned_ref, semaphores, inverse):
    copies = []
    for block in range(plan.lane_blocks):
        rows = pl.ds(block * LANES, LANES)
        parts = [
            arrived_ref[pl.ds(piece * plan.lane_blocks + block, plan.groups, stride=plan.message), :]
            for piece in range(plan.pieces)
        ]
        turned_ref[rows, :] = (jnp.concatenate(parts, axis=0) * inverse).T
        if block % 2:
            half = block // 2
            rows = pl.ds((block - 1) * LANES, 2 * LANES)
            copy = pltpu.make_async_copy(turned_ref.at[rows, :], out_ref.at[rows, :], semaphores.at[half])
            copy.start()
            copies.append(copy)
    return copies


def later_kernel(plan, keep, arrived_ref, raw_ref, previous_ref, initial_ref, place_ref, inside_ref, *refs):
    masked_refs = refs[: plan.bits]
    if keep:
        current_ref, new_ref, out_ref, moment_ref, rounded_ref = refs[plan.bits :]
        squares, overlap = totals_of(arrived_ref, 0, 1, plan.groups)
    else:
        out_ref, moment_ref, placed_ref, rounded_ref, current_ref, turned_ref, semaphores = refs[plan.bits :]
        squares, overlap = totals_of(arrived_ref, plan.body, plan.message, plan.groups)
    inverse = 1.0 / scale_of(plan, squares)
    moment_ref[...] = jnp.broadcast_to(overlap * inverse / plan.entries, moment_ref.shape)
    copies = [] if keep else place(plan, arrived_ref, placed_ref, turned_ref, semaphores, inverse)
    for block in range(plan.lane_blocks):
        lanes = pl.ds(block * LANES, LANES)
        current_ref[:, lanes] = raw_ref[:, lanes] * inverse
    squares = []
    overlap = []

    def finish(lanes, total):
        new = 2.0 * total - previous_ref[:, lanes] * inverse
        if keep:
            new_ref[:, lanes] = new
        squares.append(lane_sums(new * new))
        overlap.append(lane_sums(new * initial_ref[:, lanes]))
        for start in range(0, lanes.size, LANES):
            block = (lanes.start + start) // LANES
            for piece in range(plan.pieces):
                out_ref[pl.ds(piece * plan.lane_blocks + block, plan.groups, stride=plan.message), :] = new[
                    piece * plan.groups : (piece + 1) * plan.groups, start : start + LANES
                ]

    step(plan, current_ref, masked_refs, place_ref, inside_ref, rounded_ref, finish, plan.bits)
    put_sums(out_ref, one_row(squares), one_row(overlap), plan.body, plan.message, plan.groups)
    for copy in copies:
        copy.wait()


def arrive_kernel(plan, arrived_ref, first_ref, second_ref, out_ref, moments_ref, turned_ref, semaphores):
    squares, overlap = totals_of(arrived_ref, plan.body, plan.message, plan.groups)
    inverse = 1.0 / scale_of(plan, squares)
    copies = place(plan, arrived_ref, out_ref, turned_ref, semaphores, inverse)
    moment = overlap * inverse / plan.entries
    moments_ref[0] = first_ref[0, 0]
    moments_ref[1] = second_ref[0, 0]
    moments_ref[2] = moment[0, 0]
    for copy in copies:
        copy.wait()


def exchange(values, count):
    shaped = values.reshape(count, values.shape[0] // count, 1, LANES)
    return lax.all_to_all(shaped, AXES, 0, 0, tiled=True).reshape(values.shape)


def shards(plan, state, operators, op_mask, site_bits, field, site_coupling, mode_coupling):
    f32 = jnp.float32
    message = jax.ShapeDtypeStruct((plan.groups * plan.message, LANES), f32)
    vector = jax.ShapeDtypeStruct((plan.places, plan.rows), f32)
    moment = jax.ShapeDtypeStruct((SUBLANES, LANES), f32)
    held = jax.ShapeDtypeStruct((plan.rows, plan.columns), f32)
    rounded = pltpu.VMEM((plan.places, plan.bits * plan.rows), jnp.bfloat16)
    turned = [pltpu.VMEM((plan.rows, plan.columns), f32), pltpu.SemaphoreType.DMA((plan.lane_blocks // 2,))]
    working = pltpu.VMEM((plan.places, plan.rows), f32)
    work = 2 * plan.bits * plan.places * plan.rows * plan.rows

    def cost(flops, moved):
        return pl.CostEstimate(flops=flops, bytes_accessed=moved, transcendentals=0)

    departing = pl.pallas_call(
        functools.partial(depart_kernel, plan),
        out_shape=message,
        in_specs=[HBM],
        out_specs=VMEM,
        scratch_shapes=[pltpu.VMEM((plan.rows, plan.columns), f32), pltpu.SemaphoreType.DMA((2,))],
        compiler_params=params(60),
        name="depart",
    )(state)
    arrived = exchange(departing, plan.groups)
    operator = jax.ShapeDtypeStruct((plan.rows, plan.rows), jnp.bfloat16)
    kept = 1
    fetched = plan.bits - kept
    place, inside, *masked = pl.pallas_call(
        functools.partial(prepare_kernel, plan, kept),
        out_shape=[
            jax.ShapeDtypeStruct((3 + plan.bits, plan.places, LANES), f32),
            jax.ShapeDtypeStruct((SUBLANES, plan.rows), f32),
        ]
        + [operator] * kept,
        in_specs=[SMEM] * 5 + [HBM],
        out_specs=[VMEM] * (2 + kept),
        scratch_shapes=[
            pltpu.VMEM((kept, plan.rows, plan.rows), jnp.bfloat16),
            pltpu.SemaphoreType.DMA((kept,)),
        ],
        compiler_params=params(50),
        cost_estimate=cost(plan.rows * plan.rows, 4 * kept * plan.rows * plan.rows),
        name="prepare",
    )(site_bits, op_mask, field, site_coupling, mode_coupling, operators)
    stored = pl.pallas_call(
        functools.partial(store_kernel, plan, kept),
        out_shape=[operator] * fetched,
        in_specs=[SMEM] * 2 + [HBM],
        out_specs=[HBM] * fetched,
        scratch_shapes=[
            pltpu.VMEM((fetched, plan.rows, plan.rows), jnp.bfloat16),
            pltpu.VMEM((fetched, plan.rows, plan.rows), jnp.bfloat16),
            pltpu.SemaphoreType.DMA((fetched,)),
            pltpu.SemaphoreType.DMA((fetched,)),
        ],
        compiler_params=params(60),
        cost_estimate=cost(plan.rows * plan.rows, 4 * fetched * plan.rows * plan.rows),
        name="store",
    )(site_bits, op_mask, operators)
    initial, raw, sums, *fetched_masked = pl.pallas_call(
        functools.partial(first_kernel, plan, kept),
        out_shape=[vector, vector, jax.ShapeDtypeStruct((plan.groups, LANES), f32)] + [operator] * fetched,
        in_specs=[VMEM] * 4 + [HBM] * fetched,
        out_specs=[VMEM] * (3 + fetched),
        scratch_shapes=[rounded, pltpu.SemaphoreType.DMA((fetched, len(parts_of(plan))))],
        compiler_params=params(46),
        cost_estimate=cost(work, 4 * plan.places * plan.rows),
        name="first",
    )(arrived, place, inside, *masked, *stored)
    tables = (place, inside, *masked, *fetched_masked)
    sums = exchange(sums, plan.groups)
    current, raw, departing, moment_one = pl.pallas_call(
        functools.partial(later_kernel, plan, True),
        out_shape=[vector, vector, message, moment],
        in_specs=[VMEM] * (6 + plan.bits),
        out_specs=[VMEM] * 4,
        scratch_shapes=[rounded],
        compiler_params=params(32),
        cost_estimate=cost(work, 4 * plan.places * plan.rows),
        name="second",
    )(sums, raw, initial, initial, *tables)
    before = exchange(departing, plan.groups)
    departing, moment_two, before = pl.pallas_call(
        functools.partial(later_kernel, plan, False),
        out_shape=[message, moment, held],
        in_specs=[VMEM] * (6 + plan.bits),
        out_specs=[VMEM, VMEM, HBM],
        scratch_shapes=[rounded, working, *turned],
        compiler_params=params(32),
        cost_estimate=cost(work, 4 * plan.places * plan.rows),
        name="third",
    )(before, raw, current, initial, *tables)
    last = exchange(departing, plan.groups)
    last, moments = pl.pallas_call(
        functools.partial(arrive_kernel, plan),
        out_shape=[held, jax.ShapeDtypeStruct((STEPS,), f32)],
        in_specs=[VMEM] * 3,
        out_specs=[HBM, SMEM],
        scratch_shapes=turned,
        compiler_params=params(16),
        name="arrive_last",
    )(last, moment_one, moment_two)
    return last, before, moments


def extended_2(block, sides, width):
    for axis, dim in sides:
        count = lax.axis_size(axis)
        forward = [(i, i + 1) for i in range(count - 1)]
        backward = [(target, source) for source, target in forward]
        low = lax.ppermute(
            lax.slice_in_dim(block, block.shape[dim] - width, None, axis=dim), axis, forward
        )
        high = lax.ppermute(lax.slice_in_dim(block, 0, width, axis=dim), axis, backward)
        block = jnp.concatenate([low, block, high], axis=dim)
    return block


def partner(value, axis, bit):
    mask = 2**bit
    pairs = [(source, source ^ mask) for source in range(lax.axis_size(axis))]
    return lax.ppermute(value, axis, pairs)


def halo_shards(state, operators, op_mask, site_bits, field, site_coupling, mode_coupling):
    site_count = lax.axis_size("site")
    phonon_count = lax.axis_size("phonon")
    bit_count = site_count.bit_length() - 1
    rows_here = state.shape[0]
    columns_here = state.shape[1]
    levels_here = columns_here // MODES
    block_edge = rows_here // op_mask.shape[1]
    expanded = jnp.repeat(jnp.repeat(op_mask, block_edge, axis=1), block_edge, axis=2)
    masked = jnp.where(expanded > 0, operators, jnp.zeros((), jnp.bfloat16))
    entries = jnp.float32(rows_here * columns_here * site_count * phonon_count)
    level_total = jnp.sqrt(jnp.float32(levels_here * phonon_count))
    device = lax.axis_index("site")
    inside = lax.iota(jnp.int32, rows_here)
    weight_rows = jnp.zeros((rows_here,), jnp.float32)
    for position in range(bit_count):
        weight_rows = weight_rows + site_coupling[site_bits[position]] * (
            device >> position & 1
        ).astype(jnp.float32)
    for local_bit in range(LBITS):
        weight_rows = weight_rows + site_coupling[bit_count + local_bit] * (
            inside >> local_bit & 1
        ).astype(jnp.float32)
    levels = (
        lax.axis_index("phonon") * levels_here + lax.iota(jnp.int32, columns_here) // MODES
    ).astype(jnp.float32)
    lower_weight = jnp.sqrt(levels)
    upper_weight = jnp.sqrt(levels + 1.0)
    mode_weight = jnp.tile(mode_coupling, columns_here // MODES) / level_total
    start_squares = lax.psum(jnp.sum(state * state), ("site", "phonon"))
    initial = state / jnp.sqrt(start_squares / entries + epsilon)
    previous = initial
    current = initial
    scale_prev = jnp.float32(1.0)
    moments = []
    for iteration in range(STEPS):
        extended = extended_2(current, (("phonon", 1),), MODES)
        lower_part = extended[:, :columns_here]
        upper_part = extended[:, 2 * MODES :]
        summed = weight_rows[:, None] * (
            mode_weight * (lower_weight * lower_part + upper_weight * upper_part)
        )
        for operate_position in range(bit_count):
            chosen = site_bits[operate_position]
            flipped = partner(current, "site", operate_position)
            product = jnp.dot(
                masked[chosen], flipped.astype(jnp.bfloat16), preferred_element_type=jnp.float32
            )
            summed = summed + (field[chosen] * flipped + product)
        if iteration == 0:
            vector_new = summed
        else:
            vector_new = 2.0 * summed - previous / scale_prev
        squares, intersection = lax.psum(
            (jnp.sum(vector_new * vector_new), jnp.sum(initial * vector_new)), ("site", "phonon")
        )
        scale_now = jnp.sqrt(squares / entries + epsilon)
        updated = vector_new / scale_now
        moment = intersection / (entries * scale_now)
        moments.append(moment)
        previous = current
        current = updated
        scale_prev = scale_now
    return (current, previous, jnp.stack(moments))


def solution(mesh):
    in_specs = (P("site", "phonon"), P(), P(), P(), P(), P(), P())
    out_specs = (P("site", "phonon"), P("site", "phonon"), P())

    def whole(state, operators, op_mask, *rest):
        rows = state.shape[0] // mesh.shape["site"]
        columns = state.shape[1] // mesh.shape["phonon"]
        plan = Plan(mesh, rows, columns, op_mask.shape[1])
        body = functools.partial(shards, plan) if plan.fits() else halo_shards
        run = jax.shard_map(body, mesh=mesh, in_specs=in_specs, out_specs=out_specs, check_vma=False)
        return run(state, operators, op_mask, *rest)

    return whole
```

```python
import functools

import jax
import jax.numpy as jnp
from jax import lax
from jax.experimental import pallas as pl
from jax.experimental.pallas import tpu as pltpu
from jax.sharding import PartitionSpec as P

LBITS = 10
MODES = 64
STEPS = 3
LANES = 128
SUBLANES = 8
EXTRA = 1
AXES = ("site", "phonon")

epsilon = 1e-06


VMEM = pl.BlockSpec(memory_space=pltpu.VMEM)
SMEM = pl.BlockSpec(memory_space=pltpu.SMEM)
HBM = pl.BlockSpec(memory_space=pltpu.HBM)


class Plan:
    def __init__(self, mesh, rows, columns, blocks):
        self.sites = mesh.shape["site"]
        self.phonons = mesh.shape["phonon"]
        self.groups = self.sites * self.phonons
        self.bits = self.sites.bit_length() - 1
        self.rows = rows
        self.columns = columns
        self.blocks = blocks
        self.edge = rows // blocks
        self.levels_here = columns // MODES
        self.level_count = self.levels_here * self.phonons
        self.share = MODES // self.groups
        self.pieces = self.levels_here * self.share
        self.lane_blocks = rows // LANES
        self.body = self.pieces * self.lane_blocks
        self.message = self.body + EXTRA
        self.places = self.pieces * self.groups
        self.width = 2 * LANES
        self.parts = rows // self.width
        self.entries = float(rows * columns * self.groups)

    def fits(self):
        return (
            MODES % self.groups == 0
            and self.columns == LANES
            and self.rows % self.width == 0
            and self.edge % LANES == 0
            and self.width % self.edge == 0
            and self.groups % SUBLANES == 0
        )


def params(mib):
    return pltpu.CompilerParams(vmem_limit_bytes=mib * 2**20)


def lane_sums(values):
    return jnp.sum(values, axis=0, keepdims=True)


def folded(value):
    return value + pltpu.roll(value, LANES // 2, 1)


def put_sums(out_ref, squares, overlap, start, stride, count):
    lane = lax.broadcasted_iota(jnp.int32, (1, LANES), 1)
    row = jnp.where(lane < LANES // 2, folded(squares), folded(overlap))
    out_ref[pl.ds(start, count, stride=stride), :] = jnp.broadcast_to(row, (count, LANES))


def totals_of(ref, start, stride, count):
    lanes = lane_sums(ref[pl.ds(start, count, stride=stride), :])
    lane = lax.broadcasted_iota(jnp.int32, (1, LANES), 1)
    squares = jnp.sum(jnp.where(lane < LANES // 2, lanes, 0.0), axis=1, keepdims=True)
    overlap = jnp.sum(jnp.where(lane < LANES // 2, 0.0, lanes), axis=1, keepdims=True)
    return squares, overlap


def scale_of(plan, squares):
    return jnp.sqrt(squares / plan.entries + epsilon)


def depart_kernel(plan, state_ref, out_ref, held_ref, semaphores):
    half = plan.rows // 2
    fetches = [
        pltpu.make_async_copy(
            state_ref.at[pl.ds(index * half, half), :], held_ref.at[pl.ds(index * half, half), :], semaphores.at[index]
        )
        for index in range(2)
    ]
    for fetch in fetches:
        fetch.start()
    sums = jnp.zeros((1, LANES), jnp.float32)
    for block in range(plan.lane_blocks):
        if block * LANES % half == 0:
            fetches[block * LANES // half].wait()
        tile = held_ref[pl.ds(block * LANES, LANES), :]
        sums = sums + lane_sums(tile * tile)
        turned = tile.T
        for piece in range(plan.pieces):
            out_ref[pl.ds(piece * plan.lane_blocks + block, plan.groups, stride=plan.message), :] = turned[
                piece * plan.groups : (piece + 1) * plan.groups
            ]
    put_sums(out_ref, sums, jnp.zeros_like(sums), plan.body, plan.message, plan.groups)


def mask_operator(plan, chosen, mask_ref, held_ref, out_ref):
    for across in range(plan.blocks):
        rows = pl.ds(across * plan.edge, plan.edge)
        for along in range(plan.blocks):
            columns = pl.ds(along * plan.edge, plan.edge)
            keep = (mask_ref[chosen, across, along] > 0).astype(jnp.float32).astype(jnp.bfloat16)
            part, start = divmod(across * plan.edge, plan.width)
            out_ref[part, columns, pl.ds(start, plan.edge)] = (held_ref[rows, columns] * keep).T


def store_kernel(plan, kept, bits_ref, mask_ref, operators_ref, *refs):
    count = plan.bits - kept
    stored_refs, (held_ref, masked_ref, in_semaphores, out_semaphores) = refs[:count], refs[count:]
    fetches = [
        pltpu.make_async_copy(operators_ref.at[bits_ref[kept + index]], held_ref.at[index], in_semaphores.at[index])
        for index in range(count)
    ]
    for fetch in fetches:
        fetch.start()
    stores = []
    for index in range(count):
        fetches[index].wait()
        mask_operator(plan, bits_ref[kept + index], mask_ref, held_ref.at[index], masked_ref.at[index])
        store = pltpu.make_async_copy(masked_ref.at[index], stored_refs[index], out_semaphores.at[index])
        store.start()
        stores.append(store)
    for store in stores:
        store.wait()


def prepare_kernel(
    plan,
    kept,
    bits_ref,
    mask_ref,
    field_ref,
    coupling_ref,
    mode_ref,
    operators_ref,
    place_ref,
    inside_ref,
    *refs,
):
    masked_refs, (held_ref, semaphores) = refs[:kept], refs[kept:]
    fetches = [
        pltpu.make_async_copy(operators_ref.at[bits_ref[index]], held_ref.at[index], semaphores.at[index])
        for index in range(kept)
    ]
    for fetch in fetches:
        fetch.start()
    me = lax.axis_index("site") * plan.phonons + lax.axis_index("phonon")
    place = lax.broadcasted_iota(jnp.int32, (plan.places, LANES), 0)
    phonon = place % plan.phonons
    site = place // plan.phonons % plan.sites
    mode = place // plan.groups % plan.share
    level = phonon * plan.levels_here + place // (plan.groups * plan.share)
    occupied = jnp.zeros((plan.places, LANES), jnp.float32)
    for position in range(plan.bits):
        held = (site >> position & 1).astype(jnp.float32)
        occupied = occupied + coupling_ref[bits_ref[position]] * held
    strength = jnp.zeros((plan.places, LANES), jnp.float32)
    for index in range(plan.share):
        strength = jnp.where(mode == index, mode_ref[index * plan.groups + me], strength)
    strength = strength / jnp.sqrt(jnp.full((1, LANES), plan.level_count, jnp.float32))
    height = level.astype(jnp.float32)
    place_ref[0] = occupied
    place_ref[1] = strength * jnp.sqrt(height)
    place_ref[2] = jnp.where(level == plan.level_count - 1, 0.0, strength * jnp.sqrt(height + 1.0))
    for position in range(plan.bits):
        place_ref[3 + position] = jnp.full((plan.places, LANES), field_ref[bits_ref[position]])
    inside = lax.broadcasted_iota(jnp.int32, (SUBLANES, plan.rows), 1)
    weight = jnp.zeros((SUBLANES, plan.rows), jnp.float32)
    for local_bit in range(LBITS):
        weight = weight + coupling_ref[plan.bits + local_bit] * (inside >> local_bit & 1).astype(jnp.float32)
    inside_ref[...] = weight
    for index in range(kept):
        fetches[index].wait()
        mask_operator(plan, bits_ref[index], mask_ref, held_ref.at[index], masked_refs[index])


def flipped(values, stride):
    places, width = values.shape
    if stride % SUBLANES == 0:
        shaped = values.reshape(places // (2 * stride), 2, stride, width)
        return jnp.concatenate([shaped[:, 1:], shaped[:, :1]], axis=1).reshape(places, width)
    tiles = values.reshape(places // SUBLANES, SUBLANES, width)
    if 2 * stride == SUBLANES:
        return pltpu.roll(tiles, stride, 1).reshape(places, width)
    spot = lax.broadcasted_iota(jnp.int32, tiles.shape, 1)
    down = pltpu.roll(tiles, stride, 1)
    up = pltpu.roll(tiles, SUBLANES - stride, 1)
    return jnp.where(spot & stride > 0, down, up).reshape(places, width)


def shifted(values, by):
    places, width = values.shape
    tiles = values.reshape(places // SUBLANES, SUBLANES, width)
    return pltpu.roll(tiles, by % SUBLANES, 1).reshape(places, width)


def step(plan, vector_ref, masked_refs, place_ref, inside_ref, rounded_ref, finish, kept, ready=None, begun_ref=None):
    span = plan.places // plan.levels_here
    for block in range(plan.lane_blocks):
        vector = vector_ref[:, pl.ds(block * LANES, LANES)]
        for position in range(plan.bits):
            rounded_ref[:, pl.ds(position * plan.rows + block * LANES, LANES)] = flipped(
                vector, plan.phonons << position
            ).astype(jnp.bfloat16)

    def local(start):
        lanes = pl.ds(start, LANES)
        vector = vector_ref[:, lanes]
        levels = [vector[index * span : (index + 1) * span] for index in range(plan.levels_here)]
        lower = jnp.concatenate([shifted(levels[-1], 1)] + levels[:-1], axis=0)
        upper = jnp.concatenate(levels[1:] + [shifted(levels[0], -1)], axis=0)
        weight = place_ref[0] + inside_ref[:1, lanes]
        total = weight * (place_ref[1] * lower + place_ref[2] * upper)
        for position in range(plan.bits):
            total = total + place_ref[3 + position, :1] * flipped(vector, plan.phonons << position)
        return total

    def product(part, position):
        return jnp.dot(
            rounded_ref[:, pl.ds(position * plan.rows, plan.rows)],
            masked_refs[position][part],
            preferred_element_type=jnp.float32,
        )

    def begun(lanes, part):
        total = jnp.concatenate([local(start) for start in range(lanes.start, lanes.start + plan.width, LANES)], axis=1)
        for position in range(kept):
            total = total + product(part, position)
        return total

    parts = [pl.ds(part * plan.width, plan.width) for part in range(plan.parts)]
    if ready is None:
        for part, lanes in enumerate(parts):
            finish(lanes, begun(lanes, part))
        return
    for part, lanes in enumerate(parts):
        begun_ref[:, lanes] = begun(lanes, part)
    for part, lanes in enumerate(parts):
        total = begun_ref[:, lanes]
        for position in range(kept, plan.bits):
            ready(part, position)
            total = total + product(part, position)
        finish(lanes, total)


def first_kernel(plan, kept, arrived_ref, place_ref, inside_ref, *refs):
    masked_refs = refs[:kept]
    stored_refs = refs[kept : plan.bits]
    initial_ref, new_ref, sums_ref = refs[plan.bits : plan.bits + 3]
    fetched_refs = refs[plan.bits + 3 : -2]
    rounded_ref, semaphores = refs[-2:]
    fetches = {}
    for part in range(plan.parts):
        for index, (stored_ref, fetched_ref) in enumerate(zip(stored_refs, fetched_refs)):
            fetch = pltpu.make_async_copy(stored_ref.at[part], fetched_ref.at[part], semaphores.at[index, part])
            fetch.start()
            fetches[part, kept + index] = fetch

    def ready(part, position):
        fetches[part, position].wait()

    squares, _ = totals_of(arrived_ref, plan.body, plan.message, plan.groups)
    inverse = 1.0 / scale_of(plan, squares)
    for piece in range(plan.pieces):
        for block in range(plan.lane_blocks):
            part = arrived_ref[pl.ds(piece * plan.lane_blocks + block, plan.groups, stride=plan.message), :]
            initial_ref[pl.ds(piece * plan.groups, plan.groups), pl.ds(block * LANES, LANES)] = part * inverse
    squares = []
    overlap = []

    def finish(lanes, new):
        new_ref[:, lanes] = new
        squares.append(lane_sums(new * new))
        overlap.append(lane_sums(new * initial_ref[:, lanes]))

    tables = (place_ref, inside_ref)
    step(plan, initial_ref, (*masked_refs, *fetched_refs), *tables, rounded_ref, finish, kept, ready, new_ref)
    put_sums(sums_ref, one_row(squares), one_row(overlap), 0, 1, plan.groups)


def one_row(rows):
    total = sum(rows[1:], rows[0])
    return sum(total[:, start : start + LANES] for start in range(0, total.shape[1], LANES))


def place(plan, arrived_ref, out_ref):
    squares, overlap = totals_of(arrived_ref, plan.body, plan.message, plan.groups)
    inverse = 1.0 / scale_of(plan, squares)
    for block in range(plan.lane_blocks):
        parts = [
            arrived_ref[pl.ds(piece * plan.lane_blocks + block, plan.groups, stride=plan.message), :]
            for piece in range(plan.pieces)
        ]
        out_ref[pl.ds(block * LANES, LANES), :] = (jnp.concatenate(parts, axis=0) * inverse).T
    return overlap * inverse / plan.entries


def later_kernel(plan, keep, arrived_ref, raw_ref, previous_ref, initial_ref, place_ref, inside_ref, *refs):
    masked_refs = refs[: plan.bits]
    if keep:
        current_ref, new_ref, out_ref, moment_ref, rounded_ref = refs[plan.bits :]
        squares, overlap = totals_of(arrived_ref, 0, 1, plan.groups)
    else:
        out_ref, rounded_ref, current_ref = refs[plan.bits :]
        squares, overlap = totals_of(arrived_ref, plan.body, plan.message, plan.groups)
    inverse = 1.0 / scale_of(plan, squares)
    if keep:
        moment_ref[...] = jnp.broadcast_to(overlap * inverse / plan.entries, moment_ref.shape)
    for block in range(plan.lane_blocks):
        lanes = pl.ds(block * LANES, LANES)
        current_ref[:, lanes] = raw_ref[:, lanes] * inverse
    squares = []
    overlap = []

    def finish(lanes, total):
        new = 2.0 * total - previous_ref[:, lanes] * inverse
        if keep:
            new_ref[:, lanes] = new
        squares.append(lane_sums(new * new))
        overlap.append(lane_sums(new * initial_ref[:, lanes]))
        for start in range(0, lanes.size, LANES):
            block = (lanes.start + start) // LANES
            for piece in range(plan.pieces):
                out_ref[pl.ds(piece * plan.lane_blocks + block, plan.groups, stride=plan.message), :] = new[
                    piece * plan.groups : (piece + 1) * plan.groups, start : start + LANES
                ]

    step(plan, current_ref, masked_refs, place_ref, inside_ref, rounded_ref, finish, plan.bits)
    put_sums(out_ref, one_row(squares), one_row(overlap), plan.body, plan.message, plan.groups)


def arrive_kernel(plan, before_ref, last_ref, moment_ref, before_out_ref, last_out_ref, moments_ref):
    second = place(plan, before_ref, before_out_ref)
    third = place(plan, last_ref, last_out_ref)
    moments_ref[0] = moment_ref[0, 0]
    moments_ref[1] = second[0, 0]
    moments_ref[2] = third[0, 0]


def exchange(values, count):
    shaped = values.reshape(count, values.shape[0] // count, 1, LANES)
    return lax.all_to_all(shaped, AXES, 0, 0, tiled=True).reshape(values.shape)


def shards(plan, state, operators, op_mask, site_bits, field, site_coupling, mode_coupling):
    f32 = jnp.float32
    message = jax.ShapeDtypeStruct((plan.groups * plan.message, LANES), f32)
    vector = jax.ShapeDtypeStruct((plan.places, plan.rows), f32)
    moment = jax.ShapeDtypeStruct((SUBLANES, LANES), f32)
    held = jax.ShapeDtypeStruct((plan.rows, plan.columns), f32)
    rounded = pltpu.VMEM((plan.places, plan.bits * plan.rows), jnp.bfloat16)
    working = pltpu.VMEM((plan.places, plan.rows), f32)
    work = 2 * plan.bits * plan.places * plan.rows * plan.rows

    def cost(flops, moved):
        return pl.CostEstimate(flops=flops, bytes_accessed=moved, transcendentals=0)

    departing = pl.pallas_call(
        functools.partial(depart_kernel, plan),
        out_shape=message,
        in_specs=[HBM],
        out_specs=VMEM,
        scratch_shapes=[pltpu.VMEM((plan.rows, plan.columns), f32), pltpu.SemaphoreType.DMA((2,))],
        compiler_params=params(60),
        name="depart",
    )(state)
    arrived = exchange(departing, plan.groups)
    operator = jax.ShapeDtypeStruct((plan.parts, plan.rows, plan.width), jnp.bfloat16)
    kept = 1
    fetched = plan.bits - kept
    place, inside, *masked = pl.pallas_call(
        functools.partial(prepare_kernel, plan, kept),
        out_shape=[
            jax.ShapeDtypeStruct((3 + plan.bits, plan.places, LANES), f32),
            jax.ShapeDtypeStruct((SUBLANES, plan.rows), f32),
        ]
        + [operator] * kept,
        in_specs=[SMEM] * 5 + [HBM],
        out_specs=[VMEM] * (2 + kept),
        scratch_shapes=[
            pltpu.VMEM((kept, plan.rows, plan.rows), jnp.bfloat16),
            pltpu.SemaphoreType.DMA((kept,)),
        ],
        compiler_params=params(50),
        cost_estimate=cost(plan.rows * plan.rows, 4 * kept * plan.rows * plan.rows),
        name="prepare",
    )(site_bits, op_mask, field, site_coupling, mode_coupling, operators)
    stored = pl.pallas_call(
        functools.partial(store_kernel, plan, kept),
        out_shape=[operator] * fetched,
        in_specs=[SMEM] * 2 + [HBM],
        out_specs=[HBM] * fetched,
        scratch_shapes=[
            pltpu.VMEM((fetched, plan.rows, plan.rows), jnp.bfloat16),
            pltpu.VMEM((fetched, *operator.shape), jnp.bfloat16),
            pltpu.SemaphoreType.DMA((fetched,)),
            pltpu.SemaphoreType.DMA((fetched,)),
        ],
        compiler_params=params(60),
        cost_estimate=cost(plan.rows * plan.rows, 4 * fetched * plan.rows * plan.rows),
        name="store",
    )(site_bits, op_mask, operators)
    initial, raw, sums, *fetched_masked = pl.pallas_call(
        functools.partial(first_kernel, plan, kept),
        out_shape=[vector, vector, jax.ShapeDtypeStruct((plan.groups, LANES), f32)] + [operator] * fetched,
        in_specs=[VMEM] * 4 + [HBM] * fetched,
        out_specs=[VMEM] * (3 + fetched),
        scratch_shapes=[rounded, pltpu.SemaphoreType.DMA((fetched, plan.parts))],
        compiler_params=params(46),
        cost_estimate=cost(work, 4 * plan.places * plan.rows),
        name="first",
    )(arrived, place, inside, *masked, *stored)
    tables = (place, inside, *masked, *fetched_masked)
    sums = exchange(sums, plan.groups)
    current, raw, departing, moment_one = pl.pallas_call(
        functools.partial(later_kernel, plan, True),
        out_shape=[vector, vector, message, moment],
        in_specs=[VMEM] * (6 + plan.bits),
        out_specs=[VMEM] * 4,
        scratch_shapes=[rounded],
        compiler_params=params(32),
        cost_estimate=cost(work, 4 * plan.places * plan.rows),
        name="second",
    )(sums, raw, initial, initial, *tables)
    before = exchange(departing, plan.groups)
    departing = pl.pallas_call(
        functools.partial(later_kernel, plan, False),
        out_shape=message,
        in_specs=[VMEM] * (6 + plan.bits),
        out_specs=VMEM,
        scratch_shapes=[rounded, working],
        compiler_params=params(32),
        cost_estimate=cost(work, 4 * plan.places * plan.rows),
        name="third",
    )(before, raw, current, initial, *tables)
    last = exchange(departing, plan.groups)
    before, last, moments = pl.pallas_call(
        functools.partial(arrive_kernel, plan),
        out_shape=[held, held, jax.ShapeDtypeStruct((STEPS,), f32)],
        in_specs=[VMEM] * 3,
        out_specs=[VMEM, VMEM, SMEM],
        compiler_params=params(16),
        name="arrive",
    )(before, last, moment_one)
    return last, before, moments


def extended_2(block, sides, width):
    for axis, dim in sides:
        count = lax.axis_size(axis)
        forward = [(i, i + 1) for i in range(count - 1)]
        backward = [(target, source) for source, target in forward]
        low = lax.ppermute(
            lax.slice_in_dim(block, block.shape[dim] - width, None, axis=dim), axis, forward
        )
        high = lax.ppermute(lax.slice_in_dim(block, 0, width, axis=dim), axis, backward)
        block = jnp.concatenate([low, block, high], axis=dim)
    return block


def partner(value, axis, bit):
    mask = 2**bit
    pairs = [(source, source ^ mask) for source in range(lax.axis_size(axis))]
    return lax.ppermute(value, axis, pairs)


def halo_shards(state, operators, op_mask, site_bits, field, site_coupling, mode_coupling):
    site_count = lax.axis_size("site")
    phonon_count = lax.axis_size("phonon")
    bit_count = site_count.bit_length() - 1
    rows_here = state.shape[0]
    columns_here = state.shape[1]
    levels_here = columns_here // MODES
    block_edge = rows_here // op_mask.shape[1]
    expanded = jnp.repeat(jnp.repeat(op_mask, block_edge, axis=1), block_edge, axis=2)
    masked = jnp.where(expanded > 0, operators, jnp.zeros((), jnp.bfloat16))
    entries = jnp.float32(rows_here * columns_here * site_count * phonon_count)
    level_total = jnp.sqrt(jnp.float32(levels_here * phonon_count))
    device = lax.axis_index("site")
    inside = lax.iota(jnp.int32, rows_here)
    weight_rows = jnp.zeros((rows_here,), jnp.float32)
    for position in range(bit_count):
        weight_rows = weight_rows + site_coupling[site_bits[position]] * (
            device >> position & 1
        ).astype(jnp.float32)
    for local_bit in range(LBITS):
        weight_rows = weight_rows + site_coupling[bit_count + local_bit] * (
            inside >> local_bit & 1
        ).astype(jnp.float32)
    levels = (
        lax.axis_index("phonon") * levels_here + lax.iota(jnp.int32, columns_here) // MODES
    ).astype(jnp.float32)
    lower_weight = jnp.sqrt(levels)
    upper_weight = jnp.sqrt(levels + 1.0)
    mode_weight = jnp.tile(mode_coupling, columns_here // MODES) / level_total
    start_squares = lax.psum(jnp.sum(state * state), ("site", "phonon"))
    initial = state / jnp.sqrt(start_squares / entries + epsilon)
    previous = initial
    current = initial
    scale_prev = jnp.float32(1.0)
    moments = []
    for iteration in range(STEPS):
        extended = extended_2(current, (("phonon", 1),), MODES)
        lower_part = extended[:, :columns_here]
        upper_part = extended[:, 2 * MODES :]
        summed = weight_rows[:, None] * (
            mode_weight * (lower_weight * lower_part + upper_weight * upper_part)
        )
        for operate_position in range(bit_count):
            chosen = site_bits[operate_position]
            flipped = partner(current, "site", operate_position)
            product = jnp.dot(
                masked[chosen], flipped.astype(jnp.bfloat16), preferred_element_type=jnp.float32
            )
            summed = summed + (field[chosen] * flipped + product)
        if iteration == 0:
            vector_new = summed
        else:
            vector_new = 2.0 * summed - previous / scale_prev
        squares, intersection = lax.psum(
            (jnp.sum(vector_new * vector_new), jnp.sum(initial * vector_new)), ("site", "phonon")
        )
        scale_now = jnp.sqrt(squares / entries + epsilon)
        updated = vector_new / scale_now
        moment = intersection / (entries * scale_now)
        moments.append(moment)
        previous = current
        current = updated
        scale_prev = scale_now
    return (current, previous, jnp.stack(moments))


def solution(mesh):
    in_specs = (P("site", "phonon"), P(), P(), P(), P(), P(), P())
    out_specs = (P("site", "phonon"), P("site", "phonon"), P())

    def whole(state, operators, op_mask, *rest):
        rows = state.shape[0] // mesh.shape["site"]
        columns = state.shape[1] // mesh.shape["phonon"]
        plan = Plan(mesh, rows, columns, op_mask.shape[1])
        body = functools.partial(shards, plan) if plan.fits() else halo_shards
        run = jax.shard_map(body, mesh=mesh, in_specs=in_specs, out_specs=out_specs, check_vma=False)
        return run(state, operators, op_mask, *rest)

    return whole
```

```python
import functools

import jax
import jax.numpy as jnp
from jax import lax
from jax.experimental import pallas as pl
from jax.experimental.pallas import tpu as pltpu
from jax.sharding import PartitionSpec as P

LBITS = 10
MODES = 64
STEPS = 3
LANES = 128
SUBLANES = 8
EXTRA = 1
AXES = ("site", "phonon")

epsilon = 1e-06


VMEM = pl.BlockSpec(memory_space=pltpu.VMEM)
SMEM = pl.BlockSpec(memory_space=pltpu.SMEM)
HBM = pl.BlockSpec(memory_space=pltpu.HBM)


class Plan:
    def __init__(self, mesh, rows, columns, blocks):
        self.sites = mesh.shape["site"]
        self.phonons = mesh.shape["phonon"]
        self.groups = self.sites * self.phonons
        self.bits = self.sites.bit_length() - 1
        self.rows = rows
        self.columns = columns
        self.blocks = blocks
        self.edge = rows // blocks
        self.levels_here = columns // MODES
        self.level_count = self.levels_here * self.phonons
        self.share = MODES // self.groups
        self.pieces = self.levels_here * self.share
        self.lane_blocks = rows // LANES
        self.body = self.pieces * self.lane_blocks
        self.message = self.body + EXTRA
        self.places = self.pieces * self.groups
        self.width = 2 * LANES
        self.parts = rows // self.width
        self.entries = float(rows * columns * self.groups)

    def fits(self):
        return (
            MODES % self.groups == 0
            and self.columns == LANES
            and self.rows % self.width == 0
            and self.edge % LANES == 0
            and self.width % self.edge == 0
            and self.groups % SUBLANES == 0
        )


def params(mib):
    return pltpu.CompilerParams(vmem_limit_bytes=mib * 2**20)


def lane_sums(values):
    return jnp.sum(values, axis=0, keepdims=True)


def folded(value):
    return value + pltpu.roll(value, LANES // 2, 1)


def put_sums(out_ref, squares, overlap, start, stride, count):
    lane = lax.broadcasted_iota(jnp.int32, (1, LANES), 1)
    row = jnp.where(lane < LANES // 2, folded(squares), folded(overlap))
    out_ref[pl.ds(start, count, stride=stride), :] = jnp.broadcast_to(row, (count, LANES))


def totals_of(ref, start, stride, count):
    lanes = lane_sums(ref[pl.ds(start, count, stride=stride), :])
    lane = lax.broadcasted_iota(jnp.int32, (1, LANES), 1)
    squares = jnp.sum(jnp.where(lane < LANES // 2, lanes, 0.0), axis=1, keepdims=True)
    overlap = jnp.sum(jnp.where(lane < LANES // 2, 0.0, lanes), axis=1, keepdims=True)
    return squares, overlap


def scale_of(plan, squares):
    return jnp.sqrt(squares / plan.entries + epsilon)


def depart_kernel(plan, state_ref, out_ref, held_ref, semaphores):
    half = plan.rows // 2
    fetches = [
        pltpu.make_async_copy(
            state_ref.at[pl.ds(index * half, half), :], held_ref.at[pl.ds(index * half, half), :], semaphores.at[index]
        )
        for index in range(2)
    ]
    for fetch in fetches:
        fetch.start()
    sums = jnp.zeros((1, LANES), jnp.float32)
    for block in range(plan.lane_blocks):
        if block * LANES % half == 0:
            fetches[block * LANES // half].wait()
        tile = held_ref[pl.ds(block * LANES, LANES), :]
        sums = sums + lane_sums(tile * tile)
        turned = tile.T
        for piece in range(plan.pieces):
            out_ref[pl.ds(piece * plan.lane_blocks + block, plan.groups, stride=plan.message), :] = turned[
                piece * plan.groups : (piece + 1) * plan.groups
            ]
    put_sums(out_ref, sums, jnp.zeros_like(sums), plan.body, plan.message, plan.groups)


def mask_operator(plan, chosen, mask_ref, held_ref, out_ref):
    for across in range(plan.blocks):
        rows = pl.ds(across * plan.edge, plan.edge)
        for along in range(plan.blocks):
            columns = pl.ds(along * plan.edge, plan.edge)
            keep = (mask_ref[chosen, across, along] > 0).astype(jnp.float32).astype(jnp.bfloat16)
            part, start = divmod(across * plan.edge, plan.width)
            out_ref[part, columns, pl.ds(start, plan.edge)] = (held_ref[rows, columns] * keep).T


def store_kernel(plan, kept, bits_ref, mask_ref, operators_ref, *refs):
    count = plan.bits - kept
    stored_refs, (held_ref, masked_ref, in_semaphores, out_semaphores) = refs[:count], refs[count:]
    fetches = [
        pltpu.make_async_copy(operators_ref.at[bits_ref[kept + index]], held_ref.at[index], in_semaphores.at[index])
        for index in range(count)
    ]
    for fetch in fetches:
        fetch.start()
    stores = []
    for index in range(count):
        fetches[index].wait()
        mask_operator(plan, bits_ref[kept + index], mask_ref, held_ref.at[index], masked_ref.at[index])
        store = pltpu.make_async_copy(masked_ref.at[index], stored_refs[index], out_semaphores.at[index])
        store.start()
        stores.append(store)
    for store in stores:
        store.wait()


def prepare_kernel(
    plan,
    kept,
    bits_ref,
    mask_ref,
    field_ref,
    coupling_ref,
    mode_ref,
    operators_ref,
    place_ref,
    inside_ref,
    *refs,
):
    masked_refs, (held_ref, semaphores) = refs[:kept], refs[kept:]
    fetches = [
        pltpu.make_async_copy(operators_ref.at[bits_ref[index]], held_ref.at[index], semaphores.at[index])
        for index in range(kept)
    ]
    for fetch in fetches:
        fetch.start()
    me = lax.axis_index("site") * plan.phonons + lax.axis_index("phonon")
    place = lax.broadcasted_iota(jnp.int32, (plan.places, LANES), 0)
    phonon = place % plan.phonons
    site = place // plan.phonons % plan.sites
    mode = place // plan.groups % plan.share
    level = phonon * plan.levels_here + place // (plan.groups * plan.share)
    occupied = jnp.zeros((plan.places, LANES), jnp.float32)
    for position in range(plan.bits):
        held = (site >> position & 1).astype(jnp.float32)
        occupied = occupied + coupling_ref[bits_ref[position]] * held
    strength = jnp.zeros((plan.places, LANES), jnp.float32)
    for index in range(plan.share):
        strength = jnp.where(mode == index, mode_ref[index * plan.groups + me], strength)
    strength = strength / jnp.sqrt(jnp.full((1, LANES), plan.level_count, jnp.float32))
    height = level.astype(jnp.float32)
    place_ref[0] = occupied
    place_ref[1] = strength * jnp.sqrt(height)
    place_ref[2] = jnp.where(level == plan.level_count - 1, 0.0, strength * jnp.sqrt(height + 1.0))
    for position in range(plan.bits):
        place_ref[3 + position] = jnp.full((plan.places, LANES), field_ref[bits_ref[position]])
    inside = lax.broadcasted_iota(jnp.int32, (SUBLANES, plan.rows), 1)
    weight = jnp.zeros((SUBLANES, plan.rows), jnp.float32)
    for local_bit in range(LBITS):
        weight = weight + coupling_ref[plan.bits + local_bit] * (inside >> local_bit & 1).astype(jnp.float32)
    inside_ref[...] = weight
    for index in range(kept):
        fetches[index].wait()
        mask_operator(plan, bits_ref[index], mask_ref, held_ref.at[index], masked_refs[index])


def flipped(values, stride):
    places, width = values.shape
    if stride % SUBLANES == 0:
        shaped = values.reshape(places // (2 * stride), 2, stride, width)
        return jnp.concatenate([shaped[:, 1:], shaped[:, :1]], axis=1).reshape(places, width)
    tiles = values.reshape(places // SUBLANES, SUBLANES, width)
    if 2 * stride == SUBLANES:
        return pltpu.roll(tiles, stride, 1).reshape(places, width)
    spot = lax.broadcasted_iota(jnp.int32, tiles.shape, 1)
    down = pltpu.roll(tiles, stride, 1)
    up = pltpu.roll(tiles, SUBLANES - stride, 1)
    return jnp.where(spot & stride > 0, down, up).reshape(places, width)


def shifted(values, by):
    places, width = values.shape
    tiles = values.reshape(places // SUBLANES, SUBLANES, width)
    return pltpu.roll(tiles, by % SUBLANES, 1).reshape(places, width)


def step(plan, vector_ref, masked_refs, place_ref, inside_ref, rounded_ref, finish, kept, ready=None, begun_ref=None):
    span = plan.places // plan.levels_here
    for block in range(plan.lane_blocks):
        vector = vector_ref[:, pl.ds(block * LANES, LANES)]
        for position in range(plan.bits):
            rounded_ref[:, pl.ds(position * plan.rows + block * LANES, LANES)] = flipped(
                vector, plan.phonons << position
            ).astype(jnp.bfloat16)

    def local(start):
        lanes = pl.ds(start, LANES)
        vector = vector_ref[:, lanes]
        levels = [vector[index * span : (index + 1) * span] for index in range(plan.levels_here)]
        lower = jnp.concatenate([shifted(levels[-1], 1)] + levels[:-1], axis=0)
        upper = jnp.concatenate(levels[1:] + [shifted(levels[0], -1)], axis=0)
        weight = place_ref[0] + inside_ref[:1, lanes]
        total = weight * (place_ref[1] * lower + place_ref[2] * upper)
        for position in range(plan.bits):
            total = total + place_ref[3 + position, :1] * flipped(vector, plan.phonons << position)
        return total

    def product(part, position):
        return jnp.dot(
            rounded_ref[:, pl.ds(position * plan.rows, plan.rows)],
            masked_refs[position][part],
            preferred_element_type=jnp.float32,
        )

    def begun(lanes, part):
        total = jnp.concatenate([local(start) for start in range(lanes.start, lanes.start + plan.width, LANES)], axis=1)
        for position in range(kept):
            total = total + product(part, position)
        return total

    parts = [pl.ds(part * plan.width, plan.width) for part in range(plan.parts)]
    if ready is None:
        for part, lanes in enumerate(parts):
            finish(lanes, begun(lanes, part))
        return
    for part, lanes in enumerate(parts):
        begun_ref[:, lanes] = begun(lanes, part)
    for part, lanes in enumerate(parts):
        total = begun_ref[:, lanes]
        for position in range(kept, plan.bits):
            ready(part, position)
            total = total + product(part, position)
        finish(lanes, total)


def first_kernel(plan, kept, arrived_ref, place_ref, inside_ref, *refs):
    masked_refs = refs[:kept]
    stored_refs = refs[kept : plan.bits]
    initial_ref, new_ref, sums_ref = refs[plan.bits : plan.bits + 3]
    fetched_refs = refs[plan.bits + 3 : -2]
    rounded_ref, semaphores = refs[-2:]
    fetches = {}
    for part in range(plan.parts):
        for index, (stored_ref, fetched_ref) in enumerate(zip(stored_refs, fetched_refs)):
            fetch = pltpu.make_async_copy(stored_ref.at[part], fetched_ref.at[part], semaphores.at[index, part])
            fetch.start()
            fetches[part, kept + index] = fetch

    def ready(part, position):
        fetches[part, position].wait()

    squares, _ = totals_of(arrived_ref, plan.body, plan.message, plan.groups)
    inverse = 1.0 / scale_of(plan, squares)
    for piece in range(plan.pieces):
        for block in range(plan.lane_blocks):
            part = arrived_ref[pl.ds(piece * plan.lane_blocks + block, plan.groups, stride=plan.message), :]
            initial_ref[pl.ds(piece * plan.groups, plan.groups), pl.ds(block * LANES, LANES)] = part * inverse
    squares = []
    overlap = []

    def finish(lanes, new):
        new_ref[:, lanes] = new
        squares.append(lane_sums(new * new))
        overlap.append(lane_sums(new * initial_ref[:, lanes]))

    tables = (place_ref, inside_ref)
    step(plan, initial_ref, (*masked_refs, *fetched_refs), *tables, rounded_ref, finish, kept, ready, new_ref)
    put_sums(sums_ref, one_row(squares), one_row(overlap), 0, 1, 1)


def one_row(rows):
    total = sum(rows[1:], rows[0])
    return sum(total[:, start : start + LANES] for start in range(0, total.shape[1], LANES))


def place(plan, arrived_ref, out_ref):
    squares, overlap = totals_of(arrived_ref, plan.body, plan.message, plan.groups)
    inverse = 1.0 / scale_of(plan, squares)
    for block in range(plan.lane_blocks):
        parts = [
            arrived_ref[pl.ds(piece * plan.lane_blocks + block, plan.groups, stride=plan.message), :]
            for piece in range(plan.pieces)
        ]
        out_ref[pl.ds(block * LANES, LANES), :] = (jnp.concatenate(parts, axis=0) * inverse).T
    return overlap * inverse / plan.entries


def later_kernel(plan, keep, arrived_ref, raw_ref, previous_ref, initial_ref, place_ref, inside_ref, *refs):
    masked_refs = refs[: plan.bits]
    if keep:
        current_ref, new_ref, out_ref, moment_ref, rounded_ref = refs[plan.bits :]
        squares, overlap = totals_of(arrived_ref, 0, 1, 1)
    else:
        out_ref, rounded_ref, current_ref = refs[plan.bits :]
        squares, overlap = totals_of(arrived_ref, plan.body, plan.message, plan.groups)
    inverse = 1.0 / scale_of(plan, squares)
    if keep:
        moment_ref[...] = jnp.broadcast_to(overlap * inverse / plan.entries, moment_ref.shape)
    for block in range(plan.lane_blocks):
        lanes = pl.ds(block * LANES, LANES)
        current_ref[:, lanes] = raw_ref[:, lanes] * inverse
    squares = []
    overlap = []

    def finish(lanes, total):
        new = 2.0 * total - previous_ref[:, lanes] * inverse
        if keep:
            new_ref[:, lanes] = new
        squares.append(lane_sums(new * new))
        overlap.append(lane_sums(new * initial_ref[:, lanes]))
        for start in range(0, lanes.size, LANES):
            block = (lanes.start + start) // LANES
            for piece in range(plan.pieces):
                out_ref[pl.ds(piece * plan.lane_blocks + block, plan.groups, stride=plan.message), :] = new[
                    piece * plan.groups : (piece + 1) * plan.groups, start : start + LANES
                ]

    step(plan, current_ref, masked_refs, place_ref, inside_ref, rounded_ref, finish, plan.bits)
    put_sums(out_ref, one_row(squares), one_row(overlap), plan.body, plan.message, plan.groups)


def arrive_kernel(plan, before_ref, last_ref, moment_ref, before_out_ref, last_out_ref, moments_ref):
    second = place(plan, before_ref, before_out_ref)
    third = place(plan, last_ref, last_out_ref)
    moments_ref[0] = moment_ref[0, 0]
    moments_ref[1] = second[0, 0]
    moments_ref[2] = third[0, 0]


def exchange(values, count):
    shaped = values.reshape(count, values.shape[0] // count, 1, LANES)
    return lax.all_to_all(shaped, AXES, 0, 0, tiled=True).reshape(values.shape)


def summed(plan, values):
    for axis, size in (("phonon", plan.phonons), ("site", plan.sites)):
        bits = [1 << bit for bit in range(size.bit_length() - 1)]
        while bits:
            near, bits = bits[-2:], bits[:-2]
            first = values + swapped(values, axis, size, near[0])
            if len(near) == 2:
                first = first + (
                    swapped(values, axis, size, near[1]) + swapped(values, axis, size, near[0] ^ near[1])
                )
            values = first
    return values


def swapped(values, axis, size, mask):
    return lax.ppermute(values, axis, [(source, source ^ mask) for source in range(size)])


def shards(plan, state, operators, op_mask, site_bits, field, site_coupling, mode_coupling):
    f32 = jnp.float32
    message = jax.ShapeDtypeStruct((plan.groups * plan.message, LANES), f32)
    vector = jax.ShapeDtypeStruct((plan.places, plan.rows), f32)
    moment = jax.ShapeDtypeStruct((SUBLANES, LANES), f32)
    held = jax.ShapeDtypeStruct((plan.rows, plan.columns), f32)
    rounded = pltpu.VMEM((plan.places, plan.bits * plan.rows), jnp.bfloat16)
    working = pltpu.VMEM((plan.places, plan.rows), f32)
    work = 2 * plan.bits * plan.places * plan.rows * plan.rows

    def cost(flops, moved):
        return pl.CostEstimate(flops=flops, bytes_accessed=moved, transcendentals=0)

    departing = pl.pallas_call(
        functools.partial(depart_kernel, plan),
        out_shape=message,
        in_specs=[HBM],
        out_specs=VMEM,
        scratch_shapes=[pltpu.VMEM((plan.rows, plan.columns), f32), pltpu.SemaphoreType.DMA((2,))],
        compiler_params=params(60),
        name="depart",
    )(state)
    arrived = exchange(departing, plan.groups)
    operator = jax.ShapeDtypeStruct((plan.parts, plan.rows, plan.width), jnp.bfloat16)
    kept = 1
    fetched = plan.bits - kept
    place, inside, *masked = pl.pallas_call(
        functools.partial(prepare_kernel, plan, kept),
        out_shape=[
            jax.ShapeDtypeStruct((3 + plan.bits, plan.places, LANES), f32),
            jax.ShapeDtypeStruct((SUBLANES, plan.rows), f32),
        ]
        + [operator] * kept,
        in_specs=[SMEM] * 5 + [HBM],
        out_specs=[VMEM] * (2 + kept),
        scratch_shapes=[
            pltpu.VMEM((kept, plan.rows, plan.rows), jnp.bfloat16),
            pltpu.SemaphoreType.DMA((kept,)),
        ],
        compiler_params=params(50),
        cost_estimate=cost(plan.rows * plan.rows, 4 * kept * plan.rows * plan.rows),
        name="prepare",
    )(site_bits, op_mask, field, site_coupling, mode_coupling, operators)
    stored = pl.pallas_call(
        functools.partial(store_kernel, plan, kept),
        out_shape=[operator] * fetched,
        in_specs=[SMEM] * 2 + [HBM],
        out_specs=[HBM] * fetched,
        scratch_shapes=[
            pltpu.VMEM((fetched, plan.rows, plan.rows), jnp.bfloat16),
            pltpu.VMEM((fetched, *operator.shape), jnp.bfloat16),
            pltpu.SemaphoreType.DMA((fetched,)),
            pltpu.SemaphoreType.DMA((fetched,)),
        ],
        compiler_params=params(60),
        cost_estimate=cost(plan.rows * plan.rows, 4 * fetched * plan.rows * plan.rows),
        name="store",
    )(site_bits, op_mask, operators)
    initial, raw, sums, *fetched_masked = pl.pallas_call(
        functools.partial(first_kernel, plan, kept),
        out_shape=[vector, vector, jax.ShapeDtypeStruct((1, LANES), f32)] + [operator] * fetched,
        in_specs=[VMEM] * 4 + [HBM] * fetched,
        out_specs=[VMEM] * (3 + fetched),
        scratch_shapes=[rounded, pltpu.SemaphoreType.DMA((fetched, plan.parts))],
        compiler_params=params(46),
        cost_estimate=cost(work, 4 * plan.places * plan.rows),
        name="first",
    )(arrived, place, inside, *masked, *stored)
    tables = (place, inside, *masked, *fetched_masked)
    sums = summed(plan, sums)
    current, raw, departing, moment_one = pl.pallas_call(
        functools.partial(later_kernel, plan, True),
        out_shape=[vector, vector, message, moment],
        in_specs=[VMEM] * (6 + plan.bits),
        out_specs=[VMEM] * 4,
        scratch_shapes=[rounded],
        compiler_params=params(32),
        cost_estimate=cost(work, 4 * plan.places * plan.rows),
        name="second",
    )(sums, raw, initial, initial, *tables)
    before = exchange(departing, plan.groups)
    departing = pl.pallas_call(
        functools.partial(later_kernel, plan, False),
        out_shape=message,
        in_specs=[VMEM] * (6 + plan.bits),
        out_specs=VMEM,
        scratch_shapes=[rounded, working],
        compiler_params=params(32),
        cost_estimate=cost(work, 4 * plan.places * plan.rows),
        name="third",
    )(before, raw, current, initial, *tables)
    last = exchange(departing, plan.groups)
    before, last, moments = pl.pallas_call(
        functools.partial(arrive_kernel, plan),
        out_shape=[held, held, jax.ShapeDtypeStruct((STEPS,), f32)],
        in_specs=[VMEM] * 3,
        out_specs=[VMEM, VMEM, SMEM],
        compiler_params=params(16),
        name="arrive",
    )(before, last, moment_one)
    return last, before, moments


def extended_2(block, sides, width):
    for axis, dim in sides:
        count = lax.axis_size(axis)
        forward = [(i, i + 1) for i in range(count - 1)]
        backward = [(target, source) for source, target in forward]
        low = lax.ppermute(
            lax.slice_in_dim(block, block.shape[dim] - width, None, axis=dim), axis, forward
        )
        high = lax.ppermute(lax.slice_in_dim(block, 0, width, axis=dim), axis, backward)
        block = jnp.concatenate([low, block, high], axis=dim)
    return block


def partner(value, axis, bit):
    mask = 2**bit
    pairs = [(source, source ^ mask) for source in range(lax.axis_size(axis))]
    return lax.ppermute(value, axis, pairs)


def halo_shards(state, operators, op_mask, site_bits, field, site_coupling, mode_coupling):
    site_count = lax.axis_size("site")
    phonon_count = lax.axis_size("phonon")
    bit_count = site_count.bit_length() - 1
    rows_here = state.shape[0]
    columns_here = state.shape[1]
    levels_here = columns_here // MODES
    block_edge = rows_here // op_mask.shape[1]
    expanded = jnp.repeat(jnp.repeat(op_mask, block_edge, axis=1), block_edge, axis=2)
    masked = jnp.where(expanded > 0, operators, jnp.zeros((), jnp.bfloat16))
    entries = jnp.float32(rows_here * columns_here * site_count * phonon_count)
    level_total = jnp.sqrt(jnp.float32(levels_here * phonon_count))
    device = lax.axis_index("site")
    inside = lax.iota(jnp.int32, rows_here)
    weight_rows = jnp.zeros((rows_here,), jnp.float32)
    for position in range(bit_count):
        weight_rows = weight_rows + site_coupling[site_bits[position]] * (
            device >> position & 1
        ).astype(jnp.float32)
    for local_bit in range(LBITS):
        weight_rows = weight_rows + site_coupling[bit_count + local_bit] * (
            inside >> local_bit & 1
        ).astype(jnp.float32)
    levels = (
        lax.axis_index("phonon") * levels_here + lax.iota(jnp.int32, columns_here) // MODES
    ).astype(jnp.float32)
    lower_weight = jnp.sqrt(levels)
    upper_weight = jnp.sqrt(levels + 1.0)
    mode_weight = jnp.tile(mode_coupling, columns_here // MODES) / level_total
    start_squares = lax.psum(jnp.sum(state * state), ("site", "phonon"))
    initial = state / jnp.sqrt(start_squares / entries + epsilon)
    previous = initial
    current = initial
    scale_prev = jnp.float32(1.0)
    moments = []
    for iteration in range(STEPS):
        extended = extended_2(current, (("phonon", 1),), MODES)
        lower_part = extended[:, :columns_here]
        upper_part = extended[:, 2 * MODES :]
        summed = weight_rows[:, None] * (
            mode_weight * (lower_weight * lower_part + upper_weight * upper_part)
        )
        for operate_position in range(bit_count):
            chosen = site_bits[operate_position]
            flipped = partner(current, "site", operate_position)
            product = jnp.dot(
                masked[chosen], flipped.astype(jnp.bfloat16), preferred_element_type=jnp.float32
            )
            summed = summed + (field[chosen] * flipped + product)
        if iteration == 0:
            vector_new = summed
        else:
            vector_new = 2.0 * summed - previous / scale_prev
        squares, intersection = lax.psum(
            (jnp.sum(vector_new * vector_new), jnp.sum(initial * vector_new)), ("site", "phonon")
        )
        scale_now = jnp.sqrt(squares / entries + epsilon)
        updated = vector_new / scale_now
        moment = intersection / (entries * scale_now)
        moments.append(moment)
        previous = current
        current = updated
        scale_prev = scale_now
    return (current, previous, jnp.stack(moments))


def solution(mesh):
    in_specs = (P("site", "phonon"), P(), P(), P(), P(), P(), P())
    out_specs = (P("site", "phonon"), P("site", "phonon"), P())

    def whole(state, operators, op_mask, *rest):
        rows = state.shape[0] // mesh.shape["site"]
        columns = state.shape[1] // mesh.shape["phonon"]
        plan = Plan(mesh, rows, columns, op_mask.shape[1])
        body = functools.partial(shards, plan) if plan.fits() else halo_shards
        run = jax.shard_map(body, mesh=mesh, in_specs=in_specs, out_specs=out_specs, check_vma=False)
        return run(state, operators, op_mask, *rest)

    return whole
```

```python
import functools

import jax
import jax.numpy as jnp
from jax import lax
from jax.experimental import pallas as pl
from jax.experimental.pallas import tpu as pltpu
from jax.sharding import PartitionSpec as P

LBITS = 10
MODES = 64
STEPS = 3
LANES = 128
SUBLANES = 8
SLOTS = 4
AXES = ("site", "phonon")

epsilon = 1e-06


VMEM = pl.BlockSpec(memory_space=pltpu.VMEM)
SMEM = pl.BlockSpec(memory_space=pltpu.SMEM)
HBM = pl.BlockSpec(memory_space=pltpu.HBM)


class Plan:
    def __init__(self, mesh, rows, columns, blocks):
        self.sites = mesh.shape["site"]
        self.phonons = mesh.shape["phonon"]
        self.groups = self.sites * self.phonons
        self.bits = self.sites.bit_length() - 1
        self.rows = rows
        self.columns = columns
        self.blocks = blocks
        self.edge = rows // blocks
        self.levels_here = columns // MODES
        self.level_count = self.levels_here * self.phonons
        self.share = MODES // self.groups
        self.pieces = self.levels_here * self.share
        self.lane_blocks = rows // LANES
        self.body = self.pieces * self.lane_blocks
        self.inward = self.body + 1
        self.outward = 2 * self.body + 1
        self.places = self.pieces * self.groups
        self.width = 2 * LANES
        self.parts = rows // self.width
        self.entries = float(rows * columns * self.groups)

    def fits(self):
        return (
            MODES % self.groups == 0
            and self.columns == LANES
            and self.rows % self.width == 0
            and self.edge % LANES == 0
            and self.width % self.edge == 0
            and self.groups % SUBLANES == 0
        )


def params(mib):
    return pltpu.CompilerParams(vmem_limit_bytes=mib * 2**20)


def lane_sums(values):
    return jnp.sum(values, axis=0, keepdims=True)


def put_sums(out_ref, sums, start, stride, count):
    lane = lax.broadcasted_iota(jnp.int32, (1, LANES), 1)
    row = jnp.zeros((1, LANES), jnp.float32)
    for slot, value in enumerate(sums):
        width = LANES
        while width > LANES // SLOTS:
            width //= 2
            value = value + pltpu.roll(value, width, 1)
        row = jnp.where(lane // (LANES // SLOTS) == slot, value, row)
    out_ref[pl.ds(start, count, stride=stride), :] = jnp.broadcast_to(row, (count, LANES))


def totals_of(ref, start, stride, count):
    lanes = lane_sums(ref[pl.ds(start, count, stride=stride), :])
    lane = lax.broadcasted_iota(jnp.int32, (1, LANES), 1)
    return [
        jnp.sum(jnp.where(lane // (LANES // SLOTS) == slot, lanes, 0.0), axis=1, keepdims=True)
        for slot in range(SLOTS)
    ]


def scale_of(plan, squares):
    return jnp.sqrt(squares / plan.entries + epsilon)


def depart_kernel(plan, state_ref, out_ref, held_ref, semaphores):
    half = plan.rows // 2
    fetches = [
        pltpu.make_async_copy(
            state_ref.at[pl.ds(index * half, half), :], held_ref.at[pl.ds(index * half, half), :], semaphores.at[index]
        )
        for index in range(2)
    ]
    for fetch in fetches:
        fetch.start()
    sums = jnp.zeros((1, LANES), jnp.float32)
    for block in range(plan.lane_blocks):
        if block * LANES % half == 0:
            fetches[block * LANES // half].wait()
        tile = held_ref[pl.ds(block * LANES, LANES), :]
        sums = sums + lane_sums(tile * tile)
        turned = tile.T
        for piece in range(plan.pieces):
            out_ref[pl.ds(piece * plan.lane_blocks + block, plan.groups, stride=plan.inward), :] = turned[
                piece * plan.groups : (piece + 1) * plan.groups
            ]
    put_sums(out_ref, [sums], plan.body, plan.inward, plan.groups)


def mask_operator(plan, chosen, mask_ref, held_ref, out_ref):
    for across in range(plan.blocks):
        rows = pl.ds(across * plan.edge, plan.edge)
        for along in range(plan.blocks):
            columns = pl.ds(along * plan.edge, plan.edge)
            keep = (mask_ref[chosen, across, along] > 0).astype(jnp.float32).astype(jnp.bfloat16)
            part, start = divmod(across * plan.edge, plan.width)
            out_ref[part, columns, pl.ds(start, plan.edge)] = (held_ref[rows, columns] * keep).T


def store_kernel(plan, kept, bits_ref, mask_ref, operators_ref, *refs):
    count = plan.bits - kept
    stored_refs, (held_ref, masked_ref, in_semaphores, out_semaphores) = refs[:count], refs[count:]
    fetches = [
        pltpu.make_async_copy(operators_ref.at[bits_ref[kept + index]], held_ref.at[index], in_semaphores.at[index])
        for index in range(count)
    ]
    for fetch in fetches:
        fetch.start()
    stores = []
    for index in range(count):
        fetches[index].wait()
        mask_operator(plan, bits_ref[kept + index], mask_ref, held_ref.at[index], masked_ref.at[index])
        store = pltpu.make_async_copy(masked_ref.at[index], stored_refs[index], out_semaphores.at[index])
        store.start()
        stores.append(store)
    for store in stores:
        store.wait()


def prepare_kernel(
    plan,
    kept,
    bits_ref,
    mask_ref,
    field_ref,
    coupling_ref,
    mode_ref,
    operators_ref,
    place_ref,
    inside_ref,
    *refs,
):
    masked_refs, (held_ref, semaphores) = refs[:kept], refs[kept:]
    fetches = [
        pltpu.make_async_copy(operators_ref.at[bits_ref[index]], held_ref.at[index], semaphores.at[index])
        for index in range(kept)
    ]
    for fetch in fetches:
        fetch.start()
    me = lax.axis_index("site") * plan.phonons + lax.axis_index("phonon")
    place = lax.broadcasted_iota(jnp.int32, (plan.places, LANES), 0)
    phonon = place % plan.phonons
    site = place // plan.phonons % plan.sites
    mode = place // plan.groups % plan.share
    level = phonon * plan.levels_here + place // (plan.groups * plan.share)
    occupied = jnp.zeros((plan.places, LANES), jnp.float32)
    for position in range(plan.bits):
        held = (site >> position & 1).astype(jnp.float32)
        occupied = occupied + coupling_ref[bits_ref[position]] * held
    strength = jnp.zeros((plan.places, LANES), jnp.float32)
    for index in range(plan.share):
        strength = jnp.where(mode == index, mode_ref[index * plan.groups + me], strength)
    strength = strength / jnp.sqrt(jnp.full((1, LANES), plan.level_count, jnp.float32))
    height = level.astype(jnp.float32)
    place_ref[0] = occupied
    place_ref[1] = strength * jnp.sqrt(height)
    place_ref[2] = jnp.where(level == plan.level_count - 1, 0.0, strength * jnp.sqrt(height + 1.0))
    for position in range(plan.bits):
        place_ref[3 + position] = jnp.full((plan.places, LANES), field_ref[bits_ref[position]])
    inside = lax.broadcasted_iota(jnp.int32, (SUBLANES, plan.rows), 1)
    weight = jnp.zeros((SUBLANES, plan.rows), jnp.float32)
    for local_bit in range(LBITS):
        weight = weight + coupling_ref[plan.bits + local_bit] * (inside >> local_bit & 1).astype(jnp.float32)
    inside_ref[...] = weight
    for index in range(kept):
        fetches[index].wait()
        mask_operator(plan, bits_ref[index], mask_ref, held_ref.at[index], masked_refs[index])


def flipped(values, stride):
    places, width = values.shape
    if stride % SUBLANES == 0:
        shaped = values.reshape(places // (2 * stride), 2, stride, width)
        return jnp.concatenate([shaped[:, 1:], shaped[:, :1]], axis=1).reshape(places, width)
    tiles = values.reshape(places // SUBLANES, SUBLANES, width)
    if 2 * stride == SUBLANES:
        return pltpu.roll(tiles, stride, 1).reshape(places, width)
    spot = lax.broadcasted_iota(jnp.int32, tiles.shape, 1)
    down = pltpu.roll(tiles, stride, 1)
    up = pltpu.roll(tiles, SUBLANES - stride, 1)
    return jnp.where(spot & stride > 0, down, up).reshape(places, width)


def shifted(values, by):
    places, width = values.shape
    tiles = values.reshape(places // SUBLANES, SUBLANES, width)
    return pltpu.roll(tiles, by % SUBLANES, 1).reshape(places, width)


def step(plan, vector_ref, masked_refs, place_ref, inside_ref, rounded_ref, finish, kept, ready=None, begun_ref=None):
    span = plan.places // plan.levels_here
    for block in range(plan.lane_blocks):
        vector = vector_ref[:, pl.ds(block * LANES, LANES)]
        for position in range(plan.bits):
            rounded_ref[:, pl.ds(position * plan.rows + block * LANES, LANES)] = flipped(
                vector, plan.phonons << position
            ).astype(jnp.bfloat16)

    def local(start):
        lanes = pl.ds(start, LANES)
        vector = vector_ref[:, lanes]
        levels = [vector[index * span : (index + 1) * span] for index in range(plan.levels_here)]
        lower = jnp.concatenate([shifted(levels[-1], 1)] + levels[:-1], axis=0)
        upper = jnp.concatenate(levels[1:] + [shifted(levels[0], -1)], axis=0)
        weight = place_ref[0] + inside_ref[:1, lanes]
        total = weight * (place_ref[1] * lower + place_ref[2] * upper)
        for position in range(plan.bits):
            total = total + place_ref[3 + position, :1] * flipped(vector, plan.phonons << position)
        return total

    def product(part, position):
        return jnp.dot(
            rounded_ref[:, pl.ds(position * plan.rows, plan.rows)],
            masked_refs[position][part],
            preferred_element_type=jnp.float32,
        )

    def begun(lanes, part):
        total = jnp.concatenate([local(start) for start in range(lanes.start, lanes.start + plan.width, LANES)], axis=1)
        for position in range(kept):
            total = total + product(part, position)
        return total

    parts = [pl.ds(part * plan.width, plan.width) for part in range(plan.parts)]
    if ready is None:
        for part, lanes in enumerate(parts):
            finish(lanes, begun(lanes, part))
        return
    for part, lanes in enumerate(parts):
        begun_ref[:, lanes] = begun(lanes, part)
    for part, lanes in enumerate(parts):
        total = begun_ref[:, lanes]
        for position in range(kept, plan.bits):
            ready(part, position)
            total = total + product(part, position)
        finish(lanes, total)


def first_kernel(plan, kept, arrived_ref, place_ref, inside_ref, *refs):
    masked_refs = refs[:kept]
    stored_refs = refs[kept : plan.bits]
    initial_ref, new_ref, sums_ref = refs[plan.bits : plan.bits + 3]
    fetched_refs = refs[plan.bits + 3 : -2]
    rounded_ref, semaphores = refs[-2:]
    fetches = {}
    for part in range(plan.parts):
        for index, (stored_ref, fetched_ref) in enumerate(zip(stored_refs, fetched_refs)):
            fetch = pltpu.make_async_copy(stored_ref.at[part], fetched_ref.at[part], semaphores.at[index, part])
            fetch.start()
            fetches[part, kept + index] = fetch

    def ready(part, position):
        fetches[part, position].wait()

    squares = totals_of(arrived_ref, plan.body, plan.inward, plan.groups)[0]
    inverse = 1.0 / scale_of(plan, squares)
    for piece in range(plan.pieces):
        for block in range(plan.lane_blocks):
            part = arrived_ref[pl.ds(piece * plan.lane_blocks + block, plan.groups, stride=plan.inward), :]
            initial_ref[pl.ds(piece * plan.groups, plan.groups), pl.ds(block * LANES, LANES)] = part * inverse
    tables = ((*masked_refs, *fetched_refs), place_ref, inside_ref, rounded_ref)
    squares = []
    overlap = []
    ahead = []

    def finish(lanes, new):
        new_ref[:, lanes] = new
        squares.append(lane_sums(new * new))
        overlap.append(lane_sums(new * initial_ref[:, lanes]))

    def look_ahead(lanes, total):
        new = 2.0 * total - initial_ref[:, lanes]
        ahead.append(lane_sums(new * new))

    step(plan, initial_ref, *tables, finish, kept, ready, new_ref)
    step(plan, new_ref, *tables, look_ahead, plan.bits)
    put_sums(sums_ref, [one_row(squares), one_row(overlap), one_row(ahead)], 0, 1, plan.groups)


def one_row(rows):
    total = sum(rows[1:], rows[0])
    return sum(total[:, start : start + LANES] for start in range(0, total.shape[1], LANES))


def onward_kernel(plan, arrived_ref, raw_ref, initial_ref, place_ref, inside_ref, *refs):
    masked_refs = refs[: plan.bits]
    out_ref, known_ref, rounded_ref, second_ref, third_ref = refs[plan.bits :]
    squares, overlap, ahead, _ = totals_of(arrived_ref, 0, 1, plan.groups)
    first = 1.0 / scale_of(plan, squares)
    estimate = scale_of(plan, ahead * first * first)
    second = 1.0 / estimate
    known_ref[:1, :] = jnp.broadcast_to(overlap * first / plan.entries, (1, LANES))
    known_ref[1:, :] = jnp.broadcast_to(estimate, (SUBLANES - 1, LANES))
    for block in range(plan.lane_blocks):
        lanes = pl.ds(block * LANES, LANES)
        second_ref[:, lanes] = raw_ref[:, lanes] * first
    tables = (masked_refs, place_ref, inside_ref, rounded_ref)
    sums = [[] for _ in range(SLOTS)]

    def send(vector, lanes, new):
        sums[2 * vector].append(lane_sums(new * new))
        sums[2 * vector + 1].append(lane_sums(new * initial_ref[:, lanes]))
        for start in range(0, plan.width, LANES):
            block = (lanes.start + start) // LANES
            for piece in range(plan.pieces):
                row = vector * plan.body + piece * plan.lane_blocks + block
                out_ref[pl.ds(row, plan.groups, stride=plan.outward), :] = new[
                    piece * plan.groups : (piece + 1) * plan.groups, start : start + LANES
                ]

    def finish_second(lanes, total):
        new = 2.0 * total - initial_ref[:, lanes] * first
        third_ref[:, lanes] = new * second
        send(0, lanes, new)

    def finish_third(lanes, total):
        send(1, lanes, 2.0 * total - second_ref[:, lanes] * second)

    step(plan, second_ref, *tables, finish_second, plan.bits)
    step(plan, third_ref, *tables, finish_third, plan.bits)
    put_sums(out_ref, [one_row(rows) for rows in sums], 2 * plan.body, plan.outward, plan.groups)


def arrive_kernel(plan, arrived_ref, known_ref, before_ref, last_ref, moments_ref):
    before_squares, before_overlap, last_squares, last_overlap = totals_of(
        arrived_ref, 2 * plan.body, plan.outward, plan.groups
    )
    before = 1.0 / scale_of(plan, before_squares)
    back = known_ref[1:2, :1] * before
    last = back / scale_of(plan, last_squares * back * back)
    for vector, (out_ref, factor) in enumerate(((before_ref, before), (last_ref, last))):
        for block in range(plan.lane_blocks):
            first = vector * plan.body + block
            parts = [
                arrived_ref[pl.ds(first + piece * plan.lane_blocks, plan.groups, stride=plan.outward), :]
                for piece in range(plan.pieces)
            ]
            out_ref[pl.ds(block * LANES, LANES), :] = (jnp.concatenate(parts, axis=0) * factor).T
    moments_ref[0] = known_ref[0, 0]
    moments_ref[1] = (before_overlap * before / plan.entries)[0, 0]
    moments_ref[2] = (last_overlap * last / plan.entries)[0, 0]


def exchange(values, count):
    shaped = values.reshape(count, values.shape[0] // count, 1, LANES)
    return lax.all_to_all(shaped, AXES, 0, 0, tiled=True).reshape(values.shape)


def shards(plan, state, operators, op_mask, site_bits, field, site_coupling, mode_coupling):
    f32 = jnp.float32
    inward = jax.ShapeDtypeStruct((plan.groups * plan.inward, LANES), f32)
    outward = jax.ShapeDtypeStruct((plan.groups * plan.outward, LANES), f32)
    vector = jax.ShapeDtypeStruct((plan.places, plan.rows), f32)
    known = jax.ShapeDtypeStruct((SUBLANES, LANES), f32)
    held = jax.ShapeDtypeStruct((plan.rows, plan.columns), f32)
    rounded = pltpu.VMEM((plan.places, plan.bits * plan.rows), jnp.bfloat16)
    working = pltpu.VMEM((plan.places, plan.rows), f32)
    work = 2 * plan.bits * plan.places * plan.rows * plan.rows

    def cost(flops, moved):
        return pl.CostEstimate(flops=flops, bytes_accessed=moved, transcendentals=0)

    departing = pl.pallas_call(
        functools.partial(depart_kernel, plan),
        out_shape=inward,
        in_specs=[HBM],
        out_specs=VMEM,
        scratch_shapes=[pltpu.VMEM((plan.rows, plan.columns), f32), pltpu.SemaphoreType.DMA((2,))],
        compiler_params=params(60),
        name="depart",
    )(state)
    arrived = exchange(departing, plan.groups)
    operator = jax.ShapeDtypeStruct((plan.parts, plan.rows, plan.width), jnp.bfloat16)
    kept = 1
    fetched = plan.bits - kept
    place, inside, *masked = pl.pallas_call(
        functools.partial(prepare_kernel, plan, kept),
        out_shape=[
            jax.ShapeDtypeStruct((3 + plan.bits, plan.places, LANES), f32),
            jax.ShapeDtypeStruct((SUBLANES, plan.rows), f32),
        ]
        + [operator] * kept,
        in_specs=[SMEM] * 5 + [HBM],
        out_specs=[VMEM] * (2 + kept),
        scratch_shapes=[
            pltpu.VMEM((kept, plan.rows, plan.rows), jnp.bfloat16),
            pltpu.SemaphoreType.DMA((kept,)),
        ],
        compiler_params=params(50),
        cost_estimate=cost(plan.rows * plan.rows, 4 * kept * plan.rows * plan.rows),
        name="prepare",
    )(site_bits, op_mask, field, site_coupling, mode_coupling, operators)
    stored = pl.pallas_call(
        functools.partial(store_kernel, plan, kept),
        out_shape=[operator] * fetched,
        in_specs=[SMEM] * 2 + [HBM],
        out_specs=[HBM] * fetched,
        scratch_shapes=[
            pltpu.VMEM((fetched, plan.rows, plan.rows), jnp.bfloat16),
            pltpu.VMEM((fetched, *operator.shape), jnp.bfloat16),
            pltpu.SemaphoreType.DMA((fetched,)),
            pltpu.SemaphoreType.DMA((fetched,)),
        ],
        compiler_params=params(60),
        cost_estimate=cost(plan.rows * plan.rows, 4 * fetched * plan.rows * plan.rows),
        name="store",
    )(site_bits, op_mask, operators)
    initial, raw, sums, *fetched_masked = pl.pallas_call(
        functools.partial(first_kernel, plan, kept),
        out_shape=[vector, vector, jax.ShapeDtypeStruct((plan.groups, LANES), f32)] + [operator] * fetched,
        in_specs=[VMEM] * 4 + [HBM] * fetched,
        out_specs=[VMEM] * (3 + fetched),
        scratch_shapes=[rounded, pltpu.SemaphoreType.DMA((fetched, plan.parts))],
        compiler_params=params(46),
        cost_estimate=cost(work, 4 * plan.places * plan.rows),
        name="first",
    )(arrived, place, inside, *masked, *stored)
    tables = (place, inside, *masked, *fetched_masked)
    sums = exchange(sums, plan.groups)
    departing, told = pl.pallas_call(
        functools.partial(onward_kernel, plan),
        out_shape=[outward, known],
        in_specs=[VMEM] * (5 + plan.bits),
        out_specs=[VMEM] * 2,
        scratch_shapes=[rounded, working, working],
        compiler_params=params(32),
        cost_estimate=cost(2 * work, 8 * plan.places * plan.rows),
        name="onward",
    )(sums, raw, initial, *tables)
    arrived = exchange(departing, plan.groups)
    before, last, moments = pl.pallas_call(
        functools.partial(arrive_kernel, plan),
        out_shape=[held, held, jax.ShapeDtypeStruct((STEPS,), f32)],
        in_specs=[VMEM] * 2,
        out_specs=[VMEM, VMEM, SMEM],
        compiler_params=params(16),
        name="arrive",
    )(arrived, told)
    return last, before, moments


def extended_2(block, sides, width):
    for axis, dim in sides:
        count = lax.axis_size(axis)
        forward = [(i, i + 1) for i in range(count - 1)]
        backward = [(target, source) for source, target in forward]
        low = lax.ppermute(
            lax.slice_in_dim(block, block.shape[dim] - width, None, axis=dim), axis, forward
        )
        high = lax.ppermute(lax.slice_in_dim(block, 0, width, axis=dim), axis, backward)
        block = jnp.concatenate([low, block, high], axis=dim)
    return block


def partner(value, axis, bit):
    mask = 2**bit
    pairs = [(source, source ^ mask) for source in range(lax.axis_size(axis))]
    return lax.ppermute(value, axis, pairs)


def halo_shards(state, operators, op_mask, site_bits, field, site_coupling, mode_coupling):
    site_count = lax.axis_size("site")
    phonon_count = lax.axis_size("phonon")
    bit_count = site_count.bit_length() - 1
    rows_here = state.shape[0]
    columns_here = state.shape[1]
    levels_here = columns_here // MODES
    block_edge = rows_here // op_mask.shape[1]
    expanded = jnp.repeat(jnp.repeat(op_mask, block_edge, axis=1), block_edge, axis=2)
    masked = jnp.where(expanded > 0, operators, jnp.zeros((), jnp.bfloat16))
    entries = jnp.float32(rows_here * columns_here * site_count * phonon_count)
    level_total = jnp.sqrt(jnp.float32(levels_here * phonon_count))
    device = lax.axis_index("site")
    inside = lax.iota(jnp.int32, rows_here)
    weight_rows = jnp.zeros((rows_here,), jnp.float32)
    for position in range(bit_count):
        weight_rows = weight_rows + site_coupling[site_bits[position]] * (
            device >> position & 1
        ).astype(jnp.float32)
    for local_bit in range(LBITS):
        weight_rows = weight_rows + site_coupling[bit_count + local_bit] * (
            inside >> local_bit & 1
        ).astype(jnp.float32)
    levels = (
        lax.axis_index("phonon") * levels_here + lax.iota(jnp.int32, columns_here) // MODES
    ).astype(jnp.float32)
    lower_weight = jnp.sqrt(levels)
    upper_weight = jnp.sqrt(levels + 1.0)
    mode_weight = jnp.tile(mode_coupling, columns_here // MODES) / level_total
    start_squares = lax.psum(jnp.sum(state * state), ("site", "phonon"))
    initial = state / jnp.sqrt(start_squares / entries + epsilon)
    previous = initial
    current = initial
    scale_prev = jnp.float32(1.0)
    moments = []
    for iteration in range(STEPS):
        extended = extended_2(current, (("phonon", 1),), MODES)
        lower_part = extended[:, :columns_here]
        upper_part = extended[:, 2 * MODES :]
        summed = weight_rows[:, None] * (
            mode_weight * (lower_weight * lower_part + upper_weight * upper_part)
        )
        for operate_position in range(bit_count):
            chosen = site_bits[operate_position]
            flipped = partner(current, "site", operate_position)
            product = jnp.dot(
                masked[chosen], flipped.astype(jnp.bfloat16), preferred_element_type=jnp.float32
            )
            summed = summed + (field[chosen] * flipped + product)
        if iteration == 0:
            vector_new = summed
        else:
            vector_new = 2.0 * summed - previous / scale_prev
        squares, intersection = lax.psum(
            (jnp.sum(vector_new * vector_new), jnp.sum(initial * vector_new)), ("site", "phonon")
        )
        scale_now = jnp.sqrt(squares / entries + epsilon)
        updated = vector_new / scale_now
        moment = intersection / (entries * scale_now)
        moments.append(moment)
        previous = current
        current = updated
        scale_prev = scale_now
    return (current, previous, jnp.stack(moments))


def solution(mesh):
    in_specs = (P("site", "phonon"), P(), P(), P(), P(), P(), P())
    out_specs = (P("site", "phonon"), P("site", "phonon"), P())

    def whole(state, operators, op_mask, *rest):
        rows = state.shape[0] // mesh.shape["site"]
        columns = state.shape[1] // mesh.shape["phonon"]
        plan = Plan(mesh, rows, columns, op_mask.shape[1])
        body = functools.partial(shards, plan) if plan.fits() else halo_shards
        run = jax.shard_map(body, mesh=mesh, in_specs=in_specs, out_specs=out_specs, check_vma=False)
        return run(state, operators, op_mask, *rest)

    return whole
```

```python
import functools

import jax
import jax.numpy as jnp
from jax import lax
from jax.experimental import pallas as pl
from jax.experimental.pallas import tpu as pltpu
from jax.sharding import PartitionSpec as P

LBITS = 10
MODES = 64
STEPS = 3
LANES = 128
SUBLANES = 8
SLOTS = 4
AXES = ("site", "phonon")

epsilon = 1e-06


VMEM = pl.BlockSpec(memory_space=pltpu.VMEM)
SMEM = pl.BlockSpec(memory_space=pltpu.SMEM)
HBM = pl.BlockSpec(memory_space=pltpu.HBM)


class Plan:
    def __init__(self, mesh, rows, columns, blocks):
        self.sites = mesh.shape["site"]
        self.phonons = mesh.shape["phonon"]
        self.groups = self.sites * self.phonons
        self.bits = self.sites.bit_length() - 1
        self.rows = rows
        self.columns = columns
        self.blocks = blocks
        self.edge = rows // blocks
        self.levels_here = columns // MODES
        self.level_count = self.levels_here * self.phonons
        self.share = MODES // self.groups
        self.pieces = self.levels_here * self.share
        self.lane_blocks = rows // LANES
        self.body = self.pieces * self.lane_blocks
        self.inward = self.body + 1
        self.outward = 2 * self.body + 1
        self.places = self.pieces * self.groups
        self.width = 2 * LANES
        self.parts = rows // self.width
        self.slabs = self.bits * self.parts
        self.kept = min(self.parts + 1, self.slabs - 1)
        self.entries = float(rows * columns * self.groups)

    def fits(self):
        return (
            MODES % self.groups == 0
            and self.columns == LANES
            and self.rows % self.width == 0
            and self.edge % LANES == 0
            and self.width % self.edge == 0
            and self.bits < SUBLANES
            and self.groups % SUBLANES == 0
        )


def params(mib):
    return pltpu.CompilerParams(vmem_limit_bytes=mib * 2**20)


def lane_sums(values):
    return jnp.sum(values, axis=0, keepdims=True)


def put_sums(out_ref, sums, start, stride, count):
    lane = lax.broadcasted_iota(jnp.int32, (1, LANES), 1)
    row = jnp.zeros((1, LANES), jnp.float32)
    for slot, value in enumerate(sums):
        width = LANES
        while width > LANES // SLOTS:
            width //= 2
            value = value + pltpu.roll(value, width, 1)
        row = jnp.where(lane // (LANES // SLOTS) == slot, value, row)
    out_ref[pl.ds(start, count, stride=stride), :] = jnp.broadcast_to(row, (count, LANES))


def totals_of(ref, start, stride, count):
    lanes = lane_sums(ref[pl.ds(start, count, stride=stride), :])
    lane = lax.broadcasted_iota(jnp.int32, (1, LANES), 1)
    return [
        jnp.sum(jnp.where(lane // (LANES // SLOTS) == slot, lanes, 0.0), axis=1, keepdims=True)
        for slot in range(SLOTS)
    ]


def scale_of(plan, squares):
    return jnp.sqrt(squares / plan.entries + epsilon)


def depart_kernel(plan, state_ref, out_ref, held_ref, semaphores):
    half = plan.rows // 2
    fetches = [
        pltpu.make_async_copy(
            state_ref.at[pl.ds(index * half, half), :], held_ref.at[pl.ds(index * half, half), :], semaphores.at[index]
        )
        for index in range(2)
    ]
    for fetch in fetches:
        fetch.start()
    sums = jnp.zeros((1, LANES), jnp.float32)
    for block in range(plan.lane_blocks):
        if block * LANES % half == 0:
            fetches[block * LANES // half].wait()
        tile = held_ref[pl.ds(block * LANES, LANES), :]
        sums = sums + lane_sums(tile * tile)
        turned = tile.T
        for piece in range(plan.pieces):
            out_ref[pl.ds(piece * plan.lane_blocks + block, plan.groups, stride=plan.inward), :] = turned[
                piece * plan.groups : (piece + 1) * plan.groups
            ]
    put_sums(out_ref, [sums], plan.body, plan.inward, plan.groups)


def fetch_slabs(plan, slabs, bits_ref, operators_ref, held_ref, semaphores):
    fetches = []
    for index, slab in enumerate(slabs):
        bit, part = divmod(slab, plan.parts)
        rows = pl.ds(part * plan.width, plan.width)
        fetch = pltpu.make_async_copy(
            operators_ref.at[bits_ref[bit], rows, :], held_ref.at[index], semaphores.at[index]
        )
        fetch.start()
        fetches.append(fetch)
    return fetches


def mask_slab(plan, slab, index, bits_ref, mask_ref, held_ref, out_ref):
    bit, part = divmod(slab, plan.parts)
    chosen = bits_ref[bit]
    for start in range(0, plan.width, plan.edge):
        across = (part * plan.width + start) // plan.edge
        rows = pl.ds(start, plan.edge)
        for along in range(plan.blocks):
            columns = pl.ds(along * plan.edge, plan.edge)
            keep = (mask_ref[chosen, across, along] > 0).astype(jnp.float32).astype(jnp.bfloat16)
            out_ref[index, columns, rows] = (held_ref[index, rows, columns] * keep).T


def store_kernel(plan, bits_ref, mask_ref, operators_ref, stored_ref, held_ref, masked_ref, in_semaphores, out_semaphores):
    slabs = range(plan.kept, plan.slabs)
    fetches = fetch_slabs(plan, slabs, bits_ref, operators_ref, held_ref, in_semaphores)
    stores = []
    for index, slab in enumerate(slabs):
        fetches[index].wait()
        mask_slab(plan, slab, index, bits_ref, mask_ref, held_ref, masked_ref)
        store = pltpu.make_async_copy(masked_ref.at[index], stored_ref.at[index], out_semaphores.at[index])
        store.start()
        stores.append(store)
    for store in stores:
        store.wait()


def prepare_kernel(
    plan,
    bits_ref,
    mask_ref,
    field_ref,
    coupling_ref,
    mode_ref,
    operators_ref,
    place_ref,
    inside_ref,
    kept_ref,
    held_ref,
    semaphores,
):
    slabs = range(plan.kept)
    fetches = fetch_slabs(plan, slabs, bits_ref, operators_ref, held_ref, semaphores)
    me = lax.axis_index("site") * plan.phonons + lax.axis_index("phonon")
    place = lax.broadcasted_iota(jnp.int32, (plan.places, LANES), 0)
    phonon = place % plan.phonons
    site = place // plan.phonons % plan.sites
    mode = place // plan.groups % plan.share
    level = phonon * plan.levels_here + place // (plan.groups * plan.share)
    occupied = jnp.zeros((plan.places, LANES), jnp.float32)
    for position in range(plan.bits):
        held = (site >> position & 1).astype(jnp.float32)
        occupied = occupied + coupling_ref[bits_ref[position]] * held
    strength = jnp.zeros((plan.places, LANES), jnp.float32)
    for index in range(plan.share):
        strength = jnp.where(mode == index, mode_ref[index * plan.groups + me], strength)
    strength = strength / jnp.sqrt(jnp.full((1, LANES), plan.level_count, jnp.float32))
    height = level.astype(jnp.float32)
    place_ref[0] = occupied
    place_ref[1] = strength * jnp.sqrt(height)
    place_ref[2] = jnp.where(level == plan.level_count - 1, 0.0, strength * jnp.sqrt(height + 1.0))
    inside = lax.broadcasted_iota(jnp.int32, (1, plan.rows), 1)
    weight = jnp.zeros((1, plan.rows), jnp.float32)
    for local_bit in range(LBITS):
        weight = weight + coupling_ref[plan.bits + local_bit] * (inside >> local_bit & 1).astype(jnp.float32)
    inside_ref[...] = jnp.zeros_like(inside_ref)
    inside_ref[:1] = weight
    for position in range(plan.bits):
        inside_ref[pl.ds(1 + position, 1)] = jnp.full((1, plan.rows), field_ref[bits_ref[position]])
    for slab in slabs:
        fetches[slab].wait()
        mask_slab(plan, slab, slab, bits_ref, mask_ref, held_ref, kept_ref)


def flipped(values, stride):
    places, width = values.shape
    if stride % SUBLANES == 0:
        shaped = values.reshape(places // (2 * stride), 2, stride, width)
        return jnp.concatenate([shaped[:, 1:], shaped[:, :1]], axis=1).reshape(places, width)
    tiles = values.reshape(places // SUBLANES, SUBLANES, width)
    if 2 * stride == SUBLANES:
        return pltpu.roll(tiles, stride, 1).reshape(places, width)
    spot = lax.broadcasted_iota(jnp.int32, tiles.shape, 1)
    down = pltpu.roll(tiles, stride, 1)
    up = pltpu.roll(tiles, SUBLANES - stride, 1)
    return jnp.where(spot & stride > 0, down, up).reshape(places, width)


def shifted(values, by):
    places, width = values.shape
    tiles = values.reshape(places // SUBLANES, SUBLANES, width)
    return pltpu.roll(tiles, by % SUBLANES, 1).reshape(places, width)


def step(plan, vector_ref, kept_ref, fetched_ref, place_ref, inside_ref, rounded_ref, finish, ready=None, begun_ref=None):
    span = plan.places // plan.levels_here
    for block in range(plan.lane_blocks):
        vector = vector_ref[:, pl.ds(block * LANES, LANES)]
        for position in range(plan.bits):
            rounded_ref[:, pl.ds(position * plan.rows + block * LANES, LANES)] = flipped(
                vector, plan.phonons << position
            ).astype(jnp.bfloat16)

    def local(start):
        lanes = pl.ds(start, LANES)
        vector = vector_ref[:, lanes]
        levels = [vector[index * span : (index + 1) * span] for index in range(plan.levels_here)]
        lower = jnp.concatenate([shifted(levels[-1], 1)] + levels[:-1], axis=0)
        upper = jnp.concatenate(levels[1:] + [shifted(levels[0], -1)], axis=0)
        weight = place_ref[0] + inside_ref[:1, lanes]
        total = weight * (place_ref[1] * lower + place_ref[2] * upper)
        for position in range(plan.bits):
            total = total + inside_ref[pl.ds(1 + position, 1), lanes] * flipped(vector, plan.phonons << position)
        return total

    def added(total, part, late):
        for position in range(plan.bits):
            slab = position * plan.parts + part
            if late is not None and late != (slab >= plan.kept):
                continue
            if late:
                ready(slab)
            masked = kept_ref[slab] if slab < plan.kept else fetched_ref[slab - plan.kept]
            total = total + jnp.dot(
                rounded_ref[:, pl.ds(position * plan.rows, plan.rows)], masked, preferred_element_type=jnp.float32
            )
        return total

    def locals_of(lanes):
        return jnp.concatenate([local(start) for start in range(lanes.start, lanes.start + plan.width, LANES)], axis=1)

    parts = [pl.ds(part * plan.width, plan.width) for part in range(plan.parts)]
    if ready is None:
        for part, lanes in enumerate(parts):
            finish(lanes, added(locals_of(lanes), part, None))
        return
    for part, lanes in enumerate(parts):
        begun_ref[:, lanes] = added(locals_of(lanes), part, False)
    for part, lanes in enumerate(parts):
        finish(lanes, added(begun_ref[:, lanes], part, True))


def first_kernel(
    plan,
    arrived_ref,
    place_ref,
    inside_ref,
    kept_ref,
    stored_ref,
    initial_ref,
    new_ref,
    sums_ref,
    fetched_ref,
    rounded_ref,
    semaphores,
):
    fetches = {}
    for part in range(plan.parts):
        for slab in range(part, plan.slabs, plan.parts):
            if slab >= plan.kept:
                index = slab - plan.kept
                fetches[slab] = pltpu.make_async_copy(
                    stored_ref.at[index], fetched_ref.at[index], semaphores.at[index]
                )
                fetches[slab].start()

    def ready(slab):
        fetches[slab].wait()

    squares = totals_of(arrived_ref, plan.body, plan.inward, plan.groups)[0]
    inverse = 1.0 / scale_of(plan, squares)
    for piece in range(plan.pieces):
        for block in range(plan.lane_blocks):
            part = arrived_ref[pl.ds(piece * plan.lane_blocks + block, plan.groups, stride=plan.inward), :]
            initial_ref[pl.ds(piece * plan.groups, plan.groups), pl.ds(block * LANES, LANES)] = part * inverse
    tables = (kept_ref, fetched_ref, place_ref, inside_ref, rounded_ref)
    squares = []
    overlap = []
    ahead = []

    def finish(lanes, new):
        new_ref[:, lanes] = new
        squares.append(lane_sums(new * new))
        overlap.append(lane_sums(new * initial_ref[:, lanes]))

    def look_ahead(lanes, total):
        new = 2.0 * total - initial_ref[:, lanes]
        ahead.append(lane_sums(new * new))

    step(plan, initial_ref, *tables, finish, ready, new_ref)
    step(plan, new_ref, *tables, look_ahead)
    put_sums(sums_ref, [one_row(squares), one_row(overlap), one_row(ahead)], 0, 1, plan.groups)


def one_row(rows):
    total = sum(rows[1:], rows[0])
    return sum(total[:, start : start + LANES] for start in range(0, total.shape[1], LANES))


def onward_kernel(
    plan,
    arrived_ref,
    raw_ref,
    initial_ref,
    place_ref,
    inside_ref,
    kept_ref,
    fetched_ref,
    out_ref,
    known_ref,
    rounded_ref,
    second_ref,
    third_ref,
):
    squares, overlap, ahead, _ = totals_of(arrived_ref, 0, 1, plan.groups)
    first = 1.0 / scale_of(plan, squares)
    estimate = scale_of(plan, ahead * first * first)
    second = 1.0 / estimate
    known_ref[:1, :] = jnp.broadcast_to(overlap * first / plan.entries, (1, LANES))
    known_ref[1:, :] = jnp.broadcast_to(estimate, (SUBLANES - 1, LANES))
    for block in range(plan.lane_blocks):
        lanes = pl.ds(block * LANES, LANES)
        second_ref[:, lanes] = raw_ref[:, lanes] * first
    tables = (kept_ref, fetched_ref, place_ref, inside_ref, rounded_ref)
    sums = [[] for _ in range(SLOTS)]

    def send(vector, lanes, new):
        sums[2 * vector].append(lane_sums(new * new))
        sums[2 * vector + 1].append(lane_sums(new * initial_ref[:, lanes]))
        for start in range(0, plan.width, LANES):
            block = (lanes.start + start) // LANES
            for piece in range(plan.pieces):
                row = vector * plan.body + piece * plan.lane_blocks + block
                out_ref[pl.ds(row, plan.groups, stride=plan.outward), :] = new[
                    piece * plan.groups : (piece + 1) * plan.groups, start : start + LANES
                ]

    def finish_second(lanes, total):
        new = 2.0 * total - initial_ref[:, lanes] * first
        third_ref[:, lanes] = new * second
        send(0, lanes, new)

    def finish_third(lanes, total):
        send(1, lanes, 2.0 * total - second_ref[:, lanes] * second)

    step(plan, second_ref, *tables, finish_second)
    step(plan, third_ref, *tables, finish_third)
    put_sums(out_ref, [one_row(rows) for rows in sums], 2 * plan.body, plan.outward, plan.groups)


def arrive_kernel(plan, arrived_ref, known_ref, before_ref, last_ref, moments_ref):
    before_squares, before_overlap, last_squares, last_overlap = totals_of(
        arrived_ref, 2 * plan.body, plan.outward, plan.groups
    )
    before = 1.0 / scale_of(plan, before_squares)
    back = known_ref[1:2, :1] * before
    last = back / scale_of(plan, last_squares * back * back)
    for vector, (out_ref, factor) in enumerate(((before_ref, before), (last_ref, last))):
        for block in range(plan.lane_blocks):
            first = vector * plan.body + block
            parts = [
                arrived_ref[pl.ds(first + piece * plan.lane_blocks, plan.groups, stride=plan.outward), :]
                for piece in range(plan.pieces)
            ]
            out_ref[pl.ds(block * LANES, LANES), :] = jnp.concatenate(parts, axis=0).T * factor
    moments_ref[0] = known_ref[0, 0]
    moments_ref[1] = (before_overlap * before / plan.entries)[0, 0]
    moments_ref[2] = (last_overlap * last / plan.entries)[0, 0]


def exchange(values, count):
    shaped = values.reshape(count, values.shape[0] // count, 1, LANES)
    return lax.all_to_all(shaped, AXES, 0, 0, tiled=True).reshape(values.shape)


def shards(plan, state, operators, op_mask, site_bits, field, site_coupling, mode_coupling):
    f32 = jnp.float32
    inward = jax.ShapeDtypeStruct((plan.groups * plan.inward, LANES), f32)
    outward = jax.ShapeDtypeStruct((plan.groups * plan.outward, LANES), f32)
    vector = jax.ShapeDtypeStruct((plan.places, plan.rows), f32)
    known = jax.ShapeDtypeStruct((SUBLANES, LANES), f32)
    held = jax.ShapeDtypeStruct((plan.rows, plan.columns), f32)
    rounded = pltpu.VMEM((plan.places, plan.bits * plan.rows), jnp.bfloat16)
    working = pltpu.VMEM((plan.places, plan.rows), f32)
    work = 2 * plan.bits * plan.places * plan.rows * plan.rows

    def cost(flops, moved):
        return pl.CostEstimate(flops=flops, bytes_accessed=moved, transcendentals=0)

    departing = pl.pallas_call(
        functools.partial(depart_kernel, plan),
        out_shape=inward,
        in_specs=[HBM],
        out_specs=VMEM,
        scratch_shapes=[pltpu.VMEM((plan.rows, plan.columns), f32), pltpu.SemaphoreType.DMA((2,))],
        compiler_params=params(60),
        name="depart",
    )(state)
    arrived = exchange(departing, plan.groups)
    fetched = plan.slabs - plan.kept
    kept_slabs = (plan.kept, plan.rows, plan.width)
    fetched_slabs = (fetched, plan.rows, plan.width)

    def held_slabs(count):
        return pltpu.VMEM((count, plan.width, plan.rows), jnp.bfloat16)

    place, inside, kept = pl.pallas_call(
        functools.partial(prepare_kernel, plan),
        out_shape=[
            jax.ShapeDtypeStruct((3, plan.places, LANES), f32),
            jax.ShapeDtypeStruct((SUBLANES, plan.rows), f32),
            jax.ShapeDtypeStruct(kept_slabs, jnp.bfloat16),
        ],
        in_specs=[SMEM] * 5 + [HBM],
        out_specs=[VMEM] * 3,
        scratch_shapes=[held_slabs(plan.kept), pltpu.SemaphoreType.DMA((plan.kept,))],
        compiler_params=params(50),
        cost_estimate=cost(plan.rows * plan.rows, 4 * plan.kept * plan.rows * plan.width),
        name="prepare",
    )(site_bits, op_mask, field, site_coupling, mode_coupling, operators)
    stored = pl.pallas_call(
        functools.partial(store_kernel, plan),
        out_shape=jax.ShapeDtypeStruct(fetched_slabs, jnp.bfloat16),
        in_specs=[SMEM] * 2 + [HBM],
        out_specs=HBM,
        scratch_shapes=[
            held_slabs(fetched),
            pltpu.VMEM(fetched_slabs, jnp.bfloat16),
            pltpu.SemaphoreType.DMA((fetched,)),
            pltpu.SemaphoreType.DMA((fetched,)),
        ],
        compiler_params=params(60),
        cost_estimate=cost(plan.rows * plan.rows, 4 * fetched * plan.rows * plan.width),
        name="store",
    )(site_bits, op_mask, operators)
    initial, raw, sums, late = pl.pallas_call(
        functools.partial(first_kernel, plan),
        out_shape=[
            vector,
            vector,
            jax.ShapeDtypeStruct((plan.groups, LANES), f32),
            jax.ShapeDtypeStruct(fetched_slabs, jnp.bfloat16),
        ],
        in_specs=[VMEM] * 4 + [HBM],
        out_specs=[VMEM] * 4,
        scratch_shapes=[rounded, pltpu.SemaphoreType.DMA((fetched,))],
        compiler_params=params(46),
        cost_estimate=cost(2 * work, 4 * plan.places * plan.rows),
        name="first",
    )(arrived, place, inside, kept, stored)
    tables = (place, inside, kept, late)
    sums = exchange(sums, plan.groups)
    departing, told = pl.pallas_call(
        functools.partial(onward_kernel, plan),
        out_shape=[outward, known],
        in_specs=[VMEM] * 7,
        out_specs=[VMEM] * 2,
        scratch_shapes=[rounded, working, working],
        compiler_params=params(32),
        cost_estimate=cost(2 * work, 8 * plan.places * plan.rows),
        name="onward",
    )(sums, raw, initial, *tables)
    arrived = exchange(departing, plan.groups)
    before, last, moments = pl.pallas_call(
        functools.partial(arrive_kernel, plan),
        out_shape=[held, held, jax.ShapeDtypeStruct((STEPS,), f32)],
        in_specs=[VMEM] * 2,
        out_specs=[VMEM, VMEM, SMEM],
        compiler_params=params(16),
        name="arrive",
    )(arrived, told)
    return last, before, moments


def extended_2(block, sides, width):
    for axis, dim in sides:
        count = lax.axis_size(axis)
        forward = [(i, i + 1) for i in range(count - 1)]
        backward = [(target, source) for source, target in forward]
        low = lax.ppermute(
            lax.slice_in_dim(block, block.shape[dim] - width, None, axis=dim), axis, forward
        )
        high = lax.ppermute(lax.slice_in_dim(block, 0, width, axis=dim), axis, backward)
        block = jnp.concatenate([low, block, high], axis=dim)
    return block


def partner(value, axis, bit):
    mask = 2**bit
    pairs = [(source, source ^ mask) for source in range(lax.axis_size(axis))]
    return lax.ppermute(value, axis, pairs)


def halo_shards(state, operators, op_mask, site_bits, field, site_coupling, mode_coupling):
    site_count = lax.axis_size("site")
    phonon_count = lax.axis_size("phonon")
    bit_count = site_count.bit_length() - 1
    rows_here = state.shape[0]
    columns_here = state.shape[1]
    levels_here = columns_here // MODES
    block_edge = rows_here // op_mask.shape[1]
    expanded = jnp.repeat(jnp.repeat(op_mask, block_edge, axis=1), block_edge, axis=2)
    masked = jnp.where(expanded > 0, operators, jnp.zeros((), jnp.bfloat16))
    entries = jnp.float32(rows_here * columns_here * site_count * phonon_count)
    level_total = jnp.sqrt(jnp.float32(levels_here * phonon_count))
    device = lax.axis_index("site")
    inside = lax.iota(jnp.int32, rows_here)
    weight_rows = jnp.zeros((rows_here,), jnp.float32)
    for position in range(bit_count):
        weight_rows = weight_rows + site_coupling[site_bits[position]] * (
            device >> position & 1
        ).astype(jnp.float32)
    for local_bit in range(LBITS):
        weight_rows = weight_rows + site_coupling[bit_count + local_bit] * (
            inside >> local_bit & 1
        ).astype(jnp.float32)
    levels = (
        lax.axis_index("phonon") * levels_here + lax.iota(jnp.int32, columns_here) // MODES
    ).astype(jnp.float32)
    lower_weight = jnp.sqrt(levels)
    upper_weight = jnp.sqrt(levels + 1.0)
    mode_weight = jnp.tile(mode_coupling, columns_here // MODES) / level_total
    start_squares = lax.psum(jnp.sum(state * state), ("site", "phonon"))
    initial = state / jnp.sqrt(start_squares / entries + epsilon)
    previous = initial
    current = initial
    scale_prev = jnp.float32(1.0)
    moments = []
    for iteration in range(STEPS):
        extended = extended_2(current, (("phonon", 1),), MODES)
        lower_part = extended[:, :columns_here]
        upper_part = extended[:, 2 * MODES :]
        summed = weight_rows[:, None] * (
            mode_weight * (lower_weight * lower_part + upper_weight * upper_part)
        )
        for operate_position in range(bit_count):
            chosen = site_bits[operate_position]
            flipped = partner(current, "site", operate_position)
            product = jnp.dot(
                masked[chosen], flipped.astype(jnp.bfloat16), preferred_element_type=jnp.float32
            )
            summed = summed + (field[chosen] * flipped + product)
        if iteration == 0:
            vector_new = summed
        else:
            vector_new = 2.0 * summed - previous / scale_prev
        squares, intersection = lax.psum(
            (jnp.sum(vector_new * vector_new), jnp.sum(initial * vector_new)), ("site", "phonon")
        )
        scale_now = jnp.sqrt(squares / entries + epsilon)
        updated = vector_new / scale_now
        moment = intersection / (entries * scale_now)
        moments.append(moment)
        previous = current
        current = updated
        scale_prev = scale_now
    return (current, previous, jnp.stack(moments))


def solution(mesh):
    in_specs = (P("site", "phonon"), P(), P(), P(), P(), P(), P())
    out_specs = (P("site", "phonon"), P("site", "phonon"), P())

    def whole(state, operators, op_mask, *rest):
        rows = state.shape[0] // mesh.shape["site"]
        columns = state.shape[1] // mesh.shape["phonon"]
        plan = Plan(mesh, rows, columns, op_mask.shape[1])
        body = functools.partial(shards, plan) if plan.fits() else halo_shards
        run = jax.shard_map(body, mesh=mesh, in_specs=in_specs, out_specs=out_specs, check_vma=False)
        return run(state, operators, op_mask, *rest)

    return whole
```

```python
import functools

import jax
import jax.numpy as jnp
from jax import lax
from jax.experimental import pallas as pl
from jax.experimental.pallas import tpu as pltpu
from jax.sharding import PartitionSpec as P

LBITS = 10
MODES = 64
STEPS = 3
LANES = 128
SUBLANES = 8
SLOTS = 4
AXES = ("site", "phonon")

epsilon = 1e-06


VMEM = pl.BlockSpec(memory_space=pltpu.VMEM)
SMEM = pl.BlockSpec(memory_space=pltpu.SMEM)
HBM = pl.BlockSpec(memory_space=pltpu.HBM)


class Plan:
    def __init__(self, mesh, rows, columns, blocks):
        self.sites = mesh.shape["site"]
        self.phonons = mesh.shape["phonon"]
        self.groups = self.sites * self.phonons
        self.bits = self.sites.bit_length() - 1
        self.rows = rows
        self.columns = columns
        self.blocks = blocks
        self.edge = rows // blocks
        self.levels_here = columns // MODES
        self.level_count = self.levels_here * self.phonons
        self.share = MODES // self.groups
        self.pieces = self.levels_here * self.share
        self.lane_blocks = rows // LANES
        self.body = self.pieces * self.lane_blocks
        self.inward = self.body + 1
        self.outward = 2 * self.body + 1
        self.places = self.pieces * self.groups
        self.width = 2 * LANES
        self.parts = rows // self.width
        self.slabs = self.bits * self.parts
        self.kept = min(5, self.slabs - 1)
        self.entries = float(rows * columns * self.groups)

    def fits(self):
        return (
            MODES % self.groups == 0
            and self.columns == LANES
            and self.rows % self.width == 0
            and self.edge % LANES == 0
            and self.width % self.edge == 0
            and self.bits < SUBLANES
            and self.groups % SUBLANES == 0
        )


def params(mib):
    return pltpu.CompilerParams(vmem_limit_bytes=mib * 2**20)


def lane_sums(values):
    return jnp.sum(values, axis=0, keepdims=True)


def put_sums(out_ref, sums, start, stride, count):
    lane = lax.broadcasted_iota(jnp.int32, (1, LANES), 1)
    row = jnp.zeros((1, LANES), jnp.float32)
    for slot, value in enumerate(sums):
        width = LANES
        while width > LANES // SLOTS:
            width //= 2
            value = value + pltpu.roll(value, width, 1)
        row = jnp.where(lane // (LANES // SLOTS) == slot, value, row)
    out_ref[pl.ds(start, count, stride=stride), :] = jnp.broadcast_to(row, (count, LANES))


def totals_of(ref, start, stride, count):
    lanes = lane_sums(ref[pl.ds(start, count, stride=stride), :])
    lane = lax.broadcasted_iota(jnp.int32, (1, LANES), 1)
    return [
        jnp.sum(jnp.where(lane // (LANES // SLOTS) == slot, lanes, 0.0), axis=1, keepdims=True)
        for slot in range(SLOTS)
    ]


def scale_of(plan, squares):
    return jnp.sqrt(squares / plan.entries + epsilon)


def depart_kernel(plan, state_ref, out_ref, held_ref, semaphores):
    half = plan.rows // 2
    fetches = [
        pltpu.make_async_copy(
            state_ref.at[pl.ds(index * half, half), :], held_ref.at[pl.ds(index * half, half), :], semaphores.at[index]
        )
        for index in range(2)
    ]
    for fetch in fetches:
        fetch.start()
    sums = jnp.zeros((1, LANES), jnp.float32)
    for block in range(plan.lane_blocks):
        if block * LANES % half == 0:
            fetches[block * LANES // half].wait()
        tile = held_ref[pl.ds(block * LANES, LANES), :]
        sums = sums + lane_sums(tile * tile)
        turned = tile.T
        for piece in range(plan.pieces):
            out_ref[pl.ds(piece * plan.lane_blocks + block, plan.groups, stride=plan.inward), :] = turned[
                piece * plan.groups : (piece + 1) * plan.groups
            ]
    put_sums(out_ref, [sums], plan.body, plan.inward, plan.groups)


def fetch_slabs(plan, slabs, bits_ref, operators_ref, held_ref, semaphores):
    fetches = []
    for index, slab in enumerate(slabs):
        part, bit = divmod(slab, plan.bits)
        rows = pl.ds(part * plan.width, plan.width)
        fetch = pltpu.make_async_copy(
            operators_ref.at[bits_ref[bit], rows, :], held_ref.at[index], semaphores.at[index]
        )
        fetch.start()
        fetches.append(fetch)
    return fetches


def mask_slab(plan, slab, index, bits_ref, mask_ref, held_ref, out_ref):
    part, bit = divmod(slab, plan.bits)
    chosen = bits_ref[bit]
    for start in range(0, plan.width, plan.edge):
        across = (part * plan.width + start) // plan.edge
        rows = pl.ds(start, plan.edge)
        for along in range(plan.blocks):
            columns = pl.ds(along * plan.edge, plan.edge)
            keep = (mask_ref[chosen, across, along] > 0).astype(jnp.float32).astype(jnp.bfloat16)
            out_ref[index, columns, rows] = (held_ref[index, rows, columns] * keep).T


def store_kernel(plan, bits_ref, mask_ref, operators_ref, stored_ref, held_ref, masked_ref, in_semaphores, out_semaphores):
    slabs = range(plan.kept, plan.slabs)
    fetches = fetch_slabs(plan, slabs, bits_ref, operators_ref, held_ref, in_semaphores)
    stores = []
    for index, slab in enumerate(slabs):
        fetches[index].wait()
        mask_slab(plan, slab, index, bits_ref, mask_ref, held_ref, masked_ref)
        store = pltpu.make_async_copy(masked_ref.at[index], stored_ref.at[index], out_semaphores.at[index])
        store.start()
        stores.append(store)
    for store in stores:
        store.wait()


def prepare_kernel(
    plan,
    bits_ref,
    mask_ref,
    field_ref,
    coupling_ref,
    mode_ref,
    operators_ref,
    place_ref,
    inside_ref,
    kept_ref,
    held_ref,
    semaphores,
):
    slabs = range(plan.kept)
    fetches = fetch_slabs(plan, slabs, bits_ref, operators_ref, held_ref, semaphores)
    me = lax.axis_index("site") * plan.phonons + lax.axis_index("phonon")
    place = lax.broadcasted_iota(jnp.int32, (plan.places, LANES), 0)
    phonon = place % plan.phonons
    site = place // plan.phonons % plan.sites
    mode = place // plan.groups % plan.share
    level = phonon * plan.levels_here + place // (plan.groups * plan.share)
    occupied = jnp.zeros((plan.places, LANES), jnp.float32)
    for position in range(plan.bits):
        held = (site >> position & 1).astype(jnp.float32)
        occupied = occupied + coupling_ref[bits_ref[position]] * held
    strength = jnp.zeros((plan.places, LANES), jnp.float32)
    for index in range(plan.share):
        strength = jnp.where(mode == index, mode_ref[index * plan.groups + me], strength)
    strength = strength / jnp.sqrt(jnp.full((1, LANES), plan.level_count, jnp.float32))
    height = level.astype(jnp.float32)
    place_ref[0] = occupied
    place_ref[1] = strength * jnp.sqrt(height)
    place_ref[2] = jnp.where(level == plan.level_count - 1, 0.0, strength * jnp.sqrt(height + 1.0))
    inside = lax.broadcasted_iota(jnp.int32, (1, plan.rows), 1)
    weight = jnp.zeros((1, plan.rows), jnp.float32)
    for local_bit in range(LBITS):
        weight = weight + coupling_ref[plan.bits + local_bit] * (inside >> local_bit & 1).astype(jnp.float32)
    inside_ref[...] = jnp.zeros_like(inside_ref)
    inside_ref[:1] = weight
    for position in range(plan.bits):
        inside_ref[pl.ds(1 + position, 1)] = jnp.full((1, plan.rows), field_ref[bits_ref[position]])
    for slab in slabs:
        fetches[slab].wait()
        mask_slab(plan, slab, slab, bits_ref, mask_ref, held_ref, kept_ref)


def flipped(values, stride):
    places, width = values.shape
    if stride % SUBLANES == 0:
        shaped = values.reshape(places // (2 * stride), 2, stride, width)
        return jnp.concatenate([shaped[:, 1:], shaped[:, :1]], axis=1).reshape(places, width)
    tiles = values.reshape(places // SUBLANES, SUBLANES, width)
    if 2 * stride == SUBLANES:
        return pltpu.roll(tiles, stride, 1).reshape(places, width)
    spot = lax.broadcasted_iota(jnp.int32, tiles.shape, 1)
    down = pltpu.roll(tiles, stride, 1)
    up = pltpu.roll(tiles, SUBLANES - stride, 1)
    return jnp.where(spot & stride > 0, down, up).reshape(places, width)


def shifted(values, by):
    places, width = values.shape
    tiles = values.reshape(places // SUBLANES, SUBLANES, width)
    return pltpu.roll(tiles, by % SUBLANES, 1).reshape(places, width)


def put_rounded(plan, rounded_ref, vector, start):
    for position in range(plan.bits):
        rounded_ref[:, pl.ds(position * plan.rows + start, vector.shape[1])] = flipped(
            vector, plan.phonons << position
        ).astype(jnp.bfloat16)


def step(plan, vector_ref, rounded_ref, kept_ref, fetched_ref, place_ref, inside_ref, finish, ready=None, begun_ref=None):
    span = plan.places // plan.levels_here

    def local(start):
        lanes = pl.ds(start, LANES)
        vector = vector_ref[:, lanes]
        levels = [vector[index * span : (index + 1) * span] for index in range(plan.levels_here)]
        lower = jnp.concatenate([shifted(levels[-1], 1)] + levels[:-1], axis=0)
        upper = jnp.concatenate(levels[1:] + [shifted(levels[0], -1)], axis=0)
        weight = place_ref[0] + inside_ref[:1, lanes]
        total = weight * (place_ref[1] * lower + place_ref[2] * upper)
        for position in range(plan.bits):
            total = total + inside_ref[pl.ds(1 + position, 1), lanes] * flipped(vector, plan.phonons << position)
        return total

    def added(total, part, late):
        for ref, low, high in ((kept_ref, 0, plan.kept), (fetched_ref, plan.kept, plan.slabs)):
            fetched = low > 0
            begin = max(part * plan.bits, low)
            count = min((part + 1) * plan.bits, high) - begin
            if count <= 0 or late not in (None, fetched):
                continue
            if late:
                for slab in range(begin, begin + count):
                    ready(slab)
            first = begin - part * plan.bits
            masked = ref[pl.ds(begin - low, count)].reshape(count * plan.rows, plan.width)
            operand = rounded_ref[:, pl.ds(first * plan.rows, count * plan.rows)]
            total = total + jnp.dot(operand, masked, preferred_element_type=jnp.float32)
        return total

    def locals_of(lanes):
        return jnp.concatenate([local(start) for start in range(lanes.start, lanes.start + plan.width, LANES)], axis=1)

    parts = [pl.ds(part * plan.width, plan.width) for part in range(plan.parts)]
    if ready is None:
        for part, lanes in enumerate(parts):
            finish(lanes, added(locals_of(lanes), part, None))
        return
    for part, lanes in enumerate(parts):
        begun_ref[:, lanes] = added(locals_of(lanes), part, False)
    for part, lanes in enumerate(parts):
        finish(lanes, added(begun_ref[:, lanes], part, True))


def first_kernel(
    plan,
    arrived_ref,
    place_ref,
    inside_ref,
    kept_ref,
    stored_ref,
    initial_ref,
    new_ref,
    sums_ref,
    fetched_ref,
    rounded_ref,
    ahead_ref,
    semaphores,
):
    fetches = {}
    for slab in range(plan.kept, plan.slabs):
        index = slab - plan.kept
        fetches[slab] = pltpu.make_async_copy(stored_ref.at[index], fetched_ref.at[index], semaphores.at[index])
        fetches[slab].start()

    def ready(slab):
        fetches[slab].wait()

    squares = totals_of(arrived_ref, plan.body, plan.inward, plan.groups)[0]
    inverse = 1.0 / scale_of(plan, squares)
    for block in range(plan.lane_blocks):
        parts = [
            arrived_ref[pl.ds(piece * plan.lane_blocks + block, plan.groups, stride=plan.inward), :]
            for piece in range(plan.pieces)
        ]
        vector = jnp.concatenate(parts, axis=0) * inverse
        initial_ref[:, pl.ds(block * LANES, LANES)] = vector
        put_rounded(plan, rounded_ref, vector, block * LANES)
    tables = (kept_ref, fetched_ref, place_ref, inside_ref)
    squares = []
    overlap = []
    ahead = []

    def finish(lanes, new):
        new_ref[:, lanes] = new
        put_rounded(plan, ahead_ref, new, lanes.start)
        squares.append(lane_sums(new * new))
        overlap.append(lane_sums(new * initial_ref[:, lanes]))

    def look_ahead(lanes, total):
        new = 2.0 * total - initial_ref[:, lanes]
        ahead.append(lane_sums(new * new))

    step(plan, initial_ref, rounded_ref, *tables, finish, ready, new_ref)
    step(plan, new_ref, ahead_ref, *tables, look_ahead)
    put_sums(sums_ref, [one_row(squares), one_row(overlap), one_row(ahead)], 0, 1, plan.groups)


def one_row(rows):
    total = sum(rows[1:], rows[0])
    return sum(total[:, start : start + LANES] for start in range(0, total.shape[1], LANES))


def onward_kernel(
    plan,
    arrived_ref,
    raw_ref,
    initial_ref,
    place_ref,
    inside_ref,
    kept_ref,
    fetched_ref,
    out_ref,
    known_ref,
    rounded_ref,
    ahead_ref,
    second_ref,
    third_ref,
):
    squares, overlap, ahead, _ = totals_of(arrived_ref, 0, 1, plan.groups)
    first = 1.0 / scale_of(plan, squares)
    estimate = scale_of(plan, ahead * first * first)
    second = 1.0 / estimate
    known_ref[:1, :] = jnp.broadcast_to(overlap * first / plan.entries, (1, LANES))
    known_ref[1:, :] = jnp.broadcast_to(estimate, (SUBLANES - 1, LANES))
    for block in range(plan.lane_blocks):
        lanes = pl.ds(block * LANES, LANES)
        vector = raw_ref[:, lanes] * first
        second_ref[:, lanes] = vector
        put_rounded(plan, rounded_ref, vector, block * LANES)
    tables = (kept_ref, fetched_ref, place_ref, inside_ref)
    sums = [[] for _ in range(SLOTS)]

    def send(vector, lanes, new):
        sums[2 * vector].append(lane_sums(new * new))
        sums[2 * vector + 1].append(lane_sums(new * initial_ref[:, lanes]))
        for start in range(0, plan.width, LANES):
            block = (lanes.start + start) // LANES
            for piece in range(plan.pieces):
                row = vector * plan.body + piece * plan.lane_blocks + block
                out_ref[pl.ds(row, plan.groups, stride=plan.outward), :] = new[
                    piece * plan.groups : (piece + 1) * plan.groups, start : start + LANES
                ]

    def finish_second(lanes, total):
        new = 2.0 * total - initial_ref[:, lanes] * first
        vector = new * second
        third_ref[:, lanes] = vector
        put_rounded(plan, ahead_ref, vector, lanes.start)
        send(0, lanes, new)

    def finish_third(lanes, total):
        send(1, lanes, 2.0 * total - second_ref[:, lanes] * second)

    step(plan, second_ref, rounded_ref, *tables, finish_second)
    step(plan, third_ref, ahead_ref, *tables, finish_third)
    put_sums(out_ref, [one_row(rows) for rows in sums], 2 * plan.body, plan.outward, plan.groups)


def arrive_kernel(plan, arrived_ref, known_ref, before_ref, last_ref, moments_ref):
    before_squares, before_overlap, last_squares, last_overlap = totals_of(
        arrived_ref, 2 * plan.body, plan.outward, plan.groups
    )
    before = 1.0 / scale_of(plan, before_squares)
    back = known_ref[1:2, :1] * before
    last = back / scale_of(plan, last_squares * back * back)
    for vector, (out_ref, factor) in enumerate(((before_ref, before), (last_ref, last))):
        for block in range(plan.lane_blocks):
            first = vector * plan.body + block
            parts = [
                arrived_ref[pl.ds(first + piece * plan.lane_blocks, plan.groups, stride=plan.outward), :]
                for piece in range(plan.pieces)
            ]
            out_ref[pl.ds(block * LANES, LANES), :] = jnp.concatenate(parts, axis=0).T * factor
    moments_ref[0] = known_ref[0, 0]
    moments_ref[1] = (before_overlap * before / plan.entries)[0, 0]
    moments_ref[2] = (last_overlap * last / plan.entries)[0, 0]


def exchange(values, count):
    shaped = values.reshape(count, values.shape[0] // count, 1, LANES)
    return lax.all_to_all(shaped, AXES, 0, 0, tiled=True).reshape(values.shape)


def shards(plan, state, operators, op_mask, site_bits, field, site_coupling, mode_coupling):
    f32 = jnp.float32
    inward = jax.ShapeDtypeStruct((plan.groups * plan.inward, LANES), f32)
    outward = jax.ShapeDtypeStruct((plan.groups * plan.outward, LANES), f32)
    vector = jax.ShapeDtypeStruct((plan.places, plan.rows), f32)
    known = jax.ShapeDtypeStruct((SUBLANES, LANES), f32)
    held = jax.ShapeDtypeStruct((plan.rows, plan.columns), f32)
    rounded = pltpu.VMEM((plan.places, plan.bits * plan.rows), jnp.bfloat16)
    working = pltpu.VMEM((plan.places, plan.rows), f32)
    work = 2 * plan.bits * plan.places * plan.rows * plan.rows

    def cost(flops, moved):
        return pl.CostEstimate(flops=flops, bytes_accessed=moved, transcendentals=0)

    departing = pl.pallas_call(
        functools.partial(depart_kernel, plan),
        out_shape=inward,
        in_specs=[HBM],
        out_specs=VMEM,
        scratch_shapes=[pltpu.VMEM((plan.rows, plan.columns), f32), pltpu.SemaphoreType.DMA((2,))],
        compiler_params=params(60),
        name="depart",
    )(state)
    arrived = exchange(departing, plan.groups)
    fetched = plan.slabs - plan.kept
    kept_slabs = (plan.kept, plan.rows, plan.width)
    fetched_slabs = (fetched, plan.rows, plan.width)

    def held_slabs(count):
        return pltpu.VMEM((count, plan.width, plan.rows), jnp.bfloat16)

    place, inside, kept = pl.pallas_call(
        functools.partial(prepare_kernel, plan),
        out_shape=[
            jax.ShapeDtypeStruct((3, plan.places, LANES), f32),
            jax.ShapeDtypeStruct((SUBLANES, plan.rows), f32),
            jax.ShapeDtypeStruct(kept_slabs, jnp.bfloat16),
        ],
        in_specs=[SMEM] * 5 + [HBM],
        out_specs=[VMEM] * 3,
        scratch_shapes=[held_slabs(plan.kept), pltpu.SemaphoreType.DMA((plan.kept,))],
        compiler_params=params(50),
        cost_estimate=cost(plan.rows * plan.rows, 4 * plan.kept * plan.rows * plan.width),
        name="prepare",
    )(site_bits, op_mask, field, site_coupling, mode_coupling, operators)
    stored = pl.pallas_call(
        functools.partial(store_kernel, plan),
        out_shape=jax.ShapeDtypeStruct(fetched_slabs, jnp.bfloat16),
        in_specs=[SMEM] * 2 + [HBM],
        out_specs=HBM,
        scratch_shapes=[
            held_slabs(fetched),
            pltpu.VMEM(fetched_slabs, jnp.bfloat16),
            pltpu.SemaphoreType.DMA((fetched,)),
            pltpu.SemaphoreType.DMA((fetched,)),
        ],
        compiler_params=params(60),
        cost_estimate=cost(plan.rows * plan.rows, 4 * fetched * plan.rows * plan.width),
        name="store",
    )(site_bits, op_mask, operators)
    initial, raw, sums, late = pl.pallas_call(
        functools.partial(first_kernel, plan),
        out_shape=[
            vector,
            vector,
            jax.ShapeDtypeStruct((plan.groups, LANES), f32),
            jax.ShapeDtypeStruct(fetched_slabs, jnp.bfloat16),
        ],
        in_specs=[VMEM] * 4 + [HBM],
        out_specs=[VMEM] * 4,
        scratch_shapes=[rounded, rounded, pltpu.SemaphoreType.DMA((fetched,))],
        compiler_params=params(46),
        cost_estimate=cost(2 * work, 4 * plan.places * plan.rows),
        name="first",
    )(arrived, place, inside, kept, stored)
    tables = (place, inside, kept, late)
    sums = exchange(sums, plan.groups)
    departing, told = pl.pallas_call(
        functools.partial(onward_kernel, plan),
        out_shape=[outward, known],
        in_specs=[VMEM] * 7,
        out_specs=[VMEM] * 2,
        scratch_shapes=[rounded, rounded, working, working],
        compiler_params=params(32),
        cost_estimate=cost(2 * work, 8 * plan.places * plan.rows),
        name="onward",
    )(sums, raw, initial, *tables)
    arrived = exchange(departing, plan.groups)
    before, last, moments = pl.pallas_call(
        functools.partial(arrive_kernel, plan),
        out_shape=[held, held, jax.ShapeDtypeStruct((STEPS,), f32)],
        in_specs=[VMEM] * 2,
        out_specs=[VMEM, VMEM, SMEM],
        compiler_params=params(16),
        name="arrive",
    )(arrived, told)
    return last, before, moments


def extended_2(block, sides, width):
    for axis, dim in sides:
        count = lax.axis_size(axis)
        forward = [(i, i + 1) for i in range(count - 1)]
        backward = [(target, source) for source, target in forward]
        low = lax.ppermute(
            lax.slice_in_dim(block, block.shape[dim] - width, None, axis=dim), axis, forward
        )
        high = lax.ppermute(lax.slice_in_dim(block, 0, width, axis=dim), axis, backward)
        block = jnp.concatenate([low, block, high], axis=dim)
    return block


def partner(value, axis, bit):
    mask = 2**bit
    pairs = [(source, source ^ mask) for source in range(lax.axis_size(axis))]
    return lax.ppermute(value, axis, pairs)


def halo_shards(state, operators, op_mask, site_bits, field, site_coupling, mode_coupling):
    site_count = lax.axis_size("site")
    phonon_count = lax.axis_size("phonon")
    bit_count = site_count.bit_length() - 1
    rows_here = state.shape[0]
    columns_here = state.shape[1]
    levels_here = columns_here // MODES
    block_edge = rows_here // op_mask.shape[1]
    expanded = jnp.repeat(jnp.repeat(op_mask, block_edge, axis=1), block_edge, axis=2)
    masked = jnp.where(expanded > 0, operators, jnp.zeros((), jnp.bfloat16))
    entries = jnp.float32(rows_here * columns_here * site_count * phonon_count)
    level_total = jnp.sqrt(jnp.float32(levels_here * phonon_count))
    device = lax.axis_index("site")
    inside = lax.iota(jnp.int32, rows_here)
    weight_rows = jnp.zeros((rows_here,), jnp.float32)
    for position in range(bit_count):
        weight_rows = weight_rows + site_coupling[site_bits[position]] * (
            device >> position & 1
        ).astype(jnp.float32)
    for local_bit in range(LBITS):
        weight_rows = weight_rows + site_coupling[bit_count + local_bit] * (
            inside >> local_bit & 1
        ).astype(jnp.float32)
    levels = (
        lax.axis_index("phonon") * levels_here + lax.iota(jnp.int32, columns_here) // MODES
    ).astype(jnp.float32)
    lower_weight = jnp.sqrt(levels)
    upper_weight = jnp.sqrt(levels + 1.0)
    mode_weight = jnp.tile(mode_coupling, columns_here // MODES) / level_total
    start_squares = lax.psum(jnp.sum(state * state), ("site", "phonon"))
    initial = state / jnp.sqrt(start_squares / entries + epsilon)
    previous = initial
    current = initial
    scale_prev = jnp.float32(1.0)
    moments = []
    for iteration in range(STEPS):
        extended = extended_2(current, (("phonon", 1),), MODES)
        lower_part = extended[:, :columns_here]
        upper_part = extended[:, 2 * MODES :]
        summed = weight_rows[:, None] * (
            mode_weight * (lower_weight * lower_part + upper_weight * upper_part)
        )
        for operate_position in range(bit_count):
            chosen = site_bits[operate_position]
            flipped = partner(current, "site", operate_position)
            product = jnp.dot(
                masked[chosen], flipped.astype(jnp.bfloat16), preferred_element_type=jnp.float32
            )
            summed = summed + (field[chosen] * flipped + product)
        if iteration == 0:
            vector_new = summed
        else:
            vector_new = 2.0 * summed - previous / scale_prev
        squares, intersection = lax.psum(
            (jnp.sum(vector_new * vector_new), jnp.sum(initial * vector_new)), ("site", "phonon")
        )
        scale_now = jnp.sqrt(squares / entries + epsilon)
        updated = vector_new / scale_now
        moment = intersection / (entries * scale_now)
        moments.append(moment)
        previous = current
        current = updated
        scale_prev = scale_now
    return (current, previous, jnp.stack(moments))


def solution(mesh):
    in_specs = (P("site", "phonon"), P(), P(), P(), P(), P(), P())
    out_specs = (P("site", "phonon"), P("site", "phonon"), P())

    def whole(state, operators, op_mask, *rest):
        rows = state.shape[0] // mesh.shape["site"]
        columns = state.shape[1] // mesh.shape["phonon"]
        plan = Plan(mesh, rows, columns, op_mask.shape[1])
        body = functools.partial(shards, plan) if plan.fits() else halo_shards
        run = jax.shard_map(body, mesh=mesh, in_specs=in_specs, out_specs=out_specs, check_vma=False)
        return run(state, operators, op_mask, *rest)

    return whole
```

```python
import functools

import jax
import jax.numpy as jnp
from jax import lax
from jax.experimental import pallas as pl
from jax.experimental.pallas import tpu as pltpu
from jax.sharding import PartitionSpec as P

LBITS = 10
MODES = 64
STEPS = 3
LANES = 128
SUBLANES = 8
SLOTS = 4
AXES = ("site", "phonon")

epsilon = 1e-06


VMEM = pl.BlockSpec(memory_space=pltpu.VMEM)
SMEM = pl.BlockSpec(memory_space=pltpu.SMEM)
HBM = pl.BlockSpec(memory_space=pltpu.HBM)


class Plan:
    def __init__(self, mesh, rows, columns, blocks):
        self.sites = mesh.shape["site"]
        self.phonons = mesh.shape["phonon"]
        self.groups = self.sites * self.phonons
        self.bits = self.sites.bit_length() - 1
        self.rows = rows
        self.columns = columns
        self.blocks = blocks
        self.edge = rows // blocks
        self.levels_here = columns // MODES
        self.level_count = self.levels_here * self.phonons
        self.share = MODES // self.groups
        self.pieces = self.levels_here * self.share
        self.lane_blocks = rows // LANES
        self.body = self.pieces * self.lane_blocks
        self.inward = self.body + 1
        self.outward = 2 * self.body + 1
        self.places = self.pieces * self.groups
        self.width = 2 * LANES
        self.parts = rows // self.width
        self.slabs = self.bits * self.parts
        self.kept = min(5, self.slabs - 1)
        self.entries = float(rows * columns * self.groups)

    def fits(self):
        return (
            MODES % self.groups == 0
            and self.columns == LANES
            and self.rows % self.width == 0
            and self.edge % LANES == 0
            and self.width % self.edge == 0
            and self.bits < SUBLANES
            and self.groups % SUBLANES == 0
        )


def params(mib):
    return pltpu.CompilerParams(vmem_limit_bytes=mib * 2**20)


def lane_sums(values):
    return jnp.sum(values, axis=0, keepdims=True)


def put_sums(out_ref, sums, start, stride, count):
    lane = lax.broadcasted_iota(jnp.int32, (1, LANES), 1)
    row = jnp.zeros((1, LANES), jnp.float32)
    for slot, value in enumerate(sums):
        width = LANES
        while width > LANES // SLOTS:
            width //= 2
            value = value + pltpu.roll(value, width, 1)
        row = jnp.where(lane // (LANES // SLOTS) == slot, value, row)
    out_ref[pl.ds(start, count, stride=stride), :] = jnp.broadcast_to(row, (count, LANES))


def totals_of(ref, start, stride, count):
    lanes = lane_sums(ref[pl.ds(start, count, stride=stride), :])
    lane = lax.broadcasted_iota(jnp.int32, (1, LANES), 1)
    return [
        jnp.sum(jnp.where(lane // (LANES // SLOTS) == slot, lanes, 0.0), axis=1, keepdims=True)
        for slot in range(SLOTS)
    ]


def scale_of(plan, squares):
    return jnp.sqrt(squares / plan.entries + epsilon)


def depart_kernel(plan, state_ref, out_ref, held_ref, semaphores):
    fetches = []
    for part in range(plan.parts):
        rows = pl.ds(part * plan.width, plan.width)
        fetches.append(pltpu.make_async_copy(state_ref.at[rows, :], held_ref.at[rows, :], semaphores.at[part]))
    for fetch in fetches:
        fetch.start()
    sums = jnp.zeros((1, LANES), jnp.float32)
    for block in range(plan.lane_blocks):
        if block * LANES % plan.width == 0:
            fetches[block * LANES // plan.width].wait()
        tile = held_ref[pl.ds(block * LANES, LANES), :]
        sums = sums + lane_sums(tile * tile)
        turned = tile.T
        for piece in range(plan.pieces):
            out_ref[pl.ds(piece * plan.lane_blocks + block, plan.groups, stride=plan.inward), :] = turned[
                piece * plan.groups : (piece + 1) * plan.groups
            ]
    put_sums(out_ref, [sums], plan.body, plan.inward, plan.groups)


def fetch_slabs(plan, slabs, bits_ref, operators_ref, held_ref, semaphores):
    fetches = []
    for index, slab in enumerate(slabs):
        part, bit = divmod(slab, plan.bits)
        rows = pl.ds(part * plan.width, plan.width)
        fetch = pltpu.make_async_copy(
            operators_ref.at[bits_ref[bit], rows, :], held_ref.at[index], semaphores.at[index]
        )
        fetch.start()
        fetches.append(fetch)
    return fetches


def mask_slab(plan, slab, index, bits_ref, mask_ref, held_ref, out_ref):
    part, bit = divmod(slab, plan.bits)
    chosen = bits_ref[bit]
    for start in range(0, plan.width, plan.edge):
        across = (part * plan.width + start) // plan.edge
        rows = pl.ds(start, plan.edge)
        for along in range(plan.blocks):
            columns = pl.ds(along * plan.edge, plan.edge)
            keep = (mask_ref[chosen, across, along] > 0).astype(jnp.float32).astype(jnp.bfloat16)
            out_ref[index, columns, rows] = (held_ref[index, rows, columns] * keep).T


def store_kernel(plan, bits_ref, mask_ref, operators_ref, stored_ref, held_ref, masked_ref, in_semaphores, out_semaphores):
    slabs = range(plan.kept, plan.slabs)
    fetches = fetch_slabs(plan, slabs, bits_ref, operators_ref, held_ref, in_semaphores)
    stores = []
    for index, slab in enumerate(slabs):
        fetches[index].wait()
        mask_slab(plan, slab, index, bits_ref, mask_ref, held_ref, masked_ref)
        store = pltpu.make_async_copy(masked_ref.at[index], stored_ref.at[index], out_semaphores.at[index])
        store.start()
        stores.append(store)
    for store in stores:
        store.wait()


def prepare_kernel(
    plan,
    bits_ref,
    mask_ref,
    field_ref,
    coupling_ref,
    mode_ref,
    operators_ref,
    place_ref,
    inside_ref,
    kept_ref,
    held_ref,
    semaphores,
):
    slabs = range(plan.kept)
    fetches = fetch_slabs(plan, slabs, bits_ref, operators_ref, held_ref, semaphores)
    me = lax.axis_index("site") * plan.phonons + lax.axis_index("phonon")
    place = lax.broadcasted_iota(jnp.int32, (plan.places, LANES), 0)
    phonon = place % plan.phonons
    site = place // plan.phonons % plan.sites
    mode = place // plan.groups % plan.share
    level = phonon * plan.levels_here + place // (plan.groups * plan.share)
    occupied = jnp.zeros((plan.places, LANES), jnp.float32)
    for position in range(plan.bits):
        held = (site >> position & 1).astype(jnp.float32)
        occupied = occupied + coupling_ref[bits_ref[position]] * held
    strength = jnp.zeros((plan.places, LANES), jnp.float32)
    for index in range(plan.share):
        strength = jnp.where(mode == index, mode_ref[index * plan.groups + me], strength)
    strength = strength / jnp.sqrt(jnp.full((1, LANES), plan.level_count, jnp.float32))
    height = level.astype(jnp.float32)
    place_ref[0] = occupied
    place_ref[1] = strength * jnp.sqrt(height)
    place_ref[2] = jnp.where(level == plan.level_count - 1, 0.0, strength * jnp.sqrt(height + 1.0))
    inside = lax.broadcasted_iota(jnp.int32, (1, plan.rows), 1)
    weight = jnp.zeros((1, plan.rows), jnp.float32)
    for local_bit in range(LBITS):
        weight = weight + coupling_ref[plan.bits + local_bit] * (inside >> local_bit & 1).astype(jnp.float32)
    inside_ref[...] = jnp.zeros_like(inside_ref)
    inside_ref[:1] = weight
    for position in range(plan.bits):
        inside_ref[pl.ds(1 + position, 1)] = jnp.full((1, plan.rows), field_ref[bits_ref[position]])
    for slab in slabs:
        fetches[slab].wait()
        mask_slab(plan, slab, slab, bits_ref, mask_ref, held_ref, kept_ref)


def flipped(values, stride):
    places, width = values.shape
    if stride % SUBLANES == 0:
        shaped = values.reshape(places // (2 * stride), 2, stride, width)
        return jnp.concatenate([shaped[:, 1:], shaped[:, :1]], axis=1).reshape(places, width)
    tiles = values.reshape(places // SUBLANES, SUBLANES, width)
    if 2 * stride == SUBLANES:
        return pltpu.roll(tiles, stride, 1).reshape(places, width)
    spot = lax.broadcasted_iota(jnp.int32, tiles.shape, 1)
    down = pltpu.roll(tiles, stride, 1)
    up = pltpu.roll(tiles, SUBLANES - stride, 1)
    return jnp.where(spot & stride > 0, down, up).reshape(places, width)


def shifted(values, by):
    places, width = values.shape
    tiles = values.reshape(places // SUBLANES, SUBLANES, width)
    return pltpu.roll(tiles, by % SUBLANES, 1).reshape(places, width)


def put_rounded(plan, rounded_ref, vector, start):
    for position in range(plan.bits):
        rounded_ref[:, pl.ds(position * plan.rows + start, vector.shape[1])] = flipped(
            vector, plan.phonons << position
        ).astype(jnp.bfloat16)


def step(plan, vector_ref, rounded_ref, kept_ref, fetched_ref, place_ref, inside_ref, finish, ready=None, begun_ref=None):
    span = plan.places // plan.levels_here

    def local(start):
        lanes = pl.ds(start, LANES)
        vector = vector_ref[:, lanes]
        levels = [vector[index * span : (index + 1) * span] for index in range(plan.levels_here)]
        lower = jnp.concatenate([shifted(levels[-1], 1)] + levels[:-1], axis=0)
        upper = jnp.concatenate(levels[1:] + [shifted(levels[0], -1)], axis=0)
        weight = place_ref[0] + inside_ref[:1, lanes]
        total = weight * (place_ref[1] * lower + place_ref[2] * upper)
        for position in range(plan.bits):
            total = total + inside_ref[pl.ds(1 + position, 1), lanes] * flipped(vector, plan.phonons << position)
        return total

    def added(total, part, late):
        for ref, low, high in ((kept_ref, 0, plan.kept), (fetched_ref, plan.kept, plan.slabs)):
            fetched = low > 0
            begin = max(part * plan.bits, low)
            count = min((part + 1) * plan.bits, high) - begin
            if count <= 0 or late not in (None, fetched):
                continue
            if late:
                for slab in range(begin, begin + count):
                    ready(slab)
            first = begin - part * plan.bits
            masked = ref[pl.ds(begin - low, count)].reshape(count * plan.rows, plan.width)
            operand = rounded_ref[:, pl.ds(first * plan.rows, count * plan.rows)]
            total = total + jnp.dot(operand, masked, preferred_element_type=jnp.float32)
        return total

    def locals_of(lanes):
        return jnp.concatenate([local(start) for start in range(lanes.start, lanes.start + plan.width, LANES)], axis=1)

    parts = [pl.ds(part * plan.width, plan.width) for part in range(plan.parts)]
    if ready is None:
        for part, lanes in enumerate(parts):
            finish(lanes, added(locals_of(lanes), part, None))
        return
    for part, lanes in enumerate(parts):
        begun_ref[:, lanes] = added(locals_of(lanes), part, False)
    for part, lanes in enumerate(parts):
        finish(lanes, added(begun_ref[:, lanes], part, True))


def first_kernel(
    plan,
    arrived_ref,
    place_ref,
    inside_ref,
    kept_ref,
    stored_ref,
    initial_ref,
    new_ref,
    sums_ref,
    fetched_ref,
    rounded_ref,
    ahead_ref,
    semaphores,
):
    fetches = {}
    for slab in range(plan.kept, plan.slabs):
        index = slab - plan.kept
        fetches[slab] = pltpu.make_async_copy(stored_ref.at[index], fetched_ref.at[index], semaphores.at[index])
        fetches[slab].start()

    def ready(slab):
        fetches[slab].wait()

    squares = totals_of(arrived_ref, plan.body, plan.inward, plan.groups)[0]
    inverse = 1.0 / scale_of(plan, squares)
    for block in range(plan.lane_blocks):
        parts = [
            arrived_ref[pl.ds(piece * plan.lane_blocks + block, plan.groups, stride=plan.inward), :]
            for piece in range(plan.pieces)
        ]
        vector = jnp.concatenate(parts, axis=0) * inverse
        initial_ref[:, pl.ds(block * LANES, LANES)] = vector
        put_rounded(plan, rounded_ref, vector, block * LANES)
    tables = (kept_ref, fetched_ref, place_ref, inside_ref)
    squares = []
    overlap = []
    ahead = []

    def finish(lanes, new):
        new_ref[:, lanes] = new
        put_rounded(plan, ahead_ref, new, lanes.start)
        squares.append(lane_sums(new * new))
        overlap.append(lane_sums(new * initial_ref[:, lanes]))

    def look_ahead(lanes, total):
        new = 2.0 * total - initial_ref[:, lanes]
        ahead.append(lane_sums(new * new))

    step(plan, initial_ref, rounded_ref, *tables, finish, ready, new_ref)
    step(plan, new_ref, ahead_ref, *tables, look_ahead)
    put_sums(sums_ref, [one_row(squares), one_row(overlap), one_row(ahead)], 0, 1, plan.groups)


def one_row(rows):
    total = sum(rows[1:], rows[0])
    return sum(total[:, start : start + LANES] for start in range(0, total.shape[1], LANES))


def onward_kernel(
    plan,
    arrived_ref,
    raw_ref,
    initial_ref,
    place_ref,
    inside_ref,
    kept_ref,
    fetched_ref,
    out_ref,
    known_ref,
    rounded_ref,
    ahead_ref,
    second_ref,
    third_ref,
):
    squares, overlap, ahead, _ = totals_of(arrived_ref, 0, 1, plan.groups)
    first = 1.0 / scale_of(plan, squares)
    estimate = scale_of(plan, ahead * first * first)
    second = 1.0 / estimate
    known_ref[:1, :] = jnp.broadcast_to(overlap * first / plan.entries, (1, LANES))
    known_ref[1:, :] = jnp.broadcast_to(estimate, (SUBLANES - 1, LANES))
    for block in range(plan.lane_blocks):
        lanes = pl.ds(block * LANES, LANES)
        vector = raw_ref[:, lanes] * first
        second_ref[:, lanes] = vector
        put_rounded(plan, rounded_ref, vector, block * LANES)
    tables = (kept_ref, fetched_ref, place_ref, inside_ref)
    sums = [[] for _ in range(SLOTS)]

    def send(vector, lanes, new):
        sums[2 * vector].append(lane_sums(new * new))
        sums[2 * vector + 1].append(lane_sums(new * initial_ref[:, lanes]))
        for start in range(0, plan.width, LANES):
            block = (lanes.start + start) // LANES
            for piece in range(plan.pieces):
                row = vector * plan.body + piece * plan.lane_blocks + block
                out_ref[pl.ds(row, plan.groups, stride=plan.outward), :] = new[
                    piece * plan.groups : (piece + 1) * plan.groups, start : start + LANES
                ]

    def finish_second(lanes, total):
        new = 2.0 * total - initial_ref[:, lanes] * first
        vector = new * second
        third_ref[:, lanes] = vector
        put_rounded(plan, ahead_ref, vector, lanes.start)
        send(0, lanes, new)

    def finish_third(lanes, total):
        send(1, lanes, 2.0 * total - second_ref[:, lanes] * second)

    step(plan, second_ref, rounded_ref, *tables, finish_second)
    step(plan, third_ref, ahead_ref, *tables, finish_third)
    put_sums(out_ref, [one_row(rows) for rows in sums], 2 * plan.body, plan.outward, plan.groups)


def arrive_kernel(plan, arrived_ref, known_ref, before_ref, last_ref, moments_ref, turned_ref, semaphore):
    before_squares, before_overlap, last_squares, last_overlap = totals_of(
        arrived_ref, 2 * plan.body, plan.outward, plan.groups
    )
    before = 1.0 / scale_of(plan, before_squares)
    back = known_ref[1:2, :1] * before
    last = back / scale_of(plan, last_squares * back * back)
    leave = pltpu.make_async_copy(turned_ref, before_ref, semaphore)
    for vector, (out_ref, factor) in enumerate(((turned_ref, before), (last_ref, last))):
        for block in range(plan.lane_blocks):
            first = vector * plan.body + block
            parts = [
                arrived_ref[pl.ds(first + piece * plan.lane_blocks, plan.groups, stride=plan.outward), :]
                for piece in range(plan.pieces)
            ]
            out_ref[pl.ds(block * LANES, LANES), :] = jnp.concatenate(parts, axis=0).T * factor
        if vector == 0:
            leave.start()
    moments_ref[0] = known_ref[0, 0]
    moments_ref[1] = (before_overlap * before / plan.entries)[0, 0]
    moments_ref[2] = (last_overlap * last / plan.entries)[0, 0]
    leave.wait()


def exchange(values, count):
    shaped = values.reshape(count, values.shape[0] // count, 1, LANES)
    return lax.all_to_all(shaped, AXES, 0, 0, tiled=True).reshape(values.shape)


def shards(plan, state, operators, op_mask, site_bits, field, site_coupling, mode_coupling):
    f32 = jnp.float32
    inward = jax.ShapeDtypeStruct((plan.groups * plan.inward, LANES), f32)
    outward = jax.ShapeDtypeStruct((plan.groups * plan.outward, LANES), f32)
    vector = jax.ShapeDtypeStruct((plan.places, plan.rows), f32)
    known = jax.ShapeDtypeStruct((SUBLANES, LANES), f32)
    held = jax.ShapeDtypeStruct((plan.rows, plan.columns), f32)
    rounded = pltpu.VMEM((plan.places, plan.bits * plan.rows), jnp.bfloat16)
    working = pltpu.VMEM((plan.places, plan.rows), f32)
    work = 2 * plan.bits * plan.places * plan.rows * plan.rows

    def cost(flops, moved):
        return pl.CostEstimate(flops=flops, bytes_accessed=moved, transcendentals=0)

    departing = pl.pallas_call(
        functools.partial(depart_kernel, plan),
        out_shape=inward,
        in_specs=[HBM],
        out_specs=VMEM,
        scratch_shapes=[pltpu.VMEM((plan.rows, plan.columns), f32), pltpu.SemaphoreType.DMA((plan.parts,))],
        compiler_params=params(60),
        name="depart",
    )(state)
    arrived = exchange(departing, plan.groups)
    fetched = plan.slabs - plan.kept
    kept_slabs = (plan.kept, plan.rows, plan.width)
    fetched_slabs = (fetched, plan.rows, plan.width)

    def held_slabs(count):
        return pltpu.VMEM((count, plan.width, plan.rows), jnp.bfloat16)

    place, inside, kept = pl.pallas_call(
        functools.partial(prepare_kernel, plan),
        out_shape=[
            jax.ShapeDtypeStruct((3, plan.places, LANES), f32),
            jax.ShapeDtypeStruct((SUBLANES, plan.rows), f32),
            jax.ShapeDtypeStruct(kept_slabs, jnp.bfloat16),
        ],
        in_specs=[SMEM] * 5 + [HBM],
        out_specs=[VMEM] * 3,
        scratch_shapes=[held_slabs(plan.kept), pltpu.SemaphoreType.DMA((plan.kept,))],
        compiler_params=params(50),
        cost_estimate=cost(plan.rows * plan.rows, 4 * plan.kept * plan.rows * plan.width),
        name="prepare",
    )(site_bits, op_mask, field, site_coupling, mode_coupling, operators)
    stored = pl.pallas_call(
        functools.partial(store_kernel, plan),
        out_shape=jax.ShapeDtypeStruct(fetched_slabs, jnp.bfloat16),
        in_specs=[SMEM] * 2 + [HBM],
        out_specs=HBM,
        scratch_shapes=[
            held_slabs(fetched),
            pltpu.VMEM(fetched_slabs, jnp.bfloat16),
            pltpu.SemaphoreType.DMA((fetched,)),
            pltpu.SemaphoreType.DMA((fetched,)),
        ],
        compiler_params=params(60),
        cost_estimate=cost(plan.rows * plan.rows, 4 * fetched * plan.rows * plan.width),
        name="store",
    )(site_bits, op_mask, operators)
    initial, raw, sums, late = pl.pallas_call(
        functools.partial(first_kernel, plan),
        out_shape=[
            vector,
            vector,
            jax.ShapeDtypeStruct((plan.groups, LANES), f32),
            jax.ShapeDtypeStruct(fetched_slabs, jnp.bfloat16),
        ],
        in_specs=[VMEM] * 4 + [HBM],
        out_specs=[VMEM] * 4,
        scratch_shapes=[rounded, rounded, pltpu.SemaphoreType.DMA((fetched,))],
        compiler_params=params(46),
        cost_estimate=cost(2 * work, 4 * plan.places * plan.rows),
        name="first",
    )(arrived, place, inside, kept, stored)
    tables = (place, inside, kept, late)
    sums = exchange(sums, plan.groups)
    departing, told = pl.pallas_call(
        functools.partial(onward_kernel, plan),
        out_shape=[outward, known],
        in_specs=[VMEM] * 7,
        out_specs=[VMEM] * 2,
        scratch_shapes=[rounded, rounded, working, working],
        compiler_params=params(32),
        cost_estimate=cost(2 * work, 8 * plan.places * plan.rows),
        name="onward",
    )(sums, raw, initial, *tables)
    arrived = exchange(departing, plan.groups)
    before, last, moments = pl.pallas_call(
        functools.partial(arrive_kernel, plan),
        out_shape=[held, held, jax.ShapeDtypeStruct((STEPS,), f32)],
        in_specs=[VMEM] * 2,
        out_specs=[HBM, VMEM, SMEM],
        scratch_shapes=[pltpu.VMEM((plan.rows, plan.columns), f32), pltpu.SemaphoreType.DMA],
        compiler_params=params(16),
        name="arrive",
    )(arrived, told)
    return last, before, moments


def extended_2(block, sides, width):
    for axis, dim in sides:
        count = lax.axis_size(axis)
        forward = [(i, i + 1) for i in range(count - 1)]
        backward = [(target, source) for source, target in forward]
        low = lax.ppermute(
            lax.slice_in_dim(block, block.shape[dim] - width, None, axis=dim), axis, forward
        )
        high = lax.ppermute(lax.slice_in_dim(block, 0, width, axis=dim), axis, backward)
        block = jnp.concatenate([low, block, high], axis=dim)
    return block


def partner(value, axis, bit):
    mask = 2**bit
    pairs = [(source, source ^ mask) for source in range(lax.axis_size(axis))]
    return lax.ppermute(value, axis, pairs)


def halo_shards(state, operators, op_mask, site_bits, field, site_coupling, mode_coupling):
    site_count = lax.axis_size("site")
    phonon_count = lax.axis_size("phonon")
    bit_count = site_count.bit_length() - 1
    rows_here = state.shape[0]
    columns_here = state.shape[1]
    levels_here = columns_here // MODES
    block_edge = rows_here // op_mask.shape[1]
    expanded = jnp.repeat(jnp.repeat(op_mask, block_edge, axis=1), block_edge, axis=2)
    masked = jnp.where(expanded > 0, operators, jnp.zeros((), jnp.bfloat16))
    entries = jnp.float32(rows_here * columns_here * site_count * phonon_count)
    level_total = jnp.sqrt(jnp.float32(levels_here * phonon_count))
    device = lax.axis_index("site")
    inside = lax.iota(jnp.int32, rows_here)
    weight_rows = jnp.zeros((rows_here,), jnp.float32)
    for position in range(bit_count):
        weight_rows = weight_rows + site_coupling[site_bits[position]] * (
            device >> position & 1
        ).astype(jnp.float32)
    for local_bit in range(LBITS):
        weight_rows = weight_rows + site_coupling[bit_count + local_bit] * (
            inside >> local_bit & 1
        ).astype(jnp.float32)
    levels = (
        lax.axis_index("phonon") * levels_here + lax.iota(jnp.int32, columns_here) // MODES
    ).astype(jnp.float32)
    lower_weight = jnp.sqrt(levels)
    upper_weight = jnp.sqrt(levels + 1.0)
    mode_weight = jnp.tile(mode_coupling, columns_here // MODES) / level_total
    start_squares = lax.psum(jnp.sum(state * state), ("site", "phonon"))
    initial = state / jnp.sqrt(start_squares / entries + epsilon)
    previous = initial
    current = initial
    scale_prev = jnp.float32(1.0)
    moments = []
    for iteration in range(STEPS):
        extended = extended_2(current, (("phonon", 1),), MODES)
        lower_part = extended[:, :columns_here]
        upper_part = extended[:, 2 * MODES :]
        summed = weight_rows[:, None] * (
            mode_weight * (lower_weight * lower_part + upper_weight * upper_part)
        )
        for operate_position in range(bit_count):
            chosen = site_bits[operate_position]
            flipped = partner(current, "site", operate_position)
            product = jnp.dot(
                masked[chosen], flipped.astype(jnp.bfloat16), preferred_element_type=jnp.float32
            )
            summed = summed + (field[chosen] * flipped + product)
        if iteration == 0:
            vector_new = summed
        else:
            vector_new = 2.0 * summed - previous / scale_prev
        squares, intersection = lax.psum(
            (jnp.sum(vector_new * vector_new), jnp.sum(initial * vector_new)), ("site", "phonon")
        )
        scale_now = jnp.sqrt(squares / entries + epsilon)
        updated = vector_new / scale_now
        moment = intersection / (entries * scale_now)
        moments.append(moment)
        previous = current
        current = updated
        scale_prev = scale_now
    return (current, previous, jnp.stack(moments))


def solution(mesh):
    in_specs = (P("site", "phonon"), P(), P(), P(), P(), P(), P())
    out_specs = (P("site", "phonon"), P("site", "phonon"), P())

    def whole(state, operators, op_mask, *rest):
        rows = state.shape[0] // mesh.shape["site"]
        columns = state.shape[1] // mesh.shape["phonon"]
        plan = Plan(mesh, rows, columns, op_mask.shape[1])
        body = functools.partial(shards, plan) if plan.fits() else halo_shards
        run = jax.shard_map(body, mesh=mesh, in_specs=in_specs, out_specs=out_specs, check_vma=False)
        return run(state, operators, op_mask, *rest)

    return whole
```

```python
import functools

import jax
import jax.numpy as jnp
from jax import lax
from jax.experimental import pallas as pl
from jax.experimental.pallas import tpu as pltpu
from jax.sharding import PartitionSpec as P

LBITS = 10
MODES = 64
STEPS = 3
LANES = 128
SUBLANES = 8
SLOTS = 4
AXES = ("site", "phonon")

epsilon = 1e-06


VMEM = pl.BlockSpec(memory_space=pltpu.VMEM)
SMEM = pl.BlockSpec(memory_space=pltpu.SMEM)
HBM = pl.BlockSpec(memory_space=pltpu.HBM)


class Plan:
    def __init__(self, mesh, rows, columns, blocks):
        self.sites = mesh.shape["site"]
        self.phonons = mesh.shape["phonon"]
        self.groups = self.sites * self.phonons
        self.bits = self.sites.bit_length() - 1
        self.rows = rows
        self.columns = columns
        self.blocks = blocks
        self.edge = rows // blocks
        self.levels_here = columns // MODES
        self.level_count = self.levels_here * self.phonons
        self.share = MODES // self.groups
        self.pieces = self.levels_here * self.share
        self.lane_blocks = rows // LANES
        self.body = self.pieces * self.lane_blocks
        self.inward = self.body + 1
        self.outward = 2 * self.body + 1
        self.places = self.pieces * self.groups
        self.width = 2 * LANES
        self.parts = rows // self.width
        self.slabs = self.bits * self.parts
        self.kept = min(5, self.slabs - 1)
        self.entries = float(rows * columns * self.groups)

    def fits(self):
        return (
            MODES % self.groups == 0
            and self.columns == LANES
            and self.rows % self.width == 0
            and self.edge % LANES == 0
            and self.width % self.edge == 0
            and self.bits < SUBLANES
            and self.groups % SUBLANES == 0
        )


def params(mib):
    return pltpu.CompilerParams(vmem_limit_bytes=mib * 2**20)


def lane_sums(values):
    return jnp.sum(values, axis=0, keepdims=True)


def put_sums(out_ref, sums, start, stride, count):
    lane = lax.broadcasted_iota(jnp.int32, (1, LANES), 1)
    row = jnp.zeros((1, LANES), jnp.float32)
    for slot, value in enumerate(sums):
        width = LANES
        while width > LANES // SLOTS:
            width //= 2
            value = value + pltpu.roll(value, width, 1)
        row = jnp.where(lane // (LANES // SLOTS) == slot, value, row)
    out_ref[pl.ds(start, count, stride=stride), :] = jnp.broadcast_to(row, (count, LANES))


def totals_of(ref, start, stride, count):
    lanes = lane_sums(ref[pl.ds(start, count, stride=stride), :])
    lane = lax.broadcasted_iota(jnp.int32, (1, LANES), 1)
    return [
        jnp.sum(jnp.where(lane // (LANES // SLOTS) == slot, lanes, 0.0), axis=1, keepdims=True)
        for slot in range(SLOTS)
    ]


def scale_of(plan, squares):
    return jnp.sqrt(squares / plan.entries + epsilon)


def depart_kernel(plan, state_ref, out_ref):
    sums = jnp.zeros((1, LANES), jnp.float32)
    for block in range(plan.lane_blocks):
        tile = state_ref[pl.ds(block * LANES, LANES), :]
        sums = sums + lane_sums(tile * tile)
        turned = tile.T
        for piece in range(plan.pieces):
            out_ref[pl.ds(piece * plan.lane_blocks + block, plan.groups, stride=plan.inward), :] = turned[
                piece * plan.groups : (piece + 1) * plan.groups
            ]
    put_sums(out_ref, [sums], plan.body, plan.inward, plan.groups)


def fetch_slabs(plan, slabs, bits_ref, operators_ref, held_ref, semaphores):
    fetches = []
    for index, slab in enumerate(slabs):
        part, bit = divmod(slab, plan.bits)
        rows = pl.ds(part * plan.width, plan.width)
        fetch = pltpu.make_async_copy(
            operators_ref.at[bits_ref[bit], rows, :], held_ref.at[index], semaphores.at[index]
        )
        fetch.start()
        fetches.append(fetch)
    return fetches


def mask_slab(plan, slab, index, bits_ref, mask_ref, held_ref, out_ref):
    part, bit = divmod(slab, plan.bits)
    chosen = bits_ref[bit]
    for start in range(0, plan.width, plan.edge):
        across = (part * plan.width + start) // plan.edge
        rows = pl.ds(start, plan.edge)
        for along in range(plan.blocks):
            columns = pl.ds(along * plan.edge, plan.edge)
            keep = (mask_ref[chosen, across, along] > 0).astype(jnp.float32).astype(jnp.bfloat16)
            out_ref[index, columns, rows] = (held_ref[index, rows, columns] * keep).T


def store_kernel(plan, bits_ref, mask_ref, operators_ref, stored_ref, held_ref, masked_ref, in_semaphores, out_semaphores):
    slabs = range(plan.kept, plan.slabs)
    fetches = fetch_slabs(plan, slabs, bits_ref, operators_ref, held_ref, in_semaphores)
    stores = []
    for index, slab in enumerate(slabs):
        fetches[index].wait()
        mask_slab(plan, slab, index, bits_ref, mask_ref, held_ref, masked_ref)
        store = pltpu.make_async_copy(masked_ref.at[index], stored_ref.at[index], out_semaphores.at[index])
        store.start()
        stores.append(store)
    for store in stores:
        store.wait()


def prepare_kernel(
    plan,
    bits_ref,
    mask_ref,
    field_ref,
    coupling_ref,
    mode_ref,
    operators_ref,
    place_ref,
    inside_ref,
    kept_ref,
    held_ref,
    semaphores,
):
    slabs = range(plan.kept)
    fetches = fetch_slabs(plan, slabs, bits_ref, operators_ref, held_ref, semaphores)
    me = lax.axis_index("site") * plan.phonons + lax.axis_index("phonon")
    place = lax.broadcasted_iota(jnp.int32, (plan.places, LANES), 0)
    phonon = place % plan.phonons
    site = place // plan.phonons % plan.sites
    mode = place // plan.groups % plan.share
    level = phonon * plan.levels_here + place // (plan.groups * plan.share)
    occupied = jnp.zeros((plan.places, LANES), jnp.float32)
    for position in range(plan.bits):
        held = (site >> position & 1).astype(jnp.float32)
        occupied = occupied + coupling_ref[bits_ref[position]] * held
    strength = jnp.zeros((plan.places, LANES), jnp.float32)
    for index in range(plan.share):
        strength = jnp.where(mode == index, mode_ref[index * plan.groups + me], strength)
    strength = strength / jnp.sqrt(jnp.full((1, LANES), plan.level_count, jnp.float32))
    height = level.astype(jnp.float32)
    place_ref[0] = occupied
    place_ref[1] = strength * jnp.sqrt(height)
    place_ref[2] = jnp.where(level == plan.level_count - 1, 0.0, strength * jnp.sqrt(height + 1.0))
    inside = lax.broadcasted_iota(jnp.int32, (1, plan.rows), 1)
    weight = jnp.zeros((1, plan.rows), jnp.float32)
    for local_bit in range(LBITS):
        weight = weight + coupling_ref[plan.bits + local_bit] * (inside >> local_bit & 1).astype(jnp.float32)
    inside_ref[...] = jnp.zeros_like(inside_ref)
    inside_ref[:1] = weight
    for position in range(plan.bits):
        inside_ref[pl.ds(1 + position, 1)] = jnp.full((1, plan.rows), field_ref[bits_ref[position]])
    for slab in slabs:
        fetches[slab].wait()
        mask_slab(plan, slab, slab, bits_ref, mask_ref, held_ref, kept_ref)


def flipped(values, stride):
    places, width = values.shape
    if stride % SUBLANES == 0:
        shaped = values.reshape(places // (2 * stride), 2, stride, width)
        return jnp.concatenate([shaped[:, 1:], shaped[:, :1]], axis=1).reshape(places, width)
    tiles = values.reshape(places // SUBLANES, SUBLANES, width)
    if 2 * stride == SUBLANES:
        return pltpu.roll(tiles, stride, 1).reshape(places, width)
    spot = lax.broadcasted_iota(jnp.int32, tiles.shape, 1)
    down = pltpu.roll(tiles, stride, 1)
    up = pltpu.roll(tiles, SUBLANES - stride, 1)
    return jnp.where(spot & stride > 0, down, up).reshape(places, width)


def shifted(values, by):
    places, width = values.shape
    tiles = values.reshape(places // SUBLANES, SUBLANES, width)
    return pltpu.roll(tiles, by % SUBLANES, 1).reshape(places, width)


def put_rounded(plan, rounded_ref, vector, start):
    for position in range(plan.bits):
        rounded_ref[:, pl.ds(position * plan.rows + start, vector.shape[1])] = flipped(
            vector, plan.phonons << position
        ).astype(jnp.bfloat16)


def step(plan, vector_ref, rounded_ref, kept_ref, fetched_ref, place_ref, inside_ref, finish, ready=None, begun_ref=None):
    span = plan.places // plan.levels_here

    def local(start):
        lanes = pl.ds(start, LANES)
        vector = vector_ref[:, lanes]
        levels = [vector[index * span : (index + 1) * span] for index in range(plan.levels_here)]
        lower = jnp.concatenate([shifted(levels[-1], 1)] + levels[:-1], axis=0)
        upper = jnp.concatenate(levels[1:] + [shifted(levels[0], -1)], axis=0)
        weight = place_ref[0] + inside_ref[:1, lanes]
        total = weight * (place_ref[1] * lower + place_ref[2] * upper)
        for position in range(plan.bits):
            total = total + inside_ref[pl.ds(1 + position, 1), lanes] * flipped(vector, plan.phonons << position)
        return total

    def added(total, part, late):
        for ref, low, high in ((kept_ref, 0, plan.kept), (fetched_ref, plan.kept, plan.slabs)):
            fetched = low > 0
            begin = max(part * plan.bits, low)
            count = min((part + 1) * plan.bits, high) - begin
            if count <= 0 or late not in (None, fetched):
                continue
            if late:
                for slab in range(begin, begin + count):
                    ready(slab)
            first = begin - part * plan.bits
            masked = ref[pl.ds(begin - low, count)].reshape(count * plan.rows, plan.width)
            operand = rounded_ref[:, pl.ds(first * plan.rows, count * plan.rows)]
            total = total + jnp.dot(operand, masked, preferred_element_type=jnp.float32)
        return total

    def locals_of(lanes):
        return jnp.concatenate([local(start) for start in range(lanes.start, lanes.start + plan.width, LANES)], axis=1)

    parts = [pl.ds(part * plan.width, plan.width) for part in range(plan.parts)]
    if ready is None:
        for part, lanes in enumerate(parts):
            finish(lanes, added(locals_of(lanes), part, None))
        return
    for part, lanes in enumerate(parts):
        begun_ref[:, lanes] = added(locals_of(lanes), part, False)
    for part, lanes in enumerate(parts):
        finish(lanes, added(begun_ref[:, lanes], part, True))


def first_kernel(
    plan,
    arrived_ref,
    place_ref,
    inside_ref,
    kept_ref,
    stored_ref,
    initial_ref,
    new_ref,
    sums_ref,
    fetched_ref,
    rounded_ref,
    ahead_ref,
    semaphores,
):
    fetches = {}
    for slab in range(plan.kept, plan.slabs):
        index = slab - plan.kept
        fetches[slab] = pltpu.make_async_copy(stored_ref.at[index], fetched_ref.at[index], semaphores.at[index])
        fetches[slab].start()

    def ready(slab):
        fetches[slab].wait()

    squares = totals_of(arrived_ref, plan.body, plan.inward, plan.groups)[0]
    inverse = 1.0 / scale_of(plan, squares)
    for block in range(plan.lane_blocks):
        parts = [
            arrived_ref[pl.ds(piece * plan.lane_blocks + block, plan.groups, stride=plan.inward), :]
            for piece in range(plan.pieces)
        ]
        vector = jnp.concatenate(parts, axis=0) * inverse
        initial_ref[:, pl.ds(block * LANES, LANES)] = vector
        put_rounded(plan, rounded_ref, vector, block * LANES)
    tables = (kept_ref, fetched_ref, place_ref, inside_ref)
    squares = []
    overlap = []
    ahead = []

    def finish(lanes, new):
        new_ref[:, lanes] = new
        put_rounded(plan, ahead_ref, new, lanes.start)
        squares.append(lane_sums(new * new))
        overlap.append(lane_sums(new * initial_ref[:, lanes]))

    def look_ahead(lanes, total):
        new = 2.0 * total - initial_ref[:, lanes]
        ahead.append(lane_sums(new * new))

    step(plan, initial_ref, rounded_ref, *tables, finish, ready, new_ref)
    step(plan, new_ref, ahead_ref, *tables, look_ahead)
    put_sums(sums_ref, [one_row(squares), one_row(overlap), one_row(ahead)], 0, 1, plan.groups)


def one_row(rows):
    total = sum(rows[1:], rows[0])
    return sum(total[:, start : start + LANES] for start in range(0, total.shape[1], LANES))


def onward_kernel(
    plan,
    arrived_ref,
    raw_ref,
    initial_ref,
    place_ref,
    inside_ref,
    kept_ref,
    fetched_ref,
    out_ref,
    known_ref,
    rounded_ref,
    ahead_ref,
    second_ref,
    third_ref,
):
    squares, overlap, ahead, _ = totals_of(arrived_ref, 0, 1, plan.groups)
    first = 1.0 / scale_of(plan, squares)
    estimate = scale_of(plan, ahead * first * first)
    second = 1.0 / estimate
    known_ref[:1, :] = jnp.broadcast_to(overlap * first / plan.entries, (1, LANES))
    known_ref[1:, :] = jnp.broadcast_to(estimate, (SUBLANES - 1, LANES))
    for block in range(plan.lane_blocks):
        lanes = pl.ds(block * LANES, LANES)
        vector = raw_ref[:, lanes] * first
        second_ref[:, lanes] = vector
        put_rounded(plan, rounded_ref, vector, block * LANES)
    tables = (kept_ref, fetched_ref, place_ref, inside_ref)
    sums = [[] for _ in range(SLOTS)]

    def send(vector, lanes, new):
        sums[2 * vector].append(lane_sums(new * new))
        sums[2 * vector + 1].append(lane_sums(new * initial_ref[:, lanes]))
        for start in range(0, plan.width, LANES):
            block = (lanes.start + start) // LANES
            for piece in range(plan.pieces):
                row = vector * plan.body + piece * plan.lane_blocks + block
                out_ref[pl.ds(row, plan.groups, stride=plan.outward), :] = new[
                    piece * plan.groups : (piece + 1) * plan.groups, start : start + LANES
                ]

    def finish_second(lanes, total):
        new = 2.0 * total - initial_ref[:, lanes] * first
        vector = new * second
        third_ref[:, lanes] = vector
        put_rounded(plan, ahead_ref, vector, lanes.start)
        send(0, lanes, new)

    def finish_third(lanes, total):
        send(1, lanes, 2.0 * total - second_ref[:, lanes] * second)

    step(plan, second_ref, rounded_ref, *tables, finish_second)
    step(plan, third_ref, ahead_ref, *tables, finish_third)
    put_sums(out_ref, [one_row(rows) for rows in sums], 2 * plan.body, plan.outward, plan.groups)


def arrive_kernel(plan, arrived_ref, known_ref, before_ref, last_ref, moments_ref):
    before_squares, before_overlap, last_squares, last_overlap = totals_of(
        arrived_ref, 2 * plan.body, plan.outward, plan.groups
    )
    before = 1.0 / scale_of(plan, before_squares)
    back = known_ref[1:2, :1] * before
    last = back / scale_of(plan, last_squares * back * back)
    for vector, (out_ref, factor) in enumerate(((before_ref, before), (last_ref, last))):
        for block in range(plan.lane_blocks):
            first = vector * plan.body + block
            parts = [
                arrived_ref[pl.ds(first + piece * plan.lane_blocks, plan.groups, stride=plan.outward), :]
                for piece in range(plan.pieces)
            ]
            out_ref[pl.ds(block * LANES, LANES), :] = jnp.concatenate(parts, axis=0).T * factor
    moments_ref[0] = known_ref[0, 0]
    moments_ref[1] = (before_overlap * before / plan.entries)[0, 0]
    moments_ref[2] = (last_overlap * last / plan.entries)[0, 0]


def exchange(values, count):
    shaped = values.reshape(count, values.shape[0] // count, 1, LANES)
    return lax.all_to_all(shaped, AXES, 0, 0, tiled=True).reshape(values.shape)


def shards(plan, state, operators, op_mask, site_bits, field, site_coupling, mode_coupling):
    f32 = jnp.float32
    inward = jax.ShapeDtypeStruct((plan.groups * plan.inward, LANES), f32)
    outward = jax.ShapeDtypeStruct((plan.groups * plan.outward, LANES), f32)
    vector = jax.ShapeDtypeStruct((plan.places, plan.rows), f32)
    known = jax.ShapeDtypeStruct((SUBLANES, LANES), f32)
    held = jax.ShapeDtypeStruct((plan.rows, plan.columns), f32)
    rounded = pltpu.VMEM((plan.places, plan.bits * plan.rows), jnp.bfloat16)
    working = pltpu.VMEM((plan.places, plan.rows), f32)
    work = 2 * plan.bits * plan.places * plan.rows * plan.rows

    def cost(flops, moved):
        return pl.CostEstimate(flops=flops, bytes_accessed=moved, transcendentals=0)

    near = [(source, source ^ 1) for source in range(plan.phonons)]
    field = lax.ppermute(field, "phonon", near)
    departing = pl.pallas_call(
        functools.partial(depart_kernel, plan),
        out_shape=inward,
        in_specs=[VMEM],
        out_specs=VMEM,
        compiler_params=params(60),
        name="depart",
    )(state)
    arrived = exchange(departing, plan.groups)
    fetched = plan.slabs - plan.kept
    kept_slabs = (plan.kept, plan.rows, plan.width)
    fetched_slabs = (fetched, plan.rows, plan.width)

    def held_slabs(count):
        return pltpu.VMEM((count, plan.width, plan.rows), jnp.bfloat16)

    place, inside, kept = pl.pallas_call(
        functools.partial(prepare_kernel, plan),
        out_shape=[
            jax.ShapeDtypeStruct((3, plan.places, LANES), f32),
            jax.ShapeDtypeStruct((SUBLANES, plan.rows), f32),
            jax.ShapeDtypeStruct(kept_slabs, jnp.bfloat16),
        ],
        in_specs=[SMEM] * 5 + [HBM],
        out_specs=[VMEM] * 3,
        scratch_shapes=[held_slabs(plan.kept), pltpu.SemaphoreType.DMA((plan.kept,))],
        compiler_params=params(50),
        cost_estimate=cost(plan.rows * plan.rows, 4 * plan.kept * plan.rows * plan.width),
        name="prepare",
    )(site_bits, op_mask, field, site_coupling, mode_coupling, operators)
    stored = pl.pallas_call(
        functools.partial(store_kernel, plan),
        out_shape=jax.ShapeDtypeStruct(fetched_slabs, jnp.bfloat16),
        in_specs=[SMEM] * 2 + [HBM],
        out_specs=HBM,
        scratch_shapes=[
            held_slabs(fetched),
            pltpu.VMEM(fetched_slabs, jnp.bfloat16),
            pltpu.SemaphoreType.DMA((fetched,)),
            pltpu.SemaphoreType.DMA((fetched,)),
        ],
        compiler_params=params(60),
        cost_estimate=cost(plan.rows * plan.rows, 4 * fetched * plan.rows * plan.width),
        name="store",
    )(site_bits, op_mask, operators)
    initial, raw, sums, late = pl.pallas_call(
        functools.partial(first_kernel, plan),
        out_shape=[
            vector,
            vector,
            jax.ShapeDtypeStruct((plan.groups, LANES), f32),
            jax.ShapeDtypeStruct(fetched_slabs, jnp.bfloat16),
        ],
        in_specs=[VMEM] * 4 + [HBM],
        out_specs=[VMEM] * 4,
        scratch_shapes=[rounded, rounded, pltpu.SemaphoreType.DMA((fetched,))],
        compiler_params=params(46),
        cost_estimate=cost(2 * work, 4 * plan.places * plan.rows),
        name="first",
    )(arrived, place, inside, kept, stored)
    tables = (place, inside, kept, late)
    sums = exchange(sums, plan.groups)
    departing, told = pl.pallas_call(
        functools.partial(onward_kernel, plan),
        out_shape=[outward, known],
        in_specs=[VMEM] * 7,
        out_specs=[VMEM] * 2,
        scratch_shapes=[rounded, rounded, working, working],
        compiler_params=params(32),
        cost_estimate=cost(2 * work, 8 * plan.places * plan.rows),
        name="onward",
    )(sums, raw, initial, *tables)
    arrived = exchange(departing, plan.groups)
    before, last, moments = pl.pallas_call(
        functools.partial(arrive_kernel, plan),
        out_shape=[held, held, jax.ShapeDtypeStruct((STEPS,), f32)],
        in_specs=[VMEM] * 2,
        out_specs=[VMEM, VMEM, SMEM],
        compiler_params=params(16),
        name="arrive",
    )(arrived, told)
    return last, before, moments


def extended_2(block, sides, width):
    for axis, dim in sides:
        count = lax.axis_size(axis)
        forward = [(i, i + 1) for i in range(count - 1)]
        backward = [(target, source) for source, target in forward]
        low = lax.ppermute(
            lax.slice_in_dim(block, block.shape[dim] - width, None, axis=dim), axis, forward
        )
        high = lax.ppermute(lax.slice_in_dim(block, 0, width, axis=dim), axis, backward)
        block = jnp.concatenate([low, block, high], axis=dim)
    return block


def partner(value, axis, bit):
    mask = 2**bit
    pairs = [(source, source ^ mask) for source in range(lax.axis_size(axis))]
    return lax.ppermute(value, axis, pairs)


def halo_shards(state, operators, op_mask, site_bits, field, site_coupling, mode_coupling):
    site_count = lax.axis_size("site")
    phonon_count = lax.axis_size("phonon")
    bit_count = site_count.bit_length() - 1
    rows_here = state.shape[0]
    columns_here = state.shape[1]
    levels_here = columns_here // MODES
    block_edge = rows_here // op_mask.shape[1]
    expanded = jnp.repeat(jnp.repeat(op_mask, block_edge, axis=1), block_edge, axis=2)
    masked = jnp.where(expanded > 0, operators, jnp.zeros((), jnp.bfloat16))
    entries = jnp.float32(rows_here * columns_here * site_count * phonon_count)
    level_total = jnp.sqrt(jnp.float32(levels_here * phonon_count))
    device = lax.axis_index("site")
    inside = lax.iota(jnp.int32, rows_here)
    weight_rows = jnp.zeros((rows_here,), jnp.float32)
    for position in range(bit_count):
        weight_rows = weight_rows + site_coupling[site_bits[position]] * (
            device >> position & 1
        ).astype(jnp.float32)
    for local_bit in range(LBITS):
        weight_rows = weight_rows + site_coupling[bit_count + local_bit] * (
            inside >> local_bit & 1
        ).astype(jnp.float32)
    levels = (
        lax.axis_index("phonon") * levels_here + lax.iota(jnp.int32, columns_here) // MODES
    ).astype(jnp.float32)
    lower_weight = jnp.sqrt(levels)
    upper_weight = jnp.sqrt(levels + 1.0)
    mode_weight = jnp.tile(mode_coupling, columns_here // MODES) / level_total
    start_squares = lax.psum(jnp.sum(state * state), ("site", "phonon"))
    initial = state / jnp.sqrt(start_squares / entries + epsilon)
    previous = initial
    current = initial
    scale_prev = jnp.float32(1.0)
    moments = []
    for iteration in range(STEPS):
        extended = extended_2(current, (("phonon", 1),), MODES)
        lower_part = extended[:, :columns_here]
        upper_part = extended[:, 2 * MODES :]
        summed = weight_rows[:, None] * (
            mode_weight * (lower_weight * lower_part + upper_weight * upper_part)
        )
        for operate_position in range(bit_count):
            chosen = site_bits[operate_position]
            flipped = partner(current, "site", operate_position)
            product = jnp.dot(
                masked[chosen], flipped.astype(jnp.bfloat16), preferred_element_type=jnp.float32
            )
            summed = summed + (field[chosen] * flipped + product)
        if iteration == 0:
            vector_new = summed
        else:
            vector_new = 2.0 * summed - previous / scale_prev
        squares, intersection = lax.psum(
            (jnp.sum(vector_new * vector_new), jnp.sum(initial * vector_new)), ("site", "phonon")
        )
        scale_now = jnp.sqrt(squares / entries + epsilon)
        updated = vector_new / scale_now
        moment = intersection / (entries * scale_now)
        moments.append(moment)
        previous = current
        current = updated
        scale_prev = scale_now
    return (current, previous, jnp.stack(moments))


def solution(mesh):
    in_specs = (P("site", "phonon"), P(), P(), P(), P(), P(), P())
    out_specs = (P("site", "phonon"), P("site", "phonon"), P())

    def whole(state, operators, op_mask, *rest):
        rows = state.shape[0] // mesh.shape["site"]
        columns = state.shape[1] // mesh.shape["phonon"]
        plan = Plan(mesh, rows, columns, op_mask.shape[1])
        body = functools.partial(shards, plan) if plan.fits() else halo_shards
        run = jax.shard_map(body, mesh=mesh, in_specs=in_specs, out_specs=out_specs, check_vma=False)
        return run(state, operators, op_mask, *rest)

    return whole
```

```python
import functools

import jax
import jax.numpy as jnp
from jax import lax
from jax.experimental import pallas as pl
from jax.experimental.pallas import tpu as pltpu
from jax.sharding import PartitionSpec as P

LBITS = 10
MODES = 64
STEPS = 3
LANES = 128
SUBLANES = 8
SLOTS = 4
AXES = ("site", "phonon")

epsilon = 1e-06


VMEM = pl.BlockSpec(memory_space=pltpu.VMEM)
SMEM = pl.BlockSpec(memory_space=pltpu.SMEM)
HBM = pl.BlockSpec(memory_space=pltpu.HBM)


class Plan:
    def __init__(self, mesh, rows, columns, blocks):
        self.sites = mesh.shape["site"]
        self.phonons = mesh.shape["phonon"]
        self.groups = self.sites * self.phonons
        self.bits = self.sites.bit_length() - 1
        self.rows = rows
        self.columns = columns
        self.blocks = blocks
        self.edge = rows // blocks
        self.levels_here = columns // MODES
        self.level_count = self.levels_here * self.phonons
        self.share = MODES // self.groups
        self.pieces = self.levels_here * self.share
        self.lane_blocks = rows // LANES
        self.body = self.pieces * self.lane_blocks
        self.inward = self.body + 1
        self.outward = 2 * self.body + 1
        self.places = self.pieces * self.groups
        self.width = 2 * LANES
        self.parts = rows // self.width
        self.slabs = self.bits * self.parts
        self.kept = min(5, self.slabs - 1)
        self.entries = float(rows * columns * self.groups)

    def fits(self):
        return (
            MODES % self.groups == 0
            and self.columns == LANES
            and self.rows % self.width == 0
            and self.edge % LANES == 0
            and self.width % self.edge == 0
            and self.bits < SUBLANES
            and self.groups % SUBLANES == 0
        )


def params(mib):
    return pltpu.CompilerParams(vmem_limit_bytes=mib * 2**20)


def lane_sums(values):
    return jnp.sum(values, axis=0, keepdims=True)


def put_sums(out_ref, sums, start, stride, count):
    lane = lax.broadcasted_iota(jnp.int32, (1, LANES), 1)
    row = jnp.zeros((1, LANES), jnp.float32)
    for slot, value in enumerate(sums):
        width = LANES
        while width > LANES // SLOTS:
            width //= 2
            value = value + pltpu.roll(value, width, 1)
        row = jnp.where(lane // (LANES // SLOTS) == slot, value, row)
    out_ref[pl.ds(start, count, stride=stride), :] = jnp.broadcast_to(row, (count, LANES))


def totals_of(ref, start, stride, count):
    lanes = lane_sums(ref[pl.ds(start, count, stride=stride), :])
    lane = lax.broadcasted_iota(jnp.int32, (1, LANES), 1)
    return [
        jnp.sum(jnp.where(lane // (LANES // SLOTS) == slot, lanes, 0.0), axis=1, keepdims=True)
        for slot in range(SLOTS)
    ]


def scale_of(plan, squares):
    return jnp.sqrt(squares / plan.entries + epsilon)


def depart_kernel(plan, state_ref, out_ref, held_ref, semaphores):
    half = plan.rows // 2
    fetches = [
        pltpu.make_async_copy(
            state_ref.at[pl.ds(index * half, half), :], held_ref.at[pl.ds(index * half, half), :], semaphores.at[index]
        )
        for index in range(2)
    ]
    for fetch in fetches:
        fetch.start()
    sums = jnp.zeros((1, LANES), jnp.float32)
    for block in range(plan.lane_blocks):
        if block * LANES % half == 0:
            fetches[block * LANES // half].wait()
        tile = held_ref[pl.ds(block * LANES, LANES), :]
        sums = sums + lane_sums(tile * tile)
        turned = tile.T
        for piece in range(plan.pieces):
            out_ref[pl.ds(piece * plan.lane_blocks + block, plan.groups, stride=plan.inward), :] = turned[
                piece * plan.groups : (piece + 1) * plan.groups
            ]
    put_sums(out_ref, [sums], plan.body, plan.inward, plan.groups)


def fetch_slabs(plan, slabs, bits_ref, operators_ref, held_ref, semaphores):
    fetches = []
    for index, slab in enumerate(slabs):
        part, bit = divmod(slab, plan.bits)
        rows = pl.ds(part * plan.width, plan.width)
        fetch = pltpu.make_async_copy(
            operators_ref.at[bits_ref[bit], rows, :], held_ref.at[index], semaphores.at[index]
        )
        fetch.start()
        fetches.append(fetch)
    return fetches


def mask_slab(plan, slab, index, bits_ref, mask_ref, held_ref, out_ref):
    part, bit = divmod(slab, plan.bits)
    chosen = bits_ref[bit]
    for start in range(0, plan.width, plan.edge):
        across = (part * plan.width + start) // plan.edge
        rows = pl.ds(start, plan.edge)
        for along in range(plan.blocks):
            columns = pl.ds(along * plan.edge, plan.edge)
            keep = (mask_ref[chosen, across, along] > 0).astype(jnp.float32).astype(jnp.bfloat16)
            out_ref[index, columns, rows] = (held_ref[index, rows, columns] * keep).T


def store_kernel(plan, bits_ref, mask_ref, operators_ref, stored_ref, held_ref, masked_ref, in_semaphores, out_semaphores):
    slabs = range(plan.kept, plan.slabs)
    fetches = fetch_slabs(plan, slabs, bits_ref, operators_ref, held_ref, in_semaphores)
    stores = []
    for index, slab in enumerate(slabs):
        fetches[index].wait()
        mask_slab(plan, slab, index, bits_ref, mask_ref, held_ref, masked_ref)
        store = pltpu.make_async_copy(masked_ref.at[index], stored_ref.at[index], out_semaphores.at[index])
        store.start()
        stores.append(store)
    for store in stores:
        store.wait()


def prepare_kernel(
    plan,
    bits_ref,
    mask_ref,
    field_ref,
    coupling_ref,
    mode_ref,
    operators_ref,
    place_ref,
    inside_ref,
    kept_ref,
    held_ref,
    semaphores,
):
    slabs = range(plan.kept)
    fetches = fetch_slabs(plan, slabs, bits_ref, operators_ref, held_ref, semaphores)
    me = lax.axis_index("site") * plan.phonons + lax.axis_index("phonon")
    place = lax.broadcasted_iota(jnp.int32, (plan.places, LANES), 0)
    phonon = place % plan.phonons
    site = place // plan.phonons % plan.sites
    mode = place // plan.groups % plan.share
    level = phonon * plan.levels_here + place // (plan.groups * plan.share)
    occupied = jnp.zeros((plan.places, LANES), jnp.float32)
    for position in range(plan.bits):
        held = (site >> position & 1).astype(jnp.float32)
        occupied = occupied + coupling_ref[bits_ref[position]] * held
    strength = jnp.zeros((plan.places, LANES), jnp.float32)
    for index in range(plan.share):
        strength = jnp.where(mode == index, mode_ref[index * plan.groups + me], strength)
    strength = strength / jnp.sqrt(jnp.full((1, LANES), plan.level_count, jnp.float32))
    height = level.astype(jnp.float32)
    place_ref[0] = occupied
    place_ref[1] = strength * jnp.sqrt(height)
    place_ref[2] = jnp.where(level == plan.level_count - 1, 0.0, strength * jnp.sqrt(height + 1.0))
    inside = lax.broadcasted_iota(jnp.int32, (1, plan.rows), 1)
    weight = jnp.zeros((1, plan.rows), jnp.float32)
    for local_bit in range(LBITS):
        weight = weight + coupling_ref[plan.bits + local_bit] * (inside >> local_bit & 1).astype(jnp.float32)
    inside_ref[...] = jnp.zeros_like(inside_ref)
    inside_ref[:1] = weight
    for position in range(plan.bits):
        inside_ref[pl.ds(1 + position, 1)] = jnp.full((1, plan.rows), field_ref[bits_ref[position]])
    for slab in slabs:
        fetches[slab].wait()
        mask_slab(plan, slab, slab, bits_ref, mask_ref, held_ref, kept_ref)


def flipped(values, stride):
    places, width = values.shape
    if stride % SUBLANES == 0:
        shaped = values.reshape(places // (2 * stride), 2, stride, width)
        return jnp.concatenate([shaped[:, 1:], shaped[:, :1]], axis=1).reshape(places, width)
    tiles = values.reshape(places // SUBLANES, SUBLANES, width)
    if 2 * stride == SUBLANES:
        return pltpu.roll(tiles, stride, 1).reshape(places, width)
    spot = lax.broadcasted_iota(jnp.int32, tiles.shape, 1)
    down = pltpu.roll(tiles, stride, 1)
    up = pltpu.roll(tiles, SUBLANES - stride, 1)
    return jnp.where(spot & stride > 0, down, up).reshape(places, width)


def shifted(values, by):
    places, width = values.shape
    tiles = values.reshape(places // SUBLANES, SUBLANES, width)
    return pltpu.roll(tiles, by % SUBLANES, 1).reshape(places, width)


def put_rounded(plan, rounded_ref, vector, start):
    for position in range(plan.bits):
        rounded_ref[:, pl.ds(position * plan.rows + start, vector.shape[1])] = flipped(
            vector, plan.phonons << position
        ).astype(jnp.bfloat16)


def step(plan, vector_ref, rounded_ref, kept_ref, fetched_ref, place_ref, inside_ref, finish, ready=None, begun_ref=None):
    span = plan.places // plan.levels_here

    def local(start):
        lanes = pl.ds(start, LANES)
        vector = vector_ref[:, lanes]
        levels = [vector[index * span : (index + 1) * span] for index in range(plan.levels_here)]
        lower = jnp.concatenate([shifted(levels[-1], 1)] + levels[:-1], axis=0)
        upper = jnp.concatenate(levels[1:] + [shifted(levels[0], -1)], axis=0)
        weight = place_ref[0] + inside_ref[:1, lanes]
        total = weight * (place_ref[1] * lower + place_ref[2] * upper)
        for position in range(plan.bits):
            total = total + inside_ref[pl.ds(1 + position, 1), lanes] * flipped(vector, plan.phonons << position)
        return total

    def added(total, part, late):
        for ref, low, high in ((kept_ref, 0, plan.kept), (fetched_ref, plan.kept, plan.slabs)):
            fetched = low > 0
            begin = max(part * plan.bits, low)
            count = min((part + 1) * plan.bits, high) - begin
            if count <= 0 or late not in (None, fetched):
                continue
            if late:
                for slab in range(begin, begin + count):
                    ready(slab)
            first = begin - part * plan.bits
            masked = ref[pl.ds(begin - low, count)].reshape(count * plan.rows, plan.width)
            operand = rounded_ref[:, pl.ds(first * plan.rows, count * plan.rows)]
            total = total + jnp.dot(operand, masked, preferred_element_type=jnp.float32)
        return total

    def locals_of(lanes):
        return jnp.concatenate([local(start) for start in range(lanes.start, lanes.start + plan.width, LANES)], axis=1)

    parts = [pl.ds(part * plan.width, plan.width) for part in range(plan.parts)]
    if ready is None:
        for part, lanes in enumerate(parts):
            finish(lanes, added(locals_of(lanes), part, None))
        return
    for part, lanes in enumerate(parts):
        begun_ref[:, lanes] = added(locals_of(lanes), part, False)
    for part, lanes in enumerate(parts):
        finish(lanes, added(begun_ref[:, lanes], part, True))


def first_kernel(
    plan,
    arrived_ref,
    place_ref,
    inside_ref,
    kept_ref,
    stored_ref,
    initial_ref,
    new_ref,
    sums_ref,
    fetched_ref,
    rounded_ref,
    ahead_ref,
    semaphores,
):
    fetches = {}
    for slab in range(plan.kept, plan.slabs):
        index = slab - plan.kept
        fetches[slab] = []
        for half in range(2):
            rows = pl.ds(half * (plan.rows // 2), plan.rows // 2)
            fetch = pltpu.make_async_copy(
                stored_ref.at[index, rows, :], fetched_ref.at[index, rows, :], semaphores.at[index, half]
            )
            fetch.start()
            fetches[slab].append(fetch)

    def ready(slab):
        for fetch in fetches[slab]:
            fetch.wait()

    squares = totals_of(arrived_ref, plan.body, plan.inward, plan.groups)[0]
    inverse = 1.0 / scale_of(plan, squares)
    for block in range(plan.lane_blocks):
        parts = [
            arrived_ref[pl.ds(piece * plan.lane_blocks + block, plan.groups, stride=plan.inward), :]
            for piece in range(plan.pieces)
        ]
        vector = jnp.concatenate(parts, axis=0) * inverse
        initial_ref[:, pl.ds(block * LANES, LANES)] = vector
        put_rounded(plan, rounded_ref, vector, block * LANES)
    tables = (kept_ref, fetched_ref, place_ref, inside_ref)
    squares = []
    overlap = []
    ahead = []

    def finish(lanes, new):
        new_ref[:, lanes] = new
        put_rounded(plan, ahead_ref, new, lanes.start)
        squares.append(lane_sums(new * new))
        overlap.append(lane_sums(new * initial_ref[:, lanes]))

    def look_ahead(lanes, total):
        new = 2.0 * total - initial_ref[:, lanes]
        ahead.append(lane_sums(new * new))

    step(plan, initial_ref, rounded_ref, *tables, finish, ready, new_ref)
    step(plan, new_ref, ahead_ref, *tables, look_ahead)
    put_sums(sums_ref, [one_row(squares), one_row(overlap), one_row(ahead)], 0, 1, plan.groups)


def one_row(rows):
    total = sum(rows[1:], rows[0])
    return sum(total[:, start : start + LANES] for start in range(0, total.shape[1], LANES))


def onward_kernel(
    plan,
    arrived_ref,
    raw_ref,
    initial_ref,
    place_ref,
    inside_ref,
    kept_ref,
    fetched_ref,
    out_ref,
    known_ref,
    rounded_ref,
    ahead_ref,
    second_ref,
    third_ref,
):
    squares, overlap, ahead, _ = totals_of(arrived_ref, 0, 1, plan.groups)
    first = 1.0 / scale_of(plan, squares)
    estimate = scale_of(plan, ahead * first * first)
    second = 1.0 / estimate
    known_ref[:1, :] = jnp.broadcast_to(overlap * first / plan.entries, (1, LANES))
    known_ref[1:, :] = jnp.broadcast_to(estimate, (SUBLANES - 1, LANES))
    for block in range(plan.lane_blocks):
        lanes = pl.ds(block * LANES, LANES)
        vector = raw_ref[:, lanes] * first
        second_ref[:, lanes] = vector
        put_rounded(plan, rounded_ref, vector, block * LANES)
    tables = (kept_ref, fetched_ref, place_ref, inside_ref)
    sums = [[] for _ in range(SLOTS)]

    def send(vector, lanes, new):
        sums[2 * vector].append(lane_sums(new * new))
        sums[2 * vector + 1].append(lane_sums(new * initial_ref[:, lanes]))
        for start in range(0, plan.width, LANES):
            block = (lanes.start + start) // LANES
            for piece in range(plan.pieces):
                row = vector * plan.body + piece * plan.lane_blocks + block
                out_ref[pl.ds(row, plan.groups, stride=plan.outward), :] = new[
                    piece * plan.groups : (piece + 1) * plan.groups, start : start + LANES
                ]

    def finish_second(lanes, total):
        new = 2.0 * total - initial_ref[:, lanes] * first
        vector = new * second
        third_ref[:, lanes] = vector
        put_rounded(plan, ahead_ref, vector, lanes.start)
        send(0, lanes, new)

    def finish_third(lanes, total):
        send(1, lanes, 2.0 * total - second_ref[:, lanes] * second)

    step(plan, second_ref, rounded_ref, *tables, finish_second)
    step(plan, third_ref, ahead_ref, *tables, finish_third)
    put_sums(out_ref, [one_row(rows) for rows in sums], 2 * plan.body, plan.outward, plan.groups)


def arrive_kernel(plan, arrived_ref, known_ref, before_ref, last_ref, moments_ref):
    before_squares, before_overlap, last_squares, last_overlap = totals_of(
        arrived_ref, 2 * plan.body, plan.outward, plan.groups
    )
    before = 1.0 / scale_of(plan, before_squares)
    back = known_ref[1:2, :1] * before
    last = back / scale_of(plan, last_squares * back * back)
    for vector, (out_ref, factor) in enumerate(((before_ref, before), (last_ref, last))):
        for block in range(plan.lane_blocks):
            first = vector * plan.body + block
            parts = [
                arrived_ref[pl.ds(first + piece * plan.lane_blocks, plan.groups, stride=plan.outward), :]
                for piece in range(plan.pieces)
            ]
            out_ref[pl.ds(block * LANES, LANES), :] = jnp.concatenate(parts, axis=0).T * factor
    moments_ref[0] = known_ref[0, 0]
    moments_ref[1] = (before_overlap * before / plan.entries)[0, 0]
    moments_ref[2] = (last_overlap * last / plan.entries)[0, 0]


def exchange(values, count):
    shaped = values.reshape(count, values.shape[0] // count, 1, LANES)
    return lax.all_to_all(shaped, AXES, 0, 0, tiled=True).reshape(values.shape)


def shards(plan, state, operators, op_mask, site_bits, field, site_coupling, mode_coupling):
    f32 = jnp.float32
    inward = jax.ShapeDtypeStruct((plan.groups * plan.inward, LANES), f32)
    outward = jax.ShapeDtypeStruct((plan.groups * plan.outward, LANES), f32)
    vector = jax.ShapeDtypeStruct((plan.places, plan.rows), f32)
    known = jax.ShapeDtypeStruct((SUBLANES, LANES), f32)
    held = jax.ShapeDtypeStruct((plan.rows, plan.columns), f32)
    rounded = pltpu.VMEM((plan.places, plan.bits * plan.rows), jnp.bfloat16)
    working = pltpu.VMEM((plan.places, plan.rows), f32)
    work = 2 * plan.bits * plan.places * plan.rows * plan.rows

    def cost(flops, moved):
        return pl.CostEstimate(flops=flops, bytes_accessed=moved, transcendentals=0)

    departing = pl.pallas_call(
        functools.partial(depart_kernel, plan),
        out_shape=inward,
        in_specs=[HBM],
        out_specs=VMEM,
        scratch_shapes=[pltpu.VMEM((plan.rows, plan.columns), f32), pltpu.SemaphoreType.DMA((2,))],
        compiler_params=params(60),
        name="depart",
    )(state)
    arrived = exchange(departing, plan.groups)
    fetched = plan.slabs - plan.kept
    kept_slabs = (plan.kept, plan.rows, plan.width)
    fetched_slabs = (fetched, plan.rows, plan.width)

    def held_slabs(count):
        return pltpu.VMEM((count, plan.width, plan.rows), jnp.bfloat16)

    place, inside, kept = pl.pallas_call(
        functools.partial(prepare_kernel, plan),
        out_shape=[
            jax.ShapeDtypeStruct((3, plan.places, LANES), f32),
            jax.ShapeDtypeStruct((SUBLANES, plan.rows), f32),
            jax.ShapeDtypeStruct(kept_slabs, jnp.bfloat16),
        ],
        in_specs=[SMEM] * 5 + [HBM],
        out_specs=[VMEM] * 3,
        scratch_shapes=[held_slabs(plan.kept), pltpu.SemaphoreType.DMA((plan.kept,))],
        compiler_params=params(50),
        cost_estimate=cost(plan.rows * plan.rows, 4 * plan.kept * plan.rows * plan.width),
        name="prepare",
    )(site_bits, op_mask, field, site_coupling, mode_coupling, operators)
    stored = pl.pallas_call(
        functools.partial(store_kernel, plan),
        out_shape=jax.ShapeDtypeStruct(fetched_slabs, jnp.bfloat16),
        in_specs=[SMEM] * 2 + [HBM],
        out_specs=HBM,
        scratch_shapes=[
            held_slabs(fetched),
            pltpu.VMEM(fetched_slabs, jnp.bfloat16),
            pltpu.SemaphoreType.DMA((fetched,)),
            pltpu.SemaphoreType.DMA((fetched,)),
        ],
        compiler_params=params(60),
        cost_estimate=cost(plan.rows * plan.rows, 4 * fetched * plan.rows * plan.width),
        name="store",
    )(site_bits, op_mask, operators)
    initial, raw, sums, late = pl.pallas_call(
        functools.partial(first_kernel, plan),
        out_shape=[
            vector,
            vector,
            jax.ShapeDtypeStruct((plan.groups, LANES), f32),
            jax.ShapeDtypeStruct(fetched_slabs, jnp.bfloat16),
        ],
        in_specs=[VMEM] * 4 + [HBM],
        out_specs=[VMEM] * 4,
        scratch_shapes=[rounded, rounded, pltpu.SemaphoreType.DMA((fetched, 2))],
        compiler_params=params(46),
        cost_estimate=cost(2 * work, 4 * plan.places * plan.rows),
        name="first",
    )(arrived, place, inside, kept, stored)
    tables = (place, inside, kept, late)
    sums = exchange(sums, plan.groups)
    departing, told = pl.pallas_call(
        functools.partial(onward_kernel, plan),
        out_shape=[outward, known],
        in_specs=[VMEM] * 7,
        out_specs=[VMEM] * 2,
        scratch_shapes=[rounded, rounded, working, working],
        compiler_params=params(32),
        cost_estimate=cost(2 * work, 8 * plan.places * plan.rows),
        name="onward",
    )(sums, raw, initial, *tables)
    arrived = exchange(departing, plan.groups)
    before, last, moments = pl.pallas_call(
        functools.partial(arrive_kernel, plan),
        out_shape=[held, held, jax.ShapeDtypeStruct((STEPS,), f32)],
        in_specs=[VMEM] * 2,
        out_specs=[VMEM, VMEM, SMEM],
        compiler_params=params(16),
        name="arrive",
    )(arrived, told)
    return last, before, moments


def extended_2(block, sides, width):
    for axis, dim in sides:
        count = lax.axis_size(axis)
        forward = [(i, i + 1) for i in range(count - 1)]
        backward = [(target, source) for source, target in forward]
        low = lax.ppermute(
            lax.slice_in_dim(block, block.shape[dim] - width, None, axis=dim), axis, forward
        )
        high = lax.ppermute(lax.slice_in_dim(block, 0, width, axis=dim), axis, backward)
        block = jnp.concatenate([low, block, high], axis=dim)
    return block


def partner(value, axis, bit):
    mask = 2**bit
    pairs = [(source, source ^ mask) for source in range(lax.axis_size(axis))]
    return lax.ppermute(value, axis, pairs)


def halo_shards(state, operators, op_mask, site_bits, field, site_coupling, mode_coupling):
    site_count = lax.axis_size("site")
    phonon_count = lax.axis_size("phonon")
    bit_count = site_count.bit_length() - 1
    rows_here = state.shape[0]
    columns_here = state.shape[1]
    levels_here = columns_here // MODES
    block_edge = rows_here // op_mask.shape[1]
    expanded = jnp.repeat(jnp.repeat(op_mask, block_edge, axis=1), block_edge, axis=2)
    masked = jnp.where(expanded > 0, operators, jnp.zeros((), jnp.bfloat16))
    entries = jnp.float32(rows_here * columns_here * site_count * phonon_count)
    level_total = jnp.sqrt(jnp.float32(levels_here * phonon_count))
    device = lax.axis_index("site")
    inside = lax.iota(jnp.int32, rows_here)
    weight_rows = jnp.zeros((rows_here,), jnp.float32)
    for position in range(bit_count):
        weight_rows = weight_rows + site_coupling[site_bits[position]] * (
            device >> position & 1
        ).astype(jnp.float32)
    for local_bit in range(LBITS):
        weight_rows = weight_rows + site_coupling[bit_count + local_bit] * (
            inside >> local_bit & 1
        ).astype(jnp.float32)
    levels = (
        lax.axis_index("phonon") * levels_here + lax.iota(jnp.int32, columns_here) // MODES
    ).astype(jnp.float32)
    lower_weight = jnp.sqrt(levels)
    upper_weight = jnp.sqrt(levels + 1.0)
    mode_weight = jnp.tile(mode_coupling, columns_here // MODES) / level_total
    start_squares = lax.psum(jnp.sum(state * state), ("site", "phonon"))
    initial = state / jnp.sqrt(start_squares / entries + epsilon)
    previous = initial
    current = initial
    scale_prev = jnp.float32(1.0)
    moments = []
    for iteration in range(STEPS):
        extended = extended_2(current, (("phonon", 1),), MODES)
        lower_part = extended[:, :columns_here]
        upper_part = extended[:, 2 * MODES :]
        summed = weight_rows[:, None] * (
            mode_weight * (lower_weight * lower_part + upper_weight * upper_part)
        )
        for operate_position in range(bit_count):
            chosen = site_bits[operate_position]
            flipped = partner(current, "site", operate_position)
            product = jnp.dot(
                masked[chosen], flipped.astype(jnp.bfloat16), preferred_element_type=jnp.float32
            )
            summed = summed + (field[chosen] * flipped + product)
        if iteration == 0:
            vector_new = summed
        else:
            vector_new = 2.0 * summed - previous / scale_prev
        squares, intersection = lax.psum(
            (jnp.sum(vector_new * vector_new), jnp.sum(initial * vector_new)), ("site", "phonon")
        )
        scale_now = jnp.sqrt(squares / entries + epsilon)
        updated = vector_new / scale_now
        moment = intersection / (entries * scale_now)
        moments.append(moment)
        previous = current
        current = updated
        scale_prev = scale_now
    return (current, previous, jnp.stack(moments))


def solution(mesh):
    in_specs = (P("site", "phonon"), P(), P(), P(), P(), P(), P())
    out_specs = (P("site", "phonon"), P("site", "phonon"), P())

    def whole(state, operators, op_mask, *rest):
        rows = state.shape[0] // mesh.shape["site"]
        columns = state.shape[1] // mesh.shape["phonon"]
        plan = Plan(mesh, rows, columns, op_mask.shape[1])
        body = functools.partial(shards, plan) if plan.fits() else halo_shards
        run = jax.shard_map(body, mesh=mesh, in_specs=in_specs, out_specs=out_specs, check_vma=False)
        return run(state, operators, op_mask, *rest)

    return whole
```

```python
import functools

import jax
import jax.numpy as jnp
from jax import lax
from jax.experimental import pallas as pl
from jax.experimental.pallas import tpu as pltpu
from jax.sharding import PartitionSpec as P

LBITS = 10
MODES = 64
STEPS = 3
LANES = 128
SUBLANES = 8
SLOTS = 4
AXES = ("site", "phonon")

epsilon = 1e-06


VMEM = pl.BlockSpec(memory_space=pltpu.VMEM)
SMEM = pl.BlockSpec(memory_space=pltpu.SMEM)
HBM = pl.BlockSpec(memory_space=pltpu.HBM)


class Plan:
    def __init__(self, mesh, rows, columns, blocks):
        self.sites = mesh.shape["site"]
        self.phonons = mesh.shape["phonon"]
        self.groups = self.sites * self.phonons
        self.bits = self.sites.bit_length() - 1
        self.rows = rows
        self.columns = columns
        self.blocks = blocks
        self.edge = rows // blocks
        self.levels_here = columns // MODES
        self.level_count = self.levels_here * self.phonons
        self.share = MODES // self.groups
        self.pieces = self.levels_here * self.share
        self.lane_blocks = rows // LANES
        self.body = self.pieces * self.lane_blocks
        self.inward = self.body + 1
        self.outward = 2 * self.body + 1
        self.places = self.pieces * self.groups
        self.width = 2 * LANES
        self.parts = rows // self.width
        self.slabs = self.bits * self.parts
        self.kept = min(5, self.slabs - 1)
        self.entries = float(rows * columns * self.groups)

    def fits(self):
        return (
            MODES % self.groups == 0
            and self.columns == LANES
            and self.rows % self.width == 0
            and self.edge % LANES == 0
            and self.width % self.edge == 0
            and self.bits < SUBLANES
            and self.groups % SUBLANES == 0
        )


def params(mib):
    return pltpu.CompilerParams(vmem_limit_bytes=mib * 2**20)


def lane_sums(values):
    return jnp.sum(values, axis=0, keepdims=True)


def put_sums(out_ref, sums, start, stride, count):
    lane = lax.broadcasted_iota(jnp.int32, (1, LANES), 1)
    row = jnp.zeros((1, LANES), jnp.float32)
    for slot, value in enumerate(sums):
        width = LANES
        while width > LANES // SLOTS:
            width //= 2
            value = value + pltpu.roll(value, width, 1)
        row = jnp.where(lane // (LANES // SLOTS) == slot, value, row)
    out_ref[pl.ds(start, count, stride=stride), :] = jnp.broadcast_to(row, (count, LANES))


def totals_of(ref, start, stride, count):
    lanes = lane_sums(ref[pl.ds(start, count, stride=stride), :])
    lane = lax.broadcasted_iota(jnp.int32, (1, LANES), 1)
    return [
        jnp.sum(jnp.where(lane // (LANES // SLOTS) == slot, lanes, 0.0), axis=1, keepdims=True)
        for slot in range(SLOTS)
    ]


def scale_of(plan, squares):
    return jnp.sqrt(squares / plan.entries + epsilon)


def depart_kernel(plan, state_ref, out_ref, sums_ref):
    part = pl.program_id(0)

    @pl.when(part == 0)
    def _():
        sums_ref[...] = jnp.zeros_like(sums_ref)

    for start in range(0, plan.width, LANES):
        tile = state_ref[pl.ds(start, LANES), :]
        sums_ref[...] += lane_sums(tile * tile)
        turned = tile.T
        block = part * (plan.width // LANES) + start // LANES
        for piece in range(plan.pieces):
            out_ref[pl.ds(piece * plan.lane_blocks + block, plan.groups, stride=plan.inward), :] = turned[
                piece * plan.groups : (piece + 1) * plan.groups
            ]

    @pl.when(part == plan.parts - 1)
    def _():
        put_sums(out_ref, [sums_ref[...]], plan.body, plan.inward, plan.groups)


def fetch_slabs(plan, slabs, bits_ref, operators_ref, held_ref, semaphores):
    fetches = []
    for index, slab in enumerate(slabs):
        part, bit = divmod(slab, plan.bits)
        rows = pl.ds(part * plan.width, plan.width)
        fetch = pltpu.make_async_copy(
            operators_ref.at[bits_ref[bit], rows, :], held_ref.at[index], semaphores.at[index]
        )
        fetch.start()
        fetches.append(fetch)
    return fetches


def mask_slab(plan, slab, index, bits_ref, mask_ref, held_ref, out_ref):
    part, bit = divmod(slab, plan.bits)
    chosen = bits_ref[bit]
    for start in range(0, plan.width, plan.edge):
        across = (part * plan.width + start) // plan.edge
        rows = pl.ds(start, plan.edge)
        for along in range(plan.blocks):
            columns = pl.ds(along * plan.edge, plan.edge)
            keep = (mask_ref[chosen, across, along] > 0).astype(jnp.float32).astype(jnp.bfloat16)
            out_ref[index, columns, rows] = (held_ref[index, rows, columns] * keep).T


def store_kernel(plan, bits_ref, mask_ref, operators_ref, stored_ref, held_ref, masked_ref, in_semaphores, out_semaphores):
    slabs = range(plan.kept, plan.slabs)
    fetches = fetch_slabs(plan, slabs, bits_ref, operators_ref, held_ref, in_semaphores)
    stores = []
    for index, slab in enumerate(slabs):
        fetches[index].wait()
        mask_slab(plan, slab, index, bits_ref, mask_ref, held_ref, masked_ref)
        store = pltpu.make_async_copy(masked_ref.at[index], stored_ref.at[index], out_semaphores.at[index])
        store.start()
        stores.append(store)
    for store in stores:
        store.wait()


def prepare_kernel(
    plan,
    bits_ref,
    mask_ref,
    field_ref,
    coupling_ref,
    mode_ref,
    operators_ref,
    place_ref,
    inside_ref,
    kept_ref,
    held_ref,
    semaphores,
):
    slabs = range(plan.kept)
    fetches = fetch_slabs(plan, slabs, bits_ref, operators_ref, held_ref, semaphores)
    me = lax.axis_index("site") * plan.phonons + lax.axis_index("phonon")
    place = lax.broadcasted_iota(jnp.int32, (plan.places, LANES), 0)
    phonon = place % plan.phonons
    site = place // plan.phonons % plan.sites
    mode = place // plan.groups % plan.share
    level = phonon * plan.levels_here + place // (plan.groups * plan.share)
    occupied = jnp.zeros((plan.places, LANES), jnp.float32)
    for position in range(plan.bits):
        held = (site >> position & 1).astype(jnp.float32)
        occupied = occupied + coupling_ref[bits_ref[position]] * held
    strength = jnp.zeros((plan.places, LANES), jnp.float32)
    for index in range(plan.share):
        strength = jnp.where(mode == index, mode_ref[index * plan.groups + me], strength)
    strength = strength / jnp.sqrt(jnp.full((1, LANES), plan.level_count, jnp.float32))
    height = level.astype(jnp.float32)
    place_ref[0] = occupied
    place_ref[1] = strength * jnp.sqrt(height)
    place_ref[2] = jnp.where(level == plan.level_count - 1, 0.0, strength * jnp.sqrt(height + 1.0))
    inside = lax.broadcasted_iota(jnp.int32, (1, plan.rows), 1)
    weight = jnp.zeros((1, plan.rows), jnp.float32)
    for local_bit in range(LBITS):
        weight = weight + coupling_ref[plan.bits + local_bit] * (inside >> local_bit & 1).astype(jnp.float32)
    inside_ref[...] = jnp.zeros_like(inside_ref)
    inside_ref[:1] = weight
    for position in range(plan.bits):
        inside_ref[pl.ds(1 + position, 1)] = jnp.full((1, plan.rows), field_ref[bits_ref[position]])
    for slab in slabs:
        fetches[slab].wait()
        mask_slab(plan, slab, slab, bits_ref, mask_ref, held_ref, kept_ref)


def flipped(values, stride):
    places, width = values.shape
    if stride % SUBLANES == 0:
        shaped = values.reshape(places // (2 * stride), 2, stride, width)
        return jnp.concatenate([shaped[:, 1:], shaped[:, :1]], axis=1).reshape(places, width)
    tiles = values.reshape(places // SUBLANES, SUBLANES, width)
    if 2 * stride == SUBLANES:
        return pltpu.roll(tiles, stride, 1).reshape(places, width)
    spot = lax.broadcasted_iota(jnp.int32, tiles.shape, 1)
    down = pltpu.roll(tiles, stride, 1)
    up = pltpu.roll(tiles, SUBLANES - stride, 1)
    return jnp.where(spot & stride > 0, down, up).reshape(places, width)


def shifted(values, by):
    places, width = values.shape
    tiles = values.reshape(places // SUBLANES, SUBLANES, width)
    return pltpu.roll(tiles, by % SUBLANES, 1).reshape(places, width)


def put_rounded(plan, rounded_ref, vector, start):
    for position in range(plan.bits):
        rounded_ref[:, pl.ds(position * plan.rows + start, vector.shape[1])] = flipped(
            vector, plan.phonons << position
        ).astype(jnp.bfloat16)


def step(plan, vector_ref, rounded_ref, kept_ref, fetched_ref, place_ref, inside_ref, finish, ready=None, begun_ref=None, factor=None):
    span = plan.places // plan.levels_here

    def local(start):
        lanes = pl.ds(start, LANES)
        vector = vector_ref[:, lanes]
        levels = [vector[index * span : (index + 1) * span] for index in range(plan.levels_here)]
        lower = jnp.concatenate([shifted(levels[-1], 1)] + levels[:-1], axis=0)
        upper = jnp.concatenate(levels[1:] + [shifted(levels[0], -1)], axis=0)
        weight = place_ref[0] + inside_ref[:1, lanes]
        total = weight * (place_ref[1] * lower + place_ref[2] * upper)
        for position in range(plan.bits):
            total = total + inside_ref[pl.ds(1 + position, 1), lanes] * flipped(vector, plan.phonons << position)
        return total if factor is None else total * factor

    def added(total, part, late):
        for ref, low, high in ((kept_ref, 0, plan.kept), (fetched_ref, plan.kept, plan.slabs)):
            fetched = low > 0
            begin = max(part * plan.bits, low)
            count = min((part + 1) * plan.bits, high) - begin
            if count <= 0 or late not in (None, fetched):
                continue
            if late:
                for slab in range(begin, begin + count):
                    ready(slab)
            first = begin - part * plan.bits
            masked = ref[pl.ds(begin - low, count)].reshape(count * plan.rows, plan.width)
            operand = rounded_ref[:, pl.ds(first * plan.rows, count * plan.rows)]
            total = total + jnp.dot(operand, masked, preferred_element_type=jnp.float32)
        return total

    def locals_of(lanes):
        return jnp.concatenate([local(start) for start in range(lanes.start, lanes.start + plan.width, LANES)], axis=1)

    parts = [pl.ds(part * plan.width, plan.width) for part in range(plan.parts)]
    if ready is None:
        for part, lanes in enumerate(parts):
            finish(lanes, added(locals_of(lanes), part, None))
        return
    for part, lanes in enumerate(parts):
        begun_ref[:, lanes] = added(locals_of(lanes), part, False)
    for part, lanes in enumerate(parts):
        finish(lanes, added(begun_ref[:, lanes], part, True))


def first_kernel(
    plan,
    arrived_ref,
    place_ref,
    inside_ref,
    kept_ref,
    stored_ref,
    initial_ref,
    new_ref,
    sums_ref,
    fetched_ref,
    rounded_ref,
    ahead_ref,
    semaphores,
):
    fetches = {}
    for slab in range(plan.kept, plan.slabs):
        index = slab - plan.kept
        fetches[slab] = pltpu.make_async_copy(stored_ref.at[index], fetched_ref.at[index], semaphores.at[index])
        fetches[slab].start()

    def ready(slab):
        fetches[slab].wait()

    squares = totals_of(arrived_ref, plan.body, plan.inward, plan.groups)[0]
    inverse = 1.0 / scale_of(plan, squares)
    for block in range(plan.lane_blocks):
        parts = [
            arrived_ref[pl.ds(piece * plan.lane_blocks + block, plan.groups, stride=plan.inward), :]
            for piece in range(plan.pieces)
        ]
        vector = jnp.concatenate(parts, axis=0) * inverse
        initial_ref[:, pl.ds(block * LANES, LANES)] = vector
        put_rounded(plan, rounded_ref, vector, block * LANES)
    tables = (kept_ref, fetched_ref, place_ref, inside_ref)
    squares = []
    overlap = []
    ahead = []

    def finish(lanes, new):
        new_ref[:, lanes] = new
        put_rounded(plan, ahead_ref, new, lanes.start)
        squares.append(lane_sums(new * new))
        overlap.append(lane_sums(new * initial_ref[:, lanes]))

    def look_ahead(lanes, total):
        new = 2.0 * total - initial_ref[:, lanes]
        ahead.append(lane_sums(new * new))

    step(plan, initial_ref, rounded_ref, *tables, finish, ready, new_ref)
    step(plan, new_ref, ahead_ref, *tables, look_ahead)
    put_sums(sums_ref, [one_row(squares), one_row(overlap), one_row(ahead)], 0, 1, plan.groups)


def one_row(rows):
    total = sum(rows[1:], rows[0])
    return sum(total[:, start : start + LANES] for start in range(0, total.shape[1], LANES))


def onward_kernel(
    plan,
    arrived_ref,
    raw_ref,
    initial_ref,
    place_ref,
    inside_ref,
    kept_ref,
    fetched_ref,
    out_ref,
    known_ref,
    rounded_ref,
    ahead_ref,
    third_ref,
):
    squares, overlap, ahead, _ = totals_of(arrived_ref, 0, 1, plan.groups)
    first = 1.0 / scale_of(plan, squares)
    estimate = scale_of(plan, ahead * first * first)
    second = 1.0 / estimate
    both = first * second
    known_ref[:1, :] = jnp.broadcast_to(overlap * first / plan.entries, (1, LANES))
    known_ref[1:, :] = jnp.broadcast_to(estimate, (SUBLANES - 1, LANES))
    for block in range(plan.lane_blocks):
        lanes = pl.ds(block * LANES, LANES)
        put_rounded(plan, rounded_ref, raw_ref[:, lanes] * first, block * LANES)
    tables = (kept_ref, fetched_ref, place_ref, inside_ref)
    sums = [[] for _ in range(SLOTS)]

    def send(vector, lanes, new):
        sums[2 * vector].append(lane_sums(new * new))
        sums[2 * vector + 1].append(lane_sums(new * initial_ref[:, lanes]))
        for start in range(0, plan.width, LANES):
            block = (lanes.start + start) // LANES
            for piece in range(plan.pieces):
                row = vector * plan.body + piece * plan.lane_blocks + block
                out_ref[pl.ds(row, plan.groups, stride=plan.outward), :] = new[
                    piece * plan.groups : (piece + 1) * plan.groups, start : start + LANES
                ]

    def finish_second(lanes, total):
        new = 2.0 * total - initial_ref[:, lanes] * first
        vector = new * second
        third_ref[:, lanes] = vector
        put_rounded(plan, ahead_ref, vector, lanes.start)
        send(0, lanes, new)

    def finish_third(lanes, total):
        send(1, lanes, 2.0 * total - raw_ref[:, lanes] * both)

    step(plan, raw_ref, rounded_ref, *tables, finish_second, factor=first)
    step(plan, third_ref, ahead_ref, *tables, finish_third)
    put_sums(out_ref, [one_row(rows) for rows in sums], 2 * plan.body, plan.outward, plan.groups)


def arrive_kernel(plan, arrived_ref, known_ref, before_ref, last_ref, moments_ref, factors_ref):
    part = pl.program_id(0)

    @pl.when(part == 0)
    def _():
        before_squares, before_overlap, last_squares, last_overlap = totals_of(
            arrived_ref, 2 * plan.body, plan.outward, plan.groups
        )
        before = 1.0 / scale_of(plan, before_squares)
        back = known_ref[1:2, :1] * before
        last = back / scale_of(plan, last_squares * back * back)
        factors_ref[0:1, :] = jnp.broadcast_to(before, (1, LANES))
        factors_ref[1:2, :] = jnp.broadcast_to(last, (1, LANES))
        moments_ref[0] = known_ref[0, 0]
        moments_ref[1] = (before_overlap * before / plan.entries)[0, 0]
        moments_ref[2] = (last_overlap * last / plan.entries)[0, 0]

    for vector, out_ref in enumerate((before_ref, last_ref)):
        for start in range(0, plan.width, LANES):
            first = vector * plan.body + part * (plan.width // LANES) + start // LANES
            parts = [
                arrived_ref[pl.ds(first + piece * plan.lane_blocks, plan.groups, stride=plan.outward), :]
                for piece in range(plan.pieces)
            ]
            out_ref[pl.ds(start, LANES), :] = jnp.concatenate(parts, axis=0).T * factors_ref[vector : vector + 1, :]


def exchange(values, count):
    shaped = values.reshape(count, values.shape[0] // count, 1, LANES)
    return lax.all_to_all(shaped, AXES, 0, 0, tiled=True).reshape(values.shape)


def shards(plan, state, operators, op_mask, site_bits, field, site_coupling, mode_coupling):
    f32 = jnp.float32
    inward = jax.ShapeDtypeStruct((plan.groups * plan.inward, LANES), f32)
    outward = jax.ShapeDtypeStruct((plan.groups * plan.outward, LANES), f32)
    vector = jax.ShapeDtypeStruct((plan.places, plan.rows), f32)
    known = jax.ShapeDtypeStruct((SUBLANES, LANES), f32)
    held = jax.ShapeDtypeStruct((plan.rows, plan.columns), f32)
    rounded = pltpu.VMEM((plan.places, plan.bits * plan.rows), jnp.bfloat16)
    working = pltpu.VMEM((plan.places, plan.rows), f32)
    work = 2 * plan.bits * plan.places * plan.rows * plan.rows

    def cost(flops, moved):
        return pl.CostEstimate(flops=flops, bytes_accessed=moved, transcendentals=0)

    departing = pl.pallas_call(
        functools.partial(depart_kernel, plan),
        out_shape=inward,
        grid=(plan.parts,),
        in_specs=[pl.BlockSpec((plan.width, plan.columns), lambda part: (part, 0))],
        out_specs=pl.BlockSpec(inward.shape, lambda part: (0, 0)),
        scratch_shapes=[pltpu.VMEM((1, LANES), f32)],
        compiler_params=params(60),
        name="depart",
    )(state)
    arrived = exchange(departing, plan.groups)
    fetched = plan.slabs - plan.kept
    kept_slabs = (plan.kept, plan.rows, plan.width)
    fetched_slabs = (fetched, plan.rows, plan.width)

    def held_slabs(count):
        return pltpu.VMEM((count, plan.width, plan.rows), jnp.bfloat16)

    place, inside, kept = pl.pallas_call(
        functools.partial(prepare_kernel, plan),
        out_shape=[
            jax.ShapeDtypeStruct((3, plan.places, LANES), f32),
            jax.ShapeDtypeStruct((SUBLANES, plan.rows), f32),
            jax.ShapeDtypeStruct(kept_slabs, jnp.bfloat16),
        ],
        in_specs=[SMEM] * 5 + [HBM],
        out_specs=[VMEM] * 3,
        scratch_shapes=[held_slabs(plan.kept), pltpu.SemaphoreType.DMA((plan.kept,))],
        compiler_params=params(50),
        cost_estimate=cost(plan.rows * plan.rows, 4 * plan.kept * plan.rows * plan.width),
        name="prepare",
    )(site_bits, op_mask, field, site_coupling, mode_coupling, operators)
    stored = pl.pallas_call(
        functools.partial(store_kernel, plan),
        out_shape=jax.ShapeDtypeStruct(fetched_slabs, jnp.bfloat16),
        in_specs=[SMEM] * 2 + [HBM],
        out_specs=HBM,
        scratch_shapes=[
            held_slabs(fetched),
            pltpu.VMEM(fetched_slabs, jnp.bfloat16),
            pltpu.SemaphoreType.DMA((fetched,)),
            pltpu.SemaphoreType.DMA((fetched,)),
        ],
        compiler_params=params(60),
        cost_estimate=cost(plan.rows * plan.rows, 4 * fetched * plan.rows * plan.width),
        name="store",
    )(site_bits, op_mask, operators)
    initial, raw, sums, late = pl.pallas_call(
        functools.partial(first_kernel, plan),
        out_shape=[
            vector,
            vector,
            jax.ShapeDtypeStruct((plan.groups, LANES), f32),
            jax.ShapeDtypeStruct(fetched_slabs, jnp.bfloat16),
        ],
        in_specs=[VMEM] * 4 + [HBM],
        out_specs=[VMEM] * 4,
        scratch_shapes=[rounded, rounded, pltpu.SemaphoreType.DMA((fetched,))],
        compiler_params=params(46),
        cost_estimate=cost(2 * work, 4 * plan.places * plan.rows),
        name="first",
    )(arrived, place, inside, kept, stored)
    tables = (place, inside, kept, late)
    sums = exchange(sums, plan.groups)
    departing, told = pl.pallas_call(
        functools.partial(onward_kernel, plan),
        out_shape=[outward, known],
        in_specs=[VMEM] * 7,
        out_specs=[VMEM] * 2,
        scratch_shapes=[rounded, rounded, working],
        compiler_params=params(32),
        cost_estimate=cost(2 * work, 8 * plan.places * plan.rows),
        name="onward",
    )(sums, raw, initial, *tables)
    arrived = exchange(departing, plan.groups)
    before, last, moments = pl.pallas_call(
        functools.partial(arrive_kernel, plan),
        out_shape=[held, held, jax.ShapeDtypeStruct((STEPS,), f32)],
        grid=(plan.parts,),
        in_specs=[VMEM] * 2,
        out_specs=[pl.BlockSpec((plan.width, plan.columns), lambda part: (part, 0))] * 2 + [SMEM],
        scratch_shapes=[pltpu.VMEM((SUBLANES, LANES), f32)],
        compiler_params=params(16),
        name="arrive",
    )(arrived, told)
    return last, before, moments


def extended_2(block, sides, width):
    for axis, dim in sides:
        count = lax.axis_size(axis)
        forward = [(i, i + 1) for i in range(count - 1)]
        backward = [(target, source) for source, target in forward]
        low = lax.ppermute(
            lax.slice_in_dim(block, block.shape[dim] - width, None, axis=dim), axis, forward
        )
        high = lax.ppermute(lax.slice_in_dim(block, 0, width, axis=dim), axis, backward)
        block = jnp.concatenate([low, block, high], axis=dim)
    return block


def partner(value, axis, bit):
    mask = 2**bit
    pairs = [(source, source ^ mask) for source in range(lax.axis_size(axis))]
    return lax.ppermute(value, axis, pairs)


def halo_shards(state, operators, op_mask, site_bits, field, site_coupling, mode_coupling):
    site_count = lax.axis_size("site")
    phonon_count = lax.axis_size("phonon")
    bit_count = site_count.bit_length() - 1
    rows_here = state.shape[0]
    columns_here = state.shape[1]
    levels_here = columns_here // MODES
    block_edge = rows_here // op_mask.shape[1]
    expanded = jnp.repeat(jnp.repeat(op_mask, block_edge, axis=1), block_edge, axis=2)
    masked = jnp.where(expanded > 0, operators, jnp.zeros((), jnp.bfloat16))
    entries = jnp.float32(rows_here * columns_here * site_count * phonon_count)
    level_total = jnp.sqrt(jnp.float32(levels_here * phonon_count))
    device = lax.axis_index("site")
    inside = lax.iota(jnp.int32, rows_here)
    weight_rows = jnp.zeros((rows_here,), jnp.float32)
    for position in range(bit_count):
        weight_rows = weight_rows + site_coupling[site_bits[position]] * (
            device >> position & 1
        ).astype(jnp.float32)
    for local_bit in range(LBITS):
        weight_rows = weight_rows + site_coupling[bit_count + local_bit] * (
            inside >> local_bit & 1
        ).astype(jnp.float32)
    levels = (
        lax.axis_index("phonon") * levels_here + lax.iota(jnp.int32, columns_here) // MODES
    ).astype(jnp.float32)
    lower_weight = jnp.sqrt(levels)
    upper_weight = jnp.sqrt(levels + 1.0)
    mode_weight = jnp.tile(mode_coupling, columns_here // MODES) / level_total
    start_squares = lax.psum(jnp.sum(state * state), ("site", "phonon"))
    initial = state / jnp.sqrt(start_squares / entries + epsilon)
    previous = initial
    current = initial
    scale_prev = jnp.float32(1.0)
    moments = []
    for iteration in range(STEPS):
        extended = extended_2(current, (("phonon", 1),), MODES)
        lower_part = extended[:, :columns_here]
        upper_part = extended[:, 2 * MODES :]
        summed = weight_rows[:, None] * (
            mode_weight * (lower_weight * lower_part + upper_weight * upper_part)
        )
        for operate_position in range(bit_count):
            chosen = site_bits[operate_position]
            flipped = partner(current, "site", operate_position)
            product = jnp.dot(
                masked[chosen], flipped.astype(jnp.bfloat16), preferred_element_type=jnp.float32
            )
            summed = summed + (field[chosen] * flipped + product)
        if iteration == 0:
            vector_new = summed
        else:
            vector_new = 2.0 * summed - previous / scale_prev
        squares, intersection = lax.psum(
            (jnp.sum(vector_new * vector_new), jnp.sum(initial * vector_new)), ("site", "phonon")
        )
        scale_now = jnp.sqrt(squares / entries + epsilon)
        updated = vector_new / scale_now
        moment = intersection / (entries * scale_now)
        moments.append(moment)
        previous = current
        current = updated
        scale_prev = scale_now
    return (current, previous, jnp.stack(moments))


def solution(mesh):
    in_specs = (P("site", "phonon"), P(), P(), P(), P(), P(), P())
    out_specs = (P("site", "phonon"), P("site", "phonon"), P())

    def whole(state, operators, op_mask, *rest):
        rows = state.shape[0] // mesh.shape["site"]
        columns = state.shape[1] // mesh.shape["phonon"]
        plan = Plan(mesh, rows, columns, op_mask.shape[1])
        body = functools.partial(shards, plan) if plan.fits() else halo_shards
        run = jax.shard_map(body, mesh=mesh, in_specs=in_specs, out_specs=out_specs, check_vma=False)
        return run(state, operators, op_mask, *rest)

    return whole
```

```python
import functools

import jax
import jax.numpy as jnp
from jax import lax
from jax.experimental import pallas as pl
from jax.experimental.pallas import tpu as pltpu
from jax.sharding import PartitionSpec as P

LBITS = 10
MODES = 64
STEPS = 3
LANES = 128
SUBLANES = 8
SLOTS = 4
AXES = ("site", "phonon")

epsilon = 1e-06


VMEM = pl.BlockSpec(memory_space=pltpu.VMEM)
SMEM = pl.BlockSpec(memory_space=pltpu.SMEM)
HBM = pl.BlockSpec(memory_space=pltpu.HBM)


class Plan:
    def __init__(self, mesh, rows, columns, blocks):
        self.sites = mesh.shape["site"]
        self.phonons = mesh.shape["phonon"]
        self.groups = self.sites * self.phonons
        self.bits = self.sites.bit_length() - 1
        self.rows = rows
        self.columns = columns
        self.blocks = blocks
        self.edge = rows // blocks
        self.levels_here = columns // MODES
        self.level_count = self.levels_here * self.phonons
        self.share = MODES // self.groups
        self.pieces = self.levels_here * self.share
        self.lane_blocks = rows // LANES
        self.body = self.pieces * self.lane_blocks
        self.inward = self.body + 1
        self.outward = 2 * self.body + 1
        self.places = self.pieces * self.groups
        self.width = 2 * LANES
        self.parts = rows // self.width
        self.half = self.groups // 2
        self.slabs = self.bits * self.parts
        self.kept = min(5, self.slabs - 1)
        self.entries = float(rows * columns * self.groups)

    def fits(self):
        return (
            MODES % self.groups == 0
            and self.columns == LANES
            and self.rows % self.width == 0
            and self.edge % LANES == 0
            and self.width % self.edge == 0
            and self.bits < SUBLANES
            and self.half % SUBLANES == 0
        )


def params(mib):
    return pltpu.CompilerParams(vmem_limit_bytes=mib * 2**20)


def lane_sums(values):
    return jnp.sum(values, axis=0, keepdims=True)


def put_sums(out_ref, sums, start, stride, count):
    lane = lax.broadcasted_iota(jnp.int32, (1, LANES), 1)
    row = jnp.zeros((1, LANES), jnp.float32)
    for slot, value in enumerate(sums):
        width = LANES
        while width > LANES // SLOTS:
            width //= 2
            value = value + pltpu.roll(value, width, 1)
        row = jnp.where(lane // (LANES // SLOTS) == slot, value, row)
    out_ref[pl.ds(start, count, stride=stride), :] = jnp.broadcast_to(row, (count, LANES))


def totals_of(ref, start, stride, count):
    lanes = lane_sums(ref[pl.ds(start, count, stride=stride), :])
    lane = lax.broadcasted_iota(jnp.int32, (1, LANES), 1)
    return [
        jnp.sum(jnp.where(lane // (LANES // SLOTS) == slot, lanes, 0.0), axis=1, keepdims=True)
        for slot in range(SLOTS)
    ]


def scale_of(plan, squares):
    return jnp.sqrt(squares / plan.entries + epsilon)


def depart_kernel(plan, state_ref, out_ref, held_ref, semaphores):
    half = plan.rows // 2
    fetches = [
        pltpu.make_async_copy(
            state_ref.at[pl.ds(index * half, half), :], held_ref.at[pl.ds(index * half, half), :], semaphores.at[index]
        )
        for index in range(2)
    ]
    for fetch in fetches:
        fetch.start()
    sums = jnp.zeros((1, LANES), jnp.float32)
    for block in range(plan.lane_blocks):
        if block * LANES % half == 0:
            fetches[block * LANES // half].wait()
        tile = held_ref[pl.ds(block * LANES, LANES), :]
        sums = sums + lane_sums(tile * tile)
        turned = tile.T
        for piece in range(plan.pieces):
            out_ref[pl.ds(piece * plan.lane_blocks + block, plan.groups, stride=plan.inward), :] = turned[
                piece * plan.groups : (piece + 1) * plan.groups
            ]
    put_sums(out_ref, [sums], plan.body, plan.inward, plan.groups)


def fetch_slabs(plan, slabs, bits_ref, operators_ref, held_ref, semaphores):
    fetches = []
    for index, slab in enumerate(slabs):
        part, bit = divmod(slab, plan.bits)
        rows = pl.ds(part * plan.width, plan.width)
        fetch = pltpu.make_async_copy(
            operators_ref.at[bits_ref[bit], rows, :], held_ref.at[index], semaphores.at[index]
        )
        fetch.start()
        fetches.append(fetch)
    return fetches


def mask_slab(plan, slab, index, bits_ref, mask_ref, held_ref, out_ref):
    part, bit = divmod(slab, plan.bits)
    chosen = bits_ref[bit]
    for start in range(0, plan.width, plan.edge):
        across = (part * plan.width + start) // plan.edge
        rows = pl.ds(start, plan.edge)
        for along in range(plan.blocks):
            columns = pl.ds(along * plan.edge, plan.edge)
            keep = (mask_ref[chosen, across, along] > 0).astype(jnp.float32).astype(jnp.bfloat16)
            out_ref[index, columns, rows] = (held_ref[index, rows, columns] * keep).T


def store_kernel(plan, bits_ref, mask_ref, operators_ref, stored_ref, held_ref, masked_ref, in_semaphores, out_semaphores):
    slabs = range(plan.kept, plan.slabs)
    fetches = fetch_slabs(plan, slabs, bits_ref, operators_ref, held_ref, in_semaphores)
    stores = []
    for index, slab in enumerate(slabs):
        fetches[index].wait()
        mask_slab(plan, slab, index, bits_ref, mask_ref, held_ref, masked_ref)
        store = pltpu.make_async_copy(masked_ref.at[index], stored_ref.at[index], out_semaphores.at[index])
        store.start()
        stores.append(store)
    for store in stores:
        store.wait()


def prepare_kernel(
    plan,
    bits_ref,
    mask_ref,
    field_ref,
    coupling_ref,
    mode_ref,
    operators_ref,
    place_ref,
    partner_ref,
    inside_ref,
    kept_ref,
    held_ref,
    semaphores,
):
    slabs = range(plan.kept)
    fetches = fetch_slabs(plan, slabs, bits_ref, operators_ref, held_ref, semaphores)
    me = lax.axis_index("site") * plan.phonons + lax.axis_index("phonon")
    place = lax.broadcasted_iota(jnp.int32, (plan.places, LANES), 0)
    phonon = place % plan.phonons
    site = place // plan.phonons % plan.sites
    mode = place // plan.groups % plan.share
    level = phonon * plan.levels_here + place // (plan.groups * plan.share)
    occupied = jnp.zeros((plan.places, LANES), jnp.float32)
    for position in range(plan.bits):
        held = (site >> position & 1).astype(jnp.float32)
        occupied = occupied + coupling_ref[bits_ref[position]] * held
    height = level.astype(jnp.float32)
    lower = jnp.sqrt(height)
    upper = jnp.where(level == plan.level_count - 1, 0.0, jnp.sqrt(height + 1.0))
    place_ref[0] = occupied
    for ref, start, owner in ((place_ref, 1, me), (partner_ref, 0, me ^ plan.half)):
        strength = jnp.zeros((plan.places, LANES), jnp.float32)
        for index in range(plan.share):
            strength = jnp.where(mode == index, mode_ref[index * plan.groups + owner], strength)
        strength = strength / jnp.sqrt(jnp.full((1, LANES), plan.level_count, jnp.float32))
        ref[start] = strength * lower
        ref[start + 1] = strength * upper
    inside = lax.broadcasted_iota(jnp.int32, (1, plan.rows), 1)
    weight = jnp.zeros((1, plan.rows), jnp.float32)
    for local_bit in range(LBITS):
        weight = weight + coupling_ref[plan.bits + local_bit] * (inside >> local_bit & 1).astype(jnp.float32)
    inside_ref[...] = jnp.zeros_like(inside_ref)
    inside_ref[:1] = weight
    for position in range(plan.bits):
        inside_ref[pl.ds(1 + position, 1)] = jnp.full((1, plan.rows), field_ref[bits_ref[position]])
    for slab in slabs:
        fetches[slab].wait()
        mask_slab(plan, slab, slab, bits_ref, mask_ref, held_ref, kept_ref)


def flipped(values, stride):
    places, width = values.shape
    if stride % SUBLANES == 0:
        shaped = values.reshape(places // (2 * stride), 2, stride, width)
        return jnp.concatenate([shaped[:, 1:], shaped[:, :1]], axis=1).reshape(places, width)
    tiles = values.reshape(places // SUBLANES, SUBLANES, width)
    if 2 * stride == SUBLANES:
        return pltpu.roll(tiles, stride, 1).reshape(places, width)
    spot = lax.broadcasted_iota(jnp.int32, tiles.shape, 1)
    down = pltpu.roll(tiles, stride, 1)
    up = pltpu.roll(tiles, SUBLANES - stride, 1)
    return jnp.where(spot & stride > 0, down, up).reshape(places, width)


def shifted(values, by):
    places, width = values.shape
    tiles = values.reshape(places // SUBLANES, SUBLANES, width)
    return pltpu.roll(tiles, by % SUBLANES, 1).reshape(places, width)


def put_rounded(plan, rounded_ref, vector, start):
    for position in range(plan.bits):
        rounded_ref[:, pl.ds(position * plan.rows + start, vector.shape[1])] = flipped(
            vector, plan.phonons << position
        ).astype(jnp.bfloat16)


def step(plan, vector_ref, rounded_ref, kept_ref, fetched_ref, place, inside_ref, finish, ready=None, begun_ref=None):
    span = plan.places // plan.levels_here

    def local(start):
        lanes = pl.ds(start, LANES)
        vector = vector_ref[:, lanes]
        levels = [vector[index * span : (index + 1) * span] for index in range(plan.levels_here)]
        lower = jnp.concatenate([shifted(levels[-1], 1)] + levels[:-1], axis=0)
        upper = jnp.concatenate(levels[1:] + [shifted(levels[0], -1)], axis=0)
        occupied, (ladder_ref, first) = place
        weight = occupied[0] + inside_ref[:1, lanes]
        total = weight * (ladder_ref[first] * lower + ladder_ref[first + 1] * upper)
        for position in range(plan.bits):
            total = total + inside_ref[pl.ds(1 + position, 1), lanes] * flipped(vector, plan.phonons << position)
        return total

    def added(total, part, late):
        for ref, low, high in ((kept_ref, 0, plan.kept), (fetched_ref, plan.kept, plan.slabs)):
            fetched = low > 0
            begin = max(part * plan.bits, low)
            count = min((part + 1) * plan.bits, high) - begin
            if count <= 0 or late not in (None, fetched):
                continue
            if late:
                for slab in range(begin, begin + count):
                    ready(slab)
            first = begin - part * plan.bits
            masked = ref[pl.ds(begin - low, count)].reshape(count * plan.rows, plan.width)
            operand = rounded_ref[:, pl.ds(first * plan.rows, count * plan.rows)]
            total = total + jnp.dot(operand, masked, preferred_element_type=jnp.float32)
        return total

    def locals_of(lanes):
        return jnp.concatenate([local(start) for start in range(lanes.start, lanes.start + plan.width, LANES)], axis=1)

    parts = [pl.ds(part * plan.width, plan.width) for part in range(plan.parts)]
    if ready is None:
        for part, lanes in enumerate(parts):
            finish(lanes, added(locals_of(lanes), part, None))
        return
    for part, lanes in enumerate(parts):
        begun_ref[:, lanes] = added(locals_of(lanes), part, False)
    for part, lanes in enumerate(parts):
        finish(lanes, added(begun_ref[:, lanes], part, True))


def first_kernel(
    plan,
    arrived_ref,
    place_ref,
    inside_ref,
    kept_ref,
    stored_ref,
    initial_ref,
    new_ref,
    sums_ref,
    fetched_ref,
    rounded_ref,
    ahead_ref,
    semaphores,
):
    fetches = {}
    for slab in range(plan.kept, plan.slabs):
        index = slab - plan.kept
        fetches[slab] = pltpu.make_async_copy(stored_ref.at[index], fetched_ref.at[index], semaphores.at[index])
        fetches[slab].start()

    def ready(slab):
        fetches[slab].wait()

    squares = totals_of(arrived_ref, plan.body, plan.inward, plan.groups)[0]
    inverse = 1.0 / scale_of(plan, squares)
    for block in range(plan.lane_blocks):
        parts = [
            arrived_ref[pl.ds(piece * plan.lane_blocks + block, plan.groups, stride=plan.inward), :]
            for piece in range(plan.pieces)
        ]
        vector = jnp.concatenate(parts, axis=0) * inverse
        initial_ref[:, pl.ds(block * LANES, LANES)] = vector
        put_rounded(plan, rounded_ref, vector, block * LANES)
    tables = (kept_ref, fetched_ref, (place_ref, (place_ref, 1)), inside_ref)
    squares = []
    overlap = []
    ahead = []

    def finish(lanes, new):
        new_ref[:, lanes] = new
        put_rounded(plan, ahead_ref, new, lanes.start)
        squares.append(lane_sums(new * new))
        overlap.append(lane_sums(new * initial_ref[:, lanes]))

    def look_ahead(lanes, total):
        new = 2.0 * total - initial_ref[:, lanes]
        ahead.append(lane_sums(new * new))

    step(plan, initial_ref, rounded_ref, *tables, finish, ready, new_ref)
    step(plan, new_ref, ahead_ref, *tables, look_ahead)
    put_sums(sums_ref, [one_row(squares), one_row(overlap), one_row(ahead)], 0, 1, plan.groups)


def one_row(rows):
    total = sum(rows[1:], rows[0])
    return sum(total[:, start : start + LANES] for start in range(0, total.shape[1], LANES))


def onward_kernel(
    plan,
    arrived_ref,
    raw_ref,
    initial_ref,
    place_ref,
    inside_ref,
    kept_ref,
    fetched_ref,
    out_ref,
    known_ref,
    rounded_ref,
    ahead_ref,
    second_ref,
    third_ref,
):
    squares, overlap, ahead, _ = totals_of(arrived_ref, 0, 1, plan.groups)
    first = 1.0 / scale_of(plan, squares)
    estimate = scale_of(plan, ahead * first * first)
    second = 1.0 / estimate
    known_ref[...] = jnp.broadcast_to(first, (SUBLANES, LANES))
    known_ref[0:1, :] = jnp.broadcast_to(overlap * first / plan.entries, (1, LANES))
    known_ref[1:2, :] = jnp.broadcast_to(estimate, (1, LANES))
    for block in range(plan.lane_blocks):
        lanes = pl.ds(block * LANES, LANES)
        vector = raw_ref[:, lanes] * first
        second_ref[:, lanes] = vector
        put_rounded(plan, rounded_ref, vector, block * LANES)
    tables = (kept_ref, fetched_ref, (place_ref, (place_ref, 1)), inside_ref)
    sums = [[] for _ in range(SLOTS)]

    def note(vector, lanes, new):
        sums[2 * vector].append(lane_sums(new * new))
        sums[2 * vector + 1].append(lane_sums(new * initial_ref[:, lanes]))

    last_steps(
        plan, tables, first, second, initial_ref, second_ref, third_ref, rounded_ref, ahead_ref, out_ref, plan.outward, note
    )
    put_sums(out_ref, [one_row(rows) for rows in sums], 2 * plan.body, plan.outward, plan.half)


def last_steps(
    plan, tables, first, second, initial_ref, second_ref, third_ref, rounded_ref, ahead_ref, out_ref, stride, note
):
    upper = lax.axis_index("site") >= plan.sites // 2

    def send(vector, lanes, new):
        if note:
            note(vector, lanes, new)
        for start in range(0, plan.width, LANES):
            block = (lanes.start + start) // LANES
            for piece in range(plan.pieces):
                row = vector * plan.body + piece * plan.lane_blocks + block
                rows = new[piece * plan.groups : (piece + 1) * plan.groups, start : start + LANES]
                out_ref[pl.ds(row, plan.half, stride=stride), :] = jnp.where(
                    upper, rows[plan.half :], rows[: plan.half]
                )

    def finish_second(lanes, total):
        new = 2.0 * total - initial_ref[:, lanes] * first
        vector = new * second
        third_ref[:, lanes] = vector
        put_rounded(plan, ahead_ref, vector, lanes.start)
        send(0, lanes, new)

    def finish_third(lanes, total):
        send(1, lanes, 2.0 * total - second_ref[:, lanes] * second)

    step(plan, second_ref, rounded_ref, *tables, finish_second)
    step(plan, third_ref, ahead_ref, *tables, finish_third)


def partner_kernel(
    plan,
    state_ref,
    known_ref,
    own_ref,
    place_ref,
    partner_ref,
    inside_ref,
    kept_ref,
    fetched_ref,
    out_ref,
    sums_ref,
    first_ref,
    second_ref,
    third_ref,
    initial_ref,
    vector_ref,
    later_ref,
):
    sums_ref[...] = jnp.broadcast_to(
        lane_sums(own_ref[pl.ds(2 * plan.body, plan.half, stride=plan.outward), :]), (SUBLANES, LANES)
    )
    squares = totals_of(state_ref, plan.body, plan.inward, plan.groups)[0]
    inverse = 1.0 / scale_of(plan, squares)
    first = known_ref[2:3, :1]
    second = 1.0 / known_ref[1:2, :1]
    for block in range(plan.lane_blocks):
        parts = [
            state_ref[pl.ds(piece * plan.lane_blocks + block, plan.groups, stride=plan.inward), :]
            for piece in range(plan.pieces)
        ]
        vector = jnp.concatenate(parts, axis=0) * inverse
        initial_ref[:, pl.ds(block * LANES, LANES)] = vector
        put_rounded(plan, first_ref, vector, block * LANES)
    tables = (kept_ref, fetched_ref, (place_ref, (partner_ref, 0)), inside_ref)

    def finish(lanes, new):
        vector = new * first
        vector_ref[:, lanes] = vector
        put_rounded(plan, second_ref, vector, lanes.start)

    step(plan, initial_ref, first_ref, *tables, finish)
    last_steps(
        plan, tables, first, second, initial_ref, vector_ref, later_ref, second_ref, third_ref, out_ref, 2 * plan.body, None
    )


def arrive_kernel(
    plan, own_ref, other_ref, known_ref, sums_ref, other_sums_ref, before_ref, last_ref, moments_ref, total_ref
):
    upper = lax.axis_index("site") >= plan.sites // 2
    total_ref[...] = sums_ref[...] + other_sums_ref[...]
    before_squares, before_overlap, last_squares, last_overlap = totals_of(total_ref, 0, 1, 1)
    before = 1.0 / scale_of(plan, before_squares)
    back = known_ref[1:2, :1] * before
    last = back / scale_of(plan, last_squares * back * back)
    for vector, (out_ref, factor) in enumerate(((before_ref, before), (last_ref, last))):
        for block in range(plan.lane_blocks):
            parts = []
            for piece in range(plan.pieces):
                row = vector * plan.body + piece * plan.lane_blocks + block
                own = own_ref[pl.ds(row, plan.half, stride=plan.outward), :]
                other = other_ref[pl.ds(row, plan.half, stride=2 * plan.body), :]
                parts += [jnp.where(upper, other, own), jnp.where(upper, own, other)]
            out_ref[pl.ds(block * LANES, LANES), :] = jnp.concatenate(parts, axis=0).T * factor
    moments_ref[0] = known_ref[0, 0]
    moments_ref[1] = (before_overlap * before / plan.entries)[0, 0]
    moments_ref[2] = (last_overlap * last / plan.entries)[0, 0]


def exchange_half(plan, values):
    shaped = values.reshape(plan.half, values.shape[0] // plan.half, 1, LANES)
    halves = [list(range(start, start + plan.half)) for start in (0, plan.half)]
    return lax.all_to_all(shaped, AXES, 0, 0, axis_index_groups=halves, tiled=True).reshape(values.shape)


def crossed(plan, values):
    return lax.ppermute(values, "site", [(site, site ^ plan.sites // 2) for site in range(plan.sites)])


def exchange(values, count):
    shaped = values.reshape(count, values.shape[0] // count, 1, LANES)
    return lax.all_to_all(shaped, AXES, 0, 0, tiled=True).reshape(values.shape)


def shards(plan, state, operators, op_mask, site_bits, field, site_coupling, mode_coupling):
    f32 = jnp.float32
    inward = jax.ShapeDtypeStruct((plan.groups * plan.inward, LANES), f32)
    outward = jax.ShapeDtypeStruct((plan.half * plan.outward, LANES), f32)
    unsummed = jax.ShapeDtypeStruct((plan.half * 2 * plan.body, LANES), f32)
    vector = jax.ShapeDtypeStruct((plan.places, plan.rows), f32)
    known = jax.ShapeDtypeStruct((SUBLANES, LANES), f32)
    held = jax.ShapeDtypeStruct((plan.rows, plan.columns), f32)
    rounded = pltpu.VMEM((plan.places, plan.bits * plan.rows), jnp.bfloat16)
    working = pltpu.VMEM((plan.places, plan.rows), f32)
    work = 2 * plan.bits * plan.places * plan.rows * plan.rows

    def cost(flops, moved):
        return pl.CostEstimate(flops=flops, bytes_accessed=moved, transcendentals=0)

    departing = pl.pallas_call(
        functools.partial(depart_kernel, plan),
        out_shape=inward,
        in_specs=[HBM],
        out_specs=VMEM,
        scratch_shapes=[pltpu.VMEM((plan.rows, plan.columns), f32), pltpu.SemaphoreType.DMA((2,))],
        compiler_params=params(60),
        name="depart",
    )(state)
    arrived = exchange(departing, plan.groups)
    partner_state = crossed(plan, arrived)
    fetched = plan.slabs - plan.kept
    kept_slabs = (plan.kept, plan.rows, plan.width)
    fetched_slabs = (fetched, plan.rows, plan.width)

    def held_slabs(count):
        return pltpu.VMEM((count, plan.width, plan.rows), jnp.bfloat16)

    place, partner, inside, kept = pl.pallas_call(
        functools.partial(prepare_kernel, plan),
        out_shape=[
            jax.ShapeDtypeStruct((3, plan.places, LANES), f32),
            jax.ShapeDtypeStruct((2, plan.places, LANES), f32),
            jax.ShapeDtypeStruct((SUBLANES, plan.rows), f32),
            jax.ShapeDtypeStruct(kept_slabs, jnp.bfloat16),
        ],
        in_specs=[SMEM] * 5 + [HBM],
        out_specs=[VMEM] * 4,
        scratch_shapes=[held_slabs(plan.kept), pltpu.SemaphoreType.DMA((plan.kept,))],
        compiler_params=params(50),
        cost_estimate=cost(plan.rows * plan.rows, 4 * plan.kept * plan.rows * plan.width),
        name="prepare",
    )(site_bits, op_mask, field, site_coupling, mode_coupling, operators)
    stored = pl.pallas_call(
        functools.partial(store_kernel, plan),
        out_shape=jax.ShapeDtypeStruct(fetched_slabs, jnp.bfloat16),
        in_specs=[SMEM] * 2 + [HBM],
        out_specs=HBM,
        scratch_shapes=[
            held_slabs(fetched),
            pltpu.VMEM(fetched_slabs, jnp.bfloat16),
            pltpu.SemaphoreType.DMA((fetched,)),
            pltpu.SemaphoreType.DMA((fetched,)),
        ],
        compiler_params=params(60),
        cost_estimate=cost(plan.rows * plan.rows, 4 * fetched * plan.rows * plan.width),
        name="store",
    )(site_bits, op_mask, operators)
    initial, raw, sums, late = pl.pallas_call(
        functools.partial(first_kernel, plan),
        out_shape=[
            vector,
            vector,
            jax.ShapeDtypeStruct((plan.groups, LANES), f32),
            jax.ShapeDtypeStruct(fetched_slabs, jnp.bfloat16),
        ],
        in_specs=[VMEM] * 4 + [HBM],
        out_specs=[VMEM] * 4,
        scratch_shapes=[rounded, rounded, pltpu.SemaphoreType.DMA((fetched,))],
        compiler_params=params(46),
        cost_estimate=cost(2 * work, 4 * plan.places * plan.rows),
        name="first",
    )(arrived, place, inside, kept, stored)
    tables = (place, inside, kept, late)
    sums = exchange(sums, plan.groups)
    departing, told = pl.pallas_call(
        functools.partial(onward_kernel, plan),
        out_shape=[outward, known],
        in_specs=[VMEM] * 7,
        out_specs=[VMEM] * 2,
        scratch_shapes=[rounded, rounded, working, working],
        compiler_params=params(32),
        cost_estimate=cost(2 * work, 8 * plan.places * plan.rows),
        name="onward",
    )(sums, raw, initial, *tables)
    own = exchange_half(plan, departing)
    departing, share = pl.pallas_call(
        functools.partial(partner_kernel, plan),
        out_shape=[unsummed, known],
        in_specs=[VMEM] * 8,
        out_specs=[VMEM] * 2,
        scratch_shapes=[rounded, rounded, rounded, working, working, working],
        compiler_params=params(32),
        cost_estimate=cost(3 * work, 8 * plan.places * plan.rows),
        name="partner",
    )(partner_state, told, own, place, partner, inside, kept, late)
    other_share = crossed(plan, share)
    other = exchange_half(plan, departing)
    before, last, moments = pl.pallas_call(
        functools.partial(arrive_kernel, plan),
        out_shape=[held, held, jax.ShapeDtypeStruct((STEPS,), f32)],
        in_specs=[VMEM] * 5,
        out_specs=[VMEM, VMEM, SMEM],
        scratch_shapes=[pltpu.VMEM((SUBLANES, LANES), f32)],
        compiler_params=params(16),
        name="arrive",
    )(own, other, told, share, other_share)
    return last, before, moments


def extended_2(block, sides, width):
    for axis, dim in sides:
        count = lax.axis_size(axis)
        forward = [(i, i + 1) for i in range(count - 1)]
        backward = [(target, source) for source, target in forward]
        low = lax.ppermute(
            lax.slice_in_dim(block, block.shape[dim] - width, None, axis=dim), axis, forward
        )
        high = lax.ppermute(lax.slice_in_dim(block, 0, width, axis=dim), axis, backward)
        block = jnp.concatenate([low, block, high], axis=dim)
    return block


def partner(value, axis, bit):
    mask = 2**bit
    pairs = [(source, source ^ mask) for source in range(lax.axis_size(axis))]
    return lax.ppermute(value, axis, pairs)


def halo_shards(state, operators, op_mask, site_bits, field, site_coupling, mode_coupling):
    site_count = lax.axis_size("site")
    phonon_count = lax.axis_size("phonon")
    bit_count = site_count.bit_length() - 1
    rows_here = state.shape[0]
    columns_here = state.shape[1]
    levels_here = columns_here // MODES
    block_edge = rows_here // op_mask.shape[1]
    expanded = jnp.repeat(jnp.repeat(op_mask, block_edge, axis=1), block_edge, axis=2)
    masked = jnp.where(expanded > 0, operators, jnp.zeros((), jnp.bfloat16))
    entries = jnp.float32(rows_here * columns_here * site_count * phonon_count)
    level_total = jnp.sqrt(jnp.float32(levels_here * phonon_count))
    device = lax.axis_index("site")
    inside = lax.iota(jnp.int32, rows_here)
    weight_rows = jnp.zeros((rows_here,), jnp.float32)
    for position in range(bit_count):
        weight_rows = weight_rows + site_coupling[site_bits[position]] * (
            device >> position & 1
        ).astype(jnp.float32)
    for local_bit in range(LBITS):
        weight_rows = weight_rows + site_coupling[bit_count + local_bit] * (
            inside >> local_bit & 1
        ).astype(jnp.float32)
    levels = (
        lax.axis_index("phonon") * levels_here + lax.iota(jnp.int32, columns_here) // MODES
    ).astype(jnp.float32)
    lower_weight = jnp.sqrt(levels)
    upper_weight = jnp.sqrt(levels + 1.0)
    mode_weight = jnp.tile(mode_coupling, columns_here // MODES) / level_total
    start_squares = lax.psum(jnp.sum(state * state), ("site", "phonon"))
    initial = state / jnp.sqrt(start_squares / entries + epsilon)
    previous = initial
    current = initial
    scale_prev = jnp.float32(1.0)
    moments = []
    for iteration in range(STEPS):
        extended = extended_2(current, (("phonon", 1),), MODES)
        lower_part = extended[:, :columns_here]
        upper_part = extended[:, 2 * MODES :]
        summed = weight_rows[:, None] * (
            mode_weight * (lower_weight * lower_part + upper_weight * upper_part)
        )
        for operate_position in range(bit_count):
            chosen = site_bits[operate_position]
            flipped = partner(current, "site", operate_position)
            product = jnp.dot(
                masked[chosen], flipped.astype(jnp.bfloat16), preferred_element_type=jnp.float32
            )
            summed = summed + (field[chosen] * flipped + product)
        if iteration == 0:
            vector_new = summed
        else:
            vector_new = 2.0 * summed - previous / scale_prev
        squares, intersection = lax.psum(
            (jnp.sum(vector_new * vector_new), jnp.sum(initial * vector_new)), ("site", "phonon")
        )
        scale_now = jnp.sqrt(squares / entries + epsilon)
        updated = vector_new / scale_now
        moment = intersection / (entries * scale_now)
        moments.append(moment)
        previous = current
        current = updated
        scale_prev = scale_now
    return (current, previous, jnp.stack(moments))


def solution(mesh):
    in_specs = (P("site", "phonon"), P(), P(), P(), P(), P(), P())
    out_specs = (P("site", "phonon"), P("site", "phonon"), P())

    def whole(state, operators, op_mask, *rest):
        rows = state.shape[0] // mesh.shape["site"]
        columns = state.shape[1] // mesh.shape["phonon"]
        plan = Plan(mesh, rows, columns, op_mask.shape[1])
        body = functools.partial(shards, plan) if plan.fits() else halo_shards
        run = jax.shard_map(body, mesh=mesh, in_specs=in_specs, out_specs=out_specs, check_vma=False)
        return run(state, operators, op_mask, *rest)

    return whole
```

```python
import functools

import jax
import jax.numpy as jnp
from jax import lax
from jax.experimental import pallas as pl
from jax.experimental.pallas import tpu as pltpu
from jax.sharding import PartitionSpec as P

LBITS = 10
MODES = 64
STEPS = 3
LANES = 128
SUBLANES = 8
SLOTS = 4
AXES = ("site", "phonon")

epsilon = 1e-06


VMEM = pl.BlockSpec(memory_space=pltpu.VMEM)
SMEM = pl.BlockSpec(memory_space=pltpu.SMEM)
HBM = pl.BlockSpec(memory_space=pltpu.HBM)


class Plan:
    def __init__(self, mesh, rows, columns, blocks):
        self.sites = mesh.shape["site"]
        self.phonons = mesh.shape["phonon"]
        self.groups = self.sites * self.phonons
        self.bits = self.sites.bit_length() - 1
        self.rows = rows
        self.columns = columns
        self.blocks = blocks
        self.edge = rows // blocks
        self.levels_here = columns // MODES
        self.level_count = self.levels_here * self.phonons
        self.share = MODES // self.groups
        self.pieces = self.levels_here * self.share
        self.lane_blocks = rows // LANES
        self.body = self.pieces * self.lane_blocks
        self.inward = self.body + 1
        self.outward = 2 * self.body + 1
        self.places = self.pieces * self.groups
        self.width = 2 * LANES
        self.parts = rows // self.width
        self.slabs = self.bits * self.parts
        self.kept = min(5, self.slabs - 1)
        self.entries = float(rows * columns * self.groups)

    def stride(self, position):
        return self.phonons << (self.bits - 1 - position)

    def order(self):
        sites = [sum((site >> bit & 1) << (self.bits - 1 - bit) for bit in range(self.bits)) for site in range(self.sites)]
        return [site * self.phonons + phonon for site in sites for phonon in range(self.phonons)]

    def fits(self):
        return (
            MODES % self.groups == 0
            and self.columns == LANES
            and self.rows % self.width == 0
            and self.edge % LANES == 0
            and self.width % self.edge == 0
            and self.bits < SUBLANES
            and self.groups % SUBLANES == 0
        )


def params(mib):
    return pltpu.CompilerParams(vmem_limit_bytes=mib * 2**20)


def lane_sums(values):
    return jnp.sum(values, axis=0, keepdims=True)


def put_sums(out_ref, sums, start, stride, count):
    lane = lax.broadcasted_iota(jnp.int32, (1, LANES), 1)
    row = jnp.zeros((1, LANES), jnp.float32)
    for slot, value in enumerate(sums):
        width = LANES
        while width > LANES // SLOTS:
            width //= 2
            value = value + pltpu.roll(value, width, 1)
        row = jnp.where(lane // (LANES // SLOTS) == slot, value, row)
    out_ref[pl.ds(start, count, stride=stride), :] = jnp.broadcast_to(row, (count, LANES))


def totals_of(ref, start, stride, count):
    lanes = lane_sums(ref[pl.ds(start, count, stride=stride), :])
    lane = lax.broadcasted_iota(jnp.int32, (1, LANES), 1)
    return [
        jnp.sum(jnp.where(lane // (LANES // SLOTS) == slot, lanes, 0.0), axis=1, keepdims=True)
        for slot in range(SLOTS)
    ]


def scale_of(plan, squares):
    return jnp.sqrt(squares / plan.entries + epsilon)


def depart_kernel(plan, state_ref, out_ref, held_ref, semaphores):
    half = plan.rows // 2
    fetches = [
        pltpu.make_async_copy(
            state_ref.at[pl.ds(index * half, half), :], held_ref.at[pl.ds(index * half, half), :], semaphores.at[index]
        )
        for index in range(2)
    ]
    for fetch in fetches:
        fetch.start()
    sums = jnp.zeros((1, LANES), jnp.float32)
    for block in range(plan.lane_blocks):
        if block * LANES % half == 0:
            fetches[block * LANES // half].wait()
        tile = held_ref[pl.ds(block * LANES, LANES), :]
        sums = sums + lane_sums(tile * tile)
        turned = tile.T
        for piece in range(plan.pieces):
            out_ref[pl.ds(piece * plan.lane_blocks + block, plan.groups, stride=plan.inward), :] = turned[
                piece * plan.groups : (piece + 1) * plan.groups
            ]
    put_sums(out_ref, [sums], plan.body, plan.inward, plan.groups)


def fetch_slabs(plan, slabs, bits_ref, operators_ref, held_ref, semaphores):
    fetches = []
    for index, slab in enumerate(slabs):
        part, bit = divmod(slab, plan.bits)
        rows = pl.ds(part * plan.width, plan.width)
        fetch = pltpu.make_async_copy(
            operators_ref.at[bits_ref[bit], rows, :], held_ref.at[index], semaphores.at[index]
        )
        fetch.start()
        fetches.append(fetch)
    return fetches


def mask_slab(plan, slab, index, bits_ref, mask_ref, held_ref, out_ref):
    part, bit = divmod(slab, plan.bits)
    chosen = bits_ref[bit]
    for start in range(0, plan.width, plan.edge):
        across = (part * plan.width + start) // plan.edge
        rows = pl.ds(start, plan.edge)
        for along in range(plan.blocks):
            columns = pl.ds(along * plan.edge, plan.edge)
            keep = (mask_ref[chosen, across, along] > 0).astype(jnp.float32).astype(jnp.bfloat16)
            out_ref[index, columns, rows] = (held_ref[index, rows, columns] * keep).T


def store_kernel(plan, bits_ref, mask_ref, operators_ref, stored_ref, held_ref, masked_ref, in_semaphores, out_semaphores):
    slabs = range(plan.kept, plan.slabs)
    fetches = fetch_slabs(plan, slabs, bits_ref, operators_ref, held_ref, in_semaphores)
    stores = []
    for index, slab in enumerate(slabs):
        fetches[index].wait()
        mask_slab(plan, slab, index, bits_ref, mask_ref, held_ref, masked_ref)
        store = pltpu.make_async_copy(masked_ref.at[index], stored_ref.at[index], out_semaphores.at[index])
        store.start()
        stores.append(store)
    for store in stores:
        store.wait()


def prepare_kernel(
    plan,
    bits_ref,
    mask_ref,
    field_ref,
    coupling_ref,
    mode_ref,
    operators_ref,
    place_ref,
    inside_ref,
    kept_ref,
    held_ref,
    semaphores,
):
    slabs = range(plan.kept)
    fetches = fetch_slabs(plan, slabs, bits_ref, operators_ref, held_ref, semaphores)
    me = lax.axis_index("phonon")
    for position in range(plan.bits):
        me = me + (lax.axis_index("site") >> position & 1) * plan.stride(position)
    place = lax.broadcasted_iota(jnp.int32, (plan.places, LANES), 0)
    phonon = place % plan.phonons
    mode = place // plan.groups % plan.share
    level = phonon * plan.levels_here + place // (plan.groups * plan.share)
    occupied = jnp.zeros((plan.places, LANES), jnp.float32)
    for position in range(plan.bits):
        held = (place // plan.stride(position) % 2).astype(jnp.float32)
        occupied = occupied + coupling_ref[bits_ref[position]] * held
    strength = jnp.zeros((plan.places, LANES), jnp.float32)
    for index in range(plan.share):
        strength = jnp.where(mode == index, mode_ref[index * plan.groups + me], strength)
    strength = strength / jnp.sqrt(jnp.full((1, LANES), plan.level_count, jnp.float32))
    height = level.astype(jnp.float32)
    place_ref[0] = occupied
    place_ref[1] = strength * jnp.sqrt(height)
    place_ref[2] = jnp.where(level == plan.level_count - 1, 0.0, strength * jnp.sqrt(height + 1.0))
    inside = lax.broadcasted_iota(jnp.int32, (1, plan.rows), 1)
    weight = jnp.zeros((1, plan.rows), jnp.float32)
    for local_bit in range(LBITS):
        weight = weight + coupling_ref[plan.bits + local_bit] * (inside >> local_bit & 1).astype(jnp.float32)
    inside_ref[...] = jnp.zeros_like(inside_ref)
    inside_ref[:1] = weight
    for position in range(plan.bits):
        inside_ref[pl.ds(1 + position, 1)] = jnp.full((1, plan.rows), field_ref[bits_ref[position]])
    for slab in slabs:
        fetches[slab].wait()
        mask_slab(plan, slab, slab, bits_ref, mask_ref, held_ref, kept_ref)


def flipped(values, stride):
    places, width = values.shape
    if stride % SUBLANES == 0:
        shaped = values.reshape(places // (2 * stride), 2, stride, width)
        return jnp.concatenate([shaped[:, 1:], shaped[:, :1]], axis=1).reshape(places, width)
    tiles = values.reshape(places // SUBLANES, SUBLANES, width)
    if 2 * stride == SUBLANES:
        return pltpu.roll(tiles, stride, 1).reshape(places, width)
    spot = lax.broadcasted_iota(jnp.int32, tiles.shape, 1)
    down = pltpu.roll(tiles, stride, 1)
    up = pltpu.roll(tiles, SUBLANES - stride, 1)
    return jnp.where(spot & stride > 0, down, up).reshape(places, width)


def shifted(values, by):
    places, width = values.shape
    tiles = values.reshape(places // SUBLANES, SUBLANES, width)
    return pltpu.roll(tiles, by % SUBLANES, 1).reshape(places, width)


def put_rounded(plan, rounded_ref, vector, start):
    for position in range(plan.bits):
        rounded_ref[:, pl.ds(position * plan.rows + start, vector.shape[1])] = flipped(
            vector, plan.stride(position)
        ).astype(jnp.bfloat16)


def step(plan, vector_ref, rounded_ref, kept_ref, fetched_ref, place_ref, inside_ref, finish, ready=None, begun_ref=None):
    span = plan.places // plan.levels_here

    def local(start):
        lanes = pl.ds(start, LANES)
        vector = vector_ref[:, lanes]
        levels = [vector[index * span : (index + 1) * span] for index in range(plan.levels_here)]
        lower = jnp.concatenate([shifted(levels[-1], 1)] + levels[:-1], axis=0)
        upper = jnp.concatenate(levels[1:] + [shifted(levels[0], -1)], axis=0)
        weight = place_ref[0] + inside_ref[:1, lanes]
        total = weight * (place_ref[1] * lower + place_ref[2] * upper)
        for position in range(plan.bits):
            total = total + inside_ref[pl.ds(1 + position, 1), lanes] * flipped(vector, plan.stride(position))
        return total

    def added(total, part, late):
        for ref, low, high in ((kept_ref, 0, plan.kept), (fetched_ref, plan.kept, plan.slabs)):
            fetched = low > 0
            begin = max(part * plan.bits, low)
            count = min((part + 1) * plan.bits, high) - begin
            if count <= 0 or late not in (None, fetched):
                continue
            if late:
                for slab in range(begin, begin + count):
                    ready(slab)
            first = begin - part * plan.bits
            masked = ref[pl.ds(begin - low, count)].reshape(count * plan.rows, plan.width)
            operand = rounded_ref[:, pl.ds(first * plan.rows, count * plan.rows)]
            total = total + jnp.dot(operand, masked, preferred_element_type=jnp.float32)
        return total

    def locals_of(lanes):
        return jnp.concatenate([local(start) for start in range(lanes.start, lanes.start + plan.width, LANES)], axis=1)

    parts = [pl.ds(part * plan.width, plan.width) for part in range(plan.parts)]
    if ready is None:
        for part, lanes in enumerate(parts):
            finish(lanes, added(locals_of(lanes), part, None))
        return
    for part, lanes in enumerate(parts):
        begun_ref[:, lanes] = added(locals_of(lanes), part, False)
    for part, lanes in enumerate(parts):
        finish(lanes, added(begun_ref[:, lanes], part, True))


def first_kernel(
    plan,
    arrived_ref,
    place_ref,
    inside_ref,
    kept_ref,
    stored_ref,
    initial_ref,
    new_ref,
    sums_ref,
    fetched_ref,
    rounded_ref,
    ahead_ref,
    semaphores,
):
    fetches = {}
    for slab in range(plan.kept, plan.slabs):
        index = slab - plan.kept
        fetches[slab] = pltpu.make_async_copy(stored_ref.at[index], fetched_ref.at[index], semaphores.at[index])
        fetches[slab].start()

    def ready(slab):
        fetches[slab].wait()

    squares = totals_of(arrived_ref, plan.body, plan.inward, plan.groups)[0]
    inverse = 1.0 / scale_of(plan, squares)
    for block in range(plan.lane_blocks):
        parts = [
            arrived_ref[pl.ds(piece * plan.lane_blocks + block, plan.groups, stride=plan.inward), :]
            for piece in range(plan.pieces)
        ]
        vector = jnp.concatenate(parts, axis=0) * inverse
        initial_ref[:, pl.ds(block * LANES, LANES)] = vector
        put_rounded(plan, rounded_ref, vector, block * LANES)
    tables = (kept_ref, fetched_ref, place_ref, inside_ref)
    squares = []
    overlap = []
    ahead = []

    def finish(lanes, new):
        new_ref[:, lanes] = new
        put_rounded(plan, ahead_ref, new, lanes.start)
        squares.append(lane_sums(new * new))
        overlap.append(lane_sums(new * initial_ref[:, lanes]))

    def look_ahead(lanes, total):
        new = 2.0 * total - initial_ref[:, lanes]
        ahead.append(lane_sums(new * new))

    step(plan, initial_ref, rounded_ref, *tables, finish, ready, new_ref)
    step(plan, new_ref, ahead_ref, *tables, look_ahead)
    put_sums(sums_ref, [one_row(squares), one_row(overlap), one_row(ahead)], 0, 1, plan.groups)


def one_row(rows):
    total = sum(rows[1:], rows[0])
    return sum(total[:, start : start + LANES] for start in range(0, total.shape[1], LANES))


def onward_kernel(
    plan,
    arrived_ref,
    raw_ref,
    initial_ref,
    place_ref,
    inside_ref,
    kept_ref,
    fetched_ref,
    out_ref,
    known_ref,
    rounded_ref,
    ahead_ref,
    second_ref,
    third_ref,
):
    squares, overlap, ahead, _ = totals_of(arrived_ref, 0, 1, plan.groups)
    first = 1.0 / scale_of(plan, squares)
    estimate = scale_of(plan, ahead * first * first)
    second = 1.0 / estimate
    known_ref[:1, :] = jnp.broadcast_to(overlap * first / plan.entries, (1, LANES))
    known_ref[1:, :] = jnp.broadcast_to(estimate, (SUBLANES - 1, LANES))
    for block in range(plan.lane_blocks):
        lanes = pl.ds(block * LANES, LANES)
        vector = raw_ref[:, lanes] * first
        second_ref[:, lanes] = vector
        put_rounded(plan, rounded_ref, vector, block * LANES)
    tables = (kept_ref, fetched_ref, place_ref, inside_ref)
    sums = [[] for _ in range(SLOTS)]

    def send(vector, lanes, new):
        sums[2 * vector].append(lane_sums(new * new))
        sums[2 * vector + 1].append(lane_sums(new * initial_ref[:, lanes]))
        for start in range(0, plan.width, LANES):
            block = (lanes.start + start) // LANES
            for piece in range(plan.pieces):
                row = vector * plan.body + piece * plan.lane_blocks + block
                out_ref[pl.ds(row, plan.groups, stride=plan.outward), :] = new[
                    piece * plan.groups : (piece + 1) * plan.groups, start : start + LANES
                ]

    def finish_second(lanes, total):
        new = 2.0 * total - initial_ref[:, lanes] * first
        vector = new * second
        third_ref[:, lanes] = vector
        put_rounded(plan, ahead_ref, vector, lanes.start)
        send(0, lanes, new)

    def finish_third(lanes, total):
        send(1, lanes, 2.0 * total - second_ref[:, lanes] * second)

    step(plan, second_ref, rounded_ref, *tables, finish_second)
    step(plan, third_ref, ahead_ref, *tables, finish_third)
    put_sums(out_ref, [one_row(rows) for rows in sums], 2 * plan.body, plan.outward, plan.groups)


def arrive_kernel(plan, arrived_ref, known_ref, before_ref, last_ref, moments_ref):
    before_squares, before_overlap, last_squares, last_overlap = totals_of(
        arrived_ref, 2 * plan.body, plan.outward, plan.groups
    )
    before = 1.0 / scale_of(plan, before_squares)
    back = known_ref[1:2, :1] * before
    last = back / scale_of(plan, last_squares * back * back)
    for vector, (out_ref, factor) in enumerate(((before_ref, before), (last_ref, last))):
        for block in range(plan.lane_blocks):
            first = vector * plan.body + block
            parts = [
                arrived_ref[pl.ds(first + piece * plan.lane_blocks, plan.groups, stride=plan.outward), :]
                for piece in range(plan.pieces)
            ]
            out_ref[pl.ds(block * LANES, LANES), :] = jnp.concatenate(parts, axis=0).T * factor
    moments_ref[0] = known_ref[0, 0]
    moments_ref[1] = (before_overlap * before / plan.entries)[0, 0]
    moments_ref[2] = (last_overlap * last / plan.entries)[0, 0]


def exchange(plan, values):
    shaped = values.reshape(plan.groups, values.shape[0] // plan.groups, 1, LANES)
    return lax.all_to_all(shaped, AXES, 0, 0, axis_index_groups=[plan.order()], tiled=True).reshape(values.shape)


def shards(plan, state, operators, op_mask, site_bits, field, site_coupling, mode_coupling):
    f32 = jnp.float32
    inward = jax.ShapeDtypeStruct((plan.groups * plan.inward, LANES), f32)
    outward = jax.ShapeDtypeStruct((plan.groups * plan.outward, LANES), f32)
    vector = jax.ShapeDtypeStruct((plan.places, plan.rows), f32)
    known = jax.ShapeDtypeStruct((SUBLANES, LANES), f32)
    held = jax.ShapeDtypeStruct((plan.rows, plan.columns), f32)
    rounded = pltpu.VMEM((plan.places, plan.bits * plan.rows), jnp.bfloat16)
    working = pltpu.VMEM((plan.places, plan.rows), f32)
    work = 2 * plan.bits * plan.places * plan.rows * plan.rows

    def cost(flops, moved):
        return pl.CostEstimate(flops=flops, bytes_accessed=moved, transcendentals=0)

    departing = pl.pallas_call(
        functools.partial(depart_kernel, plan),
        out_shape=inward,
        in_specs=[HBM],
        out_specs=VMEM,
        scratch_shapes=[pltpu.VMEM((plan.rows, plan.columns), f32), pltpu.SemaphoreType.DMA((2,))],
        compiler_params=params(60),
        name="depart",
    )(state)
    arrived = exchange(plan, departing)
    fetched = plan.slabs - plan.kept
    kept_slabs = (plan.kept, plan.rows, plan.width)
    fetched_slabs = (fetched, plan.rows, plan.width)

    def held_slabs(count):
        return pltpu.VMEM((count, plan.width, plan.rows), jnp.bfloat16)

    place, inside, kept = pl.pallas_call(
        functools.partial(prepare_kernel, plan),
        out_shape=[
            jax.ShapeDtypeStruct((3, plan.places, LANES), f32),
            jax.ShapeDtypeStruct((SUBLANES, plan.rows), f32),
            jax.ShapeDtypeStruct(kept_slabs, jnp.bfloat16),
        ],
        in_specs=[SMEM] * 5 + [HBM],
        out_specs=[VMEM] * 3,
        scratch_shapes=[held_slabs(plan.kept), pltpu.SemaphoreType.DMA((plan.kept,))],
        compiler_params=params(50),
        cost_estimate=cost(plan.rows * plan.rows, 4 * plan.kept * plan.rows * plan.width),
        name="prepare",
    )(site_bits, op_mask, field, site_coupling, mode_coupling, operators)
    stored = pl.pallas_call(
        functools.partial(store_kernel, plan),
        out_shape=jax.ShapeDtypeStruct(fetched_slabs, jnp.bfloat16),
        in_specs=[SMEM] * 2 + [HBM],
        out_specs=HBM,
        scratch_shapes=[
            held_slabs(fetched),
            pltpu.VMEM(fetched_slabs, jnp.bfloat16),
            pltpu.SemaphoreType.DMA((fetched,)),
            pltpu.SemaphoreType.DMA((fetched,)),
        ],
        compiler_params=params(60),
        cost_estimate=cost(plan.rows * plan.rows, 4 * fetched * plan.rows * plan.width),
        name="store",
    )(site_bits, op_mask, operators)
    initial, raw, sums, late = pl.pallas_call(
        functools.partial(first_kernel, plan),
        out_shape=[
            vector,
            vector,
            jax.ShapeDtypeStruct((plan.groups, LANES), f32),
            jax.ShapeDtypeStruct(fetched_slabs, jnp.bfloat16),
        ],
        in_specs=[VMEM] * 4 + [HBM],
        out_specs=[VMEM] * 4,
        scratch_shapes=[rounded, rounded, pltpu.SemaphoreType.DMA((fetched,))],
        compiler_params=params(46),
        cost_estimate=cost(2 * work, 4 * plan.places * plan.rows),
        name="first",
    )(arrived, place, inside, kept, stored)
    tables = (place, inside, kept, late)
    sums = exchange(plan, sums)
    departing, told = pl.pallas_call(
        functools.partial(onward_kernel, plan),
        out_shape=[outward, known],
        in_specs=[VMEM] * 7,
        out_specs=[VMEM] * 2,
        scratch_shapes=[rounded, rounded, working, working],
        compiler_params=params(32),
        cost_estimate=cost(2 * work, 8 * plan.places * plan.rows),
        name="onward",
    )(sums, raw, initial, *tables)
    arrived = exchange(plan, departing)
    before, last, moments = pl.pallas_call(
        functools.partial(arrive_kernel, plan),
        out_shape=[held, held, jax.ShapeDtypeStruct((STEPS,), f32)],
        in_specs=[VMEM] * 2,
        out_specs=[VMEM, VMEM, SMEM],
        compiler_params=params(16),
        name="arrive",
    )(arrived, told)
    return last, before, moments


def extended_2(block, sides, width):
    for axis, dim in sides:
        count = lax.axis_size(axis)
        forward = [(i, i + 1) for i in range(count - 1)]
        backward = [(target, source) for source, target in forward]
        low = lax.ppermute(
            lax.slice_in_dim(block, block.shape[dim] - width, None, axis=dim), axis, forward
        )
        high = lax.ppermute(lax.slice_in_dim(block, 0, width, axis=dim), axis, backward)
        block = jnp.concatenate([low, block, high], axis=dim)
    return block


def partner(value, axis, bit):
    mask = 2**bit
    pairs = [(source, source ^ mask) for source in range(lax.axis_size(axis))]
    return lax.ppermute(value, axis, pairs)


def halo_shards(state, operators, op_mask, site_bits, field, site_coupling, mode_coupling):
    site_count = lax.axis_size("site")
    phonon_count = lax.axis_size("phonon")
    bit_count = site_count.bit_length() - 1
    rows_here = state.shape[0]
    columns_here = state.shape[1]
    levels_here = columns_here // MODES
    block_edge = rows_here // op_mask.shape[1]
    expanded = jnp.repeat(jnp.repeat(op_mask, block_edge, axis=1), block_edge, axis=2)
    masked = jnp.where(expanded > 0, operators, jnp.zeros((), jnp.bfloat16))
    entries = jnp.float32(rows_here * columns_here * site_count * phonon_count)
    level_total = jnp.sqrt(jnp.float32(levels_here * phonon_count))
    device = lax.axis_index("site")
    inside = lax.iota(jnp.int32, rows_here)
    weight_rows = jnp.zeros((rows_here,), jnp.float32)
    for position in range(bit_count):
        weight_rows = weight_rows + site_coupling[site_bits[position]] * (
            device >> position & 1
        ).astype(jnp.float32)
    for local_bit in range(LBITS):
        weight_rows = weight_rows + site_coupling[bit_count + local_bit] * (
            inside >> local_bit & 1
        ).astype(jnp.float32)
    levels = (
        lax.axis_index("phonon") * levels_here + lax.iota(jnp.int32, columns_here) // MODES
    ).astype(jnp.float32)
    lower_weight = jnp.sqrt(levels)
    upper_weight = jnp.sqrt(levels + 1.0)
    mode_weight = jnp.tile(mode_coupling, columns_here // MODES) / level_total
    start_squares = lax.psum(jnp.sum(state * state), ("site", "phonon"))
    initial = state / jnp.sqrt(start_squares / entries + epsilon)
    previous = initial
    current = initial
    scale_prev = jnp.float32(1.0)
    moments = []
    for iteration in range(STEPS):
        extended = extended_2(current, (("phonon", 1),), MODES)
        lower_part = extended[:, :columns_here]
        upper_part = extended[:, 2 * MODES :]
        summed = weight_rows[:, None] * (
            mode_weight * (lower_weight * lower_part + upper_weight * upper_part)
        )
        for operate_position in range(bit_count):
            chosen = site_bits[operate_position]
            flipped = partner(current, "site", operate_position)
            product = jnp.dot(
                masked[chosen], flipped.astype(jnp.bfloat16), preferred_element_type=jnp.float32
            )
            summed = summed + (field[chosen] * flipped + product)
        if iteration == 0:
            vector_new = summed
        else:
            vector_new = 2.0 * summed - previous / scale_prev
        squares, intersection = lax.psum(
            (jnp.sum(vector_new * vector_new), jnp.sum(initial * vector_new)), ("site", "phonon")
        )
        scale_now = jnp.sqrt(squares / entries + epsilon)
        updated = vector_new / scale_now
        moment = intersection / (entries * scale_now)
        moments.append(moment)
        previous = current
        current = updated
        scale_prev = scale_now
    return (current, previous, jnp.stack(moments))


def solution(mesh):
    in_specs = (P("site", "phonon"), P(), P(), P(), P(), P(), P())
    out_specs = (P("site", "phonon"), P("site", "phonon"), P())

    def whole(state, operators, op_mask, *rest):
        rows = state.shape[0] // mesh.shape["site"]
        columns = state.shape[1] // mesh.shape["phonon"]
        plan = Plan(mesh, rows, columns, op_mask.shape[1])
        body = functools.partial(shards, plan) if plan.fits() else halo_shards
        run = jax.shard_map(body, mesh=mesh, in_specs=in_specs, out_specs=out_specs, check_vma=False)
        return run(state, operators, op_mask, *rest)

    return whole
```

```python
import functools

import jax
import jax.numpy as jnp
from jax import lax
from jax.experimental import pallas as pl
from jax.experimental.pallas import tpu as pltpu
from jax.sharding import PartitionSpec as P

LBITS = 10
MODES = 64
STEPS = 3
LANES = 128
SUBLANES = 8
SLOTS = 4
AXES = ("site", "phonon")

epsilon = 1e-06


VMEM = pl.BlockSpec(memory_space=pltpu.VMEM)
SMEM = pl.BlockSpec(memory_space=pltpu.SMEM)
HBM = pl.BlockSpec(memory_space=pltpu.HBM)


class Plan:
    def __init__(self, mesh, rows, columns, blocks):
        self.sites = mesh.shape["site"]
        self.phonons = mesh.shape["phonon"]
        self.groups = self.sites * self.phonons
        self.bits = self.sites.bit_length() - 1
        self.rows = rows
        self.columns = columns
        self.blocks = blocks
        self.edge = rows // blocks
        self.levels_here = columns // MODES
        self.level_count = self.levels_here * self.phonons
        self.share = MODES // self.groups
        self.pieces = self.levels_here * self.share
        self.lane_blocks = rows // LANES
        self.body = self.pieces * self.lane_blocks
        self.inward = self.body + 1
        self.outward = 2 * self.body + 1
        self.places = self.pieces * self.groups
        self.width = 2 * LANES
        self.parts = rows // self.width
        self.slabs = self.bits * self.parts
        self.kept = min(5, self.slabs - 1)
        self.entries = float(rows * columns * self.groups)

    def fits(self):
        return (
            MODES % self.groups == 0
            and self.columns == LANES
            and self.rows % self.width == 0
            and self.edge % LANES == 0
            and self.width % self.edge == 0
            and self.bits < SUBLANES
            and self.groups % SUBLANES == 0
        )


def params(mib):
    return pltpu.CompilerParams(vmem_limit_bytes=mib * 2**20)


def lane_sums(values):
    return jnp.sum(values, axis=0, keepdims=True)


def put_sums(out_ref, sums, start, stride, count):
    lane = lax.broadcasted_iota(jnp.int32, (1, LANES), 1)
    row = jnp.zeros((1, LANES), jnp.float32)
    for slot, value in enumerate(sums):
        width = LANES
        while width > LANES // SLOTS:
            width //= 2
            value = value + pltpu.roll(value, width, 1)
        row = jnp.where(lane // (LANES // SLOTS) == slot, value, row)
    out_ref[pl.ds(start, count, stride=stride), :] = jnp.broadcast_to(row, (count, LANES))


def totals_of(ref, start, stride, count):
    lanes = lane_sums(ref[pl.ds(start, count, stride=stride), :])
    lane = lax.broadcasted_iota(jnp.int32, (1, LANES), 1)
    return [
        jnp.sum(jnp.where(lane // (LANES // SLOTS) == slot, lanes, 0.0), axis=1, keepdims=True)
        for slot in range(SLOTS)
    ]


def scale_of(plan, squares):
    return jnp.sqrt(squares / plan.entries + epsilon)


def depart_kernel(plan, state_ref, out_ref, held_ref, semaphores):
    half = plan.rows // 2
    fetches = [
        pltpu.make_async_copy(
            state_ref.at[pl.ds(index * half, half), :], held_ref.at[pl.ds(index * half, half), :], semaphores.at[index]
        )
        for index in range(2)
    ]
    for index, fetch in enumerate(fetches):
        fetch.start(priority=index)
    sums = jnp.zeros((1, LANES), jnp.float32)
    for block in range(plan.lane_blocks):
        if block * LANES % half == 0:
            fetches[block * LANES // half].wait()
        tile = held_ref[pl.ds(block * LANES, LANES), :]
        sums = sums + lane_sums(tile * tile)
        turned = tile.T
        for piece in range(plan.pieces):
            out_ref[pl.ds(piece * plan.lane_blocks + block, plan.groups, stride=plan.inward), :] = turned[
                piece * plan.groups : (piece + 1) * plan.groups
            ]
    put_sums(out_ref, [sums], plan.body, plan.inward, plan.groups)


def fetch_slabs(plan, slabs, bits_ref, operators_ref, held_ref, semaphores):
    fetches = []
    for index, slab in enumerate(slabs):
        part, bit = divmod(slab, plan.bits)
        rows = pl.ds(part * plan.width, plan.width)
        fetch = pltpu.make_async_copy(
            operators_ref.at[bits_ref[bit], rows, :], held_ref.at[index], semaphores.at[index]
        )
        fetch.start()
        fetches.append(fetch)
    return fetches


def mask_slab(plan, slab, index, bits_ref, mask_ref, held_ref, out_ref):
    part, bit = divmod(slab, plan.bits)
    chosen = bits_ref[bit]
    for start in range(0, plan.width, plan.edge):
        across = (part * plan.width + start) // plan.edge
        rows = pl.ds(start, plan.edge)
        for along in range(plan.blocks):
            columns = pl.ds(along * plan.edge, plan.edge)
            keep = (mask_ref[chosen, across, along] > 0).astype(jnp.float32).astype(jnp.bfloat16)
            out_ref[index, columns, rows] = (held_ref[index, rows, columns] * keep).T


def store_kernel(plan, bits_ref, mask_ref, operators_ref, stored_ref, held_ref, masked_ref, in_semaphores, out_semaphores):
    slabs = range(plan.kept, plan.slabs)
    fetches = fetch_slabs(plan, slabs, bits_ref, operators_ref, held_ref, in_semaphores)
    stores = []
    for index, slab in enumerate(slabs):
        fetches[index].wait()
        mask_slab(plan, slab, index, bits_ref, mask_ref, held_ref, masked_ref)
        store = pltpu.make_async_copy(masked_ref.at[index], stored_ref.at[index], out_semaphores.at[index])
        store.start()
        stores.append(store)
    for store in stores:
        store.wait()


def prepare_kernel(
    plan,
    bits_ref,
    mask_ref,
    field_ref,
    coupling_ref,
    mode_ref,
    operators_ref,
    place_ref,
    inside_ref,
    kept_ref,
    held_ref,
    semaphores,
):
    slabs = range(plan.kept)
    fetches = fetch_slabs(plan, slabs, bits_ref, operators_ref, held_ref, semaphores)
    me = lax.axis_index("site") * plan.phonons + lax.axis_index("phonon")
    place = lax.broadcasted_iota(jnp.int32, (plan.places, LANES), 0)
    phonon = place % plan.phonons
    site = place // plan.phonons % plan.sites
    mode = place // plan.groups % plan.share
    level = phonon * plan.levels_here + place // (plan.groups * plan.share)
    occupied = jnp.zeros((plan.places, LANES), jnp.float32)
    for position in range(plan.bits):
        held = (site >> position & 1).astype(jnp.float32)
        occupied = occupied + coupling_ref[bits_ref[position]] * held
    strength = jnp.zeros((plan.places, LANES), jnp.float32)
    for index in range(plan.share):
        strength = jnp.where(mode == index, mode_ref[index * plan.groups + me], strength)
    strength = strength / jnp.sqrt(jnp.full((1, LANES), plan.level_count, jnp.float32))
    height = level.astype(jnp.float32)
    place_ref[0] = occupied
    place_ref[1] = strength * jnp.sqrt(height)
    place_ref[2] = jnp.where(level == plan.level_count - 1, 0.0, strength * jnp.sqrt(height + 1.0))
    inside = lax.broadcasted_iota(jnp.int32, (1, plan.rows), 1)
    weight = jnp.zeros((1, plan.rows), jnp.float32)
    for local_bit in range(LBITS):
        weight = weight + coupling_ref[plan.bits + local_bit] * (inside >> local_bit & 1).astype(jnp.float32)
    inside_ref[...] = jnp.zeros_like(inside_ref)
    inside_ref[:1] = weight
    for position in range(plan.bits):
        inside_ref[pl.ds(1 + position, 1)] = jnp.full((1, plan.rows), field_ref[bits_ref[position]])
    for slab in slabs:
        fetches[slab].wait()
        mask_slab(plan, slab, slab, bits_ref, mask_ref, held_ref, kept_ref)


def flipped(values, stride):
    places, width = values.shape
    if stride % SUBLANES == 0:
        shaped = values.reshape(places // (2 * stride), 2, stride, width)
        return jnp.concatenate([shaped[:, 1:], shaped[:, :1]], axis=1).reshape(places, width)
    tiles = values.reshape(places // SUBLANES, SUBLANES, width)
    if 2 * stride == SUBLANES:
        return pltpu.roll(tiles, stride, 1).reshape(places, width)
    spot = lax.broadcasted_iota(jnp.int32, tiles.shape, 1)
    down = pltpu.roll(tiles, stride, 1)
    up = pltpu.roll(tiles, SUBLANES - stride, 1)
    return jnp.where(spot & stride > 0, down, up).reshape(places, width)


def shifted(values, by):
    places, width = values.shape
    tiles = values.reshape(places // SUBLANES, SUBLANES, width)
    return pltpu.roll(tiles, by % SUBLANES, 1).reshape(places, width)


def put_rounded(plan, rounded_ref, vector, start):
    for position in range(plan.bits):
        rounded_ref[:, pl.ds(position * plan.rows + start, vector.shape[1])] = flipped(
            vector, plan.phonons << position
        ).astype(jnp.bfloat16)


def step(plan, vector_ref, rounded_ref, kept_ref, fetched_ref, place_ref, inside_ref, finish, ready=None, begun_ref=None):
    span = plan.places // plan.levels_here

    def local(start):
        lanes = pl.ds(start, LANES)
        vector = vector_ref[:, lanes]
        levels = [vector[index * span : (index + 1) * span] for index in range(plan.levels_here)]
        lower = jnp.concatenate([shifted(levels[-1], 1)] + levels[:-1], axis=0)
        upper = jnp.concatenate(levels[1:] + [shifted(levels[0], -1)], axis=0)
        weight = place_ref[0] + inside_ref[:1, lanes]
        total = weight * (place_ref[1] * lower + place_ref[2] * upper)
        for position in range(plan.bits):
            total = total + inside_ref[pl.ds(1 + position, 1), lanes] * flipped(vector, plan.phonons << position)
        return total

    def added(total, part, late):
        for ref, low, high in ((kept_ref, 0, plan.kept), (fetched_ref, plan.kept, plan.slabs)):
            fetched = low > 0
            begin = max(part * plan.bits, low)
            count = min((part + 1) * plan.bits, high) - begin
            if count <= 0 or late not in (None, fetched):
                continue
            if late:
                for slab in range(begin, begin + count):
                    ready(slab)
            first = begin - part * plan.bits
            masked = ref[pl.ds(begin - low, count)].reshape(count * plan.rows, plan.width)
            operand = rounded_ref[:, pl.ds(first * plan.rows, count * plan.rows)]
            total = total + jnp.dot(operand, masked, preferred_element_type=jnp.float32)
        return total

    def locals_of(lanes):
        return jnp.concatenate([local(start) for start in range(lanes.start, lanes.start + plan.width, LANES)], axis=1)

    parts = [pl.ds(part * plan.width, plan.width) for part in range(plan.parts)]
    if ready is None:
        for part, lanes in enumerate(parts):
            finish(lanes, added(locals_of(lanes), part, None))
        return
    for part, lanes in enumerate(parts):
        begun_ref[:, lanes] = added(locals_of(lanes), part, False)
    for part, lanes in enumerate(parts):
        finish(lanes, added(begun_ref[:, lanes], part, True))


def first_kernel(
    plan,
    arrived_ref,
    place_ref,
    inside_ref,
    kept_ref,
    stored_ref,
    initial_ref,
    new_ref,
    sums_ref,
    fetched_ref,
    rounded_ref,
    ahead_ref,
    semaphores,
):
    fetches = {}
    for slab in range(plan.kept, plan.slabs):
        index = slab - plan.kept
        fetches[slab] = pltpu.make_async_copy(stored_ref.at[index], fetched_ref.at[index], semaphores.at[index])
        fetches[slab].start(priority=index % 2)

    def ready(slab):
        fetches[slab].wait()

    squares = totals_of(arrived_ref, plan.body, plan.inward, plan.groups)[0]
    inverse = 1.0 / scale_of(plan, squares)
    for block in range(plan.lane_blocks):
        parts = [
            arrived_ref[pl.ds(piece * plan.lane_blocks + block, plan.groups, stride=plan.inward), :]
            for piece in range(plan.pieces)
        ]
        vector = jnp.concatenate(parts, axis=0) * inverse
        initial_ref[:, pl.ds(block * LANES, LANES)] = vector
        put_rounded(plan, rounded_ref, vector, block * LANES)
    tables = (kept_ref, fetched_ref, place_ref, inside_ref)
    squares = []
    overlap = []
    ahead = []

    def finish(lanes, new):
        new_ref[:, lanes] = new
        put_rounded(plan, ahead_ref, new, lanes.start)
        squares.append(lane_sums(new * new))
        overlap.append(lane_sums(new * initial_ref[:, lanes]))

    def look_ahead(lanes, total):
        new = 2.0 * total - initial_ref[:, lanes]
        ahead.append(lane_sums(new * new))

    step(plan, initial_ref, rounded_ref, *tables, finish, ready, new_ref)
    step(plan, new_ref, ahead_ref, *tables, look_ahead)
    put_sums(sums_ref, [one_row(squares), one_row(overlap), one_row(ahead)], 0, 1, plan.groups)


def one_row(rows):
    total = sum(rows[1:], rows[0])
    return sum(total[:, start : start + LANES] for start in range(0, total.shape[1], LANES))


def onward_kernel(
    plan,
    arrived_ref,
    raw_ref,
    initial_ref,
    place_ref,
    inside_ref,
    kept_ref,
    fetched_ref,
    out_ref,
    known_ref,
    rounded_ref,
    ahead_ref,
    second_ref,
    third_ref,
):
    squares, overlap, ahead, _ = totals_of(arrived_ref, 0, 1, plan.groups)
    first = 1.0 / scale_of(plan, squares)
    estimate = scale_of(plan, ahead * first * first)
    second = 1.0 / estimate
    known_ref[:1, :] = jnp.broadcast_to(overlap * first / plan.entries, (1, LANES))
    known_ref[1:, :] = jnp.broadcast_to(estimate, (SUBLANES - 1, LANES))
    for block in range(plan.lane_blocks):
        lanes = pl.ds(block * LANES, LANES)
        vector = raw_ref[:, lanes] * first
        second_ref[:, lanes] = vector
        put_rounded(plan, rounded_ref, vector, block * LANES)
    tables = (kept_ref, fetched_ref, place_ref, inside_ref)
    sums = [[] for _ in range(SLOTS)]

    def send(vector, lanes, new):
        sums[2 * vector].append(lane_sums(new * new))
        sums[2 * vector + 1].append(lane_sums(new * initial_ref[:, lanes]))
        for start in range(0, plan.width, LANES):
            block = (lanes.start + start) // LANES
            for piece in range(plan.pieces):
                row = vector * plan.body + piece * plan.lane_blocks + block
                out_ref[pl.ds(row, plan.groups, stride=plan.outward), :] = new[
                    piece * plan.groups : (piece + 1) * plan.groups, start : start + LANES
                ]

    def finish_second(lanes, total):
        new = 2.0 * total - initial_ref[:, lanes] * first
        vector = new * second
        third_ref[:, lanes] = vector
        put_rounded(plan, ahead_ref, vector, lanes.start)
        send(0, lanes, new)

    def finish_third(lanes, total):
        send(1, lanes, 2.0 * total - second_ref[:, lanes] * second)

    step(plan, second_ref, rounded_ref, *tables, finish_second)
    step(plan, third_ref, ahead_ref, *tables, finish_third)
    put_sums(out_ref, [one_row(rows) for rows in sums], 2 * plan.body, plan.outward, plan.groups)


def arrive_kernel(plan, arrived_ref, known_ref, before_ref, last_ref, moments_ref):
    before_squares, before_overlap, last_squares, last_overlap = totals_of(
        arrived_ref, 2 * plan.body, plan.outward, plan.groups
    )
    before = 1.0 / scale_of(plan, before_squares)
    back = known_ref[1:2, :1] * before
    last = back / scale_of(plan, last_squares * back * back)
    for vector, (out_ref, factor) in enumerate(((before_ref, before), (last_ref, last))):
        for block in range(plan.lane_blocks):
            first = vector * plan.body + block
            parts = [
                arrived_ref[pl.ds(first + piece * plan.lane_blocks, plan.groups, stride=plan.outward), :]
                for piece in range(plan.pieces)
            ]
            out_ref[pl.ds(block * LANES, LANES), :] = jnp.concatenate(parts, axis=0).T * factor
    moments_ref[0] = known_ref[0, 0]
    moments_ref[1] = (before_overlap * before / plan.entries)[0, 0]
    moments_ref[2] = (last_overlap * last / plan.entries)[0, 0]


def exchange(values, count):
    shaped = values.reshape(count, values.shape[0] // count, 1, LANES)
    return lax.all_to_all(shaped, AXES, 0, 0, tiled=True).reshape(values.shape)


def shards(plan, state, operators, op_mask, site_bits, field, site_coupling, mode_coupling):
    f32 = jnp.float32
    inward = jax.ShapeDtypeStruct((plan.groups * plan.inward, LANES), f32)
    outward = jax.ShapeDtypeStruct((plan.groups * plan.outward, LANES), f32)
    vector = jax.ShapeDtypeStruct((plan.places, plan.rows), f32)
    known = jax.ShapeDtypeStruct((SUBLANES, LANES), f32)
    held = jax.ShapeDtypeStruct((plan.rows, plan.columns), f32)
    rounded = pltpu.VMEM((plan.places, plan.bits * plan.rows), jnp.bfloat16)
    working = pltpu.VMEM((plan.places, plan.rows), f32)
    work = 2 * plan.bits * plan.places * plan.rows * plan.rows

    def cost(flops, moved):
        return pl.CostEstimate(flops=flops, bytes_accessed=moved, transcendentals=0)

    departing = pl.pallas_call(
        functools.partial(depart_kernel, plan),
        out_shape=inward,
        in_specs=[HBM],
        out_specs=VMEM,
        scratch_shapes=[pltpu.VMEM((plan.rows, plan.columns), f32), pltpu.SemaphoreType.DMA((2,))],
        compiler_params=params(60),
        name="depart",
    )(state)
    arrived = exchange(departing, plan.groups)
    fetched = plan.slabs - plan.kept
    kept_slabs = (plan.kept, plan.rows, plan.width)
    fetched_slabs = (fetched, plan.rows, plan.width)

    def held_slabs(count):
        return pltpu.VMEM((count, plan.width, plan.rows), jnp.bfloat16)

    place, inside, kept = pl.pallas_call(
        functools.partial(prepare_kernel, plan),
        out_shape=[
            jax.ShapeDtypeStruct((3, plan.places, LANES), f32),
            jax.ShapeDtypeStruct((SUBLANES, plan.rows), f32),
            jax.ShapeDtypeStruct(kept_slabs, jnp.bfloat16),
        ],
        in_specs=[SMEM] * 5 + [HBM],
        out_specs=[VMEM] * 3,
        scratch_shapes=[held_slabs(plan.kept), pltpu.SemaphoreType.DMA((plan.kept,))],
        compiler_params=params(50),
        cost_estimate=cost(plan.rows * plan.rows, 4 * plan.kept * plan.rows * plan.width),
        name="prepare",
    )(site_bits, op_mask, field, site_coupling, mode_coupling, operators)
    stored = pl.pallas_call(
        functools.partial(store_kernel, plan),
        out_shape=jax.ShapeDtypeStruct(fetched_slabs, jnp.bfloat16),
        in_specs=[SMEM] * 2 + [HBM],
        out_specs=HBM,
        scratch_shapes=[
            held_slabs(fetched),
            pltpu.VMEM(fetched_slabs, jnp.bfloat16),
            pltpu.SemaphoreType.DMA((fetched,)),
            pltpu.SemaphoreType.DMA((fetched,)),
        ],
        compiler_params=params(60),
        cost_estimate=cost(plan.rows * plan.rows, 4 * fetched * plan.rows * plan.width),
        name="store",
    )(site_bits, op_mask, operators)
    initial, raw, sums, late = pl.pallas_call(
        functools.partial(first_kernel, plan),
        out_shape=[
            vector,
            vector,
            jax.ShapeDtypeStruct((plan.groups, LANES), f32),
            jax.ShapeDtypeStruct(fetched_slabs, jnp.bfloat16),
        ],
        in_specs=[VMEM] * 4 + [HBM],
        out_specs=[VMEM] * 4,
        scratch_shapes=[rounded, rounded, pltpu.SemaphoreType.DMA((fetched,))],
        compiler_params=params(46),
        cost_estimate=cost(2 * work, 4 * plan.places * plan.rows),
        name="first",
    )(arrived, place, inside, kept, stored)
    tables = (place, inside, kept, late)
    sums = exchange(sums, plan.groups)
    departing, told = pl.pallas_call(
        functools.partial(onward_kernel, plan),
        out_shape=[outward, known],
        in_specs=[VMEM] * 7,
        out_specs=[VMEM] * 2,
        scratch_shapes=[rounded, rounded, working, working],
        compiler_params=params(32),
        cost_estimate=cost(2 * work, 8 * plan.places * plan.rows),
        name="onward",
    )(sums, raw, initial, *tables)
    arrived = exchange(departing, plan.groups)
    before, last, moments = pl.pallas_call(
        functools.partial(arrive_kernel, plan),
        out_shape=[held, held, jax.ShapeDtypeStruct((STEPS,), f32)],
        in_specs=[VMEM] * 2,
        out_specs=[VMEM, VMEM, SMEM],
        compiler_params=params(16),
        name="arrive",
    )(arrived, told)
    return last, before, moments


def extended_2(block, sides, width):
    for axis, dim in sides:
        count = lax.axis_size(axis)
        forward = [(i, i + 1) for i in range(count - 1)]
        backward = [(target, source) for source, target in forward]
        low = lax.ppermute(
            lax.slice_in_dim(block, block.shape[dim] - width, None, axis=dim), axis, forward
        )
        high = lax.ppermute(lax.slice_in_dim(block, 0, width, axis=dim), axis, backward)
        block = jnp.concatenate([low, block, high], axis=dim)
    return block


def partner(value, axis, bit):
    mask = 2**bit
    pairs = [(source, source ^ mask) for source in range(lax.axis_size(axis))]
    return lax.ppermute(value, axis, pairs)


def halo_shards(state, operators, op_mask, site_bits, field, site_coupling, mode_coupling):
    site_count = lax.axis_size("site")
    phonon_count = lax.axis_size("phonon")
    bit_count = site_count.bit_length() - 1
    rows_here = state.shape[0]
    columns_here = state.shape[1]
    levels_here = columns_here // MODES
    block_edge = rows_here // op_mask.shape[1]
    expanded = jnp.repeat(jnp.repeat(op_mask, block_edge, axis=1), block_edge, axis=2)
    masked = jnp.where(expanded > 0, operators, jnp.zeros((), jnp.bfloat16))
    entries = jnp.float32(rows_here * columns_here * site_count * phonon_count)
    level_total = jnp.sqrt(jnp.float32(levels_here * phonon_count))
    device = lax.axis_index("site")
    inside = lax.iota(jnp.int32, rows_here)
    weight_rows = jnp.zeros((rows_here,), jnp.float32)
    for position in range(bit_count):
        weight_rows = weight_rows + site_coupling[site_bits[position]] * (
            device >> position & 1
        ).astype(jnp.float32)
    for local_bit in range(LBITS):
        weight_rows = weight_rows + site_coupling[bit_count + local_bit] * (
            inside >> local_bit & 1
        ).astype(jnp.float32)
    levels = (
        lax.axis_index("phonon") * levels_here + lax.iota(jnp.int32, columns_here) // MODES
    ).astype(jnp.float32)
    lower_weight = jnp.sqrt(levels)
    upper_weight = jnp.sqrt(levels + 1.0)
    mode_weight = jnp.tile(mode_coupling, columns_here // MODES) / level_total
    start_squares = lax.psum(jnp.sum(state * state), ("site", "phonon"))
    initial = state / jnp.sqrt(start_squares / entries + epsilon)
    previous = initial
    current = initial
    scale_prev = jnp.float32(1.0)
    moments = []
    for iteration in range(STEPS):
        extended = extended_2(current, (("phonon", 1),), MODES)
        lower_part = extended[:, :columns_here]
        upper_part = extended[:, 2 * MODES :]
        summed = weight_rows[:, None] * (
            mode_weight * (lower_weight * lower_part + upper_weight * upper_part)
        )
        for operate_position in range(bit_count):
            chosen = site_bits[operate_position]
            flipped = partner(current, "site", operate_position)
            product = jnp.dot(
                masked[chosen], flipped.astype(jnp.bfloat16), preferred_element_type=jnp.float32
            )
            summed = summed + (field[chosen] * flipped + product)
        if iteration == 0:
            vector_new = summed
        else:
            vector_new = 2.0 * summed - previous / scale_prev
        squares, intersection = lax.psum(
            (jnp.sum(vector_new * vector_new), jnp.sum(initial * vector_new)), ("site", "phonon")
        )
        scale_now = jnp.sqrt(squares / entries + epsilon)
        updated = vector_new / scale_now
        moment = intersection / (entries * scale_now)
        moments.append(moment)
        previous = current
        current = updated
        scale_prev = scale_now
    return (current, previous, jnp.stack(moments))


def solution(mesh):
    in_specs = (P("site", "phonon"), P(), P(), P(), P(), P(), P())
    out_specs = (P("site", "phonon"), P("site", "phonon"), P())

    def whole(state, operators, op_mask, *rest):
        rows = state.shape[0] // mesh.shape["site"]
        columns = state.shape[1] // mesh.shape["phonon"]
        plan = Plan(mesh, rows, columns, op_mask.shape[1])
        body = functools.partial(shards, plan) if plan.fits() else halo_shards
        run = jax.shard_map(body, mesh=mesh, in_specs=in_specs, out_specs=out_specs, check_vma=False)
        return run(state, operators, op_mask, *rest)

    return whole
```

```python
import functools

import jax
import jax.numpy as jnp
from jax import lax
from jax.experimental import pallas as pl
from jax.experimental.pallas import tpu as pltpu
from jax.sharding import PartitionSpec as P

LBITS = 10
MODES = 64
STEPS = 3
LANES = 128
SUBLANES = 8
SLOTS = 8
AXES = ("site", "phonon")

epsilon = 1e-06


VMEM = pl.BlockSpec(memory_space=pltpu.VMEM)
SMEM = pl.BlockSpec(memory_space=pltpu.SMEM)
HBM = pl.BlockSpec(memory_space=pltpu.HBM)


class Plan:
    def __init__(self, mesh, rows, columns, blocks):
        self.sites = mesh.shape["site"]
        self.phonons = mesh.shape["phonon"]
        self.groups = self.sites * self.phonons
        self.bits = self.sites.bit_length() - 1
        self.rows = rows
        self.columns = columns
        self.blocks = blocks
        self.edge = rows // blocks
        self.levels_here = columns // MODES
        self.level_count = self.levels_here * self.phonons
        self.share = MODES // self.groups
        self.pieces = self.levels_here * self.share
        self.lane_blocks = rows // LANES
        self.body = self.pieces * self.lane_blocks
        self.inward = self.body + 1
        self.outward = 2 * self.body
        self.places = self.pieces * self.groups
        self.width = 2 * LANES
        self.parts = rows // self.width
        self.slabs = self.bits * self.parts
        self.kept = min(5, self.slabs - 1)
        self.entries = float(rows * columns * self.groups)

    def fits(self):
        return (
            MODES % self.groups == 0
            and self.columns == LANES
            and self.rows % self.width == 0
            and self.edge % LANES == 0
            and self.width % self.edge == 0
            and self.bits < SUBLANES
            and self.groups % SUBLANES == 0
        )


def params(mib):
    return pltpu.CompilerParams(vmem_limit_bytes=mib * 2**20)


def lane_sums(values):
    return jnp.sum(values, axis=0, keepdims=True)


def put_sums(out_ref, sums, start, stride, count):
    lane = lax.broadcasted_iota(jnp.int32, (1, LANES), 1)
    row = jnp.zeros((1, LANES), jnp.float32)
    for slot, value in enumerate(sums):
        width = LANES
        while width > LANES // SLOTS:
            width //= 2
            value = value + pltpu.roll(value, width, 1)
        row = jnp.where(lane // (LANES // SLOTS) == slot, value, row)
    out_ref[pl.ds(start, count, stride=stride), :] = jnp.broadcast_to(row, (count, LANES))


def totals_of(ref, start, stride, count):
    lanes = lane_sums(ref[pl.ds(start, count, stride=stride), :])
    lane = lax.broadcasted_iota(jnp.int32, (1, LANES), 1)
    return [
        jnp.sum(jnp.where(lane // (LANES // SLOTS) == slot, lanes, 0.0), axis=1, keepdims=True)
        for slot in range(SLOTS)
    ]


def scale_of(plan, squares):
    return jnp.sqrt(squares / plan.entries + epsilon)


def depart_kernel(plan, state_ref, out_ref, held_ref, semaphores):
    half = plan.rows // 2
    fetches = [
        pltpu.make_async_copy(
            state_ref.at[pl.ds(index * half, half), :], held_ref.at[pl.ds(index * half, half), :], semaphores.at[index]
        )
        for index in range(2)
    ]
    for fetch in fetches:
        fetch.start()
    sums = jnp.zeros((1, LANES), jnp.float32)
    for block in range(plan.lane_blocks):
        if block * LANES % half == 0:
            fetches[block * LANES // half].wait()
        tile = held_ref[pl.ds(block * LANES, LANES), :]
        sums = sums + lane_sums(tile * tile)
        turned = tile.T
        for piece in range(plan.pieces):
            out_ref[pl.ds(piece * plan.lane_blocks + block, plan.groups, stride=plan.inward), :] = turned[
                piece * plan.groups : (piece + 1) * plan.groups
            ]
    put_sums(out_ref, [sums], plan.body, plan.inward, plan.groups)


def fetch_slabs(plan, slabs, bits_ref, operators_ref, held_ref, semaphores):
    fetches = []
    for index, slab in enumerate(slabs):
        part, bit = divmod(slab, plan.bits)
        rows = pl.ds(part * plan.width, plan.width)
        fetch = pltpu.make_async_copy(
            operators_ref.at[bits_ref[bit], rows, :], held_ref.at[index], semaphores.at[index]
        )
        fetch.start()
        fetches.append(fetch)
    return fetches


def mask_slab(plan, slab, index, bits_ref, mask_ref, held_ref, out_ref):
    part, bit = divmod(slab, plan.bits)
    chosen = bits_ref[bit]
    for start in range(0, plan.width, plan.edge):
        across = (part * plan.width + start) // plan.edge
        rows = pl.ds(start, plan.edge)
        for along in range(plan.blocks):
            columns = pl.ds(along * plan.edge, plan.edge)
            keep = (mask_ref[chosen, across, along] > 0).astype(jnp.float32).astype(jnp.bfloat16)
            out_ref[index, columns, rows] = (held_ref[index, rows, columns] * keep).T


def store_kernel(plan, bits_ref, mask_ref, operators_ref, stored_ref, held_ref, masked_ref, in_semaphores, out_semaphores):
    slabs = range(plan.kept, plan.slabs)
    fetches = fetch_slabs(plan, slabs, bits_ref, operators_ref, held_ref, in_semaphores)
    stores = []
    for index, slab in enumerate(slabs):
        fetches[index].wait()
        mask_slab(plan, slab, index, bits_ref, mask_ref, held_ref, masked_ref)
        store = pltpu.make_async_copy(masked_ref.at[index], stored_ref.at[index], out_semaphores.at[index])
        store.start()
        stores.append(store)
    for store in stores:
        store.wait()


def prepare_kernel(
    plan,
    bits_ref,
    mask_ref,
    field_ref,
    coupling_ref,
    mode_ref,
    operators_ref,
    place_ref,
    inside_ref,
    kept_ref,
    held_ref,
    semaphores,
):
    slabs = range(plan.kept)
    fetches = fetch_slabs(plan, slabs, bits_ref, operators_ref, held_ref, semaphores)
    me = lax.axis_index("site") * plan.phonons + lax.axis_index("phonon")
    place = lax.broadcasted_iota(jnp.int32, (plan.places, LANES), 0)
    phonon = place % plan.phonons
    site = place // plan.phonons % plan.sites
    mode = place // plan.groups % plan.share
    level = phonon * plan.levels_here + place // (plan.groups * plan.share)
    occupied = jnp.zeros((plan.places, LANES), jnp.float32)
    for position in range(plan.bits):
        held = (site >> position & 1).astype(jnp.float32)
        occupied = occupied + coupling_ref[bits_ref[position]] * held
    strength = jnp.zeros((plan.places, LANES), jnp.float32)
    for index in range(plan.share):
        strength = jnp.where(mode == index, mode_ref[index * plan.groups + me], strength)
    strength = strength / jnp.sqrt(jnp.full((1, LANES), plan.level_count, jnp.float32))
    height = level.astype(jnp.float32)
    place_ref[0] = occupied
    place_ref[1] = strength * jnp.sqrt(height)
    place_ref[2] = jnp.where(level == plan.level_count - 1, 0.0, strength * jnp.sqrt(height + 1.0))
    inside = lax.broadcasted_iota(jnp.int32, (1, plan.rows), 1)
    weight = jnp.zeros((1, plan.rows), jnp.float32)
    for local_bit in range(LBITS):
        weight = weight + coupling_ref[plan.bits + local_bit] * (inside >> local_bit & 1).astype(jnp.float32)
    inside_ref[...] = jnp.zeros_like(inside_ref)
    inside_ref[:1] = weight
    for position in range(plan.bits):
        inside_ref[pl.ds(1 + position, 1)] = jnp.full((1, plan.rows), field_ref[bits_ref[position]])
    for slab in slabs:
        fetches[slab].wait()
        mask_slab(plan, slab, slab, bits_ref, mask_ref, held_ref, kept_ref)


def flipped(values, stride):
    places, width = values.shape
    if stride % SUBLANES == 0:
        shaped = values.reshape(places // (2 * stride), 2, stride, width)
        return jnp.concatenate([shaped[:, 1:], shaped[:, :1]], axis=1).reshape(places, width)
    tiles = values.reshape(places // SUBLANES, SUBLANES, width)
    if 2 * stride == SUBLANES:
        return pltpu.roll(tiles, stride, 1).reshape(places, width)
    spot = lax.broadcasted_iota(jnp.int32, tiles.shape, 1)
    down = pltpu.roll(tiles, stride, 1)
    up = pltpu.roll(tiles, SUBLANES - stride, 1)
    return jnp.where(spot & stride > 0, down, up).reshape(places, width)


def shifted(values, by):
    places, width = values.shape
    tiles = values.reshape(places // SUBLANES, SUBLANES, width)
    return pltpu.roll(tiles, by % SUBLANES, 1).reshape(places, width)


def put_rounded(plan, rounded_ref, vector, start):
    for position in range(plan.bits):
        rounded_ref[:, pl.ds(position * plan.rows + start, vector.shape[1])] = flipped(
            vector, plan.phonons << position
        ).astype(jnp.bfloat16)


def step(plan, vector_ref, rounded_ref, kept_ref, fetched_ref, place_ref, inside_ref, finish, ready=None, begun_ref=None):
    span = plan.places // plan.levels_here

    def local(start):
        lanes = pl.ds(start, LANES)
        vector = vector_ref[:, lanes]
        levels = [vector[index * span : (index + 1) * span] for index in range(plan.levels_here)]
        lower = jnp.concatenate([shifted(levels[-1], 1)] + levels[:-1], axis=0)
        upper = jnp.concatenate(levels[1:] + [shifted(levels[0], -1)], axis=0)
        weight = place_ref[0] + inside_ref[:1, lanes]
        total = weight * (place_ref[1] * lower + place_ref[2] * upper)
        for position in range(plan.bits):
            total = total + inside_ref[pl.ds(1 + position, 1), lanes] * flipped(vector, plan.phonons << position)
        return total

    def added(total, part, late):
        for ref, low, high in ((kept_ref, 0, plan.kept), (fetched_ref, plan.kept, plan.slabs)):
            fetched = low > 0
            begin = max(part * plan.bits, low)
            count = min((part + 1) * plan.bits, high) - begin
            if count <= 0 or late not in (None, fetched):
                continue
            if late:
                for slab in range(begin, begin + count):
                    ready(slab)
            first = begin - part * plan.bits
            masked = ref[pl.ds(begin - low, count)].reshape(count * plan.rows, plan.width)
            operand = rounded_ref[:, pl.ds(first * plan.rows, count * plan.rows)]
            total = total + jnp.dot(operand, masked, preferred_element_type=jnp.float32)
        return total

    def locals_of(lanes):
        return jnp.concatenate([local(start) for start in range(lanes.start, lanes.start + plan.width, LANES)], axis=1)

    parts = [pl.ds(part * plan.width, plan.width) for part in range(plan.parts)]
    if ready is None:
        for part, lanes in enumerate(parts):
            finish(lanes, added(locals_of(lanes), part, None))
        return
    for part, lanes in enumerate(parts):
        begun_ref[:, lanes] = added(locals_of(lanes), part, False)
    for part, lanes in enumerate(parts):
        finish(lanes, added(begun_ref[:, lanes], part, True))


def first_kernel(
    plan,
    arrived_ref,
    place_ref,
    inside_ref,
    kept_ref,
    stored_ref,
    initial_ref,
    new_ref,
    sums_ref,
    fetched_ref,
    rounded_ref,
    ahead_ref,
    vector_ref,
    semaphores,
):
    fetches = {}
    for slab in range(plan.kept, plan.slabs):
        index = slab - plan.kept
        fetches[slab] = pltpu.make_async_copy(stored_ref.at[index], fetched_ref.at[index], semaphores.at[index])
        fetches[slab].start()

    def ready(slab):
        fetches[slab].wait()

    squares = totals_of(arrived_ref, plan.body, plan.inward, plan.groups)[0]
    inverse = 1.0 / scale_of(plan, squares)
    for block in range(plan.lane_blocks):
        parts = [
            arrived_ref[pl.ds(piece * plan.lane_blocks + block, plan.groups, stride=plan.inward), :]
            for piece in range(plan.pieces)
        ]
        vector = jnp.concatenate(parts, axis=0) * inverse
        initial_ref[:, pl.ds(block * LANES, LANES)] = vector
        put_rounded(plan, rounded_ref, vector, block * LANES)
    tables = (kept_ref, fetched_ref, place_ref, inside_ref)
    sums = [[] for _ in range(2 * STEPS)]

    def note(vector, lanes, new):
        sums[2 * vector].append(lane_sums(new * new))
        sums[2 * vector + 1].append(lane_sums(new * initial_ref[:, lanes]))

    def finish(lanes, new):
        new_ref[:, lanes] = new
        put_rounded(plan, ahead_ref, new, lanes.start)
        note(0, lanes, new)

    def look_ahead(lanes, total):
        new = 2.0 * total - initial_ref[:, lanes]
        vector_ref[:, lanes] = new
        put_rounded(plan, rounded_ref, new, lanes.start)
        note(1, lanes, new)

    def look_further(lanes, total):
        note(2, lanes, 2.0 * total - new_ref[:, lanes])

    step(plan, initial_ref, rounded_ref, *tables, finish, ready, new_ref)
    step(plan, new_ref, ahead_ref, *tables, look_ahead)
    step(plan, vector_ref, rounded_ref, *tables, look_further)
    put_sums(sums_ref, [one_row(rows) for rows in sums], 0, 1, plan.groups)


def one_row(rows):
    total = sum(rows[1:], rows[0])
    return sum(total[:, start : start + LANES] for start in range(0, total.shape[1], LANES))


def onward_kernel(
    plan,
    arrived_ref,
    raw_ref,
    initial_ref,
    place_ref,
    inside_ref,
    kept_ref,
    fetched_ref,
    out_ref,
    known_ref,
    rounded_ref,
    ahead_ref,
    second_ref,
    third_ref,
):
    totals = totals_of(arrived_ref, 0, 1, plan.groups)
    first = 1.0 / scale_of(plan, totals[0])
    second = 1.0 / scale_of(plan, totals[2] * first * first)
    both = first * second
    third = 1.0 / scale_of(plan, totals[4] * both * both)
    for row, moment in enumerate((totals[1] * first, totals[3] * both, totals[5] * both * third)):
        known_ref[pl.ds(row, 1), :] = jnp.broadcast_to(moment / plan.entries, (1, LANES))
    known_ref[STEPS:, :] = jnp.zeros((SUBLANES - STEPS, LANES), jnp.float32)
    for block in range(plan.lane_blocks):
        lanes = pl.ds(block * LANES, LANES)
        vector = raw_ref[:, lanes] * first
        second_ref[:, lanes] = vector
        put_rounded(plan, rounded_ref, vector, block * LANES)
    tables = (kept_ref, fetched_ref, place_ref, inside_ref)

    def send(vector, lanes, new):
        for start in range(0, plan.width, LANES):
            block = (lanes.start + start) // LANES
            for piece in range(plan.pieces):
                row = vector * plan.body + piece * plan.lane_blocks + block
                out_ref[pl.ds(row, plan.groups, stride=plan.outward), :] = new[
                    piece * plan.groups : (piece + 1) * plan.groups, start : start + LANES
                ]

    def finish_second(lanes, total):
        new = 2.0 * total - initial_ref[:, lanes] * first
        vector = new * second
        third_ref[:, lanes] = vector
        put_rounded(plan, ahead_ref, vector, lanes.start)
        send(0, lanes, vector)

    def finish_third(lanes, total):
        send(1, lanes, (2.0 * total - second_ref[:, lanes] * second) * third)

    step(plan, second_ref, rounded_ref, *tables, finish_second)
    step(plan, third_ref, ahead_ref, *tables, finish_third)


def arrive_kernel(plan, arrived_ref, known_ref, before_ref, last_ref, moments_ref):
    for vector, out_ref in enumerate((before_ref, last_ref)):
        for block in range(plan.lane_blocks):
            first = vector * plan.body + block
            parts = [
                arrived_ref[pl.ds(first + piece * plan.lane_blocks, plan.groups, stride=plan.outward), :]
                for piece in range(plan.pieces)
            ]
            out_ref[pl.ds(block * LANES, LANES), :] = jnp.concatenate(parts, axis=0).T
    for step_index in range(STEPS):
        moments_ref[step_index] = known_ref[step_index, 0]


def exchange(values, count):
    shaped = values.reshape(count, values.shape[0] // count, 1, LANES)
    return lax.all_to_all(shaped, AXES, 0, 0, tiled=True).reshape(values.shape)


def shards(plan, state, operators, op_mask, site_bits, field, site_coupling, mode_coupling):
    f32 = jnp.float32
    inward = jax.ShapeDtypeStruct((plan.groups * plan.inward, LANES), f32)
    outward = jax.ShapeDtypeStruct((plan.groups * plan.outward, LANES), f32)
    vector = jax.ShapeDtypeStruct((plan.places, plan.rows), f32)
    known = jax.ShapeDtypeStruct((SUBLANES, LANES), f32)
    held = jax.ShapeDtypeStruct((plan.rows, plan.columns), f32)
    rounded = pltpu.VMEM((plan.places, plan.bits * plan.rows), jnp.bfloat16)
    working = pltpu.VMEM((plan.places, plan.rows), f32)
    work = 2 * plan.bits * plan.places * plan.rows * plan.rows

    def cost(flops, moved):
        return pl.CostEstimate(flops=flops, bytes_accessed=moved, transcendentals=0)

    departing = pl.pallas_call(
        functools.partial(depart_kernel, plan),
        out_shape=inward,
        in_specs=[HBM],
        out_specs=VMEM,
        scratch_shapes=[pltpu.VMEM((plan.rows, plan.columns), f32), pltpu.SemaphoreType.DMA((2,))],
        compiler_params=params(60),
        name="depart",
    )(state)
    arrived = exchange(departing, plan.groups)
    fetched = plan.slabs - plan.kept
    kept_slabs = (plan.kept, plan.rows, plan.width)
    fetched_slabs = (fetched, plan.rows, plan.width)

    def held_slabs(count):
        return pltpu.VMEM((count, plan.width, plan.rows), jnp.bfloat16)

    place, inside, kept = pl.pallas_call(
        functools.partial(prepare_kernel, plan),
        out_shape=[
            jax.ShapeDtypeStruct((3, plan.places, LANES), f32),
            jax.ShapeDtypeStruct((SUBLANES, plan.rows), f32),
            jax.ShapeDtypeStruct(kept_slabs, jnp.bfloat16),
        ],
        in_specs=[SMEM] * 5 + [HBM],
        out_specs=[VMEM] * 3,
        scratch_shapes=[held_slabs(plan.kept), pltpu.SemaphoreType.DMA((plan.kept,))],
        compiler_params=params(50),
        cost_estimate=cost(plan.rows * plan.rows, 4 * plan.kept * plan.rows * plan.width),
        name="prepare",
    )(site_bits, op_mask, field, site_coupling, mode_coupling, operators)
    stored = pl.pallas_call(
        functools.partial(store_kernel, plan),
        out_shape=jax.ShapeDtypeStruct(fetched_slabs, jnp.bfloat16),
        in_specs=[SMEM] * 2 + [HBM],
        out_specs=HBM,
        scratch_shapes=[
            held_slabs(fetched),
            pltpu.VMEM(fetched_slabs, jnp.bfloat16),
            pltpu.SemaphoreType.DMA((fetched,)),
            pltpu.SemaphoreType.DMA((fetched,)),
        ],
        compiler_params=params(60),
        cost_estimate=cost(plan.rows * plan.rows, 4 * fetched * plan.rows * plan.width),
        name="store",
    )(site_bits, op_mask, operators)
    initial, raw, sums, late = pl.pallas_call(
        functools.partial(first_kernel, plan),
        out_shape=[
            vector,
            vector,
            jax.ShapeDtypeStruct((plan.groups, LANES), f32),
            jax.ShapeDtypeStruct(fetched_slabs, jnp.bfloat16),
        ],
        in_specs=[VMEM] * 4 + [HBM],
        out_specs=[VMEM] * 4,
        scratch_shapes=[rounded, rounded, working, pltpu.SemaphoreType.DMA((fetched,))],
        compiler_params=params(46),
        cost_estimate=cost(2 * work, 4 * plan.places * plan.rows),
        name="first",
    )(arrived, place, inside, kept, stored)
    tables = (place, inside, kept, late)
    sums = exchange(sums, plan.groups)
    departing, told = pl.pallas_call(
        functools.partial(onward_kernel, plan),
        out_shape=[outward, known],
        in_specs=[VMEM] * 7,
        out_specs=[VMEM] * 2,
        scratch_shapes=[rounded, rounded, working, working],
        compiler_params=params(32),
        cost_estimate=cost(2 * work, 8 * plan.places * plan.rows),
        name="onward",
    )(sums, raw, initial, *tables)
    arrived = exchange(departing, plan.groups)
    before, last, moments = pl.pallas_call(
        functools.partial(arrive_kernel, plan),
        out_shape=[held, held, jax.ShapeDtypeStruct((STEPS,), f32)],
        in_specs=[VMEM] * 2,
        out_specs=[VMEM, VMEM, SMEM],
        compiler_params=params(16),
        name="arrive",
    )(arrived, told)
    return last, before, moments


def extended_2(block, sides, width):
    for axis, dim in sides:
        count = lax.axis_size(axis)
        forward = [(i, i + 1) for i in range(count - 1)]
        backward = [(target, source) for source, target in forward]
        low = lax.ppermute(
            lax.slice_in_dim(block, block.shape[dim] - width, None, axis=dim), axis, forward
        )
        high = lax.ppermute(lax.slice_in_dim(block, 0, width, axis=dim), axis, backward)
        block = jnp.concatenate([low, block, high], axis=dim)
    return block


def partner(value, axis, bit):
    mask = 2**bit
    pairs = [(source, source ^ mask) for source in range(lax.axis_size(axis))]
    return lax.ppermute(value, axis, pairs)


def halo_shards(state, operators, op_mask, site_bits, field, site_coupling, mode_coupling):
    site_count = lax.axis_size("site")
    phonon_count = lax.axis_size("phonon")
    bit_count = site_count.bit_length() - 1
    rows_here = state.shape[0]
    columns_here = state.shape[1]
    levels_here = columns_here // MODES
    block_edge = rows_here // op_mask.shape[1]
    expanded = jnp.repeat(jnp.repeat(op_mask, block_edge, axis=1), block_edge, axis=2)
    masked = jnp.where(expanded > 0, operators, jnp.zeros((), jnp.bfloat16))
    entries = jnp.float32(rows_here * columns_here * site_count * phonon_count)
    level_total = jnp.sqrt(jnp.float32(levels_here * phonon_count))
    device = lax.axis_index("site")
    inside = lax.iota(jnp.int32, rows_here)
    weight_rows = jnp.zeros((rows_here,), jnp.float32)
    for position in range(bit_count):
        weight_rows = weight_rows + site_coupling[site_bits[position]] * (
            device >> position & 1
        ).astype(jnp.float32)
    for local_bit in range(LBITS):
        weight_rows = weight_rows + site_coupling[bit_count + local_bit] * (
            inside >> local_bit & 1
        ).astype(jnp.float32)
    levels = (
        lax.axis_index("phonon") * levels_here + lax.iota(jnp.int32, columns_here) // MODES
    ).astype(jnp.float32)
    lower_weight = jnp.sqrt(levels)
    upper_weight = jnp.sqrt(levels + 1.0)
    mode_weight = jnp.tile(mode_coupling, columns_here // MODES) / level_total
    start_squares = lax.psum(jnp.sum(state * state), ("site", "phonon"))
    initial = state / jnp.sqrt(start_squares / entries + epsilon)
    previous = initial
    current = initial
    scale_prev = jnp.float32(1.0)
    moments = []
    for iteration in range(STEPS):
        extended = extended_2(current, (("phonon", 1),), MODES)
        lower_part = extended[:, :columns_here]
        upper_part = extended[:, 2 * MODES :]
        summed = weight_rows[:, None] * (
            mode_weight * (lower_weight * lower_part + upper_weight * upper_part)
        )
        for operate_position in range(bit_count):
            chosen = site_bits[operate_position]
            flipped = partner(current, "site", operate_position)
            product = jnp.dot(
                masked[chosen], flipped.astype(jnp.bfloat16), preferred_element_type=jnp.float32
            )
            summed = summed + (field[chosen] * flipped + product)
        if iteration == 0:
            vector_new = summed
        else:
            vector_new = 2.0 * summed - previous / scale_prev
        squares, intersection = lax.psum(
            (jnp.sum(vector_new * vector_new), jnp.sum(initial * vector_new)), ("site", "phonon")
        )
        scale_now = jnp.sqrt(squares / entries + epsilon)
        updated = vector_new / scale_now
        moment = intersection / (entries * scale_now)
        moments.append(moment)
        previous = current
        current = updated
        scale_prev = scale_now
    return (current, previous, jnp.stack(moments))


def solution(mesh):
    in_specs = (P("site", "phonon"), P(), P(), P(), P(), P(), P())
    out_specs = (P("site", "phonon"), P("site", "phonon"), P())

    def whole(state, operators, op_mask, *rest):
        rows = state.shape[0] // mesh.shape["site"]
        columns = state.shape[1] // mesh.shape["phonon"]
        plan = Plan(mesh, rows, columns, op_mask.shape[1])
        body = functools.partial(shards, plan) if plan.fits() else halo_shards
        run = jax.shard_map(body, mesh=mesh, in_specs=in_specs, out_specs=out_specs, check_vma=False)
        return run(state, operators, op_mask, *rest)

    return whole
```

```python
import functools

import jax
import jax.numpy as jnp
from jax import lax
from jax.experimental import pallas as pl
from jax.experimental.pallas import tpu as pltpu
from jax.sharding import PartitionSpec as P

LBITS = 10
MODES = 64
STEPS = 3
LANES = 128
SUBLANES = 8
SLOTS = 8
AXES = ("site", "phonon")

epsilon = 1e-06


VMEM = pl.BlockSpec(memory_space=pltpu.VMEM)
SMEM = pl.BlockSpec(memory_space=pltpu.SMEM)
HBM = pl.BlockSpec(memory_space=pltpu.HBM)


class Plan:
    def __init__(self, mesh, rows, columns, blocks):
        self.sites = mesh.shape["site"]
        self.phonons = mesh.shape["phonon"]
        self.groups = self.sites * self.phonons
        self.bits = self.sites.bit_length() - 1
        self.rows = rows
        self.columns = columns
        self.blocks = blocks
        self.edge = rows // blocks
        self.levels_here = columns // MODES
        self.level_count = self.levels_here * self.phonons
        self.share = MODES // self.groups
        self.pieces = self.levels_here * self.share
        self.lane_blocks = rows // LANES
        self.body = self.pieces * self.lane_blocks
        self.inward = self.body + 1
        self.outward = 2 * self.body
        self.places = self.pieces * self.groups
        self.width = 2 * LANES
        self.parts = rows // self.width
        self.slabs = self.bits * self.parts
        self.kept = min(5, self.slabs - 1)
        self.entries = float(rows * columns * self.groups)

    def fits(self):
        return (
            MODES % self.groups == 0
            and self.columns == LANES
            and self.rows % self.width == 0
            and self.edge % LANES == 0
            and self.width % self.edge == 0
            and self.bits < SUBLANES
            and self.groups % SUBLANES == 0
        )


def params(mib):
    return pltpu.CompilerParams(vmem_limit_bytes=mib * 2**20)


def lane_sums(values):
    return jnp.sum(values, axis=0, keepdims=True)


def put_sums(out_ref, sums, start, stride, count):
    lane = lax.broadcasted_iota(jnp.int32, (1, LANES), 1)
    row = jnp.zeros((1, LANES), jnp.float32)
    for slot, value in enumerate(sums):
        width = LANES
        while width > LANES // SLOTS:
            width //= 2
            value = value + pltpu.roll(value, width, 1)
        row = jnp.where(lane // (LANES // SLOTS) == slot, value, row)
    out_ref[pl.ds(start, count, stride=stride), :] = jnp.broadcast_to(row, (count, LANES))


def totals_of(ref, start, stride, count):
    lanes = lane_sums(ref[pl.ds(start, count, stride=stride), :])
    width = LANES // SLOTS
    reach = width
    while reach > 1:
        reach //= 2
        lanes = lanes + pltpu.roll(lanes, LANES - reach, 1)
    return [lanes[:, slot * width : slot * width + 1] for slot in range(SLOTS)]


def scale_of(plan, squares):
    return jnp.sqrt(squares / plan.entries + epsilon)


def depart_kernel(plan, state_ref, out_ref, held_ref, semaphores):
    half = plan.rows // 2
    fetches = [
        pltpu.make_async_copy(
            state_ref.at[pl.ds(index * half, half), :], held_ref.at[pl.ds(index * half, half), :], semaphores.at[index]
        )
        for index in range(2)
    ]
    for fetch in fetches:
        fetch.start()
    sums = jnp.zeros((1, LANES), jnp.float32)
    for block in range(plan.lane_blocks):
        if block * LANES % half == 0:
            fetches[block * LANES // half].wait()
        tile = held_ref[pl.ds(block * LANES, LANES), :]
        sums = sums + lane_sums(tile * tile)
        turned = tile.T
        for piece in range(plan.pieces):
            out_ref[pl.ds(piece * plan.lane_blocks + block, plan.groups, stride=plan.inward), :] = turned[
                piece * plan.groups : (piece + 1) * plan.groups
            ]
    put_sums(out_ref, [sums], plan.body, plan.inward, plan.groups)


def fetch_slabs(plan, slabs, bits_ref, operators_ref, held_ref, semaphores):
    fetches = []
    for index, slab in enumerate(slabs):
        part, bit = divmod(slab, plan.bits)
        rows = pl.ds(part * plan.width, plan.width)
        fetch = pltpu.make_async_copy(
            operators_ref.at[bits_ref[bit], rows, :], held_ref.at[index], semaphores.at[index]
        )
        fetch.start()
        fetches.append(fetch)
    return fetches


def mask_slab(plan, slab, index, bits_ref, mask_ref, held_ref, out_ref):
    part, bit = divmod(slab, plan.bits)
    chosen = bits_ref[bit]
    for start in range(0, plan.width, plan.edge):
        across = (part * plan.width + start) // plan.edge
        rows = pl.ds(start, plan.edge)
        for along in range(plan.blocks):
            columns = pl.ds(along * plan.edge, plan.edge)
            keep = (mask_ref[chosen, across, along] > 0).astype(jnp.float32).astype(jnp.bfloat16)
            out_ref[index, columns, rows] = (held_ref[index, rows, columns] * keep).T


def store_kernel(plan, bits_ref, mask_ref, operators_ref, stored_ref, held_ref, masked_ref, in_semaphores, out_semaphores):
    slabs = range(plan.kept, plan.slabs)
    fetches = fetch_slabs(plan, slabs, bits_ref, operators_ref, held_ref, in_semaphores)
    stores = []
    for index, slab in enumerate(slabs):
        fetches[index].wait()
        mask_slab(plan, slab, index, bits_ref, mask_ref, held_ref, masked_ref)
        store = pltpu.make_async_copy(masked_ref.at[index], stored_ref.at[index], out_semaphores.at[index])
        store.start()
        stores.append(store)
    for store in stores:
        store.wait()


def prepare_kernel(
    plan,
    bits_ref,
    mask_ref,
    field_ref,
    coupling_ref,
    mode_ref,
    operators_ref,
    place_ref,
    inside_ref,
    kept_ref,
    held_ref,
    semaphores,
):
    slabs = range(plan.kept)
    fetches = fetch_slabs(plan, slabs, bits_ref, operators_ref, held_ref, semaphores)
    me = lax.axis_index("site") * plan.phonons + lax.axis_index("phonon")
    place = lax.broadcasted_iota(jnp.int32, (plan.places, LANES), 0)
    phonon = place % plan.phonons
    site = place // plan.phonons % plan.sites
    mode = place // plan.groups % plan.share
    level = phonon * plan.levels_here + place // (plan.groups * plan.share)
    occupied = jnp.zeros((plan.places, LANES), jnp.float32)
    for position in range(plan.bits):
        held = (site >> position & 1).astype(jnp.float32)
        occupied = occupied + coupling_ref[bits_ref[position]] * held
    strength = jnp.zeros((plan.places, LANES), jnp.float32)
    for index in range(plan.share):
        strength = jnp.where(mode == index, mode_ref[index * plan.groups + me], strength)
    strength = strength / jnp.sqrt(jnp.full((1, LANES), plan.level_count, jnp.float32))
    height = level.astype(jnp.float32)
    place_ref[0] = occupied
    place_ref[1] = strength * jnp.sqrt(height)
    place_ref[2] = jnp.where(level == plan.level_count - 1, 0.0, strength * jnp.sqrt(height + 1.0))
    inside = lax.broadcasted_iota(jnp.int32, (1, plan.rows), 1)
    weight = jnp.zeros((1, plan.rows), jnp.float32)
    for local_bit in range(LBITS):
        weight = weight + coupling_ref[plan.bits + local_bit] * (inside >> local_bit & 1).astype(jnp.float32)
    inside_ref[...] = jnp.zeros_like(inside_ref)
    inside_ref[:1] = weight
    for position in range(plan.bits):
        inside_ref[pl.ds(1 + position, 1)] = jnp.full((1, plan.rows), field_ref[bits_ref[position]])
    for slab in slabs:
        fetches[slab].wait()
        mask_slab(plan, slab, slab, bits_ref, mask_ref, held_ref, kept_ref)


def flipped(values, stride):
    places, width = values.shape
    if stride % SUBLANES == 0:
        shaped = values.reshape(places // (2 * stride), 2, stride, width)
        return jnp.concatenate([shaped[:, 1:], shaped[:, :1]], axis=1).reshape(places, width)
    tiles = values.reshape(places // SUBLANES, SUBLANES, width)
    if 2 * stride == SUBLANES:
        return pltpu.roll(tiles, stride, 1).reshape(places, width)
    spot = lax.broadcasted_iota(jnp.int32, tiles.shape, 1)
    down = pltpu.roll(tiles, stride, 1)
    up = pltpu.roll(tiles, SUBLANES - stride, 1)
    return jnp.where(spot & stride > 0, down, up).reshape(places, width)


def shifted(values, by):
    places, width = values.shape
    tiles = values.reshape(places // SUBLANES, SUBLANES, width)
    return pltpu.roll(tiles, by % SUBLANES, 1).reshape(places, width)


def put_rounded(plan, rounded_ref, vector, start):
    for position in range(plan.bits):
        rounded_ref[:, pl.ds(position * plan.rows + start, vector.shape[1])] = flipped(
            vector, plan.phonons << position
        ).astype(jnp.bfloat16)


def step(plan, vector_ref, rounded_ref, kept_ref, fetched_ref, place_ref, inside_ref, finish, ready=None, begun_ref=None, factor=None):
    span = plan.places // plan.levels_here

    def local(start):
        lanes = pl.ds(start, LANES)
        vector = vector_ref[:, lanes]
        levels = [vector[index * span : (index + 1) * span] for index in range(plan.levels_here)]
        lower = jnp.concatenate([shifted(levels[-1], 1)] + levels[:-1], axis=0)
        upper = jnp.concatenate(levels[1:] + [shifted(levels[0], -1)], axis=0)
        weight = place_ref[0] + inside_ref[:1, lanes]
        total = weight * (place_ref[1] * lower + place_ref[2] * upper)
        for position in range(plan.bits):
            total = total + inside_ref[pl.ds(1 + position, 1), lanes] * flipped(vector, plan.phonons << position)
        return total if factor is None else total * factor

    def added(total, part, late):
        for ref, low, high in ((kept_ref, 0, plan.kept), (fetched_ref, plan.kept, plan.slabs)):
            fetched = low > 0
            begin = max(part * plan.bits, low)
            count = min((part + 1) * plan.bits, high) - begin
            if count <= 0 or late not in (None, fetched):
                continue
            if late:
                for slab in range(begin, begin + count):
                    ready(slab)
            first = begin - part * plan.bits
            masked = ref[pl.ds(begin - low, count)].reshape(count * plan.rows, plan.width)
            operand = rounded_ref[:, pl.ds(first * plan.rows, count * plan.rows)]
            total = total + jnp.dot(operand, masked, preferred_element_type=jnp.float32)
        return total

    def locals_of(lanes):
        return jnp.concatenate([local(start) for start in range(lanes.start, lanes.start + plan.width, LANES)], axis=1)

    parts = [pl.ds(part * plan.width, plan.width) for part in range(plan.parts)]
    if ready is None:
        for part, lanes in enumerate(parts):
            finish(lanes, added(locals_of(lanes), part, None))
        return
    for part, lanes in enumerate(parts):
        begun_ref[:, lanes] = added(locals_of(lanes), part, False)
    for part, lanes in enumerate(parts):
        finish(lanes, added(begun_ref[:, lanes], part, True))


def first_kernel(
    plan,
    arrived_ref,
    place_ref,
    inside_ref,
    kept_ref,
    stored_ref,
    initial_ref,
    new_ref,
    sums_ref,
    fetched_ref,
    rounded_ref,
    ahead_ref,
    vector_ref,
    semaphores,
):
    fetches = {}
    for slab in range(plan.kept, plan.slabs):
        index = slab - plan.kept
        fetches[slab] = pltpu.make_async_copy(stored_ref.at[index], fetched_ref.at[index], semaphores.at[index])
        fetches[slab].start()

    def ready(slab):
        fetches[slab].wait()

    squares = totals_of(arrived_ref, plan.body, plan.inward, plan.groups)[0]
    inverse = 1.0 / scale_of(plan, squares)
    for block in range(plan.lane_blocks):
        parts = [
            arrived_ref[pl.ds(piece * plan.lane_blocks + block, plan.groups, stride=plan.inward), :]
            for piece in range(plan.pieces)
        ]
        vector = jnp.concatenate(parts, axis=0) * inverse
        initial_ref[:, pl.ds(block * LANES, LANES)] = vector
        put_rounded(plan, rounded_ref, vector, block * LANES)
    tables = (kept_ref, fetched_ref, place_ref, inside_ref)
    sums = [[] for _ in range(2 * STEPS)]

    def note(vector, lanes, new):
        sums[2 * vector].append(lane_sums(new * new))
        sums[2 * vector + 1].append(lane_sums(new * initial_ref[:, lanes]))

    def finish(lanes, new):
        new_ref[:, lanes] = new
        put_rounded(plan, ahead_ref, new, lanes.start)
        note(0, lanes, new)

    def look_ahead(lanes, total):
        new = 2.0 * total - initial_ref[:, lanes]
        vector_ref[:, lanes] = new
        put_rounded(plan, rounded_ref, new, lanes.start)
        note(1, lanes, new)

    def look_further(lanes, total):
        note(2, lanes, 2.0 * total - new_ref[:, lanes])

    step(plan, initial_ref, rounded_ref, *tables, finish, ready, new_ref)
    step(plan, new_ref, ahead_ref, *tables, look_ahead)
    step(plan, vector_ref, rounded_ref, *tables, look_further)
    put_sums(sums_ref, [one_row(rows) for rows in sums], 0, 1, plan.groups)


def one_row(rows):
    total = sum(rows[1:], rows[0])
    return sum(total[:, start : start + LANES] for start in range(0, total.shape[1], LANES))


def onward_kernel(
    plan,
    arrived_ref,
    raw_ref,
    initial_ref,
    place_ref,
    inside_ref,
    kept_ref,
    fetched_ref,
    out_ref,
    known_ref,
    rounded_ref,
    ahead_ref,
    third_ref,
):
    totals = totals_of(arrived_ref, 0, 1, plan.groups)
    first = 1.0 / scale_of(plan, totals[0])
    second = 1.0 / scale_of(plan, totals[2] * first * first)
    both = first * second
    third = 1.0 / scale_of(plan, totals[4] * both * both)
    for row, moment in enumerate((totals[1] * first, totals[3] * both, totals[5] * both * third)):
        known_ref[pl.ds(row, 1), :] = jnp.broadcast_to(moment / plan.entries, (1, LANES))
    known_ref[STEPS:, :] = jnp.zeros((SUBLANES - STEPS, LANES), jnp.float32)
    for block in range(plan.lane_blocks):
        lanes = pl.ds(block * LANES, LANES)
        put_rounded(plan, rounded_ref, raw_ref[:, lanes] * first, block * LANES)
    tables = (kept_ref, fetched_ref, place_ref, inside_ref)

    def send(vector, lanes, new):
        for start in range(0, plan.width, LANES):
            block = (lanes.start + start) // LANES
            for piece in range(plan.pieces):
                row = vector * plan.body + piece * plan.lane_blocks + block
                out_ref[pl.ds(row, plan.groups, stride=plan.outward), :] = new[
                    piece * plan.groups : (piece + 1) * plan.groups, start : start + LANES
                ]

    def finish_second(lanes, total):
        new = 2.0 * total - initial_ref[:, lanes] * first
        vector = new * second
        third_ref[:, lanes] = vector
        put_rounded(plan, ahead_ref, vector, lanes.start)
        send(0, lanes, vector)

    def finish_third(lanes, total):
        send(1, lanes, 2.0 * third * total - raw_ref[:, lanes] * (both * third))

    step(plan, raw_ref, rounded_ref, *tables, finish_second, factor=first)
    step(plan, third_ref, ahead_ref, *tables, finish_third)


def arrive_kernel(plan, arrived_ref, known_ref, before_ref, last_ref, moments_ref):
    for vector, out_ref in enumerate((before_ref, last_ref)):
        for block in range(plan.lane_blocks):
            first = vector * plan.body + block
            parts = [
                arrived_ref[pl.ds(first + piece * plan.lane_blocks, plan.groups, stride=plan.outward), :]
                for piece in range(plan.pieces)
            ]
            out_ref[pl.ds(block * LANES, LANES), :] = jnp.concatenate(parts, axis=0).T
    for step_index in range(STEPS):
        moments_ref[step_index] = known_ref[step_index, 0]


def exchange(values, count):
    shaped = values.reshape(count, values.shape[0] // count, 1, LANES)
    return lax.all_to_all(shaped, AXES, 0, 0, tiled=True).reshape(values.shape)


def shards(plan, state, operators, op_mask, site_bits, field, site_coupling, mode_coupling):
    f32 = jnp.float32
    inward = jax.ShapeDtypeStruct((plan.groups * plan.inward, LANES), f32)
    outward = jax.ShapeDtypeStruct((plan.groups * plan.outward, LANES), f32)
    vector = jax.ShapeDtypeStruct((plan.places, plan.rows), f32)
    known = jax.ShapeDtypeStruct((SUBLANES, LANES), f32)
    held = jax.ShapeDtypeStruct((plan.rows, plan.columns), f32)
    rounded = pltpu.VMEM((plan.places, plan.bits * plan.rows), jnp.bfloat16)
    working = pltpu.VMEM((plan.places, plan.rows), f32)
    work = 2 * plan.bits * plan.places * plan.rows * plan.rows

    def cost(flops, moved):
        return pl.CostEstimate(flops=flops, bytes_accessed=moved, transcendentals=0)

    departing = pl.pallas_call(
        functools.partial(depart_kernel, plan),
        out_shape=inward,
        in_specs=[HBM],
        out_specs=VMEM,
        scratch_shapes=[pltpu.VMEM((plan.rows, plan.columns), f32), pltpu.SemaphoreType.DMA((2,))],
        compiler_params=params(60),
        name="depart",
    )(state)
    arrived = exchange(departing, plan.groups)
    fetched = plan.slabs - plan.kept
    kept_slabs = (plan.kept, plan.rows, plan.width)
    fetched_slabs = (fetched, plan.rows, plan.width)

    def held_slabs(count):
        return pltpu.VMEM((count, plan.width, plan.rows), jnp.bfloat16)

    place, inside, kept = pl.pallas_call(
        functools.partial(prepare_kernel, plan),
        out_shape=[
            jax.ShapeDtypeStruct((3, plan.places, LANES), f32),
            jax.ShapeDtypeStruct((SUBLANES, plan.rows), f32),
            jax.ShapeDtypeStruct(kept_slabs, jnp.bfloat16),
        ],
        in_specs=[SMEM] * 5 + [HBM],
        out_specs=[VMEM] * 3,
        scratch_shapes=[held_slabs(plan.kept), pltpu.SemaphoreType.DMA((plan.kept,))],
        compiler_params=params(50),
        cost_estimate=cost(plan.rows * plan.rows, 4 * plan.kept * plan.rows * plan.width),
        name="prepare",
    )(site_bits, op_mask, field, site_coupling, mode_coupling, operators)
    stored = pl.pallas_call(
        functools.partial(store_kernel, plan),
        out_shape=jax.ShapeDtypeStruct(fetched_slabs, jnp.bfloat16),
        in_specs=[SMEM] * 2 + [HBM],
        out_specs=HBM,
        scratch_shapes=[
            held_slabs(fetched),
            pltpu.VMEM(fetched_slabs, jnp.bfloat16),
            pltpu.SemaphoreType.DMA((fetched,)),
            pltpu.SemaphoreType.DMA((fetched,)),
        ],
        compiler_params=params(60),
        cost_estimate=cost(plan.rows * plan.rows, 4 * fetched * plan.rows * plan.width),
        name="store",
    )(site_bits, op_mask, operators)
    initial, raw, sums, late = pl.pallas_call(
        functools.partial(first_kernel, plan),
        out_shape=[
            vector,
            vector,
            jax.ShapeDtypeStruct((plan.groups, LANES), f32),
            jax.ShapeDtypeStruct(fetched_slabs, jnp.bfloat16),
        ],
        in_specs=[VMEM] * 4 + [HBM],
        out_specs=[VMEM] * 4,
        scratch_shapes=[rounded, rounded, working, pltpu.SemaphoreType.DMA((fetched,))],
        compiler_params=params(46),
        cost_estimate=cost(2 * work, 4 * plan.places * plan.rows),
        name="first",
    )(arrived, place, inside, kept, stored)
    tables = (place, inside, kept, late)
    sums = exchange(sums, plan.groups)
    departing, told = pl.pallas_call(
        functools.partial(onward_kernel, plan),
        out_shape=[outward, known],
        in_specs=[VMEM] * 7,
        out_specs=[VMEM] * 2,
        scratch_shapes=[rounded, rounded, working],
        compiler_params=params(32),
        cost_estimate=cost(2 * work, 8 * plan.places * plan.rows),
        name="onward",
    )(sums, raw, initial, *tables)
    arrived = exchange(departing, plan.groups)
    before, last, moments = pl.pallas_call(
        functools.partial(arrive_kernel, plan),
        out_shape=[held, held, jax.ShapeDtypeStruct((STEPS,), f32)],
        in_specs=[VMEM] * 2,
        out_specs=[VMEM, VMEM, SMEM],
        compiler_params=params(16),
        name="arrive",
    )(arrived, told)
    return last, before, moments


def extended_2(block, sides, width):
    for axis, dim in sides:
        count = lax.axis_size(axis)
        forward = [(i, i + 1) for i in range(count - 1)]
        backward = [(target, source) for source, target in forward]
        low = lax.ppermute(
            lax.slice_in_dim(block, block.shape[dim] - width, None, axis=dim), axis, forward
        )
        high = lax.ppermute(lax.slice_in_dim(block, 0, width, axis=dim), axis, backward)
        block = jnp.concatenate([low, block, high], axis=dim)
    return block


def partner(value, axis, bit):
    mask = 2**bit
    pairs = [(source, source ^ mask) for source in range(lax.axis_size(axis))]
    return lax.ppermute(value, axis, pairs)


def halo_shards(state, operators, op_mask, site_bits, field, site_coupling, mode_coupling):
    site_count = lax.axis_size("site")
    phonon_count = lax.axis_size("phonon")
    bit_count = site_count.bit_length() - 1
    rows_here = state.shape[0]
    columns_here = state.shape[1]
    levels_here = columns_here // MODES
    block_edge = rows_here // op_mask.shape[1]
    expanded = jnp.repeat(jnp.repeat(op_mask, block_edge, axis=1), block_edge, axis=2)
    masked = jnp.where(expanded > 0, operators, jnp.zeros((), jnp.bfloat16))
    entries = jnp.float32(rows_here * columns_here * site_count * phonon_count)
    level_total = jnp.sqrt(jnp.float32(levels_here * phonon_count))
    device = lax.axis_index("site")
    inside = lax.iota(jnp.int32, rows_here)
    weight_rows = jnp.zeros((rows_here,), jnp.float32)
    for position in range(bit_count):
        weight_rows = weight_rows + site_coupling[site_bits[position]] * (
            device >> position & 1
        ).astype(jnp.float32)
    for local_bit in range(LBITS):
        weight_rows = weight_rows + site_coupling[bit_count + local_bit] * (
            inside >> local_bit & 1
        ).astype(jnp.float32)
    levels = (
        lax.axis_index("phonon") * levels_here + lax.iota(jnp.int32, columns_here) // MODES
    ).astype(jnp.float32)
    lower_weight = jnp.sqrt(levels)
    upper_weight = jnp.sqrt(levels + 1.0)
    mode_weight = jnp.tile(mode_coupling, columns_here // MODES) / level_total
    start_squares = lax.psum(jnp.sum(state * state), ("site", "phonon"))
    initial = state / jnp.sqrt(start_squares / entries + epsilon)
    previous = initial
    current = initial
    scale_prev = jnp.float32(1.0)
    moments = []
    for iteration in range(STEPS):
        extended = extended_2(current, (("phonon", 1),), MODES)
        lower_part = extended[:, :columns_here]
        upper_part = extended[:, 2 * MODES :]
        summed = weight_rows[:, None] * (
            mode_weight * (lower_weight * lower_part + upper_weight * upper_part)
        )
        for operate_position in range(bit_count):
            chosen = site_bits[operate_position]
            flipped = partner(current, "site", operate_position)
            product = jnp.dot(
                masked[chosen], flipped.astype(jnp.bfloat16), preferred_element_type=jnp.float32
            )
            summed = summed + (field[chosen] * flipped + product)
        if iteration == 0:
            vector_new = summed
        else:
            vector_new = 2.0 * summed - previous / scale_prev
        squares, intersection = lax.psum(
            (jnp.sum(vector_new * vector_new), jnp.sum(initial * vector_new)), ("site", "phonon")
        )
        scale_now = jnp.sqrt(squares / entries + epsilon)
        updated = vector_new / scale_now
        moment = intersection / (entries * scale_now)
        moments.append(moment)
        previous = current
        current = updated
        scale_prev = scale_now
    return (current, previous, jnp.stack(moments))


def solution(mesh):
    in_specs = (P("site", "phonon"), P(), P(), P(), P(), P(), P())
    out_specs = (P("site", "phonon"), P("site", "phonon"), P())

    def whole(state, operators, op_mask, *rest):
        rows = state.shape[0] // mesh.shape["site"]
        columns = state.shape[1] // mesh.shape["phonon"]
        plan = Plan(mesh, rows, columns, op_mask.shape[1])
        body = functools.partial(shards, plan) if plan.fits() else halo_shards
        run = jax.shard_map(body, mesh=mesh, in_specs=in_specs, out_specs=out_specs, check_vma=False)
        return run(state, operators, op_mask, *rest)

    return whole
```

```python
import functools

import jax
import jax.numpy as jnp
from jax import lax
from jax.experimental import pallas as pl
from jax.experimental.pallas import tpu as pltpu
from jax.sharding import PartitionSpec as P

LBITS = 10
MODES = 64
STEPS = 3
LANES = 128
SUBLANES = 8
SLOTS = 4
AXES = ("site", "phonon")

epsilon = 1e-06


VMEM = pl.BlockSpec(memory_space=pltpu.VMEM)
SMEM = pl.BlockSpec(memory_space=pltpu.SMEM)
HBM = pl.BlockSpec(memory_space=pltpu.HBM)


class Plan:
    def __init__(self, mesh, rows, columns, blocks):
        self.sites = mesh.shape["site"]
        self.phonons = mesh.shape["phonon"]
        self.groups = self.sites * self.phonons
        self.bits = self.sites.bit_length() - 1
        self.rows = rows
        self.columns = columns
        self.blocks = blocks
        self.edge = rows // blocks
        self.levels_here = columns // MODES
        self.level_count = self.levels_here * self.phonons
        self.share = MODES // self.groups
        self.pieces = self.levels_here * self.share
        self.lane_blocks = rows // LANES
        self.body = self.pieces * self.lane_blocks
        self.inward = self.body + 1
        self.outward = 2 * self.body + 1
        self.places = self.pieces * self.groups
        self.width = 2 * LANES
        self.parts = rows // self.width
        self.slabs = self.bits * self.parts
        self.kept = min(5, self.slabs - 1)
        self.entries = float(rows * columns * self.groups)

    def fits(self):
        return (
            MODES % self.groups == 0
            and self.columns == LANES
            and self.rows % self.width == 0
            and self.edge % LANES == 0
            and self.width % self.edge == 0
            and self.bits < SUBLANES
            and self.groups % SUBLANES == 0
        )


def params(mib):
    return pltpu.CompilerParams(vmem_limit_bytes=mib * 2**20)


def lane_sums(values):
    return jnp.sum(values, axis=0, keepdims=True)


def put_sums(out_ref, sums, start, stride, count):
    lane = lax.broadcasted_iota(jnp.int32, (1, LANES), 1)
    row = jnp.zeros((1, LANES), jnp.float32)
    for slot, value in enumerate(sums):
        width = LANES
        while width > LANES // SLOTS:
            width //= 2
            value = value + pltpu.roll(value, width, 1)
        row = jnp.where(lane // (LANES // SLOTS) == slot, value, row)
    out_ref[pl.ds(start, count, stride=stride), :] = jnp.broadcast_to(row, (count, LANES))


def totals_of(ref, start, stride, count):
    lanes = lane_sums(ref[pl.ds(start, count, stride=stride), :])
    width = LANES // SLOTS
    reach = width
    while reach > 1:
        reach //= 2
        lanes = lanes + pltpu.roll(lanes, LANES - reach, 1)
    return [lanes[:, slot * width : slot * width + 1] for slot in range(SLOTS)]


def scale_of(plan, squares):
    return jnp.sqrt(squares / plan.entries + epsilon)


def depart_kernel(plan, state_ref, out_ref, held_ref, semaphores):
    half = plan.rows // 2
    fetches = [
        pltpu.make_async_copy(
            state_ref.at[pl.ds(index * half, half), :], held_ref.at[pl.ds(index * half, half), :], semaphores.at[index]
        )
        for index in range(2)
    ]
    for fetch in fetches:
        fetch.start()
    sums = jnp.zeros((1, LANES), jnp.float32)
    for block in range(plan.lane_blocks):
        if block * LANES % half == 0:
            fetches[block * LANES // half].wait()
        tile = held_ref[pl.ds(block * LANES, LANES), :]
        sums = sums + lane_sums(tile * tile)
        turned = tile.T
        for piece in range(plan.pieces):
            out_ref[pl.ds(piece * plan.lane_blocks + block, plan.groups, stride=plan.inward), :] = turned[
                piece * plan.groups : (piece + 1) * plan.groups
            ]
    put_sums(out_ref, [sums], plan.body, plan.inward, plan.groups)


def fetch_slabs(plan, slabs, bits_ref, operators_ref, held_ref, semaphores):
    fetches = []
    for index, slab in enumerate(slabs):
        part, bit = divmod(slab, plan.bits)
        rows = pl.ds(part * plan.width, plan.width)
        fetch = pltpu.make_async_copy(
            operators_ref.at[bits_ref[bit], rows, :], held_ref.at[index], semaphores.at[index]
        )
        fetch.start()
        fetches.append(fetch)
    return fetches


def mask_slab(plan, slab, index, bits_ref, mask_ref, held_ref, out_ref):
    part, bit = divmod(slab, plan.bits)
    chosen = bits_ref[bit]
    for start in range(0, plan.width, plan.edge):
        across = (part * plan.width + start) // plan.edge
        rows = pl.ds(start, plan.edge)
        for along in range(plan.blocks):
            columns = pl.ds(along * plan.edge, plan.edge)
            keep = (mask_ref[chosen, across, along] > 0).astype(jnp.float32).astype(jnp.bfloat16)
            out_ref[index, columns, rows] = (held_ref[index, rows, columns] * keep).T


def store_kernel(plan, bits_ref, mask_ref, operators_ref, stored_ref, held_ref, masked_ref, in_semaphores, out_semaphores):
    slabs = range(plan.kept, plan.slabs)
    fetches = fetch_slabs(plan, slabs, bits_ref, operators_ref, held_ref, in_semaphores)
    stores = []
    for index, slab in enumerate(slabs):
        fetches[index].wait()
        mask_slab(plan, slab, index, bits_ref, mask_ref, held_ref, masked_ref)
        store = pltpu.make_async_copy(masked_ref.at[index], stored_ref.at[index], out_semaphores.at[index])
        store.start()
        stores.append(store)
    for store in stores:
        store.wait()


def prepare_kernel(
    plan,
    bits_ref,
    mask_ref,
    field_ref,
    coupling_ref,
    mode_ref,
    operators_ref,
    place_ref,
    inside_ref,
    kept_ref,
    held_ref,
    semaphores,
):
    slabs = range(plan.kept)
    fetches = fetch_slabs(plan, slabs, bits_ref, operators_ref, held_ref, semaphores)
    me = lax.axis_index("site") * plan.phonons + lax.axis_index("phonon")
    place = lax.broadcasted_iota(jnp.int32, (plan.places, LANES), 0)
    phonon = place % plan.phonons
    site = place // plan.phonons % plan.sites
    mode = place // plan.groups % plan.share
    level = phonon * plan.levels_here + place // (plan.groups * plan.share)
    occupied = jnp.zeros((plan.places, LANES), jnp.float32)
    for position in range(plan.bits):
        held = (site >> position & 1).astype(jnp.float32)
        occupied = occupied + coupling_ref[bits_ref[position]] * held
    strength = jnp.zeros((plan.places, LANES), jnp.float32)
    for index in range(plan.share):
        strength = jnp.where(mode == index, mode_ref[index * plan.groups + me], strength)
    strength = strength / jnp.sqrt(jnp.full((1, LANES), plan.level_count, jnp.float32))
    height = level.astype(jnp.float32)
    place_ref[0] = occupied
    place_ref[1] = strength * jnp.sqrt(height)
    place_ref[2] = jnp.where(level == plan.level_count - 1, 0.0, strength * jnp.sqrt(height + 1.0))
    inside = lax.broadcasted_iota(jnp.int32, (1, plan.rows), 1)
    weight = jnp.zeros((1, plan.rows), jnp.float32)
    for local_bit in range(LBITS):
        weight = weight + coupling_ref[plan.bits + local_bit] * (inside >> local_bit & 1).astype(jnp.float32)
    inside_ref[...] = jnp.zeros_like(inside_ref)
    inside_ref[:1] = weight
    for position in range(plan.bits):
        inside_ref[pl.ds(1 + position, 1)] = jnp.full((1, plan.rows), field_ref[bits_ref[position]])
    for slab in slabs:
        fetches[slab].wait()
        mask_slab(plan, slab, slab, bits_ref, mask_ref, held_ref, kept_ref)


def flipped(values, stride):
    places, width = values.shape
    if stride % SUBLANES == 0:
        shaped = values.reshape(places // (2 * stride), 2, stride, width)
        return jnp.concatenate([shaped[:, 1:], shaped[:, :1]], axis=1).reshape(places, width)
    tiles = values.reshape(places // SUBLANES, SUBLANES, width)
    if 2 * stride == SUBLANES:
        return pltpu.roll(tiles, stride, 1).reshape(places, width)
    spot = lax.broadcasted_iota(jnp.int32, tiles.shape, 1)
    down = pltpu.roll(tiles, stride, 1)
    up = pltpu.roll(tiles, SUBLANES - stride, 1)
    return jnp.where(spot & stride > 0, down, up).reshape(places, width)


def shifted(values, by):
    places, width = values.shape
    tiles = values.reshape(places // SUBLANES, SUBLANES, width)
    return pltpu.roll(tiles, by % SUBLANES, 1).reshape(places, width)


def put_rounded(plan, rounded_ref, vector, start):
    for position in range(plan.bits):
        rounded_ref[:, pl.ds(position * plan.rows + start, vector.shape[1])] = flipped(
            vector, plan.phonons << position
        ).astype(jnp.bfloat16)


def step(plan, vector_ref, rounded_ref, kept_ref, fetched_ref, place_ref, inside_ref, finish, ready=None, begun_ref=None):
    span = plan.places // plan.levels_here

    def local(start):
        lanes = pl.ds(start, LANES)
        vector = vector_ref[:, lanes]
        levels = [vector[index * span : (index + 1) * span] for index in range(plan.levels_here)]
        lower = jnp.concatenate([shifted(levels[-1], 1)] + levels[:-1], axis=0)
        upper = jnp.concatenate(levels[1:] + [shifted(levels[0], -1)], axis=0)
        weight = place_ref[0] + inside_ref[:1, lanes]
        total = weight * (place_ref[1] * lower + place_ref[2] * upper)
        for position in range(plan.bits):
            total = total + inside_ref[pl.ds(1 + position, 1), lanes] * flipped(vector, plan.phonons << position)
        return total

    def added(total, part, late):
        for ref, low, high in ((kept_ref, 0, plan.kept), (fetched_ref, plan.kept, plan.slabs)):
            fetched = low > 0
            begin = max(part * plan.bits, low)
            count = min((part + 1) * plan.bits, high) - begin
            if count <= 0 or late not in (None, fetched):
                continue
            if late:
                for slab in range(begin, begin + count):
                    ready(slab)
            first = begin - part * plan.bits
            masked = ref[pl.ds(begin - low, count)].reshape(count * plan.rows, plan.width)
            operand = rounded_ref[:, pl.ds(first * plan.rows, count * plan.rows)]
            total = total + jnp.dot(operand, masked, preferred_element_type=jnp.float32)
        return total

    def locals_of(lanes):
        return jnp.concatenate([local(start) for start in range(lanes.start, lanes.start + plan.width, LANES)], axis=1)

    parts = [pl.ds(part * plan.width, plan.width) for part in range(plan.parts)]
    if ready is None:
        for part, lanes in enumerate(parts):
            finish(lanes, added(locals_of(lanes), part, None))
        return
    for part, lanes in enumerate(parts):
        begun_ref[:, lanes] = added(locals_of(lanes), part, False)
    for part, lanes in enumerate(parts):
        finish(lanes, added(begun_ref[:, lanes], part, True))


def first_kernel(
    plan,
    arrived_ref,
    place_ref,
    inside_ref,
    kept_ref,
    stored_ref,
    initial_ref,
    new_ref,
    sums_ref,
    fetched_ref,
    rounded_ref,
    ahead_ref,
    semaphores,
):
    fetches = {}
    for slab in range(plan.kept, plan.slabs):
        index = slab - plan.kept
        fetches[slab] = pltpu.make_async_copy(stored_ref.at[index], fetched_ref.at[index], semaphores.at[index])
        fetches[slab].start()

    def ready(slab):
        fetches[slab].wait()

    squares = totals_of(arrived_ref, plan.body, plan.inward, plan.groups)[0]
    inverse = 1.0 / scale_of(plan, squares)
    for block in range(plan.lane_blocks):
        parts = [
            arrived_ref[pl.ds(piece * plan.lane_blocks + block, plan.groups, stride=plan.inward), :]
            for piece in range(plan.pieces)
        ]
        vector = jnp.concatenate(parts, axis=0) * inverse
        initial_ref[:, pl.ds(block * LANES, LANES)] = vector
        put_rounded(plan, rounded_ref, vector, block * LANES)
    tables = (kept_ref, fetched_ref, place_ref, inside_ref)
    squares = []
    overlap = []
    ahead = []

    def finish(lanes, new):
        new_ref[:, lanes] = new
        put_rounded(plan, ahead_ref, new, lanes.start)
        squares.append(lane_sums(new * new))
        overlap.append(lane_sums(new * initial_ref[:, lanes]))

    def look_ahead(lanes, total):
        new = 2.0 * total - initial_ref[:, lanes]
        ahead.append(lane_sums(new * new))

    step(plan, initial_ref, rounded_ref, *tables, finish, ready, new_ref)
    step(plan, new_ref, ahead_ref, *tables, look_ahead)
    put_sums(sums_ref, [one_row(squares), one_row(overlap), one_row(ahead)], 0, 1, plan.groups)


def one_row(rows):
    total = sum(rows[1:], rows[0])
    return sum(total[:, start : start + LANES] for start in range(0, total.shape[1], LANES))


def onward_kernel(
    plan,
    arrived_ref,
    raw_ref,
    initial_ref,
    place_ref,
    inside_ref,
    kept_ref,
    fetched_ref,
    out_ref,
    known_ref,
    rounded_ref,
    ahead_ref,
    second_ref,
    third_ref,
):
    squares, overlap, ahead, _ = totals_of(arrived_ref, 0, 1, plan.groups)
    first = 1.0 / scale_of(plan, squares)
    estimate = scale_of(plan, ahead * first * first)
    second = 1.0 / estimate
    for block in range(plan.lane_blocks):
        lanes = pl.ds(block * LANES, LANES)
        vector = raw_ref[:, lanes] * first
        second_ref[:, lanes] = vector
        put_rounded(plan, rounded_ref, vector, block * LANES)
    tables = (kept_ref, fetched_ref, place_ref, inside_ref)
    sums = [[] for _ in range(SLOTS)]

    def send(vector, lanes, new):
        sums[2 * vector].append(lane_sums(new * new))
        sums[2 * vector + 1].append(lane_sums(new * initial_ref[:, lanes]))
        for start in range(0, plan.width, LANES):
            block = (lanes.start + start) // LANES
            for piece in range(plan.pieces):
                row = vector * plan.body + piece * plan.lane_blocks + block
                out_ref[pl.ds(row, plan.groups, stride=plan.outward), :] = new[
                    piece * plan.groups : (piece + 1) * plan.groups, start : start + LANES
                ]

    def finish_second(lanes, total):
        new = 2.0 * total - initial_ref[:, lanes] * first
        vector = new * second
        third_ref[:, lanes] = vector
        put_rounded(plan, ahead_ref, vector, lanes.start)
        send(0, lanes, new)

    def finish_third(lanes, total):
        send(1, lanes, 2.0 * total - second_ref[:, lanes] * second)

    step(plan, second_ref, rounded_ref, *tables, finish_second)
    step(plan, third_ref, ahead_ref, *tables, finish_third)
    put_sums(out_ref, [one_row(rows) for rows in sums], 2 * plan.body, plan.outward, plan.groups)
    known_ref[:1, :] = jnp.broadcast_to(overlap * first / plan.entries, (1, LANES))
    known_ref[1:, :] = jnp.broadcast_to(estimate, (SUBLANES - 1, LANES))


def arrive_kernel(plan, arrived_ref, known_ref, before_ref, last_ref, moments_ref):
    before_squares, before_overlap, last_squares, last_overlap = totals_of(
        arrived_ref, 2 * plan.body, plan.outward, plan.groups
    )
    before = 1.0 / scale_of(plan, before_squares)
    back = known_ref[1:2, :1] * before
    last = back / scale_of(plan, last_squares * back * back)
    for vector, (out_ref, factor) in enumerate(((before_ref, before), (last_ref, last))):
        for block in range(plan.lane_blocks):
            first = vector * plan.body + block
            parts = [
                arrived_ref[pl.ds(first + piece * plan.lane_blocks, plan.groups, stride=plan.outward), :]
                for piece in range(plan.pieces)
            ]
            out_ref[pl.ds(block * LANES, LANES), :] = jnp.concatenate(parts, axis=0).T * factor
    moments_ref[0] = known_ref[0, 0]
    moments_ref[1] = (before_overlap * before / plan.entries)[0, 0]
    moments_ref[2] = (last_overlap * last / plan.entries)[0, 0]


def exchange(values, count):
    shaped = values.reshape(count, values.shape[0] // count, 1, LANES)
    return lax.all_to_all(shaped, AXES, 0, 0, tiled=True).reshape(values.shape)


def shards(plan, state, operators, op_mask, site_bits, field, site_coupling, mode_coupling):
    f32 = jnp.float32
    inward = jax.ShapeDtypeStruct((plan.groups * plan.inward, LANES), f32)
    outward = jax.ShapeDtypeStruct((plan.groups * plan.outward, LANES), f32)
    vector = jax.ShapeDtypeStruct((plan.places, plan.rows), f32)
    known = jax.ShapeDtypeStruct((SUBLANES, LANES), f32)
    held = jax.ShapeDtypeStruct((plan.rows, plan.columns), f32)
    rounded = pltpu.VMEM((plan.places, plan.bits * plan.rows), jnp.bfloat16)
    working = pltpu.VMEM((plan.places, plan.rows), f32)
    work = 2 * plan.bits * plan.places * plan.rows * plan.rows

    def cost(flops, moved):
        return pl.CostEstimate(flops=flops, bytes_accessed=moved, transcendentals=0)

    departing = pl.pallas_call(
        functools.partial(depart_kernel, plan),
        out_shape=inward,
        in_specs=[HBM],
        out_specs=VMEM,
        scratch_shapes=[pltpu.VMEM((plan.rows, plan.columns), f32), pltpu.SemaphoreType.DMA((2,))],
        compiler_params=params(60),
        name="depart",
    )(state)
    arrived = exchange(departing, plan.groups)
    fetched = plan.slabs - plan.kept
    kept_slabs = (plan.kept, plan.rows, plan.width)
    fetched_slabs = (fetched, plan.rows, plan.width)

    def held_slabs(count):
        return pltpu.VMEM((count, plan.width, plan.rows), jnp.bfloat16)

    place, inside, kept = pl.pallas_call(
        functools.partial(prepare_kernel, plan),
        out_shape=[
            jax.ShapeDtypeStruct((3, plan.places, LANES), f32),
            jax.ShapeDtypeStruct((SUBLANES, plan.rows), f32),
            jax.ShapeDtypeStruct(kept_slabs, jnp.bfloat16),
        ],
        in_specs=[SMEM] * 5 + [HBM],
        out_specs=[VMEM] * 3,
        scratch_shapes=[held_slabs(plan.kept), pltpu.SemaphoreType.DMA((plan.kept,))],
        compiler_params=params(50),
        cost_estimate=cost(plan.rows * plan.rows, 4 * plan.kept * plan.rows * plan.width),
        name="prepare",
    )(site_bits, op_mask, field, site_coupling, mode_coupling, operators)
    stored = pl.pallas_call(
        functools.partial(store_kernel, plan),
        out_shape=jax.ShapeDtypeStruct(fetched_slabs, jnp.bfloat16),
        in_specs=[SMEM] * 2 + [HBM],
        out_specs=HBM,
        scratch_shapes=[
            held_slabs(fetched),
            pltpu.VMEM(fetched_slabs, jnp.bfloat16),
            pltpu.SemaphoreType.DMA((fetched,)),
            pltpu.SemaphoreType.DMA((fetched,)),
        ],
        compiler_params=params(60),
        cost_estimate=cost(plan.rows * plan.rows, 4 * fetched * plan.rows * plan.width),
        name="store",
    )(site_bits, op_mask, operators)
    initial, raw, sums, late = pl.pallas_call(
        functools.partial(first_kernel, plan),
        out_shape=[
            vector,
            vector,
            jax.ShapeDtypeStruct((plan.groups, LANES), f32),
            jax.ShapeDtypeStruct(fetched_slabs, jnp.bfloat16),
        ],
        in_specs=[VMEM] * 4 + [HBM],
        out_specs=[VMEM] * 4,
        scratch_shapes=[rounded, rounded, pltpu.SemaphoreType.DMA((fetched,))],
        compiler_params=params(46),
        cost_estimate=cost(2 * work, 4 * plan.places * plan.rows),
        name="first",
    )(arrived, place, inside, kept, stored)
    tables = (place, inside, kept, late)
    sums = exchange(sums, plan.groups)
    departing, told = pl.pallas_call(
        functools.partial(onward_kernel, plan),
        out_shape=[outward, known],
        in_specs=[VMEM] * 7,
        out_specs=[VMEM] * 2,
        scratch_shapes=[rounded, rounded, working, working],
        compiler_params=params(32),
        cost_estimate=cost(2 * work, 8 * plan.places * plan.rows),
        name="onward",
    )(sums, raw, initial, *tables)
    arrived = exchange(departing, plan.groups)
    before, last, moments = pl.pallas_call(
        functools.partial(arrive_kernel, plan),
        out_shape=[held, held, jax.ShapeDtypeStruct((STEPS,), f32)],
        in_specs=[VMEM] * 2,
        out_specs=[VMEM, VMEM, SMEM],
        compiler_params=params(16),
        name="arrive",
    )(arrived, told)
    return last, before, moments


def extended_2(block, sides, width):
    for axis, dim in sides:
        count = lax.axis_size(axis)
        forward = [(i, i + 1) for i in range(count - 1)]
        backward = [(target, source) for source, target in forward]
        low = lax.ppermute(
            lax.slice_in_dim(block, block.shape[dim] - width, None, axis=dim), axis, forward
        )
        high = lax.ppermute(lax.slice_in_dim(block, 0, width, axis=dim), axis, backward)
        block = jnp.concatenate([low, block, high], axis=dim)
    return block


def partner(value, axis, bit):
    mask = 2**bit
    pairs = [(source, source ^ mask) for source in range(lax.axis_size(axis))]
    return lax.ppermute(value, axis, pairs)


def halo_shards(state, operators, op_mask, site_bits, field, site_coupling, mode_coupling):
    site_count = lax.axis_size("site")
    phonon_count = lax.axis_size("phonon")
    bit_count = site_count.bit_length() - 1
    rows_here = state.shape[0]
    columns_here = state.shape[1]
    levels_here = columns_here // MODES
    block_edge = rows_here // op_mask.shape[1]
    expanded = jnp.repeat(jnp.repeat(op_mask, block_edge, axis=1), block_edge, axis=2)
    masked = jnp.where(expanded > 0, operators, jnp.zeros((), jnp.bfloat16))
    entries = jnp.float32(rows_here * columns_here * site_count * phonon_count)
    level_total = jnp.sqrt(jnp.float32(levels_here * phonon_count))
    device = lax.axis_index("site")
    inside = lax.iota(jnp.int32, rows_here)
    weight_rows = jnp.zeros((rows_here,), jnp.float32)
    for position in range(bit_count):
        weight_rows = weight_rows + site_coupling[site_bits[position]] * (
            device >> position & 1
        ).astype(jnp.float32)
    for local_bit in range(LBITS):
        weight_rows = weight_rows + site_coupling[bit_count + local_bit] * (
            inside >> local_bit & 1
        ).astype(jnp.float32)
    levels = (
        lax.axis_index("phonon") * levels_here + lax.iota(jnp.int32, columns_here) // MODES
    ).astype(jnp.float32)
    lower_weight = jnp.sqrt(levels)
    upper_weight = jnp.sqrt(levels + 1.0)
    mode_weight = jnp.tile(mode_coupling, columns_here // MODES) / level_total
    start_squares = lax.psum(jnp.sum(state * state), ("site", "phonon"))
    initial = state / jnp.sqrt(start_squares / entries + epsilon)
    previous = initial
    current = initial
    scale_prev = jnp.float32(1.0)
    moments = []
    for iteration in range(STEPS):
        extended = extended_2(current, (("phonon", 1),), MODES)
        lower_part = extended[:, :columns_here]
        upper_part = extended[:, 2 * MODES :]
        summed = weight_rows[:, None] * (
            mode_weight * (lower_weight * lower_part + upper_weight * upper_part)
        )
        for operate_position in range(bit_count):
            chosen = site_bits[operate_position]
            flipped = partner(current, "site", operate_position)
            product = jnp.dot(
                masked[chosen], flipped.astype(jnp.bfloat16), preferred_element_type=jnp.float32
            )
            summed = summed + (field[chosen] * flipped + product)
        if iteration == 0:
            vector_new = summed
        else:
            vector_new = 2.0 * summed - previous / scale_prev
        squares, intersection = lax.psum(
            (jnp.sum(vector_new * vector_new), jnp.sum(initial * vector_new)), ("site", "phonon")
        )
        scale_now = jnp.sqrt(squares / entries + epsilon)
        updated = vector_new / scale_now
        moment = intersection / (entries * scale_now)
        moments.append(moment)
        previous = current
        current = updated
        scale_prev = scale_now
    return (current, previous, jnp.stack(moments))


def solution(mesh):
    in_specs = (P("site", "phonon"), P(), P(), P(), P(), P(), P())
    out_specs = (P("site", "phonon"), P("site", "phonon"), P())

    def whole(state, operators, op_mask, *rest):
        rows = state.shape[0] // mesh.shape["site"]
        columns = state.shape[1] // mesh.shape["phonon"]
        plan = Plan(mesh, rows, columns, op_mask.shape[1])
        body = functools.partial(shards, plan) if plan.fits() else halo_shards
        run = jax.shard_map(body, mesh=mesh, in_specs=in_specs, out_specs=out_specs, check_vma=False)
        return run(state, operators, op_mask, *rest)

    return whole
```

```python
import functools

import jax
import jax.numpy as jnp
from jax import lax
from jax.experimental import pallas as pl
from jax.experimental.pallas import tpu as pltpu
from jax.sharding import PartitionSpec as P

LBITS = 10
MODES = 64
STEPS = 3
LANES = 128
SUBLANES = 8
SLOTS = 4
SMALL = 3
AXES = ("site", "phonon")

epsilon = 1e-06


VMEM = pl.BlockSpec(memory_space=pltpu.VMEM)
SMEM = pl.BlockSpec(memory_space=pltpu.SMEM)
HBM = pl.BlockSpec(memory_space=pltpu.HBM)


class Plan:
    def __init__(self, mesh, rows, columns, blocks):
        self.sites = mesh.shape["site"]
        self.phonons = mesh.shape["phonon"]
        self.groups = self.sites * self.phonons
        self.bits = self.sites.bit_length() - 1
        self.rows = rows
        self.columns = columns
        self.blocks = blocks
        self.edge = rows // blocks
        self.levels_here = columns // MODES
        self.level_count = self.levels_here * self.phonons
        self.share = MODES // self.groups
        self.pieces = self.levels_here * self.share
        self.lane_blocks = rows // LANES
        self.body = self.pieces * self.lane_blocks
        self.inward = self.body + 1
        self.outward = 2 * self.body + 1
        self.places = self.pieces * self.groups
        self.width = 2 * LANES
        self.parts = rows // self.width
        self.slabs = self.bits * self.parts
        self.kept = min(5, self.slabs - 1)
        self.entries = float(rows * columns * self.groups)

    def fits(self):
        return (
            MODES % self.groups == 0
            and self.columns == LANES
            and self.rows % self.width == 0
            and self.edge % LANES == 0
            and self.width % self.edge == 0
            and self.bits < SUBLANES
            and self.groups % SUBLANES == 0
        )


def params(mib):
    return pltpu.CompilerParams(vmem_limit_bytes=mib * 2**20)


def lane_sums(values):
    return jnp.sum(values, axis=0, keepdims=True)


def put_sums(out_ref, sums, start, stride, count):
    lane = lax.broadcasted_iota(jnp.int32, (1, LANES), 1)
    row = jnp.zeros((1, LANES), jnp.float32)
    for slot, value in enumerate(sums):
        width = LANES
        while width > LANES // SLOTS:
            width //= 2
            value = value + pltpu.roll(value, width, 1)
        row = jnp.where(lane // (LANES // SLOTS) == slot, value, row)
    out_ref[pl.ds(start, count, stride=stride), :] = jnp.broadcast_to(row, (count, LANES))


def put_rows(out_ref, sums, start, stride, count):
    for index, value in enumerate(sums):
        out_ref[pl.ds(start + index, count, stride=stride), :] = jnp.broadcast_to(value, (count, LANES))


def total_of(ref, start, stride, count):
    return jnp.sum(lane_sums(ref[pl.ds(start, count, stride=stride), :]), axis=1, keepdims=True)


def totals_of(ref, start, stride, count):
    lanes = lane_sums(ref[pl.ds(start, count, stride=stride), :])
    lane = lax.broadcasted_iota(jnp.int32, (1, LANES), 1)
    return [
        jnp.sum(jnp.where(lane // (LANES // SLOTS) == slot, lanes, 0.0), axis=1, keepdims=True)
        for slot in range(SLOTS)
    ]


def scale_of(plan, squares):
    return jnp.sqrt(squares / plan.entries + epsilon)


def depart_kernel(plan, state_ref, out_ref, held_ref, semaphores):
    half = plan.rows // 2
    fetches = [
        pltpu.make_async_copy(
            state_ref.at[pl.ds(index * half, half), :], held_ref.at[pl.ds(index * half, half), :], semaphores.at[index]
        )
        for index in range(2)
    ]
    for fetch in fetches:
        fetch.start()
    sums = jnp.zeros((1, LANES), jnp.float32)
    for block in range(plan.lane_blocks):
        if block * LANES % half == 0:
            fetches[block * LANES // half].wait()
        tile = held_ref[pl.ds(block * LANES, LANES), :]
        sums = sums + lane_sums(tile * tile)
        turned = tile.T
        for piece in range(plan.pieces):
            out_ref[pl.ds(piece * plan.lane_blocks + block, plan.groups, stride=plan.inward), :] = turned[
                piece * plan.groups : (piece + 1) * plan.groups
            ]
    put_rows(out_ref, [sums], plan.body, plan.inward, plan.groups)


def fetch_slabs(plan, slabs, bits_ref, operators_ref, held_ref, semaphores):
    fetches = []
    for index, slab in enumerate(slabs):
        part, bit = divmod(slab, plan.bits)
        rows = pl.ds(part * plan.width, plan.width)
        fetch = pltpu.make_async_copy(
            operators_ref.at[bits_ref[bit], rows, :], held_ref.at[index], semaphores.at[index]
        )
        fetch.start()
        fetches.append(fetch)
    return fetches


def mask_slab(plan, slab, index, bits_ref, mask_ref, held_ref, out_ref):
    part, bit = divmod(slab, plan.bits)
    chosen = bits_ref[bit]
    for start in range(0, plan.width, plan.edge):
        across = (part * plan.width + start) // plan.edge
        rows = pl.ds(start, plan.edge)
        for along in range(plan.blocks):
            columns = pl.ds(along * plan.edge, plan.edge)
            keep = (mask_ref[chosen, across, along] > 0).astype(jnp.float32).astype(jnp.bfloat16)
            out_ref[index, columns, rows] = (held_ref[index, rows, columns] * keep).T


def store_kernel(plan, bits_ref, mask_ref, operators_ref, stored_ref, held_ref, masked_ref, in_semaphores, out_semaphores):
    slabs = range(plan.kept, plan.slabs)
    fetches = fetch_slabs(plan, slabs, bits_ref, operators_ref, held_ref, in_semaphores)
    stores = []
    for index, slab in enumerate(slabs):
        fetches[index].wait()
        mask_slab(plan, slab, index, bits_ref, mask_ref, held_ref, masked_ref)
        store = pltpu.make_async_copy(masked_ref.at[index], stored_ref.at[index], out_semaphores.at[index])
        store.start()
        stores.append(store)
    for store in stores:
        store.wait()


def prepare_kernel(
    plan,
    bits_ref,
    mask_ref,
    field_ref,
    coupling_ref,
    mode_ref,
    operators_ref,
    place_ref,
    inside_ref,
    kept_ref,
    held_ref,
    semaphores,
):
    slabs = range(plan.kept)
    fetches = fetch_slabs(plan, slabs, bits_ref, operators_ref, held_ref, semaphores)
    me = lax.axis_index("site") * plan.phonons + lax.axis_index("phonon")
    place = lax.broadcasted_iota(jnp.int32, (plan.places, LANES), 0)
    phonon = place % plan.phonons
    site = place // plan.phonons % plan.sites
    mode = place // plan.groups % plan.share
    level = phonon * plan.levels_here + place // (plan.groups * plan.share)
    occupied = jnp.zeros((plan.places, LANES), jnp.float32)
    for position in range(plan.bits):
        held = (site >> position & 1).astype(jnp.float32)
        occupied = occupied + coupling_ref[bits_ref[position]] * held
    strength = jnp.zeros((plan.places, LANES), jnp.float32)
    for index in range(plan.share):
        strength = jnp.where(mode == index, mode_ref[index * plan.groups + me], strength)
    strength = strength / jnp.sqrt(jnp.full((1, LANES), plan.level_count, jnp.float32))
    height = level.astype(jnp.float32)
    place_ref[0] = occupied
    place_ref[1] = strength * jnp.sqrt(height)
    place_ref[2] = jnp.where(level == plan.level_count - 1, 0.0, strength * jnp.sqrt(height + 1.0))
    inside = lax.broadcasted_iota(jnp.int32, (1, plan.rows), 1)
    weight = jnp.zeros((1, plan.rows), jnp.float32)
    for local_bit in range(LBITS):
        weight = weight + coupling_ref[plan.bits + local_bit] * (inside >> local_bit & 1).astype(jnp.float32)
    inside_ref[...] = jnp.zeros_like(inside_ref)
    inside_ref[:1] = weight
    for position in range(plan.bits):
        inside_ref[pl.ds(1 + position, 1)] = jnp.full((1, plan.rows), field_ref[bits_ref[position]])
    for slab in slabs:
        fetches[slab].wait()
        mask_slab(plan, slab, slab, bits_ref, mask_ref, held_ref, kept_ref)


def flipped(values, stride):
    places, width = values.shape
    if stride % SUBLANES == 0:
        shaped = values.reshape(places // (2 * stride), 2, stride, width)
        return jnp.concatenate([shaped[:, 1:], shaped[:, :1]], axis=1).reshape(places, width)
    tiles = values.reshape(places // SUBLANES, SUBLANES, width)
    if 2 * stride == SUBLANES:
        return pltpu.roll(tiles, stride, 1).reshape(places, width)
    spot = lax.broadcasted_iota(jnp.int32, tiles.shape, 1)
    down = pltpu.roll(tiles, stride, 1)
    up = pltpu.roll(tiles, SUBLANES - stride, 1)
    return jnp.where(spot & stride > 0, down, up).reshape(places, width)


def shifted(values, by):
    places, width = values.shape
    tiles = values.reshape(places // SUBLANES, SUBLANES, width)
    return pltpu.roll(tiles, by % SUBLANES, 1).reshape(places, width)


def put_rounded(plan, rounded_ref, vector, start):
    for position in range(plan.bits):
        rounded_ref[:, pl.ds(position * plan.rows + start, vector.shape[1])] = flipped(
            vector, plan.phonons << position
        ).astype(jnp.bfloat16)


def step(plan, vector_ref, rounded_ref, kept_ref, fetched_ref, place_ref, inside_ref, finish, ready=None, begun_ref=None):
    span = plan.places // plan.levels_here

    def local(start):
        lanes = pl.ds(start, LANES)
        vector = vector_ref[:, lanes]
        levels = [vector[index * span : (index + 1) * span] for index in range(plan.levels_here)]
        lower = jnp.concatenate([shifted(levels[-1], 1)] + levels[:-1], axis=0)
        upper = jnp.concatenate(levels[1:] + [shifted(levels[0], -1)], axis=0)
        weight = place_ref[0] + inside_ref[:1, lanes]
        total = weight * (place_ref[1] * lower + place_ref[2] * upper)
        for position in range(plan.bits):
            total = total + inside_ref[pl.ds(1 + position, 1), lanes] * flipped(vector, plan.phonons << position)
        return total

    def added(total, part, late):
        for ref, low, high in ((kept_ref, 0, plan.kept), (fetched_ref, plan.kept, plan.slabs)):
            fetched = low > 0
            begin = max(part * plan.bits, low)
            count = min((part + 1) * plan.bits, high) - begin
            if count <= 0 or late not in (None, fetched):
                continue
            if late:
                for slab in range(begin, begin + count):
                    ready(slab)
            first = begin - part * plan.bits
            masked = ref[pl.ds(begin - low, count)].reshape(count * plan.rows, plan.width)
            operand = rounded_ref[:, pl.ds(first * plan.rows, count * plan.rows)]
            total = total + jnp.dot(operand, masked, preferred_element_type=jnp.float32)
        return total

    def locals_of(lanes):
        return jnp.concatenate([local(start) for start in range(lanes.start, lanes.start + plan.width, LANES)], axis=1)

    parts = [pl.ds(part * plan.width, plan.width) for part in range(plan.parts)]
    if ready is None:
        for part, lanes in enumerate(parts):
            finish(lanes, added(locals_of(lanes), part, None))
        return
    for part, lanes in enumerate(parts):
        begun_ref[:, lanes] = added(locals_of(lanes), part, False)
    for part, lanes in enumerate(parts):
        finish(lanes, added(begun_ref[:, lanes], part, True))


def first_kernel(
    plan,
    arrived_ref,
    place_ref,
    inside_ref,
    kept_ref,
    stored_ref,
    initial_ref,
    new_ref,
    sums_ref,
    fetched_ref,
    rounded_ref,
    ahead_ref,
    semaphores,
):
    fetches = {}
    for slab in range(plan.kept, plan.slabs):
        index = slab - plan.kept
        fetches[slab] = pltpu.make_async_copy(stored_ref.at[index], fetched_ref.at[index], semaphores.at[index])
        fetches[slab].start()

    def ready(slab):
        fetches[slab].wait()

    squares = total_of(arrived_ref, plan.body, plan.inward, plan.groups)
    inverse = 1.0 / scale_of(plan, squares)
    for block in range(plan.lane_blocks):
        parts = [
            arrived_ref[pl.ds(piece * plan.lane_blocks + block, plan.groups, stride=plan.inward), :]
            for piece in range(plan.pieces)
        ]
        vector = jnp.concatenate(parts, axis=0) * inverse
        initial_ref[:, pl.ds(block * LANES, LANES)] = vector
        put_rounded(plan, rounded_ref, vector, block * LANES)
    tables = (kept_ref, fetched_ref, place_ref, inside_ref)
    squares = []
    overlap = []
    ahead = []

    def finish(lanes, new):
        new_ref[:, lanes] = new
        put_rounded(plan, ahead_ref, new, lanes.start)
        squares.append(lane_sums(new * new))
        overlap.append(lane_sums(new * initial_ref[:, lanes]))

    def look_ahead(lanes, total):
        new = 2.0 * total - initial_ref[:, lanes]
        ahead.append(lane_sums(new * new))

    step(plan, initial_ref, rounded_ref, *tables, finish, ready, new_ref)
    step(plan, new_ref, ahead_ref, *tables, look_ahead)
    put_rows(sums_ref, [one_row(squares), one_row(overlap), one_row(ahead)], 0, SMALL, plan.groups)


def one_row(rows):
    total = sum(rows[1:], rows[0])
    return sum(total[:, start : start + LANES] for start in range(0, total.shape[1], LANES))


def onward_kernel(
    plan,
    arrived_ref,
    raw_ref,
    initial_ref,
    place_ref,
    inside_ref,
    kept_ref,
    fetched_ref,
    out_ref,
    known_ref,
    rounded_ref,
    ahead_ref,
    second_ref,
    third_ref,
):
    squares, overlap, ahead = [total_of(arrived_ref, row, SMALL, plan.groups) for row in range(SMALL)]
    first = 1.0 / scale_of(plan, squares)
    estimate = scale_of(plan, ahead * first * first)
    second = 1.0 / estimate
    known_ref[:1, :] = jnp.broadcast_to(overlap * first / plan.entries, (1, LANES))
    known_ref[1:, :] = jnp.broadcast_to(estimate, (SUBLANES - 1, LANES))
    for block in range(plan.lane_blocks):
        lanes = pl.ds(block * LANES, LANES)
        vector = raw_ref[:, lanes] * first
        second_ref[:, lanes] = vector
        put_rounded(plan, rounded_ref, vector, block * LANES)
    tables = (kept_ref, fetched_ref, place_ref, inside_ref)
    sums = [[] for _ in range(SLOTS)]

    def send(vector, lanes, new):
        sums[2 * vector].append(lane_sums(new * new))
        sums[2 * vector + 1].append(lane_sums(new * initial_ref[:, lanes]))
        for start in range(0, plan.width, LANES):
            block = (lanes.start + start) // LANES
            for piece in range(plan.pieces):
                row = vector * plan.body + piece * plan.lane_blocks + block
                out_ref[pl.ds(row, plan.groups, stride=plan.outward), :] = new[
                    piece * plan.groups : (piece + 1) * plan.groups, start : start + LANES
                ]

    def finish_second(lanes, total):
        new = 2.0 * total - initial_ref[:, lanes] * first
        vector = new * second
        third_ref[:, lanes] = vector
        put_rounded(plan, ahead_ref, vector, lanes.start)
        send(0, lanes, new)

    def finish_third(lanes, total):
        send(1, lanes, 2.0 * total - second_ref[:, lanes] * second)

    step(plan, second_ref, rounded_ref, *tables, finish_second)
    step(plan, third_ref, ahead_ref, *tables, finish_third)
    put_sums(out_ref, [one_row(rows) for rows in sums], 2 * plan.body, plan.outward, plan.groups)


def arrive_kernel(plan, arrived_ref, known_ref, before_ref, last_ref, moments_ref):
    before_squares, before_overlap, last_squares, last_overlap = totals_of(
        arrived_ref, 2 * plan.body, plan.outward, plan.groups
    )
    before = 1.0 / scale_of(plan, before_squares)
    back = known_ref[1:2, :1] * before
    last = back / scale_of(plan, last_squares * back * back)
    for vector, (out_ref, factor) in enumerate(((before_ref, before), (last_ref, last))):
        for block in range(plan.lane_blocks):
            first = vector * plan.body + block
            parts = [
                arrived_ref[pl.ds(first + piece * plan.lane_blocks, plan.groups, stride=plan.outward), :]
                for piece in range(plan.pieces)
            ]
            out_ref[pl.ds(block * LANES, LANES), :] = jnp.concatenate(parts, axis=0).T * factor
    moments_ref[0] = known_ref[0, 0]
    moments_ref[1] = (before_overlap * before / plan.entries)[0, 0]
    moments_ref[2] = (last_overlap * last / plan.entries)[0, 0]


def exchange(values, count):
    shaped = values.reshape(count, values.shape[0] // count, 1, LANES)
    return lax.all_to_all(shaped, AXES, 0, 0, tiled=True).reshape(values.shape)


def shards(plan, state, operators, op_mask, site_bits, field, site_coupling, mode_coupling):
    f32 = jnp.float32
    inward = jax.ShapeDtypeStruct((plan.groups * plan.inward, LANES), f32)
    outward = jax.ShapeDtypeStruct((plan.groups * plan.outward, LANES), f32)
    vector = jax.ShapeDtypeStruct((plan.places, plan.rows), f32)
    known = jax.ShapeDtypeStruct((SUBLANES, LANES), f32)
    held = jax.ShapeDtypeStruct((plan.rows, plan.columns), f32)
    rounded = pltpu.VMEM((plan.places, plan.bits * plan.rows), jnp.bfloat16)
    working = pltpu.VMEM((plan.places, plan.rows), f32)
    work = 2 * plan.bits * plan.places * plan.rows * plan.rows

    def cost(flops, moved):
        return pl.CostEstimate(flops=flops, bytes_accessed=moved, transcendentals=0)

    departing = pl.pallas_call(
        functools.partial(depart_kernel, plan),
        out_shape=inward,
        in_specs=[HBM],
        out_specs=VMEM,
        scratch_shapes=[pltpu.VMEM((plan.rows, plan.columns), f32), pltpu.SemaphoreType.DMA((2,))],
        compiler_params=params(60),
        name="depart",
    )(state)
    arrived = exchange(departing, plan.groups)
    fetched = plan.slabs - plan.kept
    kept_slabs = (plan.kept, plan.rows, plan.width)
    fetched_slabs = (fetched, plan.rows, plan.width)

    def held_slabs(count):
        return pltpu.VMEM((count, plan.width, plan.rows), jnp.bfloat16)

    place, inside, kept = pl.pallas_call(
        functools.partial(prepare_kernel, plan),
        out_shape=[
            jax.ShapeDtypeStruct((3, plan.places, LANES), f32),
            jax.ShapeDtypeStruct((SUBLANES, plan.rows), f32),
            jax.ShapeDtypeStruct(kept_slabs, jnp.bfloat16),
        ],
        in_specs=[SMEM] * 5 + [HBM],
        out_specs=[VMEM] * 3,
        scratch_shapes=[held_slabs(plan.kept), pltpu.SemaphoreType.DMA((plan.kept,))],
        compiler_params=params(50),
        cost_estimate=cost(plan.rows * plan.rows, 4 * plan.kept * plan.rows * plan.width),
        name="prepare",
    )(site_bits, op_mask, field, site_coupling, mode_coupling, operators)
    stored = pl.pallas_call(
        functools.partial(store_kernel, plan),
        out_shape=jax.ShapeDtypeStruct(fetched_slabs, jnp.bfloat16),
        in_specs=[SMEM] * 2 + [HBM],
        out_specs=HBM,
        scratch_shapes=[
            held_slabs(fetched),
            pltpu.VMEM(fetched_slabs, jnp.bfloat16),
            pltpu.SemaphoreType.DMA((fetched,)),
            pltpu.SemaphoreType.DMA((fetched,)),
        ],
        compiler_params=params(60),
        cost_estimate=cost(plan.rows * plan.rows, 4 * fetched * plan.rows * plan.width),
        name="store",
    )(site_bits, op_mask, operators)
    initial, raw, sums, late = pl.pallas_call(
        functools.partial(first_kernel, plan),
        out_shape=[
            vector,
            vector,
            jax.ShapeDtypeStruct((plan.groups * SMALL, LANES), f32),
            jax.ShapeDtypeStruct(fetched_slabs, jnp.bfloat16),
        ],
        in_specs=[VMEM] * 4 + [HBM],
        out_specs=[VMEM] * 4,
        scratch_shapes=[rounded, rounded, pltpu.SemaphoreType.DMA((fetched,))],
        compiler_params=params(46),
        cost_estimate=cost(2 * work, 4 * plan.places * plan.rows),
        name="first",
    )(arrived, place, inside, kept, stored)
    tables = (place, inside, kept, late)
    sums = exchange(sums, plan.groups)
    departing, told = pl.pallas_call(
        functools.partial(onward_kernel, plan),
        out_shape=[outward, known],
        in_specs=[VMEM] * 7,
        out_specs=[VMEM] * 2,
        scratch_shapes=[rounded, rounded, working, working],
        compiler_params=params(32),
        cost_estimate=cost(2 * work, 8 * plan.places * plan.rows),
        name="onward",
    )(sums, raw, initial, *tables)
    arrived = exchange(departing, plan.groups)
    before, last, moments = pl.pallas_call(
        functools.partial(arrive_kernel, plan),
        out_shape=[held, held, jax.ShapeDtypeStruct((STEPS,), f32)],
        in_specs=[VMEM] * 2,
        out_specs=[VMEM, VMEM, SMEM],
        compiler_params=params(16),
        name="arrive",
    )(arrived, told)
    return last, before, moments


def extended_2(block, sides, width):
    for axis, dim in sides:
        count = lax.axis_size(axis)
        forward = [(i, i + 1) for i in range(count - 1)]
        backward = [(target, source) for source, target in forward]
        low = lax.ppermute(
            lax.slice_in_dim(block, block.shape[dim] - width, None, axis=dim), axis, forward
        )
        high = lax.ppermute(lax.slice_in_dim(block, 0, width, axis=dim), axis, backward)
        block = jnp.concatenate([low, block, high], axis=dim)
    return block


def partner(value, axis, bit):
    mask = 2**bit
    pairs = [(source, source ^ mask) for source in range(lax.axis_size(axis))]
    return lax.ppermute(value, axis, pairs)


def halo_shards(state, operators, op_mask, site_bits, field, site_coupling, mode_coupling):
    site_count = lax.axis_size("site")
    phonon_count = lax.axis_size("phonon")
    bit_count = site_count.bit_length() - 1
    rows_here = state.shape[0]
    columns_here = state.shape[1]
    levels_here = columns_here // MODES
    block_edge = rows_here // op_mask.shape[1]
    expanded = jnp.repeat(jnp.repeat(op_mask, block_edge, axis=1), block_edge, axis=2)
    masked = jnp.where(expanded > 0, operators, jnp.zeros((), jnp.bfloat16))
    entries = jnp.float32(rows_here * columns_here * site_count * phonon_count)
    level_total = jnp.sqrt(jnp.float32(levels_here * phonon_count))
    device = lax.axis_index("site")
    inside = lax.iota(jnp.int32, rows_here)
    weight_rows = jnp.zeros((rows_here,), jnp.float32)
    for position in range(bit_count):
        weight_rows = weight_rows + site_coupling[site_bits[position]] * (
            device >> position & 1
        ).astype(jnp.float32)
    for local_bit in range(LBITS):
        weight_rows = weight_rows + site_coupling[bit_count + local_bit] * (
            inside >> local_bit & 1
        ).astype(jnp.float32)
    levels = (
        lax.axis_index("phonon") * levels_here + lax.iota(jnp.int32, columns_here) // MODES
    ).astype(jnp.float32)
    lower_weight = jnp.sqrt(levels)
    upper_weight = jnp.sqrt(levels + 1.0)
    mode_weight = jnp.tile(mode_coupling, columns_here // MODES) / level_total
    start_squares = lax.psum(jnp.sum(state * state), ("site", "phonon"))
    initial = state / jnp.sqrt(start_squares / entries + epsilon)
    previous = initial
    current = initial
    scale_prev = jnp.float32(1.0)
    moments = []
    for iteration in range(STEPS):
        extended = extended_2(current, (("phonon", 1),), MODES)
        lower_part = extended[:, :columns_here]
        upper_part = extended[:, 2 * MODES :]
        summed = weight_rows[:, None] * (
            mode_weight * (lower_weight * lower_part + upper_weight * upper_part)
        )
        for operate_position in range(bit_count):
            chosen = site_bits[operate_position]
            flipped = partner(current, "site", operate_position)
            product = jnp.dot(
                masked[chosen], flipped.astype(jnp.bfloat16), preferred_element_type=jnp.float32
            )
            summed = summed + (field[chosen] * flipped + product)
        if iteration == 0:
            vector_new = summed
        else:
            vector_new = 2.0 * summed - previous / scale_prev
        squares, intersection = lax.psum(
            (jnp.sum(vector_new * vector_new), jnp.sum(initial * vector_new)), ("site", "phonon")
        )
        scale_now = jnp.sqrt(squares / entries + epsilon)
        updated = vector_new / scale_now
        moment = intersection / (entries * scale_now)
        moments.append(moment)
        previous = current
        current = updated
        scale_prev = scale_now
    return (current, previous, jnp.stack(moments))


def solution(mesh):
    in_specs = (P("site", "phonon"), P(), P(), P(), P(), P(), P())
    out_specs = (P("site", "phonon"), P("site", "phonon"), P())

    def whole(state, operators, op_mask, *rest):
        rows = state.shape[0] // mesh.shape["site"]
        columns = state.shape[1] // mesh.shape["phonon"]
        plan = Plan(mesh, rows, columns, op_mask.shape[1])
        body = functools.partial(shards, plan) if plan.fits() else halo_shards
        run = jax.shard_map(body, mesh=mesh, in_specs=in_specs, out_specs=out_specs, check_vma=False)
        return run(state, operators, op_mask, *rest)

    return whole
```

```python
import functools

import jax
import jax.numpy as jnp
from jax import lax
from jax.experimental import pallas as pl
from jax.experimental.pallas import tpu as pltpu
from jax.sharding import PartitionSpec as P

LBITS = 10
MODES = 64
STEPS = 3
LANES = 128
SUBLANES = 8
HOME = (32, 32, 32, 32)
SMALL = (32, 32, 64)
AXES = ("site", "phonon")

epsilon = 1e-06


VMEM = pl.BlockSpec(memory_space=pltpu.VMEM)
SMEM = pl.BlockSpec(memory_space=pltpu.SMEM)
HBM = pl.BlockSpec(memory_space=pltpu.HBM)


class Plan:
    def __init__(self, mesh, rows, columns, blocks):
        self.sites = mesh.shape["site"]
        self.phonons = mesh.shape["phonon"]
        self.groups = self.sites * self.phonons
        self.bits = self.sites.bit_length() - 1
        self.rows = rows
        self.columns = columns
        self.blocks = blocks
        self.edge = rows // blocks
        self.levels_here = columns // MODES
        self.level_count = self.levels_here * self.phonons
        self.share = MODES // self.groups
        self.pieces = self.levels_here * self.share
        self.lane_blocks = rows // LANES
        self.body = self.pieces * self.lane_blocks
        self.inward = self.body + 1
        self.outward = 2 * self.body + 1
        self.places = self.pieces * self.groups
        self.width = 2 * LANES
        self.parts = rows // self.width
        self.slabs = self.bits * self.parts
        self.kept = min(5, self.slabs - 1)
        self.entries = float(rows * columns * self.groups)

    def fits(self):
        return (
            MODES % self.groups == 0
            and self.columns == LANES
            and self.rows % self.width == 0
            and self.edge % LANES == 0
            and self.width % self.edge == 0
            and self.bits < SUBLANES
            and self.groups % SUBLANES == 0
        )


def params(mib):
    return pltpu.CompilerParams(vmem_limit_bytes=mib * 2**20)


def lane_sums(values):
    return jnp.sum(values, axis=0, keepdims=True)


def slots_of(widths):
    lane = lax.broadcasted_iota(jnp.int32, (1, LANES), 1)
    starts = [sum(widths[:index]) for index in range(len(widths))]
    return [(width, (lane >= start) & (lane < start + width)) for width, start in zip(widths, starts)]


def put_sums(out_ref, sums, widths, start, stride, count):
    row = jnp.zeros((1, LANES), jnp.float32)
    for value, (width, inside) in zip(sums, slots_of(widths)):
        reach = LANES
        while reach > width:
            reach //= 2
            value = value + pltpu.roll(value, reach, 1)
        row = jnp.where(inside, value, row)
    out_ref[pl.ds(start, count, stride=stride), :] = jnp.broadcast_to(row, (count, LANES))


def total_of(ref, start, stride, count):
    return jnp.sum(lane_sums(ref[pl.ds(start, count, stride=stride), :]), axis=1, keepdims=True)


def totals_of(ref, widths, start, stride, count):
    lanes = lane_sums(ref[pl.ds(start, count, stride=stride), :])
    return [jnp.sum(jnp.where(inside, lanes, 0.0), axis=1, keepdims=True) for _, inside in slots_of(widths)]


def scale_of(plan, squares):
    return jnp.sqrt(squares / plan.entries + epsilon)


def depart_kernel(plan, state_ref, out_ref, held_ref, semaphores):
    half = plan.rows // 2
    fetches = [
        pltpu.make_async_copy(
            state_ref.at[pl.ds(index * half, half), :], held_ref.at[pl.ds(index * half, half), :], semaphores.at[index]
        )
        for index in range(2)
    ]
    for fetch in fetches:
        fetch.start()
    sums = jnp.zeros((1, LANES), jnp.float32)
    for block in range(plan.lane_blocks):
        if block * LANES % half == 0:
            fetches[block * LANES // half].wait()
        tile = held_ref[pl.ds(block * LANES, LANES), :]
        sums = sums + lane_sums(tile * tile)
        turned = tile.T
        for piece in range(plan.pieces):
            out_ref[pl.ds(piece * plan.lane_blocks + block, plan.groups, stride=plan.inward), :] = turned[
                piece * plan.groups : (piece + 1) * plan.groups
            ]
    put_sums(out_ref, [sums], (LANES,), plan.body, plan.inward, plan.groups)


def fetch_slabs(plan, slabs, bits_ref, operators_ref, held_ref, semaphores):
    fetches = []
    for index, slab in enumerate(slabs):
        part, bit = divmod(slab, plan.bits)
        rows = pl.ds(part * plan.width, plan.width)
        fetch = pltpu.make_async_copy(
            operators_ref.at[bits_ref[bit], rows, :], held_ref.at[index], semaphores.at[index]
        )
        fetch.start()
        fetches.append(fetch)
    return fetches


def mask_slab(plan, slab, index, bits_ref, mask_ref, held_ref, out_ref):
    part, bit = divmod(slab, plan.bits)
    chosen = bits_ref[bit]
    for start in range(0, plan.width, plan.edge):
        across = (part * plan.width + start) // plan.edge
        rows = pl.ds(start, plan.edge)
        for along in range(plan.blocks):
            columns = pl.ds(along * plan.edge, plan.edge)
            keep = (mask_ref[chosen, across, along] > 0).astype(jnp.float32).astype(jnp.bfloat16)
            out_ref[index, columns, rows] = (held_ref[index, rows, columns] * keep).T


def store_kernel(plan, bits_ref, mask_ref, operators_ref, stored_ref, held_ref, masked_ref, in_semaphores, out_semaphores):
    slabs = range(plan.kept, plan.slabs)
    fetches = fetch_slabs(plan, slabs, bits_ref, operators_ref, held_ref, in_semaphores)
    stores = []
    for index, slab in enumerate(slabs):
        fetches[index].wait()
        mask_slab(plan, slab, index, bits_ref, mask_ref, held_ref, masked_ref)
        store = pltpu.make_async_copy(masked_ref.at[index], stored_ref.at[index], out_semaphores.at[index])
        store.start()
        stores.append(store)
    for store in stores:
        store.wait()


def prepare_kernel(
    plan,
    bits_ref,
    mask_ref,
    field_ref,
    coupling_ref,
    mode_ref,
    operators_ref,
    place_ref,
    inside_ref,
    kept_ref,
    held_ref,
    semaphores,
):
    slabs = range(plan.kept)
    fetches = fetch_slabs(plan, slabs, bits_ref, operators_ref, held_ref, semaphores)
    me = lax.axis_index("site") * plan.phonons + lax.axis_index("phonon")
    place = lax.broadcasted_iota(jnp.int32, (plan.places, LANES), 0)
    phonon = place % plan.phonons
    site = place // plan.phonons % plan.sites
    mode = place // plan.groups % plan.share
    level = phonon * plan.levels_here + place // (plan.groups * plan.share)
    occupied = jnp.zeros((plan.places, LANES), jnp.float32)
    for position in range(plan.bits):
        held = (site >> position & 1).astype(jnp.float32)
        occupied = occupied + coupling_ref[bits_ref[position]] * held
    strength = jnp.zeros((plan.places, LANES), jnp.float32)
    for index in range(plan.share):
        strength = jnp.where(mode == index, mode_ref[index * plan.groups + me], strength)
    strength = strength / jnp.sqrt(jnp.full((1, LANES), plan.level_count, jnp.float32))
    height = level.astype(jnp.float32)
    place_ref[0] = occupied
    place_ref[1] = strength * jnp.sqrt(height)
    place_ref[2] = jnp.where(level == plan.level_count - 1, 0.0, strength * jnp.sqrt(height + 1.0))
    inside = lax.broadcasted_iota(jnp.int32, (1, plan.rows), 1)
    weight = jnp.zeros((1, plan.rows), jnp.float32)
    for local_bit in range(LBITS):
        weight = weight + coupling_ref[plan.bits + local_bit] * (inside >> local_bit & 1).astype(jnp.float32)
    inside_ref[...] = jnp.zeros_like(inside_ref)
    inside_ref[:1] = weight
    for position in range(plan.bits):
        inside_ref[pl.ds(1 + position, 1)] = jnp.full((1, plan.rows), field_ref[bits_ref[position]])
    for slab in slabs:
        fetches[slab].wait()
        mask_slab(plan, slab, slab, bits_ref, mask_ref, held_ref, kept_ref)


def flipped(values, stride):
    places, width = values.shape
    if stride % SUBLANES == 0:
        shaped = values.reshape(places // (2 * stride), 2, stride, width)
        return jnp.concatenate([shaped[:, 1:], shaped[:, :1]], axis=1).reshape(places, width)
    tiles = values.reshape(places // SUBLANES, SUBLANES, width)
    if 2 * stride == SUBLANES:
        return pltpu.roll(tiles, stride, 1).reshape(places, width)
    spot = lax.broadcasted_iota(jnp.int32, tiles.shape, 1)
    down = pltpu.roll(tiles, stride, 1)
    up = pltpu.roll(tiles, SUBLANES - stride, 1)
    return jnp.where(spot & stride > 0, down, up).reshape(places, width)


def shifted(values, by):
    places, width = values.shape
    tiles = values.reshape(places // SUBLANES, SUBLANES, width)
    return pltpu.roll(tiles, by % SUBLANES, 1).reshape(places, width)


def put_rounded(plan, rounded_ref, vector, start):
    for position in range(plan.bits):
        rounded_ref[:, pl.ds(position * plan.rows + start, vector.shape[1])] = flipped(
            vector, plan.phonons << position
        ).astype(jnp.bfloat16)


def step(plan, vector_ref, rounded_ref, kept_ref, fetched_ref, place_ref, inside_ref, finish, ready=None, begun_ref=None):
    span = plan.places // plan.levels_here

    def local(start):
        lanes = pl.ds(start, LANES)
        vector = vector_ref[:, lanes]
        levels = [vector[index * span : (index + 1) * span] for index in range(plan.levels_here)]
        lower = jnp.concatenate([shifted(levels[-1], 1)] + levels[:-1], axis=0)
        upper = jnp.concatenate(levels[1:] + [shifted(levels[0], -1)], axis=0)
        weight = place_ref[0] + inside_ref[:1, lanes]
        total = weight * (place_ref[1] * lower + place_ref[2] * upper)
        for position in range(plan.bits):
            total = total + inside_ref[pl.ds(1 + position, 1), lanes] * flipped(vector, plan.phonons << position)
        return total

    def added(total, part, late):
        for ref, low, high in ((kept_ref, 0, plan.kept), (fetched_ref, plan.kept, plan.slabs)):
            fetched = low > 0
            begin = max(part * plan.bits, low)
            count = min((part + 1) * plan.bits, high) - begin
            if count <= 0 or late not in (None, fetched):
                continue
            if late:
                for slab in range(begin, begin + count):
                    ready(slab)
            first = begin - part * plan.bits
            masked = ref[pl.ds(begin - low, count)].reshape(count * plan.rows, plan.width)
            operand = rounded_ref[:, pl.ds(first * plan.rows, count * plan.rows)]
            total = total + jnp.dot(operand, masked, preferred_element_type=jnp.float32)
        return total

    def locals_of(lanes):
        return jnp.concatenate([local(start) for start in range(lanes.start, lanes.start + plan.width, LANES)], axis=1)

    parts = [pl.ds(part * plan.width, plan.width) for part in range(plan.parts)]
    if ready is None:
        for part, lanes in enumerate(parts):
            finish(lanes, added(locals_of(lanes), part, None))
        return
    for part, lanes in enumerate(parts):
        begun_ref[:, lanes] = added(locals_of(lanes), part, False)
    for part, lanes in enumerate(parts):
        finish(lanes, added(begun_ref[:, lanes], part, True))


def first_kernel(
    plan,
    arrived_ref,
    place_ref,
    inside_ref,
    kept_ref,
    stored_ref,
    initial_ref,
    new_ref,
    sums_ref,
    fetched_ref,
    rounded_ref,
    ahead_ref,
    semaphores,
):
    fetches = {}
    for slab in range(plan.kept, plan.slabs):
        index = slab - plan.kept
        fetches[slab] = pltpu.make_async_copy(stored_ref.at[index], fetched_ref.at[index], semaphores.at[index])
        fetches[slab].start()

    def ready(slab):
        fetches[slab].wait()

    squares = total_of(arrived_ref, plan.body, plan.inward, plan.groups)
    inverse = 1.0 / scale_of(plan, squares)
    for block in range(plan.lane_blocks):
        parts = [
            arrived_ref[pl.ds(piece * plan.lane_blocks + block, plan.groups, stride=plan.inward), :]
            for piece in range(plan.pieces)
        ]
        vector = jnp.concatenate(parts, axis=0) * inverse
        initial_ref[:, pl.ds(block * LANES, LANES)] = vector
        put_rounded(plan, rounded_ref, vector, block * LANES)
    tables = (kept_ref, fetched_ref, place_ref, inside_ref)
    squares = []
    overlap = []
    ahead = []

    def finish(lanes, new):
        new_ref[:, lanes] = new
        put_rounded(plan, ahead_ref, new, lanes.start)
        squares.append(lane_sums(new * new))
        overlap.append(lane_sums(new * initial_ref[:, lanes]))

    def look_ahead(lanes, total):
        new = 2.0 * total - initial_ref[:, lanes]
        ahead.append(lane_sums(new * new))

    step(plan, initial_ref, rounded_ref, *tables, finish, ready, new_ref)
    step(plan, new_ref, ahead_ref, *tables, look_ahead)
    put_sums(sums_ref, [one_row(squares), one_row(overlap), one_row(ahead)], SMALL, 0, 1, plan.groups)


def one_row(rows):
    total = sum(rows[1:], rows[0])
    return sum(total[:, start : start + LANES] for start in range(0, total.shape[1], LANES))


def onward_kernel(
    plan,
    arrived_ref,
    raw_ref,
    initial_ref,
    place_ref,
    inside_ref,
    kept_ref,
    fetched_ref,
    out_ref,
    known_ref,
    rounded_ref,
    ahead_ref,
    second_ref,
    third_ref,
):
    squares, overlap, ahead = totals_of(arrived_ref, SMALL, 0, 1, plan.groups)
    first = 1.0 / scale_of(plan, squares)
    estimate = scale_of(plan, ahead * first * first)
    second = 1.0 / estimate
    known_ref[:1, :] = jnp.broadcast_to(overlap * first / plan.entries, (1, LANES))
    known_ref[1:, :] = jnp.broadcast_to(estimate, (SUBLANES - 1, LANES))
    for block in range(plan.lane_blocks):
        lanes = pl.ds(block * LANES, LANES)
        vector = raw_ref[:, lanes] * first
        second_ref[:, lanes] = vector
        put_rounded(plan, rounded_ref, vector, block * LANES)
    tables = (kept_ref, fetched_ref, place_ref, inside_ref)
    sums = [[] for _ in HOME]

    def send(vector, lanes, new):
        sums[2 * vector].append(lane_sums(new * new))
        sums[2 * vector + 1].append(lane_sums(new * initial_ref[:, lanes]))
        for start in range(0, plan.width, LANES):
            block = (lanes.start + start) // LANES
            for piece in range(plan.pieces):
                row = vector * plan.body + piece * plan.lane_blocks + block
                out_ref[pl.ds(row, plan.groups, stride=plan.outward), :] = new[
                    piece * plan.groups : (piece + 1) * plan.groups, start : start + LANES
                ]

    def finish_second(lanes, total):
        new = 2.0 * total - initial_ref[:, lanes] * first
        vector = new * second
        third_ref[:, lanes] = vector
        put_rounded(plan, ahead_ref, vector, lanes.start)
        send(0, lanes, new)

    def finish_third(lanes, total):
        send(1, lanes, 2.0 * total - second_ref[:, lanes] * second)

    step(plan, second_ref, rounded_ref, *tables, finish_second)
    step(plan, third_ref, ahead_ref, *tables, finish_third)
    put_sums(out_ref, [one_row(rows) for rows in sums], HOME, 2 * plan.body, plan.outward, plan.groups)


def arrive_kernel(plan, arrived_ref, known_ref, before_ref, last_ref, moments_ref):
    before_squares, before_overlap, last_squares, last_overlap = totals_of(
        arrived_ref, HOME, 2 * plan.body, plan.outward, plan.groups
    )
    before = 1.0 / scale_of(plan, before_squares)
    back = known_ref[1:2, :1] * before
    last = back / scale_of(plan, last_squares * back * back)
    for vector, (out_ref, factor) in enumerate(((before_ref, before), (last_ref, last))):
        for block in range(plan.lane_blocks):
            first = vector * plan.body + block
            parts = [
                arrived_ref[pl.ds(first + piece * plan.lane_blocks, plan.groups, stride=plan.outward), :]
                for piece in range(plan.pieces)
            ]
            out_ref[pl.ds(block * LANES, LANES), :] = jnp.concatenate(parts, axis=0).T * factor
    moments_ref[0] = known_ref[0, 0]
    moments_ref[1] = (before_overlap * before / plan.entries)[0, 0]
    moments_ref[2] = (last_overlap * last / plan.entries)[0, 0]


def exchange(values, count):
    shaped = values.reshape(count, values.shape[0] // count, 1, LANES)
    return lax.all_to_all(shaped, AXES, 0, 0, tiled=True).reshape(values.shape)


def shards(plan, state, operators, op_mask, site_bits, field, site_coupling, mode_coupling):
    f32 = jnp.float32
    inward = jax.ShapeDtypeStruct((plan.groups * plan.inward, LANES), f32)
    outward = jax.ShapeDtypeStruct((plan.groups * plan.outward, LANES), f32)
    vector = jax.ShapeDtypeStruct((plan.places, plan.rows), f32)
    known = jax.ShapeDtypeStruct((SUBLANES, LANES), f32)
    held = jax.ShapeDtypeStruct((plan.rows, plan.columns), f32)
    rounded = pltpu.VMEM((plan.places, plan.bits * plan.rows), jnp.bfloat16)
    working = pltpu.VMEM((plan.places, plan.rows), f32)
    work = 2 * plan.bits * plan.places * plan.rows * plan.rows

    def cost(flops, moved):
        return pl.CostEstimate(flops=flops, bytes_accessed=moved, transcendentals=0)

    departing = pl.pallas_call(
        functools.partial(depart_kernel, plan),
        out_shape=inward,
        in_specs=[HBM],
        out_specs=VMEM,
        scratch_shapes=[pltpu.VMEM((plan.rows, plan.columns), f32), pltpu.SemaphoreType.DMA((2,))],
        compiler_params=params(60),
        name="depart",
    )(state)
    arrived = exchange(departing, plan.groups)
    fetched = plan.slabs - plan.kept
    kept_slabs = (plan.kept, plan.rows, plan.width)
    fetched_slabs = (fetched, plan.rows, plan.width)

    def held_slabs(count):
        return pltpu.VMEM((count, plan.width, plan.rows), jnp.bfloat16)

    place, inside, kept = pl.pallas_call(
        functools.partial(prepare_kernel, plan),
        out_shape=[
            jax.ShapeDtypeStruct((3, plan.places, LANES), f32),
            jax.ShapeDtypeStruct((SUBLANES, plan.rows), f32),
            jax.ShapeDtypeStruct(kept_slabs, jnp.bfloat16),
        ],
        in_specs=[SMEM] * 5 + [HBM],
        out_specs=[VMEM] * 3,
        scratch_shapes=[held_slabs(plan.kept), pltpu.SemaphoreType.DMA((plan.kept,))],
        compiler_params=params(50),
        cost_estimate=cost(plan.rows * plan.rows, 4 * plan.kept * plan.rows * plan.width),
        name="prepare",
    )(site_bits, op_mask, field, site_coupling, mode_coupling, operators)
    stored = pl.pallas_call(
        functools.partial(store_kernel, plan),
        out_shape=jax.ShapeDtypeStruct(fetched_slabs, jnp.bfloat16),
        in_specs=[SMEM] * 2 + [HBM],
        out_specs=HBM,
        scratch_shapes=[
            held_slabs(fetched),
            pltpu.VMEM(fetched_slabs, jnp.bfloat16),
            pltpu.SemaphoreType.DMA((fetched,)),
            pltpu.SemaphoreType.DMA((fetched,)),
        ],
        compiler_params=params(60),
        cost_estimate=cost(plan.rows * plan.rows, 4 * fetched * plan.rows * plan.width),
        name="store",
    )(site_bits, op_mask, operators)
    initial, raw, sums, late = pl.pallas_call(
        functools.partial(first_kernel, plan),
        out_shape=[
            vector,
            vector,
            jax.ShapeDtypeStruct((plan.groups, LANES), f32),
            jax.ShapeDtypeStruct(fetched_slabs, jnp.bfloat16),
        ],
        in_specs=[VMEM] * 4 + [HBM],
        out_specs=[VMEM] * 4,
        scratch_shapes=[rounded, rounded, pltpu.SemaphoreType.DMA((fetched,))],
        compiler_params=params(46),
        cost_estimate=cost(2 * work, 4 * plan.places * plan.rows),
        name="first",
    )(arrived, place, inside, kept, stored)
    tables = (place, inside, kept, late)
    sums = exchange(sums, plan.groups)
    departing, told = pl.pallas_call(
        functools.partial(onward_kernel, plan),
        out_shape=[outward, known],
        in_specs=[VMEM] * 7,
        out_specs=[VMEM] * 2,
        scratch_shapes=[rounded, rounded, working, working],
        compiler_params=params(32),
        cost_estimate=cost(2 * work, 8 * plan.places * plan.rows),
        name="onward",
    )(sums, raw, initial, *tables)
    arrived = exchange(departing, plan.groups)
    before, last, moments = pl.pallas_call(
        functools.partial(arrive_kernel, plan),
        out_shape=[held, held, jax.ShapeDtypeStruct((STEPS,), f32)],
        in_specs=[VMEM] * 2,
        out_specs=[VMEM, VMEM, SMEM],
        compiler_params=params(16),
        name="arrive",
    )(arrived, told)
    return last, before, moments


def extended_2(block, sides, width):
    for axis, dim in sides:
        count = lax.axis_size(axis)
        forward = [(i, i + 1) for i in range(count - 1)]
        backward = [(target, source) for source, target in forward]
        low = lax.ppermute(
            lax.slice_in_dim(block, block.shape[dim] - width, None, axis=dim), axis, forward
        )
        high = lax.ppermute(lax.slice_in_dim(block, 0, width, axis=dim), axis, backward)
        block = jnp.concatenate([low, block, high], axis=dim)
    return block


def partner(value, axis, bit):
    mask = 2**bit
    pairs = [(source, source ^ mask) for source in range(lax.axis_size(axis))]
    return lax.ppermute(value, axis, pairs)


def halo_shards(state, operators, op_mask, site_bits, field, site_coupling, mode_coupling):
    site_count = lax.axis_size("site")
    phonon_count = lax.axis_size("phonon")
    bit_count = site_count.bit_length() - 1
    rows_here = state.shape[0]
    columns_here = state.shape[1]
    levels_here = columns_here // MODES
    block_edge = rows_here // op_mask.shape[1]
    expanded = jnp.repeat(jnp.repeat(op_mask, block_edge, axis=1), block_edge, axis=2)
    masked = jnp.where(expanded > 0, operators, jnp.zeros((), jnp.bfloat16))
    entries = jnp.float32(rows_here * columns_here * site_count * phonon_count)
    level_total = jnp.sqrt(jnp.float32(levels_here * phonon_count))
    device = lax.axis_index("site")
    inside = lax.iota(jnp.int32, rows_here)
    weight_rows = jnp.zeros((rows_here,), jnp.float32)
    for position in range(bit_count):
        weight_rows = weight_rows + site_coupling[site_bits[position]] * (
            device >> position & 1
        ).astype(jnp.float32)
    for local_bit in range(LBITS):
        weight_rows = weight_rows + site_coupling[bit_count + local_bit] * (
            inside >> local_bit & 1
        ).astype(jnp.float32)
    levels = (
        lax.axis_index("phonon") * levels_here + lax.iota(jnp.int32, columns_here) // MODES
    ).astype(jnp.float32)
    lower_weight = jnp.sqrt(levels)
    upper_weight = jnp.sqrt(levels + 1.0)
    mode_weight = jnp.tile(mode_coupling, columns_here // MODES) / level_total
    start_squares = lax.psum(jnp.sum(state * state), ("site", "phonon"))
    initial = state / jnp.sqrt(start_squares / entries + epsilon)
    previous = initial
    current = initial
    scale_prev = jnp.float32(1.0)
    moments = []
    for iteration in range(STEPS):
        extended = extended_2(current, (("phonon", 1),), MODES)
        lower_part = extended[:, :columns_here]
        upper_part = extended[:, 2 * MODES :]
        summed = weight_rows[:, None] * (
            mode_weight * (lower_weight * lower_part + upper_weight * upper_part)
        )
        for operate_position in range(bit_count):
            chosen = site_bits[operate_position]
            flipped = partner(current, "site", operate_position)
            product = jnp.dot(
                masked[chosen], flipped.astype(jnp.bfloat16), preferred_element_type=jnp.float32
            )
            summed = summed + (field[chosen] * flipped + product)
        if iteration == 0:
            vector_new = summed
        else:
            vector_new = 2.0 * summed - previous / scale_prev
        squares, intersection = lax.psum(
            (jnp.sum(vector_new * vector_new), jnp.sum(initial * vector_new)), ("site", "phonon")
        )
        scale_now = jnp.sqrt(squares / entries + epsilon)
        updated = vector_new / scale_now
        moment = intersection / (entries * scale_now)
        moments.append(moment)
        previous = current
        current = updated
        scale_prev = scale_now
    return (current, previous, jnp.stack(moments))


def solution(mesh):
    in_specs = (P("site", "phonon"), P(), P(), P(), P(), P(), P())
    out_specs = (P("site", "phonon"), P("site", "phonon"), P())

    def whole(state, operators, op_mask, *rest):
        rows = state.shape[0] // mesh.shape["site"]
        columns = state.shape[1] // mesh.shape["phonon"]
        plan = Plan(mesh, rows, columns, op_mask.shape[1])
        body = functools.partial(shards, plan) if plan.fits() else halo_shards
        run = jax.shard_map(body, mesh=mesh, in_specs=in_specs, out_specs=out_specs, check_vma=False)
        return run(state, operators, op_mask, *rest)

    return whole
```

```python
import functools

import jax
import jax.numpy as jnp
from jax import lax
from jax.experimental import pallas as pl
from jax.experimental.pallas import tpu as pltpu
from jax.sharding import PartitionSpec as P

LBITS = 10
MODES = 64
STEPS = 3
LANES = 128
SUBLANES = 8
HOME = (32, 32, 32, 32)
SMALL = (32, 32, 64)
AXES = ("site", "phonon")

epsilon = 1e-06


VMEM = pl.BlockSpec(memory_space=pltpu.VMEM)
SMEM = pl.BlockSpec(memory_space=pltpu.SMEM)
HBM = pl.BlockSpec(memory_space=pltpu.HBM)


class Plan:
    def __init__(self, mesh, rows, columns, blocks):
        self.sites = mesh.shape["site"]
        self.phonons = mesh.shape["phonon"]
        self.groups = self.sites * self.phonons
        self.bits = self.sites.bit_length() - 1
        self.rows = rows
        self.columns = columns
        self.blocks = blocks
        self.edge = rows // blocks
        self.levels_here = columns // MODES
        self.level_count = self.levels_here * self.phonons
        self.share = MODES // self.groups
        self.pieces = self.levels_here * self.share
        self.lane_blocks = rows // LANES
        self.body = self.pieces * self.lane_blocks
        self.inward = self.body + 1
        self.outward = 2 * self.body + 1
        self.places = self.pieces * self.groups
        self.width = 2 * LANES
        self.parts = rows // self.width
        self.slabs = self.bits * self.parts
        self.kept = min(5, self.slabs - 1)
        self.entries = float(rows * columns * self.groups)

    def fits(self):
        return (
            MODES % self.groups == 0
            and self.columns == LANES
            and self.rows % self.width == 0
            and self.edge % LANES == 0
            and self.width % self.edge == 0
            and self.bits < SUBLANES
            and self.groups % SUBLANES == 0
        )


def params(mib):
    return pltpu.CompilerParams(vmem_limit_bytes=mib * 2**20)


def lane_sums(values):
    return jnp.sum(values, axis=0, keepdims=True)


def slots_of(widths):
    lane = lax.broadcasted_iota(jnp.int32, (1, LANES), 1)
    starts = [sum(widths[:index]) for index in range(len(widths))]
    return [(width, (lane >= start) & (lane < start + width)) for width, start in zip(widths, starts)]


def put_sums(out_ref, sums, widths, start, stride, count):
    row = jnp.zeros((1, LANES), jnp.float32)
    for value, (width, inside) in zip(sums, slots_of(widths)):
        reach = LANES
        while reach > width:
            reach //= 2
            value = value + pltpu.roll(value, reach, 1)
        row = jnp.where(inside, value, row)
    out_ref[pl.ds(start, count, stride=stride), :] = jnp.broadcast_to(row, (count, LANES))


def total_of(ref, start, stride, count):
    return jnp.sum(lane_sums(ref[pl.ds(start, count, stride=stride), :]), axis=1, keepdims=True)


def totals_of(ref, widths, start, stride, count):
    lanes = lane_sums(ref[pl.ds(start, count, stride=stride), :])
    return [jnp.sum(jnp.where(inside, lanes, 0.0), axis=1, keepdims=True) for _, inside in slots_of(widths)]


def scale_of(plan, squares):
    return jnp.sqrt(squares / plan.entries + epsilon)


def depart_kernel(plan, state_ref, out_ref, held_ref, semaphores):
    half = plan.rows // 2
    fetches = [
        pltpu.make_async_copy(
            state_ref.at[pl.ds(index * half, half), :], held_ref.at[pl.ds(index * half, half), :], semaphores.at[index]
        )
        for index in range(2)
    ]
    for fetch in fetches:
        fetch.start()
    sums = jnp.zeros((1, LANES), jnp.float32)
    for block in range(plan.lane_blocks):
        if block * LANES % half == 0:
            fetches[block * LANES // half].wait()
        tile = held_ref[pl.ds(block * LANES, LANES), :]
        sums = sums + lane_sums(tile * tile)
        turned = tile.T
        for piece in range(plan.pieces):
            out_ref[pl.ds(piece * plan.lane_blocks + block, plan.groups, stride=plan.inward), :] = turned[
                piece * plan.groups : (piece + 1) * plan.groups
            ]
    put_sums(out_ref, [sums], (LANES,), plan.body, plan.inward, plan.groups)


def fetch_slabs(plan, slabs, bits_ref, operators_ref, held_ref, semaphores):
    fetches = []
    for index, slab in enumerate(slabs):
        part, bit = divmod(slab, plan.bits)
        rows = pl.ds(part * plan.width, plan.width)
        fetch = pltpu.make_async_copy(
            operators_ref.at[bits_ref[bit], rows, :], held_ref.at[index], semaphores.at[index]
        )
        fetch.start()
        fetches.append(fetch)
    return fetches


def mask_slab(plan, slab, index, bits_ref, mask_ref, held_ref, out_ref):
    part, bit = divmod(slab, plan.bits)
    chosen = bits_ref[bit]
    for start in range(0, plan.width, plan.edge):
        across = (part * plan.width + start) // plan.edge
        rows = pl.ds(start, plan.edge)
        for along in range(plan.blocks):
            columns = pl.ds(along * plan.edge, plan.edge)
            keep = (mask_ref[chosen, across, along] > 0).astype(jnp.float32).astype(jnp.bfloat16)
            out_ref[index, columns, rows] = (held_ref[index, rows, columns] * keep).T


def store_kernel(plan, bits_ref, mask_ref, operators_ref, stored_ref, held_ref, masked_ref, in_semaphores, out_semaphores):
    slabs = range(plan.kept, plan.slabs)
    fetches = fetch_slabs(plan, slabs, bits_ref, operators_ref, held_ref, in_semaphores)
    stores = []
    for index, slab in enumerate(slabs):
        fetches[index].wait()
        mask_slab(plan, slab, index, bits_ref, mask_ref, held_ref, masked_ref)
        store = pltpu.make_async_copy(masked_ref.at[index], stored_ref.at[index], out_semaphores.at[index])
        store.start()
        stores.append(store)
    for store in stores:
        store.wait()


def prepare_kernel(
    plan,
    bits_ref,
    mask_ref,
    field_ref,
    coupling_ref,
    mode_ref,
    operators_ref,
    place_ref,
    inside_ref,
    kept_ref,
    held_ref,
    semaphores,
):
    slabs = range(plan.kept)
    fetches = fetch_slabs(plan, slabs, bits_ref, operators_ref, held_ref, semaphores)
    me = lax.axis_index("site") * plan.phonons + lax.axis_index("phonon")
    place = lax.broadcasted_iota(jnp.int32, (plan.places, LANES), 0)
    phonon = place % plan.phonons
    site = place // plan.phonons % plan.sites
    mode = place // plan.groups % plan.share
    level = phonon * plan.levels_here + place // (plan.groups * plan.share)
    occupied = jnp.zeros((plan.places, LANES), jnp.float32)
    for position in range(plan.bits):
        held = (site >> position & 1).astype(jnp.float32)
        occupied = occupied + coupling_ref[bits_ref[position]] * held
    strength = jnp.zeros((plan.places, LANES), jnp.float32)
    for index in range(plan.share):
        strength = jnp.where(mode == index, mode_ref[index * plan.groups + me], strength)
    strength = strength / jnp.sqrt(jnp.full((1, LANES), plan.level_count, jnp.float32))
    height = level.astype(jnp.float32)
    place_ref[0] = occupied
    place_ref[1] = strength * jnp.sqrt(height)
    place_ref[2] = jnp.where(level == plan.level_count - 1, 0.0, strength * jnp.sqrt(height + 1.0))
    inside = lax.broadcasted_iota(jnp.int32, (1, plan.rows), 1)
    weight = jnp.zeros((1, plan.rows), jnp.float32)
    for local_bit in range(LBITS):
        weight = weight + coupling_ref[plan.bits + local_bit] * (inside >> local_bit & 1).astype(jnp.float32)
    inside_ref[...] = jnp.zeros_like(inside_ref)
    inside_ref[:1] = weight
    for position in range(plan.bits):
        inside_ref[pl.ds(1 + position, 1)] = jnp.full((1, plan.rows), field_ref[bits_ref[position]])
    for slab in slabs:
        fetches[slab].wait()
        mask_slab(plan, slab, slab, bits_ref, mask_ref, held_ref, kept_ref)


def flipped(values, stride):
    places, width = values.shape
    if stride % SUBLANES == 0:
        shaped = values.reshape(places // (2 * stride), 2, stride, width)
        return jnp.concatenate([shaped[:, 1:], shaped[:, :1]], axis=1).reshape(places, width)
    tiles = values.reshape(places // SUBLANES, SUBLANES, width)
    if 2 * stride == SUBLANES:
        return pltpu.roll(tiles, stride, 1).reshape(places, width)
    spot = lax.broadcasted_iota(jnp.int32, tiles.shape, 1)
    down = pltpu.roll(tiles, stride, 1)
    up = pltpu.roll(tiles, SUBLANES - stride, 1)
    return jnp.where(spot & stride > 0, down, up).reshape(places, width)


def shifted(values, by):
    places, width = values.shape
    tiles = values.reshape(places // SUBLANES, SUBLANES, width)
    return pltpu.roll(tiles, by % SUBLANES, 1).reshape(places, width)


def put_rounded(plan, rounded_ref, vector, start):
    for position in range(plan.bits):
        rounded_ref[:, pl.ds(position * plan.rows + start, vector.shape[1])] = flipped(
            vector, plan.phonons << position
        ).astype(jnp.bfloat16)


def step(plan, vector_ref, rounded_ref, kept_ref, fetched_ref, place_ref, inside_ref, finish, ready=None, begun_ref=None, factor=None):
    span = plan.places // plan.levels_here

    def local(start):
        lanes = pl.ds(start, LANES)
        vector = vector_ref[:, lanes]
        levels = [vector[index * span : (index + 1) * span] for index in range(plan.levels_here)]
        lower = jnp.concatenate([shifted(levels[-1], 1)] + levels[:-1], axis=0)
        upper = jnp.concatenate(levels[1:] + [shifted(levels[0], -1)], axis=0)
        weight = place_ref[0] + inside_ref[:1, lanes]
        total = weight * (place_ref[1] * lower + place_ref[2] * upper)
        for position in range(plan.bits):
            total = total + inside_ref[pl.ds(1 + position, 1), lanes] * flipped(vector, plan.phonons << position)
        return total if factor is None else total * factor

    def added(total, part, late):
        for ref, low, high in ((kept_ref, 0, plan.kept), (fetched_ref, plan.kept, plan.slabs)):
            fetched = low > 0
            begin = max(part * plan.bits, low)
            count = min((part + 1) * plan.bits, high) - begin
            if count <= 0 or late not in (None, fetched):
                continue
            if late:
                for slab in range(begin, begin + count):
                    ready(slab)
            first = begin - part * plan.bits
            masked = ref[pl.ds(begin - low, count)].reshape(count * plan.rows, plan.width)
            operand = rounded_ref[:, pl.ds(first * plan.rows, count * plan.rows)]
            total = total + jnp.dot(operand, masked, preferred_element_type=jnp.float32)
        return total

    def locals_of(lanes):
        return jnp.concatenate([local(start) for start in range(lanes.start, lanes.start + plan.width, LANES)], axis=1)

    parts = [pl.ds(part * plan.width, plan.width) for part in range(plan.parts)]
    if ready is None:
        for part, lanes in enumerate(parts):
            finish(lanes, added(locals_of(lanes), part, None))
        return
    for part, lanes in enumerate(parts):
        begun_ref[:, lanes] = added(locals_of(lanes), part, False)
    for part, lanes in enumerate(parts):
        finish(lanes, added(begun_ref[:, lanes], part, True))


def first_kernel(
    plan,
    arrived_ref,
    place_ref,
    inside_ref,
    kept_ref,
    stored_ref,
    initial_ref,
    new_ref,
    sums_ref,
    fetched_ref,
    rounded_ref,
    ahead_ref,
    semaphores,
):
    fetches = {}
    for slab in range(plan.kept, plan.slabs):
        index = slab - plan.kept
        fetches[slab] = pltpu.make_async_copy(stored_ref.at[index], fetched_ref.at[index], semaphores.at[index])
        fetches[slab].start()

    def ready(slab):
        fetches[slab].wait()

    squares = total_of(arrived_ref, plan.body, plan.inward, plan.groups)
    inverse = 1.0 / scale_of(plan, squares)
    for block in range(plan.lane_blocks):
        parts = [
            arrived_ref[pl.ds(piece * plan.lane_blocks + block, plan.groups, stride=plan.inward), :]
            for piece in range(plan.pieces)
        ]
        vector = jnp.concatenate(parts, axis=0) * inverse
        initial_ref[:, pl.ds(block * LANES, LANES)] = vector
        put_rounded(plan, rounded_ref, vector, block * LANES)
    tables = (kept_ref, fetched_ref, place_ref, inside_ref)
    squares = []
    overlap = []
    ahead = []

    def finish(lanes, new):
        new_ref[:, lanes] = new
        put_rounded(plan, ahead_ref, new, lanes.start)
        squares.append(lane_sums(new * new))
        overlap.append(lane_sums(new * initial_ref[:, lanes]))

    def look_ahead(lanes, total):
        new = 2.0 * total - initial_ref[:, lanes]
        ahead.append(lane_sums(new * new))

    step(plan, initial_ref, rounded_ref, *tables, finish, ready, new_ref)
    step(plan, new_ref, ahead_ref, *tables, look_ahead)
    put_sums(sums_ref, [one_row(squares), one_row(overlap), one_row(ahead)], SMALL, 0, 1, plan.groups)


def one_row(rows):
    total = sum(rows[1:], rows[0])
    return sum(total[:, start : start + LANES] for start in range(0, total.shape[1], LANES))


def onward_kernel(
    plan,
    arrived_ref,
    raw_ref,
    initial_ref,
    place_ref,
    inside_ref,
    kept_ref,
    fetched_ref,
    out_ref,
    known_ref,
    rounded_ref,
    ahead_ref,
    third_ref,
):
    squares, overlap, ahead = totals_of(arrived_ref, SMALL, 0, 1, plan.groups)
    first = 1.0 / scale_of(plan, squares)
    estimate = scale_of(plan, ahead * first * first)
    second = 1.0 / estimate
    both = first * second
    known_ref[:1, :] = jnp.broadcast_to(overlap * first / plan.entries, (1, LANES))
    known_ref[1:, :] = jnp.broadcast_to(estimate, (SUBLANES - 1, LANES))
    for block in range(plan.lane_blocks):
        lanes = pl.ds(block * LANES, LANES)
        put_rounded(plan, rounded_ref, raw_ref[:, lanes] * first, block * LANES)
    tables = (kept_ref, fetched_ref, place_ref, inside_ref)
    sums = [[] for _ in HOME]

    def send(vector, lanes, new):
        sums[2 * vector].append(lane_sums(new * new))
        sums[2 * vector + 1].append(lane_sums(new * initial_ref[:, lanes]))
        for start in range(0, plan.width, LANES):
            block = (lanes.start + start) // LANES
            for piece in range(plan.pieces):
                row = vector * plan.body + piece * plan.lane_blocks + block
                out_ref[pl.ds(row, plan.groups, stride=plan.outward), :] = new[
                    piece * plan.groups : (piece + 1) * plan.groups, start : start + LANES
                ]

    def finish_second(lanes, total):
        new = 2.0 * total - initial_ref[:, lanes] * first
        vector = new * second
        third_ref[:, lanes] = vector
        put_rounded(plan, ahead_ref, vector, lanes.start)
        send(0, lanes, new)

    def finish_third(lanes, total):
        send(1, lanes, 2.0 * total - raw_ref[:, lanes] * both)

    step(plan, raw_ref, rounded_ref, *tables, finish_second, factor=first)
    step(plan, third_ref, ahead_ref, *tables, finish_third)
    put_sums(out_ref, [one_row(rows) for rows in sums], HOME, 2 * plan.body, plan.outward, plan.groups)


def arrive_kernel(plan, arrived_ref, known_ref, before_ref, last_ref, moments_ref):
    before_squares, before_overlap, last_squares, last_overlap = totals_of(
        arrived_ref, HOME, 2 * plan.body, plan.outward, plan.groups
    )
    before = 1.0 / scale_of(plan, before_squares)
    back = known_ref[1:2, :1] * before
    last = back / scale_of(plan, last_squares * back * back)
    for vector, (out_ref, factor) in enumerate(((before_ref, before), (last_ref, last))):
        for block in range(plan.lane_blocks):
            first = vector * plan.body + block
            parts = [
                arrived_ref[pl.ds(first + piece * plan.lane_blocks, plan.groups, stride=plan.outward), :]
                for piece in range(plan.pieces)
            ]
            out_ref[pl.ds(block * LANES, LANES), :] = jnp.concatenate(parts, axis=0).T * factor
    moments_ref[0] = known_ref[0, 0]
    moments_ref[1] = (before_overlap * before / plan.entries)[0, 0]
    moments_ref[2] = (last_overlap * last / plan.entries)[0, 0]


def exchange(values, count):
    shaped = values.reshape(count, values.shape[0] // count, 1, LANES)
    return lax.all_to_all(shaped, AXES, 0, 0, tiled=True).reshape(values.shape)


def shards(plan, state, operators, op_mask, site_bits, field, site_coupling, mode_coupling):
    f32 = jnp.float32
    inward = jax.ShapeDtypeStruct((plan.groups * plan.inward, LANES), f32)
    outward = jax.ShapeDtypeStruct((plan.groups * plan.outward, LANES), f32)
    vector = jax.ShapeDtypeStruct((plan.places, plan.rows), f32)
    known = jax.ShapeDtypeStruct((SUBLANES, LANES), f32)
    held = jax.ShapeDtypeStruct((plan.rows, plan.columns), f32)
    rounded = pltpu.VMEM((plan.places, plan.bits * plan.rows), jnp.bfloat16)
    working = pltpu.VMEM((plan.places, plan.rows), f32)
    work = 2 * plan.bits * plan.places * plan.rows * plan.rows

    def cost(flops, moved):
        return pl.CostEstimate(flops=flops, bytes_accessed=moved, transcendentals=0)

    departing = pl.pallas_call(
        functools.partial(depart_kernel, plan),
        out_shape=inward,
        in_specs=[HBM],
        out_specs=VMEM,
        scratch_shapes=[pltpu.VMEM((plan.rows, plan.columns), f32), pltpu.SemaphoreType.DMA((2,))],
        compiler_params=params(60),
        name="depart",
    )(state)
    arrived = exchange(departing, plan.groups)
    fetched = plan.slabs - plan.kept
    kept_slabs = (plan.kept, plan.rows, plan.width)
    fetched_slabs = (fetched, plan.rows, plan.width)

    def held_slabs(count):
        return pltpu.VMEM((count, plan.width, plan.rows), jnp.bfloat16)

    place, inside, kept = pl.pallas_call(
        functools.partial(prepare_kernel, plan),
        out_shape=[
            jax.ShapeDtypeStruct((3, plan.places, LANES), f32),
            jax.ShapeDtypeStruct((SUBLANES, plan.rows), f32),
            jax.ShapeDtypeStruct(kept_slabs, jnp.bfloat16),
        ],
        in_specs=[SMEM] * 5 + [HBM],
        out_specs=[VMEM] * 3,
        scratch_shapes=[held_slabs(plan.kept), pltpu.SemaphoreType.DMA((plan.kept,))],
        compiler_params=params(50),
        cost_estimate=cost(plan.rows * plan.rows, 4 * plan.kept * plan.rows * plan.width),
        name="prepare",
    )(site_bits, op_mask, field, site_coupling, mode_coupling, operators)
    stored = pl.pallas_call(
        functools.partial(store_kernel, plan),
        out_shape=jax.ShapeDtypeStruct(fetched_slabs, jnp.bfloat16),
        in_specs=[SMEM] * 2 + [HBM],
        out_specs=HBM,
        scratch_shapes=[
            held_slabs(fetched),
            pltpu.VMEM(fetched_slabs, jnp.bfloat16),
            pltpu.SemaphoreType.DMA((fetched,)),
            pltpu.SemaphoreType.DMA((fetched,)),
        ],
        compiler_params=params(60),
        cost_estimate=cost(plan.rows * plan.rows, 4 * fetched * plan.rows * plan.width),
        name="store",
    )(site_bits, op_mask, operators)
    initial, raw, sums, late = pl.pallas_call(
        functools.partial(first_kernel, plan),
        out_shape=[
            vector,
            vector,
            jax.ShapeDtypeStruct((plan.groups, LANES), f32),
            jax.ShapeDtypeStruct(fetched_slabs, jnp.bfloat16),
        ],
        in_specs=[VMEM] * 4 + [HBM],
        out_specs=[VMEM] * 4,
        scratch_shapes=[rounded, rounded, pltpu.SemaphoreType.DMA((fetched,))],
        compiler_params=params(46),
        cost_estimate=cost(2 * work, 4 * plan.places * plan.rows),
        name="first",
    )(arrived, place, inside, kept, stored)
    tables = (place, inside, kept, late)
    sums = exchange(sums, plan.groups)
    departing, told = pl.pallas_call(
        functools.partial(onward_kernel, plan),
        out_shape=[outward, known],
        in_specs=[VMEM] * 7,
        out_specs=[VMEM] * 2,
        scratch_shapes=[rounded, rounded, working],
        compiler_params=params(32),
        cost_estimate=cost(2 * work, 8 * plan.places * plan.rows),
        name="onward",
    )(sums, raw, initial, *tables)
    arrived = exchange(departing, plan.groups)
    before, last, moments = pl.pallas_call(
        functools.partial(arrive_kernel, plan),
        out_shape=[held, held, jax.ShapeDtypeStruct((STEPS,), f32)],
        in_specs=[VMEM] * 2,
        out_specs=[VMEM, VMEM, SMEM],
        compiler_params=params(16),
        name="arrive",
    )(arrived, told)
    return last, before, moments


def extended_2(block, sides, width):
    for axis, dim in sides:
        count = lax.axis_size(axis)
        forward = [(i, i + 1) for i in range(count - 1)]
        backward = [(target, source) for source, target in forward]
        low = lax.ppermute(
            lax.slice_in_dim(block, block.shape[dim] - width, None, axis=dim), axis, forward
        )
        high = lax.ppermute(lax.slice_in_dim(block, 0, width, axis=dim), axis, backward)
        block = jnp.concatenate([low, block, high], axis=dim)
    return block


def partner(value, axis, bit):
    mask = 2**bit
    pairs = [(source, source ^ mask) for source in range(lax.axis_size(axis))]
    return lax.ppermute(value, axis, pairs)


def halo_shards(state, operators, op_mask, site_bits, field, site_coupling, mode_coupling):
    site_count = lax.axis_size("site")
    phonon_count = lax.axis_size("phonon")
    bit_count = site_count.bit_length() - 1
    rows_here = state.shape[0]
    columns_here = state.shape[1]
    levels_here = columns_here // MODES
    block_edge = rows_here // op_mask.shape[1]
    expanded = jnp.repeat(jnp.repeat(op_mask, block_edge, axis=1), block_edge, axis=2)
    masked = jnp.where(expanded > 0, operators, jnp.zeros((), jnp.bfloat16))
    entries = jnp.float32(rows_here * columns_here * site_count * phonon_count)
    level_total = jnp.sqrt(jnp.float32(levels_here * phonon_count))
    device = lax.axis_index("site")
    inside = lax.iota(jnp.int32, rows_here)
    weight_rows = jnp.zeros((rows_here,), jnp.float32)
    for position in range(bit_count):
        weight_rows = weight_rows + site_coupling[site_bits[position]] * (
            device >> position & 1
        ).astype(jnp.float32)
    for local_bit in range(LBITS):
        weight_rows = weight_rows + site_coupling[bit_count + local_bit] * (
            inside >> local_bit & 1
        ).astype(jnp.float32)
    levels = (
        lax.axis_index("phonon") * levels_here + lax.iota(jnp.int32, columns_here) // MODES
    ).astype(jnp.float32)
    lower_weight = jnp.sqrt(levels)
    upper_weight = jnp.sqrt(levels + 1.0)
    mode_weight = jnp.tile(mode_coupling, columns_here // MODES) / level_total
    start_squares = lax.psum(jnp.sum(state * state), ("site", "phonon"))
    initial = state / jnp.sqrt(start_squares / entries + epsilon)
    previous = initial
    current = initial
    scale_prev = jnp.float32(1.0)
    moments = []
    for iteration in range(STEPS):
        extended = extended_2(current, (("phonon", 1),), MODES)
        lower_part = extended[:, :columns_here]
        upper_part = extended[:, 2 * MODES :]
        summed = weight_rows[:, None] * (
            mode_weight * (lower_weight * lower_part + upper_weight * upper_part)
        )
        for operate_position in range(bit_count):
            chosen = site_bits[operate_position]
            flipped = partner(current, "site", operate_position)
            product = jnp.dot(
                masked[chosen], flipped.astype(jnp.bfloat16), preferred_element_type=jnp.float32
            )
            summed = summed + (field[chosen] * flipped + product)
        if iteration == 0:
            vector_new = summed
        else:
            vector_new = 2.0 * summed - previous / scale_prev
        squares, intersection = lax.psum(
            (jnp.sum(vector_new * vector_new), jnp.sum(initial * vector_new)), ("site", "phonon")
        )
        scale_now = jnp.sqrt(squares / entries + epsilon)
        updated = vector_new / scale_now
        moment = intersection / (entries * scale_now)
        moments.append(moment)
        previous = current
        current = updated
        scale_prev = scale_now
    return (current, previous, jnp.stack(moments))


def solution(mesh):
    in_specs = (P("site", "phonon"), P(), P(), P(), P(), P(), P())
    out_specs = (P("site", "phonon"), P("site", "phonon"), P())

    def whole(state, operators, op_mask, *rest):
        rows = state.shape[0] // mesh.shape["site"]
        columns = state.shape[1] // mesh.shape["phonon"]
        plan = Plan(mesh, rows, columns, op_mask.shape[1])
        body = functools.partial(shards, plan) if plan.fits() else halo_shards
        run = jax.shard_map(body, mesh=mesh, in_specs=in_specs, out_specs=out_specs, check_vma=False)
        return run(state, operators, op_mask, *rest)

    return whole
```

```python
import functools

import jax
import jax.numpy as jnp
from jax import lax
from jax.experimental import pallas as pl
from jax.experimental.pallas import tpu as pltpu
from jax.sharding import PartitionSpec as P

LBITS = 10
MODES = 64
STEPS = 3
LANES = 128
SUBLANES = 8
SLOTS = 4
SMALL = 3
AXES = ("site", "phonon")

epsilon = 1e-06


VMEM = pl.BlockSpec(memory_space=pltpu.VMEM)
SMEM = pl.BlockSpec(memory_space=pltpu.SMEM)
HBM = pl.BlockSpec(memory_space=pltpu.HBM)


class Plan:
    def __init__(self, mesh, rows, columns, blocks):
        self.sites = mesh.shape["site"]
        self.phonons = mesh.shape["phonon"]
        self.groups = self.sites * self.phonons
        self.bits = self.sites.bit_length() - 1
        self.rows = rows
        self.columns = columns
        self.blocks = blocks
        self.edge = rows // blocks
        self.levels_here = columns // MODES
        self.level_count = self.levels_here * self.phonons
        self.share = MODES // self.groups
        self.pieces = self.levels_here * self.share
        self.lane_blocks = rows // LANES
        self.body = self.pieces * self.lane_blocks
        self.inward = self.body + 1
        self.outward = 2 * self.body + 1
        self.places = self.pieces * self.groups
        self.width = 2 * LANES
        self.parts = rows // self.width
        self.slabs = self.bits * self.parts
        self.kept = min(5, self.slabs - 1)
        self.entries = float(rows * columns * self.groups)

    def fits(self):
        return (
            MODES % self.groups == 0
            and self.columns == LANES
            and self.rows % self.width == 0
            and self.edge % LANES == 0
            and self.width % self.edge == 0
            and self.bits < SUBLANES
            and self.groups % SUBLANES == 0
        )


def params(mib):
    return pltpu.CompilerParams(vmem_limit_bytes=mib * 2**20)


def lane_sums(values):
    return jnp.sum(values, axis=0, keepdims=True)


def put_sums(out_ref, sums, start, stride, count):
    lane = lax.broadcasted_iota(jnp.int32, (1, LANES), 1)
    row = jnp.zeros((1, LANES), jnp.float32)
    for slot, value in enumerate(sums):
        width = LANES
        while width > LANES // SLOTS:
            width //= 2
            value = value + pltpu.roll(value, width, 1)
        row = jnp.where(lane // (LANES // SLOTS) == slot, value, row)
    out_ref[pl.ds(start, count, stride=stride), :] = jnp.broadcast_to(row, (count, LANES))


def put_rows(out_ref, sums, start, stride, count):
    for index, value in enumerate(sums):
        out_ref[pl.ds(start + index, count, stride=stride), :] = jnp.broadcast_to(value, (count, LANES))


def total_of(ref, start, stride, count):
    return jnp.sum(lane_sums(ref[pl.ds(start, count, stride=stride), :]), axis=1, keepdims=True)


def totals_of(ref, start, stride, count):
    lanes = lane_sums(ref[pl.ds(start, count, stride=stride), :])
    lane = lax.broadcasted_iota(jnp.int32, (1, LANES), 1)
    return [
        jnp.sum(jnp.where(lane // (LANES // SLOTS) == slot, lanes, 0.0), axis=1, keepdims=True)
        for slot in range(SLOTS)
    ]


def scale_of(plan, squares):
    return jnp.sqrt(squares / plan.entries + epsilon)


def depart_kernel(plan, state_ref, out_ref, held_ref, semaphores):
    half = plan.rows // 2
    fetches = [
        pltpu.make_async_copy(
            state_ref.at[pl.ds(index * half, half), :], held_ref.at[pl.ds(index * half, half), :], semaphores.at[index]
        )
        for index in range(2)
    ]
    for fetch in fetches:
        fetch.start()
    sums = jnp.zeros((1, LANES), jnp.float32)
    for block in range(plan.lane_blocks):
        if block * LANES % half == 0:
            fetches[block * LANES // half].wait()
        tile = held_ref[pl.ds(block * LANES, LANES), :]
        sums = sums + lane_sums(tile * tile)
        turned = tile.T
        for piece in range(plan.pieces):
            out_ref[pl.ds(piece * plan.lane_blocks + block, plan.groups, stride=plan.inward), :] = turned[
                piece * plan.groups : (piece + 1) * plan.groups
            ]
    put_rows(out_ref, [sums], plan.body, plan.inward, plan.groups)


def fetch_slabs(plan, slabs, bits_ref, operators_ref, held_ref, semaphores):
    fetches = []
    for index, slab in enumerate(slabs):
        part, bit = divmod(slab, plan.bits)
        rows = pl.ds(part * plan.width, plan.width)
        fetch = pltpu.make_async_copy(
            operators_ref.at[bits_ref[bit], rows, :], held_ref.at[index], semaphores.at[index]
        )
        fetch.start()
        fetches.append(fetch)
    return fetches


def mask_slab(plan, slab, index, bits_ref, mask_ref, held_ref, out_ref):
    part, bit = divmod(slab, plan.bits)
    chosen = bits_ref[bit]
    for start in range(0, plan.width, plan.edge):
        across = (part * plan.width + start) // plan.edge
        rows = pl.ds(start, plan.edge)
        for along in range(plan.blocks):
            columns = pl.ds(along * plan.edge, plan.edge)
            keep = (mask_ref[chosen, across, along] > 0).astype(jnp.float32).astype(jnp.bfloat16)
            out_ref[index, columns, rows] = (held_ref[index, rows, columns] * keep).T


def store_kernel(plan, bits_ref, mask_ref, operators_ref, stored_ref, held_ref, masked_ref, in_semaphores, out_semaphores):
    slabs = range(plan.kept, plan.slabs)
    fetches = fetch_slabs(plan, slabs, bits_ref, operators_ref, held_ref, in_semaphores)
    stores = []
    for index, slab in enumerate(slabs):
        fetches[index].wait()
        mask_slab(plan, slab, index, bits_ref, mask_ref, held_ref, masked_ref)
        store = pltpu.make_async_copy(masked_ref.at[index], stored_ref.at[index], out_semaphores.at[index])
        store.start()
        stores.append(store)
    for store in stores:
        store.wait()


def prepare_kernel(
    plan,
    bits_ref,
    mask_ref,
    field_ref,
    coupling_ref,
    mode_ref,
    operators_ref,
    place_ref,
    inside_ref,
    kept_ref,
    held_ref,
    semaphores,
):
    slabs = range(plan.kept)
    fetches = fetch_slabs(plan, slabs, bits_ref, operators_ref, held_ref, semaphores)
    me = lax.axis_index("site") * plan.phonons + lax.axis_index("phonon")
    place = lax.broadcasted_iota(jnp.int32, (plan.places, LANES), 0)
    phonon = place % plan.phonons
    site = place // plan.phonons % plan.sites
    mode = place // plan.groups % plan.share
    level = phonon * plan.levels_here + place // (plan.groups * plan.share)
    occupied = jnp.zeros((plan.places, LANES), jnp.float32)
    for position in range(plan.bits):
        held = (site >> position & 1).astype(jnp.float32)
        occupied = occupied + coupling_ref[bits_ref[position]] * held
    strength = jnp.zeros((plan.places, LANES), jnp.float32)
    for index in range(plan.share):
        strength = jnp.where(mode == index, mode_ref[index * plan.groups + me], strength)
    strength = strength / jnp.sqrt(jnp.full((1, LANES), plan.level_count, jnp.float32))
    height = level.astype(jnp.float32)
    place_ref[0] = occupied
    place_ref[1] = strength * jnp.sqrt(height)
    place_ref[2] = jnp.where(level == plan.level_count - 1, 0.0, strength * jnp.sqrt(height + 1.0))
    inside = lax.broadcasted_iota(jnp.int32, (1, plan.rows), 1)
    weight = jnp.zeros((1, plan.rows), jnp.float32)
    for local_bit in range(LBITS):
        weight = weight + coupling_ref[plan.bits + local_bit] * (inside >> local_bit & 1).astype(jnp.float32)
    inside_ref[...] = jnp.zeros_like(inside_ref)
    inside_ref[:1] = weight
    for position in range(plan.bits):
        inside_ref[pl.ds(1 + position, 1)] = jnp.full((1, plan.rows), field_ref[bits_ref[position]])
    for slab in slabs:
        fetches[slab].wait()
        mask_slab(plan, slab, slab, bits_ref, mask_ref, held_ref, kept_ref)


def flipped(values, stride):
    places, width = values.shape
    if stride % SUBLANES == 0:
        shaped = values.reshape(places // (2 * stride), 2, stride, width)
        return jnp.concatenate([shaped[:, 1:], shaped[:, :1]], axis=1).reshape(places, width)
    tiles = values.reshape(places // SUBLANES, SUBLANES, width)
    if 2 * stride == SUBLANES:
        return pltpu.roll(tiles, stride, 1).reshape(places, width)
    spot = lax.broadcasted_iota(jnp.int32, tiles.shape, 1)
    down = pltpu.roll(tiles, stride, 1)
    up = pltpu.roll(tiles, SUBLANES - stride, 1)
    return jnp.where(spot & stride > 0, down, up).reshape(places, width)


def shifted(values, by):
    places, width = values.shape
    tiles = values.reshape(places // SUBLANES, SUBLANES, width)
    return pltpu.roll(tiles, by % SUBLANES, 1).reshape(places, width)


def put_rounded(plan, rounded_ref, vector, start):
    for position in range(plan.bits):
        rounded_ref[:, pl.ds(position * plan.rows + start, vector.shape[1])] = flipped(
            vector, plan.phonons << position
        ).astype(jnp.bfloat16)


def step(plan, vector_ref, rounded_ref, kept_ref, fetched_ref, place_ref, inside_ref, finish, ready=None, begun_ref=None, factor=None):
    span = plan.places // plan.levels_here

    def local(start):
        lanes = pl.ds(start, LANES)
        vector = vector_ref[:, lanes]
        levels = [vector[index * span : (index + 1) * span] for index in range(plan.levels_here)]
        lower = jnp.concatenate([shifted(levels[-1], 1)] + levels[:-1], axis=0)
        upper = jnp.concatenate(levels[1:] + [shifted(levels[0], -1)], axis=0)
        weight = place_ref[0] + inside_ref[:1, lanes]
        total = weight * (place_ref[1] * lower + place_ref[2] * upper)
        for position in range(plan.bits):
            total = total + inside_ref[pl.ds(1 + position, 1), lanes] * flipped(vector, plan.phonons << position)
        return total if factor is None else total * factor

    def added(total, part, late):
        for ref, low, high in ((kept_ref, 0, plan.kept), (fetched_ref, plan.kept, plan.slabs)):
            fetched = low > 0
            begin = max(part * plan.bits, low)
            count = min((part + 1) * plan.bits, high) - begin
            if count <= 0 or late not in (None, fetched):
                continue
            if late:
                for slab in range(begin, begin + count):
                    ready(slab)
            first = begin - part * plan.bits
            masked = ref[pl.ds(begin - low, count)].reshape(count * plan.rows, plan.width)
            operand = rounded_ref[:, pl.ds(first * plan.rows, count * plan.rows)]
            total = total + jnp.dot(operand, masked, preferred_element_type=jnp.float32)
        return total

    def locals_of(lanes):
        return jnp.concatenate([local(start) for start in range(lanes.start, lanes.start + plan.width, LANES)], axis=1)

    parts = [pl.ds(part * plan.width, plan.width) for part in range(plan.parts)]
    if ready is None:
        for part, lanes in enumerate(parts):
            finish(lanes, added(locals_of(lanes), part, None))
        return
    for part, lanes in enumerate(parts):
        begun_ref[:, lanes] = added(locals_of(lanes), part, False)
    for part, lanes in enumerate(parts):
        finish(lanes, added(begun_ref[:, lanes], part, True))


def first_kernel(
    plan,
    arrived_ref,
    place_ref,
    inside_ref,
    kept_ref,
    stored_ref,
    initial_ref,
    new_ref,
    sums_ref,
    fetched_ref,
    rounded_ref,
    ahead_ref,
    semaphores,
):
    fetches = {}
    for slab in range(plan.kept, plan.slabs):
        index = slab - plan.kept
        fetches[slab] = pltpu.make_async_copy(stored_ref.at[index], fetched_ref.at[index], semaphores.at[index])
        fetches[slab].start()

    def ready(slab):
        fetches[slab].wait()

    squares = total_of(arrived_ref, plan.body, plan.inward, plan.groups)
    inverse = 1.0 / scale_of(plan, squares)
    for block in range(plan.lane_blocks):
        parts = [
            arrived_ref[pl.ds(piece * plan.lane_blocks + block, plan.groups, stride=plan.inward), :]
            for piece in range(plan.pieces)
        ]
        vector = jnp.concatenate(parts, axis=0) * inverse
        initial_ref[:, pl.ds(block * LANES, LANES)] = vector
        put_rounded(plan, rounded_ref, vector, block * LANES)
    tables = (kept_ref, fetched_ref, place_ref, inside_ref)
    squares = []
    overlap = []
    ahead = []

    def finish(lanes, new):
        new_ref[:, lanes] = new
        put_rounded(plan, ahead_ref, new, lanes.start)
        squares.append(lane_sums(new * new))
        overlap.append(lane_sums(new * initial_ref[:, lanes]))

    def look_ahead(lanes, total):
        new = 2.0 * total - initial_ref[:, lanes]
        ahead.append(lane_sums(new * new))

    step(plan, initial_ref, rounded_ref, *tables, finish, ready, new_ref)
    step(plan, new_ref, ahead_ref, *tables, look_ahead)
    put_rows(sums_ref, [one_row(squares), one_row(overlap), one_row(ahead)], 0, SMALL, plan.groups)


def one_row(rows):
    total = sum(rows[1:], rows[0])
    return sum(total[:, start : start + LANES] for start in range(0, total.shape[1], LANES))


def onward_kernel(
    plan,
    arrived_ref,
    raw_ref,
    initial_ref,
    place_ref,
    inside_ref,
    kept_ref,
    fetched_ref,
    out_ref,
    known_ref,
    rounded_ref,
    ahead_ref,
    third_ref,
):
    squares, overlap, ahead = [total_of(arrived_ref, row, SMALL, plan.groups) for row in range(SMALL)]
    first = 1.0 / scale_of(plan, squares)
    estimate = scale_of(plan, ahead * first * first)
    second = 1.0 / estimate
    both = first * second
    known_ref[:1, :] = jnp.broadcast_to(overlap * first / plan.entries, (1, LANES))
    known_ref[1:, :] = jnp.broadcast_to(estimate, (SUBLANES - 1, LANES))
    for block in range(plan.lane_blocks):
        lanes = pl.ds(block * LANES, LANES)
        put_rounded(plan, rounded_ref, raw_ref[:, lanes] * first, block * LANES)
    tables = (kept_ref, fetched_ref, place_ref, inside_ref)
    sums = [[] for _ in range(SLOTS)]

    def send(vector, lanes, new):
        sums[2 * vector].append(lane_sums(new * new))
        sums[2 * vector + 1].append(lane_sums(new * initial_ref[:, lanes]))
        for start in range(0, plan.width, LANES):
            block = (lanes.start + start) // LANES
            for piece in range(plan.pieces):
                row = vector * plan.body + piece * plan.lane_blocks + block
                out_ref[pl.ds(row, plan.groups, stride=plan.outward), :] = new[
                    piece * plan.groups : (piece + 1) * plan.groups, start : start + LANES
                ]

    def finish_second(lanes, total):
        new = 2.0 * total - initial_ref[:, lanes] * first
        vector = new * second
        third_ref[:, lanes] = vector
        put_rounded(plan, ahead_ref, vector, lanes.start)
        send(0, lanes, new)

    def finish_third(lanes, total):
        send(1, lanes, 2.0 * total - raw_ref[:, lanes] * both)

    step(plan, raw_ref, rounded_ref, *tables, finish_second, factor=first)
    step(plan, third_ref, ahead_ref, *tables, finish_third)
    put_sums(out_ref, [one_row(rows) for rows in sums], 2 * plan.body, plan.outward, plan.groups)


def arrive_kernel(plan, arrived_ref, known_ref, before_ref, last_ref, moments_ref):
    before_squares, before_overlap, last_squares, last_overlap = totals_of(
        arrived_ref, 2 * plan.body, plan.outward, plan.groups
    )
    before = 1.0 / scale_of(plan, before_squares)
    back = known_ref[1:2, :1] * before
    last = back / scale_of(plan, last_squares * back * back)
    for vector, (out_ref, factor) in enumerate(((before_ref, before), (last_ref, last))):
        for block in range(plan.lane_blocks):
            first = vector * plan.body + block
            parts = [
                arrived_ref[pl.ds(first + piece * plan.lane_blocks, plan.groups, stride=plan.outward), :]
                for piece in range(plan.pieces)
            ]
            out_ref[pl.ds(block * LANES, LANES), :] = jnp.concatenate(parts, axis=0).T * factor
    moments_ref[0] = known_ref[0, 0]
    moments_ref[1] = (before_overlap * before / plan.entries)[0, 0]
    moments_ref[2] = (last_overlap * last / plan.entries)[0, 0]


def exchange(values, count):
    shaped = values.reshape(count, values.shape[0] // count, 1, LANES)
    return lax.all_to_all(shaped, AXES, 0, 0, tiled=True).reshape(values.shape)


def shards(plan, state, operators, op_mask, site_bits, field, site_coupling, mode_coupling):
    f32 = jnp.float32
    inward = jax.ShapeDtypeStruct((plan.groups * plan.inward, LANES), f32)
    outward = jax.ShapeDtypeStruct((plan.groups * plan.outward, LANES), f32)
    vector = jax.ShapeDtypeStruct((plan.places, plan.rows), f32)
    known = jax.ShapeDtypeStruct((SUBLANES, LANES), f32)
    held = jax.ShapeDtypeStruct((plan.rows, plan.columns), f32)
    rounded = pltpu.VMEM((plan.places, plan.bits * plan.rows), jnp.bfloat16)
    working = pltpu.VMEM((plan.places, plan.rows), f32)
    work = 2 * plan.bits * plan.places * plan.rows * plan.rows

    def cost(flops, moved):
        return pl.CostEstimate(flops=flops, bytes_accessed=moved, transcendentals=0)

    departing = pl.pallas_call(
        functools.partial(depart_kernel, plan),
        out_shape=inward,
        in_specs=[HBM],
        out_specs=VMEM,
        scratch_shapes=[pltpu.VMEM((plan.rows, plan.columns), f32), pltpu.SemaphoreType.DMA((2,))],
        compiler_params=params(60),
        name="depart",
    )(state)
    arrived = exchange(departing, plan.groups)
    fetched = plan.slabs - plan.kept
    kept_slabs = (plan.kept, plan.rows, plan.width)
    fetched_slabs = (fetched, plan.rows, plan.width)

    def held_slabs(count):
        return pltpu.VMEM((count, plan.width, plan.rows), jnp.bfloat16)

    place, inside, kept = pl.pallas_call(
        functools.partial(prepare_kernel, plan),
        out_shape=[
            jax.ShapeDtypeStruct((3, plan.places, LANES), f32),
            jax.ShapeDtypeStruct((SUBLANES, plan.rows), f32),
            jax.ShapeDtypeStruct(kept_slabs, jnp.bfloat16),
        ],
        in_specs=[SMEM] * 5 + [HBM],
        out_specs=[VMEM] * 3,
        scratch_shapes=[held_slabs(plan.kept), pltpu.SemaphoreType.DMA((plan.kept,))],
        compiler_params=params(50),
        cost_estimate=cost(plan.rows * plan.rows, 4 * plan.kept * plan.rows * plan.width),
        name="prepare",
    )(site_bits, op_mask, field, site_coupling, mode_coupling, operators)
    stored = pl.pallas_call(
        functools.partial(store_kernel, plan),
        out_shape=jax.ShapeDtypeStruct(fetched_slabs, jnp.bfloat16),
        in_specs=[SMEM] * 2 + [HBM],
        out_specs=HBM,
        scratch_shapes=[
            held_slabs(fetched),
            pltpu.VMEM(fetched_slabs, jnp.bfloat16),
            pltpu.SemaphoreType.DMA((fetched,)),
            pltpu.SemaphoreType.DMA((fetched,)),
        ],
        compiler_params=params(60),
        cost_estimate=cost(plan.rows * plan.rows, 4 * fetched * plan.rows * plan.width),
        name="store",
    )(site_bits, op_mask, operators)
    initial, raw, sums, late = pl.pallas_call(
        functools.partial(first_kernel, plan),
        out_shape=[
            vector,
            vector,
            jax.ShapeDtypeStruct((plan.groups * SMALL, LANES), f32),
            jax.ShapeDtypeStruct(fetched_slabs, jnp.bfloat16),
        ],
        in_specs=[VMEM] * 4 + [HBM],
        out_specs=[VMEM] * 4,
        scratch_shapes=[rounded, rounded, pltpu.SemaphoreType.DMA((fetched,))],
        compiler_params=params(46),
        cost_estimate=cost(2 * work, 4 * plan.places * plan.rows),
        name="first",
    )(arrived, place, inside, kept, stored)
    tables = (place, inside, kept, late)
    sums = exchange(sums, plan.groups)
    departing, told = pl.pallas_call(
        functools.partial(onward_kernel, plan),
        out_shape=[outward, known],
        in_specs=[VMEM] * 7,
        out_specs=[VMEM] * 2,
        scratch_shapes=[rounded, rounded, working],
        compiler_params=params(32),
        cost_estimate=cost(2 * work, 8 * plan.places * plan.rows),
        name="onward",
    )(sums, raw, initial, *tables)
    arrived = exchange(departing, plan.groups)
    before, last, moments = pl.pallas_call(
        functools.partial(arrive_kernel, plan),
        out_shape=[held, held, jax.ShapeDtypeStruct((STEPS,), f32)],
        in_specs=[VMEM] * 2,
        out_specs=[VMEM, VMEM, SMEM],
        compiler_params=params(16),
        name="arrive",
    )(arrived, told)
    return last, before, moments


def extended_2(block, sides, width):
    for axis, dim in sides:
        count = lax.axis_size(axis)
        forward = [(i, i + 1) for i in range(count - 1)]
        backward = [(target, source) for source, target in forward]
        low = lax.ppermute(
            lax.slice_in_dim(block, block.shape[dim] - width, None, axis=dim), axis, forward
        )
        high = lax.ppermute(lax.slice_in_dim(block, 0, width, axis=dim), axis, backward)
        block = jnp.concatenate([low, block, high], axis=dim)
    return block


def partner(value, axis, bit):
    mask = 2**bit
    pairs = [(source, source ^ mask) for source in range(lax.axis_size(axis))]
    return lax.ppermute(value, axis, pairs)


def halo_shards(state, operators, op_mask, site_bits, field, site_coupling, mode_coupling):
    site_count = lax.axis_size("site")
    phonon_count = lax.axis_size("phonon")
    bit_count = site_count.bit_length() - 1
    rows_here = state.shape[0]
    columns_here = state.shape[1]
    levels_here = columns_here // MODES
    block_edge = rows_here // op_mask.shape[1]
    expanded = jnp.repeat(jnp.repeat(op_mask, block_edge, axis=1), block_edge, axis=2)
    masked = jnp.where(expanded > 0, operators, jnp.zeros((), jnp.bfloat16))
    entries = jnp.float32(rows_here * columns_here * site_count * phonon_count)
    level_total = jnp.sqrt(jnp.float32(levels_here * phonon_count))
    device = lax.axis_index("site")
    inside = lax.iota(jnp.int32, rows_here)
    weight_rows = jnp.zeros((rows_here,), jnp.float32)
    for position in range(bit_count):
        weight_rows = weight_rows + site_coupling[site_bits[position]] * (
            device >> position & 1
        ).astype(jnp.float32)
    for local_bit in range(LBITS):
        weight_rows = weight_rows + site_coupling[bit_count + local_bit] * (
            inside >> local_bit & 1
        ).astype(jnp.float32)
    levels = (
        lax.axis_index("phonon") * levels_here + lax.iota(jnp.int32, columns_here) // MODES
    ).astype(jnp.float32)
    lower_weight = jnp.sqrt(levels)
    upper_weight = jnp.sqrt(levels + 1.0)
    mode_weight = jnp.tile(mode_coupling, columns_here // MODES) / level_total
    start_squares = lax.psum(jnp.sum(state * state), ("site", "phonon"))
    initial = state / jnp.sqrt(start_squares / entries + epsilon)
    previous = initial
    current = initial
    scale_prev = jnp.float32(1.0)
    moments = []
    for iteration in range(STEPS):
        extended = extended_2(current, (("phonon", 1),), MODES)
        lower_part = extended[:, :columns_here]
        upper_part = extended[:, 2 * MODES :]
        summed = weight_rows[:, None] * (
            mode_weight * (lower_weight * lower_part + upper_weight * upper_part)
        )
        for operate_position in range(bit_count):
            chosen = site_bits[operate_position]
            flipped = partner(current, "site", operate_position)
            product = jnp.dot(
                masked[chosen], flipped.astype(jnp.bfloat16), preferred_element_type=jnp.float32
            )
            summed = summed + (field[chosen] * flipped + product)
        if iteration == 0:
            vector_new = summed
        else:
            vector_new = 2.0 * summed - previous / scale_prev
        squares, intersection = lax.psum(
            (jnp.sum(vector_new * vector_new), jnp.sum(initial * vector_new)), ("site", "phonon")
        )
        scale_now = jnp.sqrt(squares / entries + epsilon)
        updated = vector_new / scale_now
        moment = intersection / (entries * scale_now)
        moments.append(moment)
        previous = current
        current = updated
        scale_prev = scale_now
    return (current, previous, jnp.stack(moments))


def solution(mesh):
    in_specs = (P("site", "phonon"), P(), P(), P(), P(), P(), P())
    out_specs = (P("site", "phonon"), P("site", "phonon"), P())

    def whole(state, operators, op_mask, *rest):
        rows = state.shape[0] // mesh.shape["site"]
        columns = state.shape[1] // mesh.shape["phonon"]
        plan = Plan(mesh, rows, columns, op_mask.shape[1])
        body = functools.partial(shards, plan) if plan.fits() else halo_shards
        run = jax.shard_map(body, mesh=mesh, in_specs=in_specs, out_specs=out_specs, check_vma=False)
        return run(state, operators, op_mask, *rest)

    return whole
```
